32 devices in a mesh: pix: 8 (over z, y), plane: 4 (over x, core).
Axes of the slice: x: 2, y: 2, z: 4, core: 2. Of those that a mesh axis runs over, the one named last changes fastest.
Arguments:
- movie: bfloat16 [4, 256, 256, 256], P('plane', 'pix'), may hold values from -6 to 6
- footprints: bfloat16 [4, 1024, 1024], P('plane', 'pix'), may hold values from 0 to 0.019897461
- traces: bfloat16 [4, 1024, 256], P('plane', 'pix'), may hold values from 0 to 2
- stripe: int32 [4, 1024, 1], P('plane', 'pix'), may hold values from 0 to 7; in each aligned block of 128 rows (0 to 127, 128 to 255, ..., all dimensions but the last counted through in order) at most 32 rows name the same one
- column: int32 [4, 1024], P('plane', 'pix'), may hold values from 0 to 224
- annulus_gain: float32 [4, 256], P('plane'), may hold values from 1 to 8
- decay_slow: float32 [4, 1024], P('plane', 'pix'), may hold values from 0.4 to 0.9
- decay_fast: float32 [4, 1024], P('plane', 'pix'), may hold values from 0.05 to 0.3
Outputs:
- background: bfloat16 [4, 256, 256, 256], P('plane', 'pix')
- traces_new: float32 [4, 1024, 256], P('plane', 'pix')
The draws below stay inside these ranges and needn't reach their ends.
Inputs may be any that keep to these rules, and one draw needn't show every extreme that they name: Among the 128 neurons of one device (aligned blocks of 128 neurons of a plane), no stripe is named more than 32 times, and some device names one stripe exactly 32 times.
All inputs are finite; a program needn't handle non-finite values.
Results may differ from the reference program's by a relative error of at most 0.001.
The reference program's roundings to bfloat16 on the way count: a program that leaves them out, or rounds other values in their place, can miss the bound.
Values may be sent and summed in bfloat16 or wider, within the bound.
No kernel may reach another device: no remote copies, remote signals or barrier semaphores. Data moves between devices by JAX's collectives and lax.ppermute only.
A program may use at most 128 MiB of HBM per device.

```python
import math
import jax
import jax.numpy as jnp
import numpy as np
from jax import lax

FOOT = 32
RAD = 12
GR = 3
COLS = 256
FRAMES = 256
NEUR_DEV = 128
PLANES = 4
HEIGHT = 256
NEUR = 1024
CAP = 32
N_PIX = 8


def touch_ends(drawn, stream_key, smallest, largest):
    shape = drawn.shape
    spot = [jax.random.randint(jax.random.fold_in(stream_key, axis), (), 0, shape[axis]) for axis in range(len(shape))]
    drawn = drawn.at[tuple(spot)].set(smallest)
    longest = shape.index(max(shape))
    spot[longest] = (spot[longest] + 1) % shape[longest]
    return drawn.at[tuple(spot)].set(largest)


def levels(key, extent, shards, low, top_value):
    loudness, own = 1.0, jax.random.fold_in(key, 6)
    for position, parts in shards:
        draws = jnp.exp(jax.random.uniform(jax.random.fold_in(own, position), (parts,), jnp.float32, low / len(shards), top_value / len(shards)))
        loudness = loudness * jnp.repeat(draws, extent[position] // parts).reshape([-1 if axis == position else 1 for axis in range(len(extent))])
    return loudness


def deal_out(key, own, number, rows, amount, top, most, skew):
    ranking = jax.random.permutation(key, amount)
    packed, ordinary = load_shares(amount, rows * top, most, skew, True), load_shares(amount, rows * top, most, skew, False)
    places = jnp.arange(amount)

    def named(tallies, turn):
        used = int((tallies > 0).sum())
        fixed = max(1, used // 4)
        moved = fixed + (places - fixed + turn * (used - fixed)) % max(1, amount - fixed)
        return jnp.zeros((amount,), jnp.int32).at[ranking[jnp.where(places < fixed, places, moved)]].set(jnp.asarray(tallies, jnp.int32))

    tallies = jnp.where(number % 4 == 0, named(packed, number // 4), named(ordinary, number - number // 4 - 1))
    mixed = jax.random.permutation(jax.random.fold_in(own, 3), amount)
    donor, sink = mixed[0:amount // 2 * 2:2], mixed[1:amount // 2 * 2:2]
    room = jnp.minimum(tallies[donor] - 1, most - tallies[sink]) // 2
    room = jnp.where((donor == ranking[0]) | (sink == ranking[0]) | (tallies[sink] == 0), 0, jnp.maximum(room, 0))
    moved = jax.random.randint(jax.random.fold_in(own, 4), (amount // 2,), 0, 1 << 20) % (room + 1)
    tallies = tallies.at[donor].add(-moved).at[sink].add(moved)
    members = jnp.searchsorted(jnp.cumsum(tallies), jnp.arange(rows * top), side="right").astype(jnp.int32)
    listing = members.reshape(top, rows).T
    listing = listing[jax.random.permutation(jax.random.fold_in(own, 1), rows)]
    turn = jax.random.randint(jax.random.fold_in(own, 2), (rows, 1), 0, top)
    return jnp.take_along_axis(listing, (jnp.arange(top)[None, :] + turn) % top, axis=1)


def load_shares(amount, total, reach, skew, full):
    loads = [(1 << 20) // math.isqrt(rank ** skew) + 1 for rank in range(1, amount + 1)]
    largest = reach if full else min(reach, max(-(-total // amount), total * loads[0] // sum(loads)))
    least = 1 if total - largest >= amount - 1 else 0
    holding, rest = [largest] + [least] * (amount - 1), total - largest - least * (amount - 1)
    while rest > 0:
        candidates = [i for i in range(1, amount) if holding[i] < largest] or [i for i in range(1, amount) if holding[i] < reach]
        whole, left = sum([loads[i] for i in candidates]), rest
        for i in candidates:
            more = min(reach - holding[i], max(1, left * loads[i] // whole), rest)
            holding[i] = holding[i] + more
            rest = rest - more
    return np.array(holding)


def normal_values(rng, shape, width, most, cuts=(), dtype=jnp.bfloat16):
    result = jax.random.normal(rng, shape, jnp.float32) * width
    if len(cuts) > 0:
        result = levels(rng, shape, cuts, -0.22, 0.18) * result
    return jnp.clip(result, min=-most, max=most).astype(dtype)


def setup_inputs(seed: int = 0) -> dict:
    seeds = jax.random.split(jax.random.key(seed), 9)
    movie = normal_values(seeds[0], (PLANES, HEIGHT, COLS, FRAMES), 1.0, 6.0, ((0, 4), (1, 8)))
    footprints = jnp.clip(0.019897461 * jax.random.uniform(seeds[1], (PLANES, NEUR, FOOT * FOOT), jnp.float32) ** levels(seeds[1], (PLANES, NEUR, FOOT * FOOT), ((0, 4), (1, 8)), -0.2, 0.2), 0.0, 0.019897461).astype(jnp.bfloat16)
    traces = jnp.clip(2.0 * jax.random.uniform(seeds[2], (PLANES, NEUR, FRAMES), jnp.float32) ** levels(seeds[2], (PLANES, NEUR, FRAMES), ((0, 4), (1, 8)), -0.2, 0.2), 0.0, 2.0).astype(jnp.bfloat16)
    stripe_keys = jax.random.split(jax.random.fold_in(seeds[3], 1), PLANES * NEUR // NEUR_DEV)
    stripe_turns = jax.random.permutation(jax.random.fold_in(seeds[3], 3), PLANES * NEUR // NEUR_DEV)
    stripe = jax.vmap(lambda own, number: deal_out(jax.random.fold_in(seeds[3], 2), own, number, NEUR_DEV, N_PIX, 1, CAP, 2))(stripe_keys, stripe_turns).reshape((PLANES, NEUR, 1))
    column = touch_ends(jax.random.randint(seeds[4], (PLANES, NEUR), 0, COLS - FOOT + 1), jax.random.fold_in(seeds[4], 1), 0, COLS - FOOT).astype(jnp.int32)
    annulus_gain = jnp.clip(jnp.exp(math.log(8.0) - 2.0794415 * jax.random.uniform(seeds[5], (PLANES, COLS), jnp.float32) ** levels(seeds[5], (PLANES, COLS), ((0, 4),), -0.2, 0.2)), 1.0, 8.0)
    decay_slow = jnp.clip(jnp.exp(math.log(0.9) - 0.8109302 * jax.random.uniform(seeds[6], (PLANES, NEUR), jnp.float32) ** levels(seeds[6], (PLANES, NEUR), ((0, 4), (1, 8)), -0.2, 0.2)), 0.4, 0.9)
    decay_fast = jnp.clip(jnp.exp(math.log(0.3) - 1.7917595 * jax.random.uniform(seeds[7], (PLANES, NEUR), jnp.float32) ** levels(seeds[7], (PLANES, NEUR), ((0, 4), (1, 8)), -0.2, 0.2)), 0.05, 0.3)
    return dict(movie=movie, footprints=footprints, traces=traces, stripe=stripe, column=column, annulus_gain=annulus_gain, decay_slow=decay_slow, decay_fast=decay_fast)


lam_floor = 0.1
noise_eps = 1e-05
norm_eps = 1e-05
sigma_twice = 4.5

def kernel_taps(radius):
    offsets = jnp.arange(-radius, radius + 1).astype(jnp.float32)
    shape_raw = jnp.exp(-offsets * offsets / sigma_twice)
    return (shape_raw / jnp.sum(shape_raw)).astype(jnp.bfloat16)

def deconvolve(updated, decay_slow, decay_fast):
    lag_one = jnp.pad(updated, ((0, 0), (1, 0)))[:, :-1]
    lag_two = jnp.pad(updated, ((0, 0), (2, 0)))[:, :-2]
    driven = updated - (decay_slow + decay_fast)[:, None] * lag_one + (decay_slow * decay_fast)[:, None] * lag_two
    return jnp.maximum(driven - lam_floor, 0.0)

def reconvolve(spikes, decay_slow, decay_fast):
    frame_count = spikes.shape[1]
    frame_index = jnp.arange(frame_count)
    frame_lag = frame_index[:, None] - frame_index[None, :]
    exponent = (jnp.maximum(frame_lag, 0) + 1).astype(jnp.float32)
    kernel_rise = jnp.exp(exponent[None] * jnp.log(decay_slow)[:, None, None]) - jnp.exp(exponent[None] * jnp.log(decay_fast)[:, None, None])
    kernel_scale = (1.0 - decay_slow) * (1.0 - decay_fast) / (decay_slow - decay_fast)
    kernel = jnp.where(frame_lag[None] >= 0, kernel_rise * kernel_scale[:, None, None], 0.0)
    return jnp.einsum('ntk,nk->nt', kernel, spikes, precision=lax.Precision.HIGHEST)

def box_sum(field_values, half_width, along_axis):
    length_along = field_values.shape[along_axis]
    pad_spec = [(0, 0)] * field_values.ndim
    pad_spec[along_axis] = (half_width + 1, half_width)
    running = jnp.cumsum(jnp.pad(field_values, pad_spec), axis=along_axis)
    upper_part = lax.slice_in_dim(running, 2 * half_width + 1, 2 * half_width + 1 + length_along, axis=along_axis)
    lower_part = lax.slice_in_dim(running, 0, length_along, axis=along_axis)
    return upper_part - lower_part

def blur_along(field_values, weights, along_axis):
    length_along = field_values.shape[along_axis]
    pad_spec = [(0, 0)] * field_values.ndim
    pad_spec[along_axis] = (GR, GR)
    padded_values = jnp.pad(field_values, pad_spec)
    running_total = jnp.zeros_like(field_values)
    for offset in range(2 * GR + 1):
        running_total = running_total + weights[offset] * lax.slice_in_dim(padded_values, offset, offset + length_along, axis=along_axis)
    return running_total

def reference(movie, footprints, traces, stripe, column, annulus_gain, decay_slow, decay_fast):
    height = movie.shape[1]
    col_count = movie.shape[2]
    frame_count = movie.shape[3]
    weights = kernel_taps(GR).astype(jnp.float32)
    backgrounds = []
    detrended_list = []
    noise_list = []
    for plane_index in range(PLANES):

        def add_tile(model_image, item_parts):
            tile_values, trace_values, stripe_value, column_value = item_parts
            patch = tile_values.astype(jnp.float32).reshape(FOOT, FOOT)[:, :, None] * trace_values.astype(jnp.float32)[None, None, :]
            start = ((stripe_value * FOOT).astype(jnp.int32), column_value.astype(jnp.int32), jnp.int32(0))
            current = lax.dynamic_slice(model_image, start, (FOOT, FOOT, frame_count))
            return (lax.dynamic_update_slice(model_image, current + patch, start), None)
        model_image, _ = lax.scan(add_tile, jnp.zeros((height, col_count, frame_count), jnp.float32), (footprints[plane_index], traces[plane_index], stripe[plane_index, :, 0], column[plane_index]))
        residual = (movie[plane_index].astype(jnp.float32) - model_image).astype(jnp.bfloat16)
        residual_f = residual.astype(jnp.float32)
        row_level = box_sum(residual_f, RAD, 1)
        level_pad = jnp.pad(row_level, ((RAD, RAD), (0, 0), (0, 0)))
        annulus_total = level_pad[0:height] + level_pad[2 * RAD:2 * RAD + height]
        upright = box_sum(residual_f, RAD - 1, 0)
        side_pad = jnp.pad(upright, ((0, 0), (RAD, RAD), (0, 0)))
        annulus_total = annulus_total + side_pad[:, 0:col_count] + side_pad[:, 2 * RAD:2 * RAD + col_count]
        annulus_fit = annulus_gain[plane_index][None, :, None] * annulus_total / (8.0 * RAD)
        backgrounds.append(annulus_fit.astype(jnp.bfloat16))
        detrended_list.append((residual_f - annulus_fit).astype(jnp.bfloat16))
        frame_step = residual_f[:, :, 1:] - residual_f[:, :, :-1]
        noise_list.append(lax.optimization_barrier(jnp.sum(frame_step * frame_step, axis=2)) / (frame_count - 1))
    traces_out = []
    for plane_index in range(PLANES):
        pooled = 2.0 * noise_list[plane_index]
        if plane_index > 0:
            pooled = pooled + noise_list[plane_index - 1]
        if plane_index + 1 < PLANES:
            pooled = pooled + noise_list[plane_index + 1]
        pooled = pooled / 4.0
        blurred = blur_along(detrended_list[plane_index].astype(jnp.float32), weights, 1)
        smoothed = blur_along(blurred, weights, 0)
        normalized = (smoothed / jnp.sqrt(pooled + noise_eps)[:, :, None]).astype(jnp.bfloat16)

        def project(item_parts):
            tile_values, stripe_value, column_value = item_parts
            start = ((stripe_value * FOOT).astype(jnp.int32), column_value.astype(jnp.int32), jnp.int32(0))
            window = lax.dynamic_slice(normalized, start, (FOOT, FOOT, frame_count))
            return jnp.einsum('yx,yxt->t', tile_values.reshape(FOOT, FOOT).astype(jnp.float32), window.astype(jnp.float32), precision=lax.Precision.HIGHEST)
        gradient = lax.map(project, (footprints[plane_index], stripe[plane_index, :, 0], column[plane_index]))
        foot_f = footprints[plane_index].astype(jnp.float32)
        step_size = 1.0 / (lax.optimization_barrier(jnp.sum(foot_f * foot_f, axis=1)) + norm_eps)
        updated = traces[plane_index].astype(jnp.float32) + step_size[:, None] * gradient
        spikes = deconvolve(updated, decay_slow[plane_index], decay_fast[plane_index])

        def convolve_block(item_parts):
            return reconvolve(item_parts[0], item_parts[1], item_parts[2])
        blocked = lax.map(convolve_block, (spikes.reshape(N_PIX, NEUR_DEV, frame_count), decay_slow[plane_index].reshape(N_PIX, NEUR_DEV), decay_fast[plane_index].reshape(N_PIX, NEUR_DEV)))
        traces_out.append(blocked.reshape(NEUR, frame_count))
    return (jnp.stack(backgrounds), jnp.stack(traces_out))
```

```python
import functools

import jax
import jax.numpy as jnp
import ml_dtypes
import numpy as np
from jax import lax
from jax.experimental import pallas as pl
from jax.experimental.pallas import tpu as pltpu
from jax.sharding import PartitionSpec as P

FOOT = 32
RAD = 12
GR = 3
LANES = 128
PER = LANES // FOOT

lam_floor = 0.1
noise_eps = 1e-05
norm_eps = 1e-05
sigma_twice = 4.5

F32 = jnp.float32
BF16 = jnp.bfloat16
MIB = 1 << 20


def tap_values():
    offsets = np.arange(-GR, GR + 1).astype(np.float32)
    raw = np.exp(-offsets * offsets / np.float32(sigma_twice)).astype(np.float32)
    return (raw / raw.sum(dtype=np.float32)).astype(ml_dtypes.bfloat16).astype(np.float32)


def params(mib, **more):
    return pltpu.CompilerParams(vmem_limit_bytes=mib * MIB, **more)


def dot(a, b):
    return jnp.dot(a, b, preferred_element_type=F32)


def outbox_kernel(capacity, stripe_col, stripe_row, column, foot, traces, main, halo, step):
    count = stripe_row.shape[1]
    slots = main.shape[0]
    before = lax.broadcasted_iota(jnp.int32, (count, count), 0) < lax.broadcasted_iota(
        jnp.int32, (count, count), 1
    )
    same = (stripe_col[...] == stripe_row[...]) & before
    rank = jnp.sum(jnp.where(same, 1.0, 0.0), axis=0, keepdims=True).astype(jnp.int32)
    slot = stripe_row[...] * capacity + rank
    place = lax.broadcasted_iota(jnp.int32, (slots, count), 0)

    def onehot(shift):
        return jnp.where(place + shift == slot, 1.0, 0.0).astype(BF16)

    col = jnp.broadcast_to(column[...].astype(F32), (count, LANES)).astype(BF16)
    tiles = foot.shape[1]
    frames = traces.shape[1]
    edge = RAD * FOOT
    here, after, ahead = onehot(0), onehot(capacity), onehot(-capacity)
    main[:, 0:tiles] = dot(here, foot[...]).astype(BF16)
    main[:, tiles : tiles + frames] = dot(here, traces[...]).astype(BF16)
    main[:, tiles + frames :] = dot(here, col).astype(BF16)
    half = frames + edge + LANES
    for base, hot, first in ((0, after, 0), (half, ahead, tiles - edge)):
        halo[:, base : base + frames] = dot(hot, traces[...]).astype(BF16)
        halo[:, base + frames : base + frames + edge] = dot(
            hot, foot[:, first : first + edge]
        ).astype(BF16)
        halo[:, base + frames + edge : base + half] = dot(hot, col).astype(BF16)
    foot_f = foot[...].astype(F32)
    total = jnp.sum(foot_f * foot_f, axis=1, keepdims=True)
    step[...] = jnp.broadcast_to(1.0 / (total + norm_eps), step.shape)


def make_outbox(stripe, column, foot, traces, capacity, slots):
    count, tiles = foot.shape
    frames = traces.shape[1]
    edge = RAD * FOOT
    return pl.pallas_call(
        functools.partial(outbox_kernel, capacity),
        out_shape=(
            jax.ShapeDtypeStruct((slots, tiles + frames + LANES), BF16),
            jax.ShapeDtypeStruct((slots, 2 * (frames + edge + LANES)), BF16),
            jax.ShapeDtypeStruct((count, LANES), F32),
        ),
        compiler_params=params(16),
        cost_estimate=pl.CostEstimate(
            flops=2 * slots * count * 3000, bytes_accessed=2 * MIB, transcendentals=0
        ),
        name="outbox",
    )(stripe.reshape(count, 1), stripe.reshape(1, count), column.reshape(count, 1), foot, traces)


def spread(block, col):
    lane = lax.broadcasted_iota(jnp.int32, block.shape, 1)
    low = lane < FOOT
    high = (lane >= 2 * FOOT) & (lane < 3 * FOOT)
    pairs = [
        jnp.where(low, block, 0.0) + jnp.where(high, pltpu.roll(block, FOOT, 1), 0.0),
        jnp.where(low, pltpu.roll(block, 2 * FOOT, 1), 0.0)
        + jnp.where(high, pltpu.roll(block, 3 * FOOT, 1), 0.0),
    ]
    bits = [((col >> k) & 1) == 1 for k in range(7)]
    right = col >= LANES
    straight = lane >= ((col >> 5) & 3) * FOOT
    in_left = straight & ~right
    in_right = (straight & right) | (~straight & ~right)
    rows = []
    for pair in pairs:
        for k in range(5):
            pair = jnp.where(bits[k], pltpu.roll(pair, 1 << k, 1), pair)
        for moved in (pair, pltpu.roll(pair, 2 * FOOT, 1)):
            moved = jnp.where(lane < 2 * FOOT, moved, 0.0)
            for k in (5, 6):
                moved = jnp.where(bits[k], pltpu.roll(moved, 1 << k, 1), moved)
            rows.append(
                jnp.concatenate(
                    [jnp.where(in_left, moved, 0.0), jnp.where(in_right, moved, 0.0)], axis=1
                ).astype(BF16)
            )
    return rows


def model_row(row, traces):
    return lax.dot_general(row, traces, (((0,), (0,)), ((), ())), preferred_element_type=F32)


def residual_kernel(tile, traces, col, movie, foot_rows, residual, noise):
    rows = spread(tile[...].astype(F32), col[...].astype(F32).astype(jnp.int32))
    frames = movie.shape[-1]
    lane = lax.broadcasted_iota(jnp.int32, movie.shape[1:], 1)
    for q, row in enumerate(rows):
        foot_rows[q] = row
        left = (movie[q].astype(F32) - model_row(row, traces[...])).astype(BF16)
        residual[q] = left
        left = left.astype(F32)
        change = jnp.where(lane < frames - 1, pltpu.roll(left, frames - 1, 1) - left, 0.0)
        change = change * change
        part = change[:, 0:LANES]
        for k in range(1, frames // LANES):
            part = part + change[:, k * LANES : (k + 1) * LANES]
        noise[q : q + 1, :] = jnp.sum(part.T, axis=0, keepdims=True) / (frames - 1)


def make_residual(inbox, movie):
    slots = inbox.shape[0]
    rows, cols, frames = movie.shape[1:]
    trace_block = FOOT * FOOT // frames
    col_block = (FOOT * FOOT + frames) // LANES
    groups = rows // PER
    foot_rows, residual, noise = pl.pallas_call(
        residual_kernel,
        grid=(groups,),
        in_specs=[
            pl.BlockSpec((slots, LANES), lambda g: (0, g)),
            pl.BlockSpec((slots, frames), lambda g: (0, trace_block)),
            pl.BlockSpec((slots, LANES), lambda g: (0, col_block)),
            pl.BlockSpec((None, PER, cols, frames), lambda g: (0, g, 0, 0)),
        ],
        out_specs=[
            pl.BlockSpec((PER, slots, cols), lambda g: (g, 0, 0)),
            pl.BlockSpec((PER, cols, frames), lambda g: (g, 0, 0)),
            pl.BlockSpec((None, PER, cols), lambda g: (g, 0, 0)),
        ],
        out_shape=(
            jax.ShapeDtypeStruct((rows, slots, cols), BF16),
            jax.ShapeDtypeStruct((rows, cols, frames), BF16),
            jax.ShapeDtypeStruct((groups, PER, cols), F32),
        ),
        compiler_params=params(24),
        cost_estimate=pl.CostEstimate(
            flops=2 * rows * cols * slots * frames, bytes_accessed=14 * MIB, transcendentals=0
        ),
        name="residual",
    )(inbox, inbox, inbox, movie)
    return foot_rows, residual, noise.reshape(rows, cols)


def halo_kernel(tile, traces, col, foot_rows, model):
    rows = spread(tile[...].astype(F32), col[...].astype(F32).astype(jnp.int32))
    for q, row in enumerate(rows):
        foot_rows[q] = row
        model[q] = model_row(row, traces[...])


def make_halo_model(inbox, cols, frames):
    slots = inbox.shape[0]
    edge = RAD * FOOT
    groups = RAD // PER
    half = (frames + edge + LANES) // LANES
    return pl.pallas_call(
        halo_kernel,
        grid=(2 * groups,),
        in_specs=[
            pl.BlockSpec(
                (slots, LANES),
                lambda g: (0, (g // groups) * half + frames // LANES + g % groups),
            ),
            pl.BlockSpec((slots, frames), lambda g: (0, (g // groups) * (half * LANES // frames))),
            pl.BlockSpec((slots, LANES), lambda g: (0, (g // groups) * half + half - 1)),
        ],
        out_specs=[
            pl.BlockSpec((PER, slots, cols), lambda g: (g, 0, 0)),
            pl.BlockSpec((PER, cols, frames), lambda g: (g, 0, 0)),
        ],
        out_shape=(
            jax.ShapeDtypeStruct((2 * RAD, slots, cols), BF16),
            jax.ShapeDtypeStruct((2 * RAD, cols, frames), F32),
        ),
        compiler_params=params(24),
        cost_estimate=pl.CostEstimate(
            flops=4 * RAD * cols * slots * frames, bytes_accessed=10 * MIB, transcendentals=0
        ),
        name="halo_model",
    )(inbox, inbox, inbox)


def weights_kernel(taps, own, nxt, prev, scale, scale_next, scale_prev, band, out, out_next, out_prev):
    rows, slots, cols = own.shape

    def across(foot, inv):
        scaled = (foot.astype(F32) * inv[:, None, :]).astype(BF16)
        count = foot.shape[0]
        return dot(scaled.reshape(count * slots, cols), band[...]).reshape(count, slots, cols)

    blurred = across(own[...], scale[...])
    for r in range(rows):
        total = taps[GR] * blurred[r]
        for k in range(1, GR + 1):
            if r - k >= 0 and r + k < rows:
                total = total + taps[GR + k] * (blurred[r - k] + blurred[r + k])
            elif r - k >= 0:
                total = total + taps[GR + k] * blurred[r - k]
            elif r + k < rows:
                total = total + taps[GR + k] * blurred[r + k]
        out[r] = total.astype(BF16)
    after = across(nxt[0:GR], scale_next[...])
    ahead = across(prev[PER - GR : PER], scale_prev[...])
    for a in range(GR):
        total = taps[2 * GR] * after[0] if a == 0 else taps[2 * GR - a] * after[0]
        for r in range(1, a + 1):
            total = total + taps[2 * GR + r - a] * after[r]
        out_next[a] = total.astype(BF16)
        total = taps[2 * GR] * ahead[a]
        for b in range(a + 1, GR):
            total = total + taps[2 * GR + a - b] * ahead[b]
        out_prev[a] = total.astype(BF16)


def make_weights(foot_rows, halo_rows, scale, scale_next, scale_prev):
    rows, slots, cols = foot_rows.shape
    taps = tap_values()
    lag = np.arange(cols)[:, None] - np.arange(cols)[None, :]
    band = np.where(np.abs(lag) <= GR, taps[np.clip(lag + GR, 0, 2 * GR)], 0.0)
    band = jnp.asarray(band.astype(ml_dtypes.bfloat16))
    part = 32
    last = 2 * RAD // PER - 1
    return pl.pallas_call(
        functools.partial(weights_kernel, [float(t) for t in taps]),
        grid=(slots // part,),
        in_specs=[
            pl.BlockSpec((rows, part, cols), lambda i: (0, i, 0)),
            pl.BlockSpec((PER, part, cols), lambda i: (0, i, 0)),
            pl.BlockSpec((PER, part, cols), lambda i: (last, i, 0)),
            pl.BlockSpec((rows, cols), lambda i: (0, 0)),
            pl.BlockSpec((GR, cols), lambda i: (0, 0)),
            pl.BlockSpec((GR, cols), lambda i: (0, 0)),
            pl.BlockSpec((cols, cols), lambda i: (0, 0)),
        ],
        out_specs=[
            pl.BlockSpec((rows, part, cols), lambda i: (0, i, 0)),
            pl.BlockSpec((GR, part, cols), lambda i: (0, i, 0)),
            pl.BlockSpec((GR, part, cols), lambda i: (0, i, 0)),
        ],
        out_shape=(
            jax.ShapeDtypeStruct((rows, slots, cols), BF16),
            jax.ShapeDtypeStruct((GR, slots, cols), BF16),
            jax.ShapeDtypeStruct((GR, slots, cols), BF16),
        ),
        compiler_params=params(24),
        cost_estimate=pl.CostEstimate(
            flops=2 * rows * slots * cols * cols, bytes_accessed=10 * MIB, transcendentals=0
        ),
        name="weights",
    )(foot_rows, halo_rows, halo_rows, scale, scale_next, scale_prev, band)


def annulus_kernel(
    own, movie_prev, movie_next, model, weight, weight_next, weight_prev, gain, band,
    background, gradient,
    field, stage, stage_model, upright, det, total, side, sems,
):
    step = pl.program_id(0)
    steps = pl.num_programs(0)
    rows = own.shape[0]
    cols, frames = own.shape[1:]

    def copies():
        return (
            pltpu.make_async_copy(own, field.at[pl.ds(RAD, rows)], sems.at[0]),
            pltpu.make_async_copy(movie_prev, stage.at[1], sems.at[1]),
            pltpu.make_async_copy(model.at[pl.ds(RAD, RAD)], stage_model.at[1], sems.at[2]),
            pltpu.make_async_copy(movie_next, stage.at[0], sems.at[3]),
            pltpu.make_async_copy(model.at[pl.ds(0, RAD)], stage_model.at[0], sems.at[4]),
        )

    def subtract(which, first):
        def one(r, carry):
            field[first + r] = (stage[which, r].astype(F32) - stage_model[which, r]).astype(BF16)
            return carry

        lax.fori_loop(0, RAD, one, 0)

    @pl.when(step == 0)
    def _():
        every = copies()
        for copy in every:
            copy.start()
        for copy in every[0:3]:
            copy.wait()
        subtract(1, 0)
        total[...] = jnp.zeros_like(total)
        upright[...] = jnp.zeros_like(upright)

        def add(r, carry):
            upright[...] += field[r].astype(F32)
            return carry

        lax.fori_loop(0, 2 * RAD - 1, add, 0)

    @pl.when(step == (rows - RAD) // PER)
    def _():
        every = copies()
        for copy in every[3:5]:
            copy.wait()
        subtract(0, RAD + rows)

    top = lax.broadcasted_iota(jnp.int32, (cols // 8, 8, LANES), 1) < 4
    blank = jnp.zeros((2, 8, LANES), F32)
    for q in range(PER):
        y = step * PER + q
        level = dot(band[...], field[y]) + dot(band[...], field[y + 2 * RAD])
        for h in range(frames // LANES):
            part = slice(h * LANES, (h + 1) * LANES)
            column = (
                upright[:, part]
                + field[y + 2 * RAD - 1, :, part].astype(F32)
                - field[y, :, part].astype(F32)
            )
            upright[:, part] = column
            turned = pltpu.roll(column.reshape(cols // 8, 8, LANES), 4, 1)
            turned = jnp.concatenate([blank, turned, blank], axis=0)
            both = turned[0 : cols // 8 + 1] + turned[3 : cols // 8 + 4]
            sides = jnp.where(top, both[0 : cols // 8], both[1 : cols // 8 + 1])
            fit = (level[:, part] + sides.reshape(cols, LANES)) * gain[...]
            background[q, :, part] = fit.astype(BF16)
            det[q, :, part] = (field[y + RAD, :, part].astype(F32) - fit).astype(BF16)
    grown = total[...]
    for q in range(PER):
        grown = grown + dot(weight[q], det[q])
    total[...] = grown

    @pl.when(step == 0)
    def _():
        edge = dot(weight_prev[0], det[0])
        for a in range(1, GR):
            edge = edge + dot(weight_prev[a], det[a])
        side[...] = edge.astype(BF16)

    @pl.when(step == steps - 1)
    def _():
        edge = dot(weight_next[0], det[PER - GR])
        for a in range(1, GR):
            edge = edge + dot(weight_next[a], det[PER - GR + a])
        whole = total[...]
        upper = whole.astype(BF16)
        gradient[:, 0:frames] = upper
        gradient[:, frames : 2 * frames] = (whole - upper.astype(F32)).astype(BF16)
        gradient[:, 2 * frames : 3 * frames] = edge.astype(BF16)
        gradient[:, 3 * frames : 4 * frames] = side[...]


def make_annulus(own, movie_prev, movie_next, model, weight, weight_next, weight_prev, gain):
    rows, cols, frames = own.shape
    slots = weight.shape[1]
    lag = np.arange(cols)[:, None] - np.arange(cols)[None, :]
    band = jnp.asarray((np.abs(lag) <= RAD).astype(ml_dtypes.bfloat16))
    any_space = pl.BlockSpec(memory_space=pl.ANY)
    return pl.pallas_call(
        annulus_kernel,
        grid=(rows // PER,),
        in_specs=[
            any_space,
            any_space,
            any_space,
            any_space,
            pl.BlockSpec((PER, slots, cols), lambda g: (g, 0, 0)),
            pl.BlockSpec((GR, slots, cols), lambda g: (0, 0, 0)),
            pl.BlockSpec((GR, slots, cols), lambda g: (0, 0, 0)),
            pl.BlockSpec((cols, LANES), lambda g: (0, 0)),
            pl.BlockSpec((cols, cols), lambda g: (0, 0)),
        ],
        out_specs=[
            pl.BlockSpec((None, PER, cols, frames), lambda g: (0, g, 0, 0)),
            pl.BlockSpec((slots, 4 * frames), lambda g: (0, 0)),
        ],
        out_shape=(
            jax.ShapeDtypeStruct((1, rows, cols, frames), BF16),
            jax.ShapeDtypeStruct((slots, 4 * frames), BF16),
        ),
        scratch_shapes=[
            pltpu.VMEM((rows + 2 * RAD, cols, frames), BF16),
            pltpu.VMEM((2, RAD, cols, frames), BF16),
            pltpu.VMEM((2, RAD, cols, frames), F32),
            pltpu.VMEM((cols, frames), F32),
            pltpu.VMEM((PER, cols, frames), BF16),
            pltpu.VMEM((slots, frames), F32),
            pltpu.VMEM((slots, frames), BF16),
            pltpu.SemaphoreType.DMA((5,)),
        ],
        compiler_params=params(40),
        cost_estimate=pl.CostEstimate(
            flops=6 * rows * cols * cols * frames, bytes_accessed=20 * MIB, transcendentals=0
        ),
        name="annulus",
    )(own, movie_prev, movie_next, model, weight, weight_next, weight_prev, gain, band)


def traces_kernel(capacity, stripe_col, stripe_row, inbox, traces, step, slow, fast, out):
    count, frames = traces.shape
    slots = inbox.shape[0]
    before = lax.broadcasted_iota(jnp.int32, (count, count), 1) < lax.broadcasted_iota(
        jnp.int32, (count, count), 0
    )
    same = (stripe_col[...] == stripe_row[...]) & before
    rank = jnp.sum(jnp.where(same, 1.0, 0.0), axis=1, keepdims=True).astype(jnp.int32)
    slot = stripe_col[...] * capacity + rank
    place = lax.broadcasted_iota(jnp.int32, (count, slots), 1)

    def onehot(shift):
        return jnp.where(place + shift == slot, 1.0, 0.0).astype(BF16)

    here = onehot(0)
    gradient = (
        dot(here, inbox[:, 0:frames])
        + dot(here, inbox[:, frames : 2 * frames])
        + dot(onehot(capacity), inbox[:, 2 * frames : 3 * frames])
        + dot(onehot(-capacity), inbox[:, 3 * frames : 4 * frames])
    )
    updated = traces[...].astype(F32) + step[:, 0:1] * gradient
    lane = lax.broadcasted_iota(jnp.int32, (count, frames), 1)

    def lagged(value, lag):
        return jnp.where(lane >= lag, pltpu.roll(value, lag, 1), 0.0)

    a, b = slow[...], fast[...]
    driven = updated - (a + b) * lagged(updated, 1) + (a * b) * lagged(updated, 2)
    value = jnp.maximum(driven - lam_floor, 0.0) * ((1.0 - a) * (1.0 - b))
    for root in (a, b):
        lag = 1
        while lag < frames:
            value = value + root * lagged(value, lag)
            root = root * root
            lag *= 2
    out[...] = value


def make_traces(stripe, inbox, traces, step, slow, fast, capacity):
    count, frames = traces.shape
    return pl.pallas_call(
        functools.partial(traces_kernel, capacity),
        out_shape=jax.ShapeDtypeStruct((count, frames), F32),
        compiler_params=params(16),
        cost_estimate=pl.CostEstimate(
            flops=10 * count * frames * frames, bytes_accessed=MIB, transcendentals=0
        ),
        name="traces",
    )(
        stripe.reshape(count, 1),
        stripe.reshape(1, count),
        inbox,
        traces,
        step,
        slow.reshape(count, 1),
        fast.reshape(count, 1),
    )


def neighbours(axis):
    devices = lax.axis_size(axis)
    up = [(i, i + 1) for i in range(devices - 1)]
    return up, [(j, i) for i, j in up]


def on_device(movie, footprints, traces, stripe, column, annulus_gain, decay_slow, decay_fast):
    pix_count = lax.axis_size("pix")
    rows, cols, frames = movie.shape[1:]
    count = footprints.shape[1]
    capacity = max(2, 2 * count // pix_count)
    slots = pix_count * capacity
    pix_up, pix_down = neighbours("pix")
    plane_up, plane_down = neighbours("plane")

    movie_prev = lax.ppermute(movie[0, rows - RAD :], "pix", pix_up)
    movie_next = lax.ppermute(movie[0, :RAD], "pix", pix_down)

    main_outbox, halo_outbox, step = make_outbox(
        stripe[0], column[0], footprints[0], traces[0], capacity, slots
    )
    inbox = lax.all_to_all(main_outbox, "pix", split_axis=0, concat_axis=0, tiled=True)
    halo_inbox = lax.all_to_all(halo_outbox, "pix", split_axis=0, concat_axis=0, tiled=True)

    foot_rows, residual, noise = make_residual(inbox, movie)
    noise_before = lax.ppermute(noise, "plane", plane_up)
    noise_after = lax.ppermute(noise, "plane", plane_down)
    pooled = (noise_before + 2.0 * noise + noise_after) / 4.0
    scale = 1.0 / jnp.sqrt(pooled + noise_eps)
    scale_prev = lax.ppermute(scale[rows - GR :], "pix", pix_up)
    scale_next = lax.ppermute(scale[:GR], "pix", pix_down)

    halo_rows, halo_model = make_halo_model(halo_inbox, cols, frames)
    weight, weight_next, weight_prev = make_weights(
        foot_rows, halo_rows, scale, scale_next, scale_prev
    )

    gain = jnp.broadcast_to((annulus_gain[0] / (8.0 * RAD))[:, None], (cols, LANES))
    background, gradient = make_annulus(
        residual, movie_prev, movie_next, halo_model, weight, weight_next, weight_prev, gain
    )
    home = lax.all_to_all(gradient, "pix", split_axis=0, concat_axis=0, tiled=True)
    traces_new = make_traces(
        stripe[0], home, traces[0], step, decay_slow[0], decay_fast[0], capacity
    )
    return (background, traces_new[None])


def solution(mesh):
    placed = (
        P("plane", "pix", None, None),
        P("plane", "pix", None),
        P("plane", "pix", None),
        P("plane", "pix", None),
        P("plane", "pix"),
        P("plane", None),
        P("plane", "pix"),
        P("plane", "pix"),
    )
    return jax.shard_map(
        on_device,
        mesh=mesh,
        in_specs=placed,
        out_specs=(P("plane", "pix", None, None), P("plane", "pix", None)),
        check_vma=False,
    )
```

```python
import functools

import jax
import jax.numpy as jnp
import ml_dtypes
import numpy as np
from jax import lax
from jax.experimental import pallas as pl
from jax.experimental.pallas import tpu as pltpu
from jax.sharding import PartitionSpec as P

FOOT = 32
RAD = 12
GR = 3
LANES = 128
PER = LANES // FOOT
NEAR = PER

lam_floor = 0.1
noise_eps = 1e-05
norm_eps = 1e-05
sigma_twice = 4.5

F32 = jnp.float32
BF16 = jnp.bfloat16
MIB = 1 << 20
ANY = pl.BlockSpec(memory_space=pl.ANY)


def tap_values():
    offsets = np.arange(-GR, GR + 1).astype(np.float32)
    raw = np.exp(-offsets * offsets / np.float32(sigma_twice)).astype(np.float32)
    return (raw / raw.sum(dtype=np.float32)).astype(ml_dtypes.bfloat16).astype(np.float32)


def params(mib=56):
    return pltpu.CompilerParams(vmem_limit_bytes=mib * MIB)


def dot(a, b):
    return jnp.dot(a, b, preferred_element_type=F32)


def cut_kernel(movie, up, down, sems):
    rows = movie.shape[1]
    copies = [
        pltpu.make_async_copy(movie.at[0, pl.ds(rows - NEAR, NEAR)], up, sems.at[0]),
        pltpu.make_async_copy(movie.at[0, pl.ds(0, NEAR)], down, sems.at[1]),
    ]
    for copy in copies:
        copy.start()
    for copy in copies:
        copy.wait()


def cut_near(movie):
    cols, frames = movie.shape[2:]
    piece = jax.ShapeDtypeStruct((NEAR, cols, frames), BF16)
    return pl.pallas_call(
        cut_kernel,
        in_specs=[ANY],
        out_specs=[ANY, ANY],
        out_shape=(piece, piece),
        scratch_shapes=[pltpu.SemaphoreType.DMA((2,))],
        compiler_params=params(),
        name="cut_near",
    )(movie)


def outbox_kernel(capacity, stripe, column, foot, traces, movie, near, outbox, step, *rest):
    far, sems = rest[:-1], rest[-1]
    del near
    rows, _, frames = movie.shape[1:]
    copies = []
    for h in range(frames // LANES):
        lanes = pl.ds(h * LANES, LANES)
        for k, first in enumerate((rows - RAD, NEAR)):
            copies.append(
                pltpu.make_async_copy(
                    movie.at[0, pl.ds(first, RAD - NEAR), :, lanes],
                    far[2 * h + k],
                    sems.at[2 * h + k],
                )
            )
    for copy in copies:
        copy.start()

    count = stripe.shape[1]
    slots = outbox.shape[0]
    before = lax.broadcasted_iota(jnp.int32, (count, count), 0) < lax.broadcasted_iota(
        jnp.int32, (count, count), 1
    )
    named = jnp.broadcast_to(stripe[...].astype(F32), (count, count))
    same = (named == named.T) & before
    rank = jnp.sum(jnp.where(same, 1.0, 0.0), axis=0, keepdims=True).astype(jnp.int32)
    slot = stripe[...] * capacity + rank
    place = lax.broadcasted_iota(jnp.int32, (slots, count), 0)
    left = jnp.broadcast_to(column[...].astype(F32), (LANES, count)).T.astype(BF16)
    tiles = foot.shape[1]
    edge = RAD * FOOT
    lane = lax.broadcasted_iota(jnp.int32, (slots, LANES), 1)
    lefts = jnp.zeros((slots, LANES), F32)
    at = 3 * frames
    pieces = ((0, 0, tiles), (capacity, 0, edge), (-capacity, tiles - edge, edge))
    for k, (shift, first, width) in enumerate(pieces):
        hot = jnp.where(place + shift == slot, 1.0, 0.0).astype(BF16)
        outbox[:, k * frames : (k + 1) * frames] = dot(hot, traces[...]).astype(BF16)
        outbox[:, at : at + width] = dot(hot, foot[:, first : first + width]).astype(BF16)
        lefts = jnp.where(lane == k, dot(hot, left), lefts)
        at += width
    outbox[:, at:] = lefts.astype(BF16)
    foot_f = foot[...].astype(F32)
    total = jnp.sum(foot_f * foot_f, axis=1, keepdims=True)
    step[...] = jnp.broadcast_to(1.0 / (total + norm_eps), step.shape)
    for copy in copies:
        copy.wait()


def make_outbox(stripe, column, foot, traces, movie, near, capacity, slots):
    count, tiles = foot.shape
    cols, frames = movie.shape[2:]
    parts = frames // LANES
    width = 3 * frames + tiles + 2 * RAD * FOOT + LANES
    vmem = pl.BlockSpec(memory_space=pltpu.VMEM)
    piece = jax.ShapeDtypeStruct((RAD - NEAR, cols, LANES), BF16)
    outbox, step, *far = pl.pallas_call(
        functools.partial(outbox_kernel, capacity),
        in_specs=[vmem] * 4 + [ANY, ANY],
        out_specs=[vmem, vmem] + [ANY] * (2 * parts),
        out_shape=(
            jax.ShapeDtypeStruct((slots, width), BF16),
            jax.ShapeDtypeStruct((count, LANES), F32),
        )
        + (piece,) * (2 * parts),
        scratch_shapes=[pltpu.SemaphoreType.DMA((2 * parts,))],
        compiler_params=params(),
        cost_estimate=pl.CostEstimate(
            flops=2 * slots * count * 3000, bytes_accessed=2 * MIB, transcendentals=0
        ),
        name="outbox",
    )(stripe, column, foot, traces, movie, near)
    return outbox, step, far


def spread(block, col):
    lane = lax.broadcasted_iota(jnp.int32, block.shape, 1)
    low = lane < FOOT
    high = (lane >= 2 * FOOT) & (lane < 3 * FOOT)
    pairs = [
        jnp.where(low, block, 0.0) + jnp.where(high, pltpu.roll(block, FOOT, 1), 0.0),
        jnp.where(low, pltpu.roll(block, 2 * FOOT, 1), 0.0)
        + jnp.where(high, pltpu.roll(block, 3 * FOOT, 1), 0.0),
    ]
    bits = [((col >> k) & 1) == 1 for k in range(7)]
    right = col >= LANES
    straight = lane >= ((col >> 5) & 3) * FOOT
    in_left = straight & ~right
    in_right = (straight & right) | (~straight & ~right)
    rows = []
    for pair in pairs:
        for k in range(5):
            pair = jnp.where(bits[k], pltpu.roll(pair, 1 << k, 1), pair)
        for moved in (pair, pltpu.roll(pair, 2 * FOOT, 1)):
            moved = jnp.where(lane < 2 * FOOT, moved, 0.0)
            for k in (5, 6):
                moved = jnp.where(bits[k], pltpu.roll(moved, 1 << k, 1), moved)
            rows.append(
                jnp.concatenate(
                    [jnp.where(in_left, moved, 0.0), jnp.where(in_right, moved, 0.0)], axis=1
                ).astype(BF16)
            )
    return rows


def model_row(row, traces):
    return lax.dot_general(row, traces, (((0,), (0,)), ((), ())), preferred_element_type=F32)


def columns(lefts, which):
    return jnp.broadcast_to(lefts[:, which : which + 1].astype(F32), lefts.shape).astype(jnp.int32)


def subtract_rows(rows, traces, movie_row, foot_rows, residual, noise):
    cols, frames = residual.shape[1:]
    lane = lax.broadcasted_iota(jnp.int32, (cols, frames), 1)
    for q, row in enumerate(rows):
        foot_rows[q] = row
        left = (movie_row(q).astype(F32) - model_row(row, traces[...])).astype(BF16)
        residual[q] = left
        left = left.astype(F32)
        change = jnp.where(lane < frames - 1, pltpu.roll(left, frames - 1, 1) - left, 0.0)
        change = change * change
        part = change[:, 0:LANES]
        for k in range(1, frames // LANES):
            part = part + change[:, k * LANES : (k + 1) * LANES]
        noise[q : q + 1, :] = jnp.sum(part.T, axis=0, keepdims=True) / (frames - 1)


def residual_kernel(tile, traces, lefts, movie, foot_rows, residual, noise):
    rows = spread(tile[...].astype(F32), columns(lefts, 0))
    subtract_rows(rows, traces, lambda q: movie[q], foot_rows, residual, noise)


def near_kernel(tile, traces, lefts, movie_next, movie_prev, foot_rows, residual, noise):
    after = pl.program_id(0) == 0
    col = jnp.where(after, columns(lefts, 1), columns(lefts, 2))
    rows = spread(tile[...].astype(F32), col)
    subtract_rows(
        rows,
        traces,
        lambda q: jnp.where(after, movie_next[q].astype(F32), movie_prev[q].astype(F32)),
        foot_rows,
        residual,
        noise,
    )


def far_kernel(tile, traces, lefts, model):
    after = pl.program_id(0) < pl.num_programs(0) // 2
    col = jnp.where(after, columns(lefts, 1), columns(lefts, 2))
    for q, row in enumerate(spread(tile[...].astype(F32), col)):
        model[q] = model_row(row, traces[...])


def inbox_specs(inbox, frames, tile_block, trace_block):
    slots, width = inbox.shape
    tiles = 3 * frames // LANES
    return [
        pl.BlockSpec((slots, LANES), lambda g: (0, tiles + tile_block(g))),
        pl.BlockSpec((slots, frames), lambda g: (0, trace_block(g))),
        pl.BlockSpec((slots, LANES), lambda g: (0, width // LANES - 1)),
    ]


def row_outputs(groups, slots, cols, frames):
    specs = [
        pl.BlockSpec((PER, slots, cols), lambda g: (g, 0, 0)),
        pl.BlockSpec((PER, cols, frames), lambda g: (g, 0, 0)),
        pl.BlockSpec((None, PER, cols), lambda g: (g, 0, 0)),
    ]
    shapes = (
        jax.ShapeDtypeStruct((groups * PER, slots, cols), BF16),
        jax.ShapeDtypeStruct((groups * PER, cols, frames), BF16),
        jax.ShapeDtypeStruct((groups, PER, cols), F32),
    )
    return specs, shapes


def make_residual(inbox, movie):
    slots = inbox.shape[0]
    rows, cols, frames = movie.shape[1:]
    groups = rows // PER
    specs, shapes = row_outputs(groups, slots, cols, frames)
    foot_rows, residual, noise = pl.pallas_call(
        residual_kernel,
        grid=(groups,),
        in_specs=inbox_specs(inbox, frames, lambda g: g, lambda g: 0)
        + [pl.BlockSpec((None, PER, cols, frames), lambda g: (0, g, 0, 0))],
        out_specs=specs,
        out_shape=shapes,
        compiler_params=params(),
        cost_estimate=pl.CostEstimate(
            flops=2 * rows * cols * slots * frames, bytes_accessed=14 * MIB, transcendentals=0
        ),
        name="residual",
    )(inbox, inbox, inbox, movie)
    return foot_rows, residual, noise.reshape(rows, cols)


def make_near(inbox, movie_next, movie_prev):
    slots = inbox.shape[0]
    cols, frames = movie_next.shape[1:]
    own = FOOT // PER
    specs, shapes = row_outputs(2, slots, cols, frames)
    whole = pl.BlockSpec((NEAR, cols, frames), lambda g: (0, 0, 0))
    foot_rows, residual, noise = pl.pallas_call(
        near_kernel,
        grid=(2,),
        in_specs=inbox_specs(
            inbox, frames, lambda g: own + g * (2 * RAD // PER - 1), lambda g: 1 + g
        )
        + [whole, whole],
        out_specs=specs,
        out_shape=shapes,
        compiler_params=params(),
        cost_estimate=pl.CostEstimate(
            flops=4 * NEAR * cols * slots * frames, bytes_accessed=5 * MIB, transcendentals=0
        ),
        name="near",
    )(inbox, inbox, inbox, movie_next, movie_prev)
    return foot_rows, residual, noise.reshape(2 * NEAR, cols)


def make_far_model(inbox, cols, frames):
    slots = inbox.shape[0]
    groups = (RAD - NEAR) // PER
    first = (FOOT + NEAR) // PER
    return pl.pallas_call(
        far_kernel,
        grid=(2 * groups,),
        in_specs=inbox_specs(inbox, frames, lambda g: first + g, lambda g: 1 + g // groups),
        out_specs=pl.BlockSpec((PER, cols, frames), lambda g: (g, 0, 0)),
        out_shape=jax.ShapeDtypeStruct((2 * (RAD - NEAR), cols, frames), F32),
        compiler_params=params(),
        cost_estimate=pl.CostEstimate(
            flops=4 * RAD * cols * slots * frames, bytes_accessed=5 * MIB, transcendentals=0
        ),
        name="far_model",
    )(inbox, inbox, inbox)


def weights_kernel(taps, own, nxt, prev, scale, band, out, out_next, out_prev):
    rows, slots, cols = own.shape

    def across(foot, inv):
        scaled = (foot.astype(F32) * inv[:, None, :]).astype(BF16)
        count = foot.shape[0]
        return dot(scaled.reshape(count * slots, cols), band[...]).reshape(count, slots, cols)

    blurred = across(own[...], scale[NEAR : NEAR + rows])
    for r in range(rows):
        total = taps[GR] * blurred[r]
        for k in range(1, GR + 1):
            if r - k >= 0 and r + k < rows:
                total = total + taps[GR + k] * (blurred[r - k] + blurred[r + k])
            elif r - k >= 0:
                total = total + taps[GR + k] * blurred[r - k]
            elif r + k < rows:
                total = total + taps[GR + k] * blurred[r + k]
        out[r] = total.astype(BF16)
    after = across(nxt[0:GR], scale[0:GR])
    ahead = across(prev[NEAR - GR : NEAR], scale[rows + 2 * NEAR - GR :])
    for a in range(GR):
        total = taps[2 * GR - a] * after[0]
        for r in range(1, a + 1):
            total = total + taps[2 * GR + r - a] * after[r]
        out_next[a] = total.astype(BF16)
        total = taps[2 * GR] * ahead[a]
        for b in range(a + 1, GR):
            total = total + taps[2 * GR + a - b] * ahead[b]
        out_prev[a] = total.astype(BF16)


def make_weights(foot_rows, near_rows, scale):
    rows, slots, cols = foot_rows.shape
    taps = tap_values()
    lag = np.arange(cols)[:, None] - np.arange(cols)[None, :]
    band = np.where(np.abs(lag) <= GR, taps[np.clip(lag + GR, 0, 2 * GR)], 0.0)
    band = jnp.asarray(band.astype(ml_dtypes.bfloat16))
    part = 32
    return pl.pallas_call(
        functools.partial(weights_kernel, [float(t) for t in taps]),
        grid=(slots // part,),
        in_specs=[
            pl.BlockSpec((rows, part, cols), lambda i: (0, i, 0)),
            pl.BlockSpec((NEAR, part, cols), lambda i: (0, i, 0)),
            pl.BlockSpec((NEAR, part, cols), lambda i: (1, i, 0)),
            pl.BlockSpec((rows + 2 * NEAR, cols), lambda i: (0, 0)),
            pl.BlockSpec((cols, cols), lambda i: (0, 0)),
        ],
        out_specs=[
            pl.BlockSpec((rows, part, cols), lambda i: (0, i, 0)),
            pl.BlockSpec((GR, part, cols), lambda i: (0, i, 0)),
            pl.BlockSpec((GR, part, cols), lambda i: (0, i, 0)),
        ],
        out_shape=(
            jax.ShapeDtypeStruct((rows, slots, cols), BF16),
            jax.ShapeDtypeStruct((GR, slots, cols), BF16),
            jax.ShapeDtypeStruct((GR, slots, cols), BF16),
        ),
        compiler_params=params(),
        cost_estimate=pl.CostEstimate(
            flops=2 * rows * slots * cols * cols, bytes_accessed=10 * MIB, transcendentals=0
        ),
        name="weights",
    )(foot_rows, near_rows, near_rows, scale, band)


def annulus_kernel(
    half, own, near, far_prev, far_next, model, weight, weight_next, weight_prev, gain, band, *rest
):
    (background, gradient, field, stage, stage_model, upright, det, total, side, sems) = rest[-10:]
    step = pl.program_id(0)
    steps = pl.num_programs(0)
    rows, cols = own.shape[0:2]
    far = RAD - NEAR
    early = 2 * RAD - PER
    lanes = pl.ds(half * LANES, LANES)

    def copy(k):
        source, target = (
            (far_prev, stage.at[1]),
            (model.at[pl.ds(far, far), :, lanes], stage_model.at[1]),
            (near.at[pl.ds(NEAR, NEAR), :, lanes], field.at[pl.ds(far, NEAR)]),
            (own.at[pl.ds(0, early), :, lanes], field.at[pl.ds(RAD, early)]),
            (
                own.at[pl.ds(early, rows - early), :, lanes],
                field.at[pl.ds(RAD + early, rows - early)],
            ),
            (far_next, stage.at[0]),
            (model.at[pl.ds(0, far), :, lanes], stage_model.at[0]),
            (near.at[pl.ds(0, NEAR), :, lanes], field.at[pl.ds(RAD + rows, NEAR)]),
        )[k]
        return pltpu.make_async_copy(source, target, sems.at[k])

    def subtract(which, first):
        for r in range(far):
            field[first + r] = (stage[which, r].astype(F32) - stage_model[which, r]).astype(BF16)

    @pl.when(step == 0)
    def _():
        for k in range(8):
            copy(k).start()
        for k in range(4):
            copy(k).wait()
        subtract(1, 0)
        total[...] = jnp.zeros_like(total)
        start = field[0].astype(F32)
        for r in range(1, 2 * RAD - 1):
            start = start + field[r].astype(F32)
        upright[...] = start

    @pl.when(step == 1)
    def _():
        copy(4).wait()

    @pl.when(step == (rows - RAD) // PER)
    def _():
        for k in range(5, 8):
            copy(k).wait()
        subtract(0, RAD + rows + NEAR)

    top = lax.broadcasted_iota(jnp.int32, (cols // 8, 8, LANES), 1) < 4
    blank = jnp.zeros((2, 8, LANES), F32)
    for pair in range(0, PER, 2):
        y = step * PER + pair
        above = jnp.concatenate([field[y], field[y + 1]], axis=1)
        below = jnp.concatenate([field[y + 2 * RAD], field[y + 2 * RAD + 1]], axis=1)
        level = dot(band[...], above) + dot(band[...], below)
        for q in (pair, pair + 1):
            y = step * PER + q
            column = upright[...] + field[y + 2 * RAD - 1].astype(F32) - field[y].astype(F32)
            upright[...] = column
            turned = pltpu.roll(column.reshape(cols // 8, 8, LANES), 4, 1)
            turned = jnp.concatenate([blank, turned, blank], axis=0)
            both = turned[0 : cols // 8 + 1] + turned[3 : cols // 8 + 4]
            sides = jnp.where(top, both[0 : cols // 8], both[1 : cols // 8 + 1])
            across = level[:, (q - pair) * LANES : (q - pair + 1) * LANES]
            fit = (across + sides.reshape(cols, LANES)) * gain[...]
            background[q] = fit.astype(BF16)
            det[q] = (field[y + RAD].astype(F32) - fit).astype(BF16)
    grown = total[...]
    for q in range(PER):
        grown = grown + dot(weight[q], det[q])
    total[...] = grown

    @pl.when(step == 0)
    def _():
        edge = dot(weight_prev[0], det[0])
        for a in range(1, GR):
            edge = edge + dot(weight_prev[a], det[a])
        side[...] = edge.astype(BF16)

    @pl.when(step == steps - 1)
    def _():
        edge = dot(weight_next[0], det[PER - GR])
        for a in range(1, GR):
            edge = edge + dot(weight_next[a], det[PER - GR + a])
        whole = total[...]
        upper = whole.astype(BF16)
        gradient[:, 0:LANES] = upper
        gradient[:, LANES : 2 * LANES] = (whole - upper.astype(F32)).astype(BF16)
        gradient[:, 2 * LANES : 3 * LANES] = edge.astype(BF16)
        gradient[:, 3 * LANES : 4 * LANES] = side[...]


def make_annulus(half, own, near, far_prev, far_next, model, weights, gain, background):
    rows, cols, frames = own.shape
    slots = weights[0].shape[1]
    lag = np.arange(cols)[:, None] - np.arange(cols)[None, :]
    band = jnp.asarray((np.abs(lag) <= RAD).astype(ml_dtypes.bfloat16))
    args = (own, near, far_prev, far_next, model, *weights, gain, band)
    earlier = () if background is None else (background,)
    return pl.pallas_call(
        functools.partial(annulus_kernel, half),
        grid=(rows // PER,),
        in_specs=[ANY] * 5
        + [
            pl.BlockSpec((PER, slots, cols), lambda g: (g, 0, 0)),
            pl.BlockSpec((GR, slots, cols), lambda g: (0, 0, 0)),
            pl.BlockSpec((GR, slots, cols), lambda g: (0, 0, 0)),
            pl.BlockSpec((cols, LANES), lambda g: (0, 0)),
            pl.BlockSpec((cols, cols), lambda g: (0, 0)),
        ]
        + [ANY] * len(earlier),
        out_specs=[
            pl.BlockSpec((None, PER, cols, LANES), lambda g: (0, g, 0, half)),
            pl.BlockSpec((slots, 4 * LANES), lambda g: (0, 0)),
        ],
        out_shape=(
            jax.ShapeDtypeStruct((1, rows, cols, frames), BF16),
            jax.ShapeDtypeStruct((slots, 4 * LANES), BF16),
        ),
        scratch_shapes=[
            pltpu.VMEM((rows + 2 * RAD, cols, LANES), BF16),
            pltpu.VMEM((2, RAD - NEAR, cols, LANES), BF16),
            pltpu.VMEM((2, RAD - NEAR, cols, LANES), F32),
            pltpu.VMEM((cols, LANES), F32),
            pltpu.VMEM((PER, cols, LANES), BF16),
            pltpu.VMEM((slots, LANES), F32),
            pltpu.VMEM((slots, LANES), BF16),
            pltpu.SemaphoreType.DMA((8,)),
        ],
        input_output_aliases={len(args): 0} if earlier else {},
        compiler_params=params(),
        cost_estimate=pl.CostEstimate(
            flops=3 * rows * cols * cols * frames, bytes_accessed=10 * MIB, transcendentals=0
        ),
        name="annulus",
    )(*args, *earlier)


def traces_kernel(capacity, stripe, slow, fast, traces, step, *rest):
    inboxes, out = rest[:-1], rest[-1]
    count, frames = traces.shape
    slots = inboxes[0].shape[0]

    def upended(row):
        return jnp.broadcast_to(row[...].astype(F32), (LANES, count)).T

    before = lax.broadcasted_iota(jnp.int32, (count, count), 1) < lax.broadcasted_iota(
        jnp.int32, (count, count), 0
    )
    named = upended(stripe)
    same = (named == stripe[...].astype(F32)) & before
    rank = jnp.sum(jnp.where(same, 1.0, 0.0), axis=1, keepdims=True)
    slot = (named[:, 0:1] * capacity + rank).astype(jnp.int32)
    place = lax.broadcasted_iota(jnp.int32, (count, slots), 1)

    def onehot(shift):
        return jnp.where(place + shift == slot, 1.0, 0.0).astype(BF16)

    here, after, ahead = onehot(0), onehot(capacity), onehot(-capacity)
    gradient = jnp.concatenate(
        [
            dot(here, inbox[:, 0:LANES])
            + dot(here, inbox[:, LANES : 2 * LANES])
            + dot(after, inbox[:, 2 * LANES : 3 * LANES])
            + dot(ahead, inbox[:, 3 * LANES : 4 * LANES])
            for inbox in inboxes
        ],
        axis=1,
    )
    updated = traces[...].astype(F32) + step[:, 0:1] * gradient
    lane = lax.broadcasted_iota(jnp.int32, (count, frames), 1)

    def lagged(value, lag):
        return jnp.where(lane >= lag, pltpu.roll(value, lag, 1), 0.0)

    a, b = [jnp.concatenate([upended(row)] * (frames // LANES), axis=1) for row in (slow, fast)]
    driven = updated - (a + b) * lagged(updated, 1) + (a * b) * lagged(updated, 2)
    value = jnp.maximum(driven - lam_floor, 0.0) * ((1.0 - a) * (1.0 - b))
    for root in (a, b):
        lag = 1
        while lag < frames:
            value = value + root * lagged(value, lag)
            root = root * root
            lag *= 2
    out[...] = value


def make_traces(stripe, slow, fast, traces, step, inboxes, capacity):
    count, frames = traces.shape
    return pl.pallas_call(
        functools.partial(traces_kernel, capacity),
        out_shape=jax.ShapeDtypeStruct((count, frames), F32),
        compiler_params=params(),
        cost_estimate=pl.CostEstimate(
            flops=10 * count * frames * frames, bytes_accessed=MIB, transcendentals=0
        ),
        name="traces",
    )(stripe, slow, fast, traces, step, *inboxes)


def neighbours(axis):
    devices = lax.axis_size(axis)
    up = [(i, i + 1) for i in range(devices - 1)]
    return up, [(j, i) for i, j in up]


def on_device(movie, footprints, traces, stripe, column, annulus_gain, decay_slow, decay_fast):
    pix_count = lax.axis_size("pix")
    rows, cols, frames = movie.shape[1:]
    count = footprints.shape[1]
    capacity = max(2, 2 * count // pix_count)
    slots = pix_count * capacity
    pix_up, pix_down = neighbours("pix")
    plane_up, plane_down = neighbours("plane")

    near_up, near_down = cut_near(movie)
    near_prev = lax.ppermute(near_up, "pix", pix_up)
    near_next = lax.ppermute(near_down, "pix", pix_down)

    stripe_row = stripe.reshape(1, count)
    outbox, step, far = make_outbox(
        stripe_row, column, footprints[0], traces[0], movie, near_up, capacity, slots
    )
    inbox = lax.all_to_all(outbox, "pix", split_axis=0, concat_axis=0, tiled=True)
    halves = range(frames // LANES)
    far_prev = [lax.ppermute(far[2 * h], "pix", pix_up) for h in halves]
    far_next = [lax.ppermute(far[2 * h + 1], "pix", pix_down) for h in halves]

    foot_rows, residual, noise = make_residual(inbox, movie)
    near_rows, near_residual, near_noise = make_near(inbox, near_next, near_prev)
    noise = jnp.concatenate([near_noise[:NEAR], noise, near_noise[NEAR:]], axis=0)
    noise_before = lax.ppermute(noise, "plane", plane_up)
    noise_after = lax.ppermute(noise, "plane", plane_down)
    pooled = (noise_before + 2.0 * noise + noise_after) / 4.0
    scale = 1.0 / jnp.sqrt(pooled + noise_eps)

    weights = make_weights(foot_rows, near_rows, scale)
    far_model = make_far_model(inbox, cols, frames)

    gain = jnp.broadcast_to((annulus_gain[0] / (8.0 * RAD))[:, None], (cols, LANES))
    background = None
    home = []
    for h in halves:
        background, gradient = make_annulus(
            h, residual, near_residual, far_prev[h], far_next[h], far_model, weights, gain,
            background,
        )
        home.append(lax.all_to_all(gradient, "pix", split_axis=0, concat_axis=0, tiled=True))
    traces_new = make_traces(
        stripe_row, decay_slow, decay_fast, traces[0], step, home, capacity
    )
    return (background, traces_new[None])


def solution(mesh):
    placed = (
        P("plane", "pix", None, None),
        P("plane", "pix", None),
        P("plane", "pix", None),
        P("plane", "pix", None),
        P("plane", "pix"),
        P("plane", None),
        P("plane", "pix"),
        P("plane", "pix"),
    )
    return jax.shard_map(
        on_device,
        mesh=mesh,
        in_specs=placed,
        out_specs=(P("plane", "pix", None, None), P("plane", "pix", None)),
        check_vma=False,
    )
```

```python
import functools

import jax
import jax.numpy as jnp
import ml_dtypes
import numpy as np
from jax import lax
from jax.experimental import pallas as pl
from jax.experimental.pallas import tpu as pltpu
from jax.sharding import PartitionSpec as P

FOOT = 32
RAD = 12
GR = 3
LANES = 128
PER = LANES // FOOT
NEAR = PER
FAR = RAD - NEAR

lam_floor = 0.1
noise_eps = 1e-05
norm_eps = 1e-05
sigma_twice = 4.5

F32 = jnp.float32
BF16 = jnp.bfloat16
MIB = 1 << 20
ANY = pl.BlockSpec(memory_space=pl.ANY)
VMEM = pl.BlockSpec(memory_space=pltpu.VMEM)


def tap_values():
    offsets = np.arange(-GR, GR + 1).astype(np.float32)
    raw = np.exp(-offsets * offsets / np.float32(sigma_twice)).astype(np.float32)
    return (raw / raw.sum(dtype=np.float32)).astype(ml_dtypes.bfloat16).astype(np.float32)


def params(mib=16):
    return pltpu.CompilerParams(vmem_limit_bytes=mib * MIB)


def cost(flops, mib):
    return pl.CostEstimate(flops=flops, bytes_accessed=mib * MIB, transcendentals=0)


def dot(a, b):
    return jnp.dot(a, b, preferred_element_type=F32)


def pick_kernel(place, foot, rest, inbox):
    capacity = inbox.shape[0]
    count, tiles = foot.shape
    frames = rest.shape[1] - LANES
    here = place[0]
    marks = rest[:, frames:].astype(F32)
    named = marks.T[0:1, :]
    before = lax.broadcasted_iota(jnp.int32, (count, count), 0) < lax.broadcasted_iota(
        jnp.int32, (count, count), 1
    )
    same = (marks[:, 0:1] == named) & before
    rank = jnp.sum(jnp.where(same, 1.0, 0.0), axis=0, keepdims=True).astype(jnp.int32)
    stripe = named.astype(jnp.int32)
    row = lax.broadcasted_iota(jnp.int32, (capacity, count), 0)
    lane = lax.broadcasted_iota(jnp.int32, (capacity, LANES), 1)
    edge = RAD * FOOT
    lefts = jnp.zeros((capacity, LANES), F32)
    at = 3 * frames
    for k, (shift, first, width) in enumerate(
        ((0, 0, tiles), (1, 0, edge), (-1, tiles - edge, edge))
    ):
        hot = jnp.where((row == rank) & (stripe == here + shift), 1.0, 0.0).astype(BF16)
        inbox[:, k * frames : (k + 1) * frames] = dot(hot, rest[:, 0:frames]).astype(BF16)
        inbox[:, at : at + width] = dot(hot, foot[:, first : first + width]).astype(BF16)
        lefts = jnp.where(lane == k, dot(hot, rest[:, frames:])[:, 1:2], lefts)
        at += width
    inbox[:, at:] = lefts.astype(BF16)


def pick(foot, rest, count, capacity):
    sources = foot.shape[0] // count
    tiles = foot.shape[1]
    frames = rest.shape[1] - LANES
    width = 3 * frames + tiles + 2 * RAD * FOOT + LANES
    inbox = pl.pallas_call(
        pick_kernel,
        grid=(sources,),
        in_specs=[
            pl.BlockSpec(memory_space=pltpu.SMEM),
            pl.BlockSpec((count, tiles), lambda d: (d, 0)),
            pl.BlockSpec((count, frames + LANES), lambda d: (d, 0)),
        ],
        out_specs=pl.BlockSpec((None, capacity, width), lambda d: (d, 0, 0)),
        out_shape=jax.ShapeDtypeStruct((sources, capacity, width), BF16),
        compiler_params=params(),
        cost_estimate=cost(2 * sources * capacity * count * width, 5),
        name="pick",
    )(lax.axis_index("pix").astype(jnp.int32).reshape(1), foot, rest)
    return inbox.reshape(sources * capacity, width)


def spread(block, col):
    lane = lax.broadcasted_iota(jnp.int32, block.shape, 1)
    for k in range(7):
        block = jnp.where(((col >> k) & 1) == 1, pltpu.roll(block, 1 << k, 1), block)
    inside = ((lane - col) & (LANES - 1)) < FOOT
    left = inside & (lane >= col)
    right = inside & (lane < col)
    rows = []
    for q in range(PER):
        moved = block if q == 0 else pltpu.roll(block, LANES - q * FOOT, 1)
        rows.append(
            jnp.concatenate(
                [jnp.where(left, moved, 0.0), jnp.where(right, moved, 0.0)], axis=1
            ).astype(BF16)
        )
    return rows


def tile_rows(inbox, which, block, frames):
    lefts = inbox[:, inbox.shape[1] - LANES :].astype(F32)
    col = jnp.broadcast_to(lefts[:, which : which + 1], lefts.shape).astype(jnp.int32)
    start = 3 * frames + block * LANES
    if not isinstance(start, int):
        start = pl.multiple_of(start, LANES)
    return spread(inbox[:, pl.ds(start, LANES)].astype(F32), col)


def model_row(row, inbox, which, frames):
    traces = inbox[:, which * frames : (which + 1) * frames]
    return lax.dot_general(row, traces, (((0,), (0,)), ((), ())), preferred_element_type=F32)


def noise_row(left, change):
    frames = left.shape[1]
    steps = dot(left, change)
    steps = steps * steps
    part = steps[:, 0:LANES]
    for k in range(1, frames // LANES):
        part = part + steps[:, k * LANES : (k + 1) * LANES]
    return jnp.sum(part.T, axis=0, keepdims=True) / (frames - 1)


def change_matrix(frames):
    earlier, later = np.arange(frames)[:, None], np.arange(frames)[None, :]
    steps = (earlier == later + 1).astype(np.float32) - (earlier == later)
    return jnp.asarray(np.where(later < frames - 1, steps, 0.0).astype(ml_dtypes.bfloat16))


def residual_kernel(inbox, movie, change, foot_rows, residual, noise):
    rows, _, frames = movie.shape[1:]

    def group(g, carry):
        noises = []
        for q, row in enumerate(tile_rows(inbox, 0, g, frames)):
            y = g * PER + q
            foot_rows[y] = row
            left = (movie[0, y].astype(F32) - model_row(row, inbox, 0, frames)).astype(BF16)
            residual[y] = left
            noises.append(noise_row(left, change[...]))
        noise[g] = jnp.concatenate(noises, axis=0)
        return carry

    lax.fori_loop(0, rows // PER, group, 0)


def make_residual(inbox, movie, change):
    slots = inbox.shape[0]
    rows, cols, frames = movie.shape[1:]
    foot_rows, residual, noise = pl.pallas_call(
        residual_kernel,
        out_shape=(
            jax.ShapeDtypeStruct((rows, slots, cols), BF16),
            jax.ShapeDtypeStruct((rows, cols, frames), BF16),
            jax.ShapeDtypeStruct((rows // PER, PER, cols), F32),
        ),
        compiler_params=params(),
        cost_estimate=cost(2 * rows * cols * slots * frames, 14),
        name="residual",
    )(inbox, movie, change)
    return foot_rows, residual, noise.reshape(rows, cols)


def near_kernel(inbox, movie_next, movie_prev, change, foot_rows, residual, noise):
    frames = movie_next.shape[2]
    own = FOOT // PER
    for side, (block, movie) in enumerate(
        ((own, movie_next), (own + 2 * RAD // PER - 1, movie_prev))
    ):
        for q, row in enumerate(tile_rows(inbox, 1 + side, block, frames)):
            y = side * NEAR + q
            foot_rows[y] = row
            left = movie[q].astype(F32) - model_row(row, inbox, 1 + side, frames)
            left = left.astype(BF16)
            residual[y] = left
            noise[y : y + 1, :] = noise_row(left, change[...])


def make_near(inbox, movie_next, movie_prev, change):
    slots = inbox.shape[0]
    cols, frames = movie_next.shape[1:]
    return pl.pallas_call(
        near_kernel,
        out_shape=(
            jax.ShapeDtypeStruct((2 * NEAR, slots, cols), BF16),
            jax.ShapeDtypeStruct((2 * NEAR, cols, frames), BF16),
            jax.ShapeDtypeStruct((2 * NEAR, cols), F32),
        ),
        compiler_params=params(),
        cost_estimate=cost(4 * NEAR * cols * slots * frames, 5),
        name="near",
    )(inbox, movie_next, movie_prev, change)


def far_kernel(inbox, model):
    frames = model.shape[2]
    groups = FAR // PER
    first = (FOOT + NEAR) // PER
    for side in range(2):

        def group(g, carry, side=side):
            block = first + side * groups + g
            for q, row in enumerate(tile_rows(inbox, 1 + side, block, frames)):
                model[side * FAR + g * PER + q] = model_row(row, inbox, 1 + side, frames)
            return carry

        lax.fori_loop(0, groups, group, 0)


def make_far_model(inbox, cols, frames):
    return pl.pallas_call(
        far_kernel,
        out_shape=jax.ShapeDtypeStruct((2 * FAR, cols, frames), F32),
        compiler_params=params(),
        cost_estimate=cost(4 * FAR * cols * inbox.shape[0] * frames, 5),
        name="far_model",
    )(inbox)


def weights_kernel(taps, part, own, near, scale, band, out, out_next, out_prev):
    rows, slots, cols = own.shape

    def across(foot, inv):
        scaled = (foot.astype(F32) * inv[:, None, :]).astype(BF16)
        count = foot.shape[0]
        return dot(scaled.reshape(count * part, cols), band[...]).reshape(count, part, cols)

    def some(i, carry):
        these = pl.ds(pl.multiple_of(i * part, part), part)
        blurred = across(own[:, these, :], scale[NEAR : NEAR + rows])
        for r in range(rows):
            total = taps[GR] * blurred[r]
            for k in range(1, GR + 1):
                if r - k >= 0 and r + k < rows:
                    total = total + taps[GR + k] * (blurred[r - k] + blurred[r + k])
                elif r - k >= 0:
                    total = total + taps[GR + k] * blurred[r - k]
                elif r + k < rows:
                    total = total + taps[GR + k] * blurred[r + k]
            out[r, these, :] = total.astype(BF16)
        after = across(near[0:GR, these, :], scale[0:GR])
        ahead = across(near[2 * NEAR - GR : 2 * NEAR, these, :], scale[rows + 2 * NEAR - GR :])
        for a in range(GR):
            total = taps[2 * GR - a] * after[0]
            for r in range(1, a + 1):
                total = total + taps[2 * GR + r - a] * after[r]
            out_next[a, these, :] = total.astype(BF16)
            total = taps[2 * GR] * ahead[a]
            for b in range(a + 1, GR):
                total = total + taps[2 * GR + a - b] * ahead[b]
            out_prev[a, these, :] = total.astype(BF16)
        return carry

    lax.fori_loop(0, slots // part, some, 0)


def make_weights(foot_rows, near_rows, scale):
    rows, slots, cols = foot_rows.shape
    taps = tap_values()
    lag = np.arange(cols)[:, None] - np.arange(cols)[None, :]
    band = np.where(np.abs(lag) <= GR, taps[np.clip(lag + GR, 0, 2 * GR)], 0.0)
    band = jnp.asarray(band.astype(ml_dtypes.bfloat16))
    return pl.pallas_call(
        functools.partial(weights_kernel, [float(t) for t in taps], 32),
        out_shape=(
            jax.ShapeDtypeStruct((rows, slots, cols), BF16),
            jax.ShapeDtypeStruct((GR, slots, cols), BF16),
            jax.ShapeDtypeStruct((GR, slots, cols), BF16),
        ),
        compiler_params=params(),
        cost_estimate=cost(2 * rows * slots * cols * cols, 10),
        name="weights",
    )(foot_rows, near_rows, scale, band)


def annulus_kernel(
    own, near, far_prev, far_next, model, weight, weight_next, weight_prev, gain, band,
    background, gradient,
    column, det, total, outgoing, sems,
):
    rows, cols, frames = own.shape
    groups = rows // PER
    top = lax.broadcasted_iota(jnp.int32, (cols // 8, 8, LANES), 1) < 4
    blank = jnp.zeros((2, 8, LANES), F32)

    def above(r):
        return (far_prev[r].astype(F32) - model[FAR + r]).astype(BF16)

    def below(r):
        return (far_next[r].astype(F32) - model[r]).astype(BF16)

    def send(g, slot):
        return pltpu.make_async_copy(
            outgoing.at[slot], background.at[0, pl.ds(g * PER, PER)], sems.at[slot]
        )

    def group(g, slot, leaving, entering, first=False, last=False):
        if isinstance(g, int):
            if g >= 2:
                send(g - 2, slot).wait()
        else:
            pl.when(g >= 2)(lambda: send(g - 2, slot).wait())
        for q in range(PER):
            y = g * PER + q
            out, new = leaving(y), entering(y)
            level = dot(band[...], out) + dot(band[...], new)
            for h in range(frames // LANES):
                part = slice(h * LANES, (h + 1) * LANES)
                inner = column[:, part] - out[:, part].astype(F32)
                column[:, part] = inner + new[:, part].astype(F32)
                turned = pltpu.roll(inner.reshape(cols // 8, 8, LANES), 4, 1)
                turned = jnp.concatenate([blank, turned, blank], axis=0)
                both = turned[0 : cols // 8 + 1] + turned[3 : cols // 8 + 4]
                sides = jnp.where(top, both[0 : cols // 8], both[1 : cols // 8 + 1])
                fit = (level[:, part] + sides.reshape(cols, LANES)) * gain[...]
                outgoing[slot, q, :, part] = fit.astype(BF16)
                det[q, :, part] = (own[y, :, part].astype(F32) - fit).astype(BF16)
        send(g, slot).start()
        grown = dot(weight[g * PER], det[0])
        for q in range(1, PER):
            grown = grown + dot(weight[g * PER + q], det[q])
        total[...] += grown

    def edge(edge_weight, first):
        value = dot(edge_weight[0], det[first])
        for a in range(1, GR):
            value = value + dot(edge_weight[a], det[first + a])
        return value.astype(BF16)

    def pair(first, leaving, entering):
        def one(g, carry):
            group(g, lax.rem(g, 2), leaving, entering)
            return carry

        lax.fori_loop(first, first + 2, one, 0)

    start = above(0).astype(F32)
    for r in range(1, FAR):
        start = start + above(r).astype(F32)
    for r in range(NEAR):
        start = start + near[NEAR + r].astype(F32)
    for r in range(RAD):
        start = start + own[r].astype(F32)
    column[...] = start
    total[...] = jnp.zeros_like(total)

    upper, lower = lambda y: own[y - RAD], lambda y: own[y + RAD]
    group(0, 0, above, lower)
    gradient[:, 3 * frames : 4 * frames] = edge(weight_prev, 0)
    group(1, 1, above, lower)
    group(2, 0, lambda y: near[NEAR + y - FAR], lower)

    def middle(g, carry):
        group(g, lax.rem(g, 2), upper, lower)
        return carry

    lax.fori_loop(RAD // PER, (rows - RAD) // PER, middle, 0)
    group(groups - 3, (groups - 3) % 2, upper, lambda y: near[y - (rows - RAD)])

    def final(g, carry):
        group(g, lax.rem(g, 2), upper, lambda y: below(y - (rows - FAR)))
        return carry

    lax.fori_loop(groups - 2, groups, final, 0)
    gradient[:, 2 * frames : 3 * frames] = edge(weight_next, PER - GR)
    whole = total[...]
    high = whole.astype(BF16)
    gradient[:, 0:frames] = high
    gradient[:, frames : 2 * frames] = (whole - high.astype(F32)).astype(BF16)
    for g in (groups - 2, groups - 1):
        send(g, g % 2).wait()


def make_annulus(own, near, far_prev, far_next, model, weights, gain):
    rows, cols, frames = own.shape
    slots = weights[0].shape[1]
    lag = np.arange(cols)[:, None] - np.arange(cols)[None, :]
    band = jnp.asarray((np.abs(lag) <= RAD).astype(ml_dtypes.bfloat16))
    return pl.pallas_call(
        annulus_kernel,
        in_specs=[VMEM] * 10,
        out_specs=[ANY, VMEM],
        out_shape=(
            jax.ShapeDtypeStruct((1, rows, cols, frames), BF16),
            jax.ShapeDtypeStruct((slots, 4 * frames), BF16),
        ),
        scratch_shapes=[
            pltpu.VMEM((cols, frames), F32),
            pltpu.VMEM((PER, cols, frames), BF16),
            pltpu.VMEM((slots, frames), F32),
            pltpu.VMEM((2, PER, cols, frames), BF16),
            pltpu.SemaphoreType.DMA((2,)),
        ],
        compiler_params=params(),
        cost_estimate=cost(6 * rows * cols * cols * frames, 20),
        name="annulus",
    )(own, near, far_prev, far_next, model, *weights, gain, band)


def traces_kernel(capacity, stripe, slow, fast, step, traces, inbox, out):
    count, frames = traces.shape
    slots = inbox.shape[0]

    def upended(row):
        return jnp.broadcast_to(row[...].astype(F32), (LANES, count)).T

    before = lax.broadcasted_iota(jnp.int32, (count, count), 1) < lax.broadcasted_iota(
        jnp.int32, (count, count), 0
    )
    named = upended(stripe)
    same = (named == stripe[...].astype(F32)) & before
    rank = jnp.sum(jnp.where(same, 1.0, 0.0), axis=1, keepdims=True)
    slot = (named[:, 0:1] * capacity + rank).astype(jnp.int32)
    place = lax.broadcasted_iota(jnp.int32, (count, slots), 1)

    def onehot(shift):
        return jnp.where(place + shift == slot, 1.0, 0.0).astype(BF16)

    here = onehot(0)
    gradient = (
        dot(here, inbox[:, 0:frames])
        + dot(here, inbox[:, frames : 2 * frames])
        + dot(onehot(capacity), inbox[:, 2 * frames : 3 * frames])
        + dot(onehot(-capacity), inbox[:, 3 * frames : 4 * frames])
    )

    def wide(row):
        return jnp.concatenate([upended(row)] * (frames // LANES), axis=1)

    updated = traces[...].astype(F32) + wide(step) * gradient
    lane = lax.broadcasted_iota(jnp.int32, (count, frames), 1)

    def lagged(value, lag):
        return jnp.where(lane >= lag, pltpu.roll(value, lag, 1), 0.0)

    a, b = wide(slow), wide(fast)
    driven = updated - (a + b) * lagged(updated, 1) + (a * b) * lagged(updated, 2)
    value = jnp.maximum(driven - lam_floor, 0.0) * ((1.0 - a) * (1.0 - b))
    for root in (a, b):
        lag = 1
        while lag < frames:
            value = value + root * lagged(value, lag)
            root = root * root
            lag *= 2
    out[...] = value


def make_traces(stripe, slow, fast, step, traces, inbox, capacity):
    count, frames = traces.shape
    return pl.pallas_call(
        functools.partial(traces_kernel, capacity),
        out_shape=jax.ShapeDtypeStruct((count, frames), F32),
        compiler_params=params(),
        cost_estimate=cost(10 * count * frames * frames, 1),
        name="traces",
    )(stripe, slow, fast, step, traces, inbox)


def neighbours(axis):
    devices = lax.axis_size(axis)
    up = [(i, i + 1) for i in range(devices - 1)]
    return up, [(j, i) for i, j in up]


def on_device(movie, footprints, traces, stripe, column, annulus_gain, decay_slow, decay_fast):
    pix_count = lax.axis_size("pix")
    rows, cols, frames = movie.shape[1:]
    count = footprints.shape[1]
    capacity = max(2, 2 * count // pix_count)
    pix_up, pix_down = neighbours("pix")
    plane_up, plane_down = neighbours("plane")

    near_prev = lax.ppermute(movie[0, rows - NEAR :], "pix", pix_up)
    near_next = lax.ppermute(movie[0, :NEAR], "pix", pix_down)
    marks = jnp.concatenate([stripe[0], column[0][:, None]], axis=1).astype(BF16)
    marks = jnp.pad(marks, ((0, 0), (0, LANES - 2)))
    rest = jnp.concatenate([traces[0], marks], axis=1)
    all_foot = lax.all_gather(footprints[0], "pix", axis=0, tiled=True)
    all_rest = lax.all_gather(rest, "pix", axis=0, tiled=True)

    far_up, far_down, all_foot, all_rest = lax.optimization_barrier(
        (movie[0, rows - RAD : rows - NEAR], movie[0, NEAR:RAD], all_foot, all_rest)
    )
    far_prev = lax.ppermute(far_up, "pix", pix_up)
    far_next = lax.ppermute(far_down, "pix", pix_down)

    inbox = pick(all_foot, all_rest, count, capacity)
    change = change_matrix(frames)
    foot_rows, residual, noise = make_residual(inbox, movie, change)
    near_rows, near_residual, near_noise = make_near(inbox, near_next, near_prev, change)
    noise = jnp.concatenate([near_noise[:NEAR], noise, near_noise[NEAR:]], axis=0)
    noise_before = lax.ppermute(noise, "plane", plane_up)
    noise_after = lax.ppermute(noise, "plane", plane_down)
    pooled = (noise_before + 2.0 * noise + noise_after) / 4.0
    scale = 1.0 / jnp.sqrt(pooled + noise_eps)

    weights = make_weights(foot_rows, near_rows, scale)
    far_model = make_far_model(inbox, cols, frames)

    gain = jnp.broadcast_to((annulus_gain[0] / (8.0 * RAD))[:, None], (cols, LANES))
    background, gradient = make_annulus(
        residual, near_residual, far_prev, far_next, far_model, weights, gain
    )
    home = lax.all_to_all(gradient, "pix", split_axis=0, concat_axis=0, tiled=True)
    foot_f = footprints[0].astype(F32)
    step = 1.0 / (jnp.sum(foot_f * foot_f, axis=1) + norm_eps)
    traces_new = make_traces(
        stripe.reshape(1, count), decay_slow, decay_fast, step[None], traces[0], home, capacity
    )
    return (background, traces_new[None])


def solution(mesh):
    placed = (
        P("plane", "pix", None, None),
        P("plane", "pix", None),
        P("plane", "pix", None),
        P("plane", "pix", None),
        P("plane", "pix"),
        P("plane", None),
        P("plane", "pix"),
        P("plane", "pix"),
    )
    return jax.shard_map(
        on_device,
        mesh=mesh,
        in_specs=placed,
        out_specs=(P("plane", "pix", None, None), P("plane", "pix", None)),
        check_vma=False,
    )
```

```python
import functools

import jax
import jax.numpy as jnp
import ml_dtypes
import numpy as np
from jax import lax
from jax.experimental import pallas as pl
from jax.experimental.pallas import tpu as pltpu
from jax.sharding import PartitionSpec as P

FOOT = 32
RAD = 12
GR = 3
LANES = 128
PER = LANES // FOOT
NEAR = PER

lam_floor = 0.1
noise_eps = 1e-05
norm_eps = 1e-05
sigma_twice = 4.5

F32 = jnp.float32
BF16 = jnp.bfloat16
MIB = 1 << 20
ANY = pl.BlockSpec(memory_space=pl.ANY)
VMEM = pl.BlockSpec(memory_space=pltpu.VMEM)


def tap_values():
    offsets = np.arange(-GR, GR + 1).astype(np.float32)
    raw = np.exp(-offsets * offsets / np.float32(sigma_twice)).astype(np.float32)
    return (raw / raw.sum(dtype=np.float32)).astype(ml_dtypes.bfloat16).astype(np.float32)


def params(mib=16):
    return pltpu.CompilerParams(vmem_limit_bytes=mib * MIB)


def cost(flops, mib):
    return pl.CostEstimate(flops=flops, bytes_accessed=mib * MIB, transcendentals=0)


def dot(a, b):
    return jnp.dot(a, b, preferred_element_type=F32)


def outbox_kernel(capacity, stripe, column, foot, traces, outbox):
    slots = outbox.shape[0]
    count, tiles = foot.shape
    frames = traces.shape[1]
    before = lax.broadcasted_iota(jnp.int32, (count, count), 0) < lax.broadcasted_iota(
        jnp.int32, (count, count), 1
    )
    named = jnp.broadcast_to(stripe[...].astype(F32), (count, count))
    same = (named == named.T) & before
    rank = jnp.sum(jnp.where(same, 1.0, 0.0), axis=0, keepdims=True).astype(jnp.int32)
    slot = stripe[...] * capacity + rank
    place = lax.broadcasted_iota(jnp.int32, (slots, count), 0)
    left = jnp.broadcast_to(column[...].astype(F32), (LANES, count)).T.astype(BF16)
    lane = lax.broadcasted_iota(jnp.int32, (slots, LANES), 1)
    edge = RAD * FOOT
    lefts = jnp.zeros((slots, LANES), F32)
    at = 3 * frames
    for k, (shift, first, width) in enumerate(
        ((0, 0, tiles), (capacity, 0, edge), (-capacity, tiles - edge, edge))
    ):
        hot = jnp.where(place + shift == slot, 1.0, 0.0).astype(BF16)
        outbox[:, k * frames : (k + 1) * frames] = dot(hot, traces[...]).astype(BF16)
        outbox[:, at : at + width] = dot(hot, foot[:, first : first + width]).astype(BF16)
        lefts = jnp.where(lane == k, dot(hot, left), lefts)
        at += width
    outbox[:, at:] = lefts.astype(BF16)


def make_outbox(stripe, column, foot, traces, capacity, slots):
    count, tiles = foot.shape
    frames = traces.shape[1]
    width = 3 * frames + tiles + 2 * RAD * FOOT + LANES
    return pl.pallas_call(
        functools.partial(outbox_kernel, capacity),
        out_shape=jax.ShapeDtypeStruct((slots, width), BF16),
        compiler_params=params(),
        cost_estimate=cost(2 * slots * count * width, 2),
        name="outbox",
    )(stripe, column, foot, traces)


def spread(block, col):
    lane = lax.broadcasted_iota(jnp.int32, block.shape, 1)
    for k in range(7):
        block = jnp.where(((col >> k) & 1) == 1, pltpu.roll(block, 1 << k, 1), block)
    inside = ((lane - col) & (LANES - 1)) < FOOT
    left = inside & (lane >= col)
    right = inside & (lane < col)
    rows = []
    for q in range(PER):
        moved = block if q == 0 else pltpu.roll(block, LANES - q * FOOT, 1)
        rows.append(
            jnp.concatenate(
                [jnp.where(left, moved, 0.0), jnp.where(right, moved, 0.0)], axis=1
            ).astype(BF16)
        )
    return rows


def tile_rows(inbox, which, block, frames):
    lefts = inbox[:, inbox.shape[1] - LANES :].astype(F32)
    col = jnp.broadcast_to(lefts[:, which : which + 1], lefts.shape).astype(jnp.int32)
    start = 3 * frames + block * LANES
    if not isinstance(start, int):
        start = pl.multiple_of(start, LANES)
    return spread(inbox[:, pl.ds(start, LANES)].astype(F32), col)


def model_row(row, inbox, which, frames):
    traces = inbox[:, which * frames : (which + 1) * frames]
    return lax.dot_general(row, traces, (((0,), (0,)), ((), ())), preferred_element_type=F32)


def noise_row(left, change):
    frames = left.shape[1]
    steps = dot(left, change)
    steps = steps * steps
    part = steps[:, 0:LANES]
    for k in range(1, frames // LANES):
        part = part + steps[:, k * LANES : (k + 1) * LANES]
    return jnp.sum(part.T, axis=0, keepdims=True) / (frames - 1)


def change_matrix(frames):
    earlier, later = np.arange(frames)[:, None], np.arange(frames)[None, :]
    steps = (earlier == later + 1).astype(np.float32) - (earlier == later)
    return jnp.asarray(np.where(later < frames - 1, steps, 0.0).astype(ml_dtypes.bfloat16))


def residual_kernel(inbox, movie, change, foot_rows, residual, noise):
    rows, _, frames = movie.shape[1:]

    def group(g, carry):
        noises = []
        for q, row in enumerate(tile_rows(inbox, 0, g, frames)):
            y = g * PER + q
            foot_rows[y] = row
            left = (movie[0, y].astype(F32) - model_row(row, inbox, 0, frames)).astype(BF16)
            residual[y] = left
            noises.append(noise_row(left, change[...]))
        noise[g] = jnp.concatenate(noises, axis=0)
        return carry

    lax.fori_loop(0, rows // PER, group, 0)


def make_residual(inbox, movie, change):
    slots = inbox.shape[0]
    rows, cols, frames = movie.shape[1:]
    foot_rows, residual, noise = pl.pallas_call(
        residual_kernel,
        out_shape=(
            jax.ShapeDtypeStruct((rows, slots, cols), BF16),
            jax.ShapeDtypeStruct((rows, cols, frames), BF16),
            jax.ShapeDtypeStruct((rows // PER, PER, cols), F32),
        ),
        compiler_params=params(),
        cost_estimate=cost(2 * rows * cols * slots * frames, 14),
        name="residual",
    )(inbox, movie, change)
    return foot_rows, residual, noise.reshape(rows, cols)


def near_kernel(inbox, movie_next, movie_prev, change, foot_rows, residual, noise):
    frames = movie_next.shape[2]
    own = FOOT // PER
    for side, (block, movie) in enumerate(
        ((own, movie_next), (own + 2 * RAD // PER - 1, movie_prev))
    ):
        for q, row in enumerate(tile_rows(inbox, 1 + side, block, frames)):
            y = side * NEAR + q
            foot_rows[y] = row
            left = movie[q].astype(F32) - model_row(row, inbox, 1 + side, frames)
            left = left.astype(BF16)
            residual[y] = left
            noise[y : y + 1, :] = noise_row(left, change[...])


def make_near(inbox, movie_next, movie_prev, change):
    slots = inbox.shape[0]
    cols, frames = movie_next.shape[1:]
    return pl.pallas_call(
        near_kernel,
        out_shape=(
            jax.ShapeDtypeStruct((2 * NEAR, slots, cols), BF16),
            jax.ShapeDtypeStruct((2 * NEAR, cols, frames), BF16),
            jax.ShapeDtypeStruct((2 * NEAR, cols), F32),
        ),
        compiler_params=params(),
        cost_estimate=cost(4 * NEAR * cols * slots * frames, 5),
        name="near",
    )(inbox, movie_next, movie_prev, change)


def outer_kernel(inbox, *models):
    frames = models[0].shape[2]
    own = FOOT // PER
    groups = RAD // PER
    for piece, model in enumerate(models, 1):
        for side, block in enumerate((own + piece, own + 2 * groups - 1 - piece)):
            for q, row in enumerate(tile_rows(inbox, 1 + side, block, frames)):
                model[side * PER + q] = model_row(row, inbox, 1 + side, frames)


def make_outer_models(inbox, cols, frames):
    piece = jax.ShapeDtypeStruct((2 * PER, cols, frames), F32)
    return pl.pallas_call(
        outer_kernel,
        out_shape=(piece,) * (RAD // PER - 1),
        compiler_params=params(),
        cost_estimate=cost(4 * RAD * cols * inbox.shape[0] * frames, 5),
        name="outer_models",
    )(inbox)


def weights_kernel(taps, part, own, near, scale, band, out, out_next, out_prev):
    rows, slots, cols = own.shape

    def across(foot, inv):
        scaled = (foot.astype(F32) * inv[:, None, :]).astype(BF16)
        count = foot.shape[0]
        return dot(scaled.reshape(count * part, cols), band[...]).reshape(count, part, cols)

    def some(i, carry):
        these = pl.ds(pl.multiple_of(i * part, part), part)
        blurred = across(own[:, these, :], scale[NEAR : NEAR + rows])
        for r in range(rows):
            total = taps[GR] * blurred[r]
            for k in range(1, GR + 1):
                if r - k >= 0 and r + k < rows:
                    total = total + taps[GR + k] * (blurred[r - k] + blurred[r + k])
                elif r - k >= 0:
                    total = total + taps[GR + k] * blurred[r - k]
                elif r + k < rows:
                    total = total + taps[GR + k] * blurred[r + k]
            out[r, these, :] = total.astype(BF16)
        after = across(near[0:GR, these, :], scale[0:GR])
        ahead = across(near[2 * NEAR - GR : 2 * NEAR, these, :], scale[rows + 2 * NEAR - GR :])
        for a in range(GR):
            total = taps[2 * GR - a] * after[0]
            for r in range(1, a + 1):
                total = total + taps[2 * GR + r - a] * after[r]
            out_next[a, these, :] = total.astype(BF16)
            total = taps[2 * GR] * ahead[a]
            for b in range(a + 1, GR):
                total = total + taps[2 * GR + a - b] * ahead[b]
            out_prev[a, these, :] = total.astype(BF16)
        return carry

    lax.fori_loop(0, slots // part, some, 0)


def make_weights(foot_rows, near_rows, scale):
    rows, slots, cols = foot_rows.shape
    taps = tap_values()
    lag = np.arange(cols)[:, None] - np.arange(cols)[None, :]
    band = np.where(np.abs(lag) <= GR, taps[np.clip(lag + GR, 0, 2 * GR)], 0.0)
    band = jnp.asarray(band.astype(ml_dtypes.bfloat16))
    return pl.pallas_call(
        functools.partial(weights_kernel, [float(t) for t in taps], 32),
        out_shape=(
            jax.ShapeDtypeStruct((rows, slots, cols), BF16),
            jax.ShapeDtypeStruct((GR, slots, cols), BF16),
            jax.ShapeDtypeStruct((GR, slots, cols), BF16),
        ),
        compiler_params=params(),
        cost_estimate=cost(2 * rows * slots * cols * cols, 10),
        name="weights",
    )(foot_rows, near_rows, scale, band)


def annulus_group(g, own, leaving, entering, weight, gain, band, column, total, outgoing):
    cols, frames = own.shape[1:]
    top = lax.broadcasted_iota(jnp.int32, (cols // 8, 8, LANES), 1) < 4
    blank = jnp.zeros((2, 8, LANES), F32)
    outs = [leaving(q) for q in range(PER)]
    news = [entering(q) for q in range(PER)]
    levels = [dot(band, jnp.concatenate([o, n], axis=0)) for o, n in zip(outs, news)]
    column = list(column)
    dets = []
    for q in range(PER):
        det = []
        for h in range(frames // LANES):
            part = slice(h * LANES, (h + 1) * LANES)
            inner = column[h] - outs[q][:, part].astype(F32)
            column[h] = inner + news[q][:, part].astype(F32)
            turned = pltpu.roll(inner.reshape(cols // 8, 8, LANES), 4, 1)
            turned = jnp.concatenate([blank, turned, blank], axis=0)
            both = turned[0 : cols // 8 + 1] + turned[3 : cols // 8 + 4]
            sides = jnp.where(top, both[0 : cols // 8], both[1 : cols // 8 + 1])
            fit = (levels[q][:, part] + sides.reshape(cols, LANES)) * gain
            outgoing[g, q, :, part] = fit.astype(BF16)
            det.append((own[g * PER + q, :, part].astype(F32) - fit).astype(BF16))
        dets.append(jnp.concatenate(det, axis=1))
    weights = jnp.concatenate([weight[g * PER + q] for q in range(PER)], axis=1)
    total = total + dot(weights, jnp.concatenate(dets, axis=0))
    return column, total, dets


def halves(ref):
    return [ref[:, h * LANES : (h + 1) * LANES] for h in range(ref.shape[1] // LANES)]


def add_rows(column, rows, sign=1.0):
    for row in rows:
        column = [c + sign * r.astype(F32) for c, r in zip(column, halves(row))]
    return column


def put(ref, column):
    for h, value in enumerate(column):
        ref[:, h * LANES : (h + 1) * LANES] = value


def subtracted(movie, model, first):
    return [(movie[r].astype(F32) - model[first + r]).astype(BF16) for r in range(PER)]


def sender(outgoing, background, sems):
    def send(g, slot):
        return pltpu.make_async_copy(
            outgoing.at[g], background.at[0, pl.ds(g * PER, PER)], sems.at[slot]
        )

    return send


def middle_kernel(
    own, near, weight, gain, band, background, upper, lower, total, outgoing, sems
):
    rows, cols, frames = own.shape
    first, last = RAD // PER - 1, (rows - RAD) // PER + 1
    send = sender(outgoing, background, sems)
    column = add_rows([jnp.zeros((cols, LANES), F32)] * (frames // LANES), [
        near[NEAR + r] for r in range(NEAR)
    ])
    column = add_rows(column, [own[r] for r in range(RAD + NEAR)])
    put(upper, column)
    column = add_rows(column, [own[RAD + NEAR + r] for r in range(PER)])
    grown = jnp.zeros(total.shape, F32)
    for k, g in enumerate(range(first, last)):
        y = g * PER
        column, grown, _ = annulus_group(
            g,
            own,
            (lambda q: near[NEAR + q]) if g == first else (lambda q: own[y - RAD + q]),
            (lambda q: near[q]) if g == last - 1 else (lambda q: own[y + RAD + q]),
            weight, gain[...], band[...], column, grown, outgoing,
        )
        send(g, k).start()
    put(lower, column)
    total[...] = grown
    for k, g in enumerate(range(first, last)):
        send(g, k).wait()


def mid_kernel(
    own, near, movie_prev, movie_next, model, weight, gain, band, before, upper, lower, total,
    background, new_upper, new_lower, new_total, outgoing, sems,
):
    del before
    rows = own.shape[0]
    low, high = RAD // PER - 2, (rows - RAD) // PER + 1
    send = sender(outgoing, background, sems)
    above, below = subtracted(movie_prev, model, PER), subtracted(movie_next, model, 0)
    column = add_rows(halves(upper), above)
    put(new_upper, add_rows(column, [own[RAD + r] for r in range(PER)], -1.0))
    y = low * PER
    _, grown, _ = annulus_group(
        low, own, lambda q: above[q], lambda q: own[y + RAD + q],
        weight, gain[...], band[...], column, total[...], outgoing,
    )
    send(low, 0).start()
    z = high * PER
    column, grown, _ = annulus_group(
        high, own, lambda q: own[z - RAD + q], lambda q: below[q],
        weight, gain[...], band[...], halves(lower), grown, outgoing,
    )
    send(high, 1).start()
    put(new_lower, column)
    new_total[...] = grown
    send(low, 0).wait()
    send(high, 1).wait()


def end_kernel(
    own, movie_prev, movie_next, model, weight, weight_next, weight_prev, gain, band, before,
    upper, lower, total, background, gradient, outgoing, sems,
):
    del before
    rows, _, frames = own.shape
    low, high = 0, rows // PER - 1
    send = sender(outgoing, background, sems)
    above, below = subtracted(movie_prev, model, PER), subtracted(movie_next, model, 0)
    _, grown, low_dets = annulus_group(
        low, own, lambda q: above[q], lambda q: own[RAD + q],
        weight, gain[...], band[...], add_rows(halves(upper), above), total[...], outgoing,
    )
    send(low, 0).start()
    z = high * PER
    _, grown, high_dets = annulus_group(
        high, own, lambda q: own[z - RAD + q], lambda q: below[q],
        weight, gain[...], band[...], halves(lower), grown, outgoing,
    )
    send(high, 1).start()
    for at, edge, dets in ((2, weight_next, high_dets[PER - GR :]), (3, weight_prev, low_dets[:GR])):
        value = dot(
            jnp.concatenate([edge[a] for a in range(GR)], axis=1), jnp.concatenate(dets, axis=0)
        )
        gradient[:, at * frames : (at + 1) * frames] = value.astype(BF16)
    upper_half = grown.astype(BF16)
    gradient[:, 0:frames] = upper_half
    gradient[:, frames : 2 * frames] = (grown - upper_half.astype(F32)).astype(BF16)
    send(low, 0).wait()
    send(high, 1).wait()


def make_annulus(own, near, movies, models, weights, gain):
    rows, cols, frames = own.shape
    weight, weight_next, weight_prev = weights
    slots = weight.shape[1]
    lag = np.arange(cols)[:, None] - np.arange(cols)[None, :]
    band = (np.abs(lag) <= RAD).astype(ml_dtypes.bfloat16)
    band = jnp.asarray(np.concatenate([band, band], axis=1))
    background = jax.ShapeDtypeStruct((1, rows, cols, frames), BF16)
    column = jax.ShapeDtypeStruct((cols, frames), F32)
    total = jax.ShapeDtypeStruct((slots, frames), F32)
    gradient = jax.ShapeDtypeStruct((slots, 4 * frames), BF16)

    def call(kernel, name, args, outs, done, share):
        specs = [VMEM] * len(args)
        if done is not None:
            specs[done] = ANY
        return pl.pallas_call(
            kernel,
            in_specs=specs,
            out_specs=[ANY] + [VMEM] * (len(outs) - 1),
            out_shape=outs,
            scratch_shapes=[
                pltpu.VMEM((rows // PER, PER, cols, frames), BF16),
                pltpu.SemaphoreType.DMA((rows // PER,)),
            ],
            input_output_aliases={} if done is None else {done: 0},
            compiler_params=params(),
            cost_estimate=cost(6 * rows * cols * cols * frames // share, 20 // share),
            name=name,
        )(*args)

    done, upper, lower, grown = call(
        middle_kernel, "annulus_middle", (own, near, weight, gain, band),
        (background, column, column, total), None, 2,
    )
    done, upper, lower, grown = call(
        mid_kernel, "annulus_mid",
        (own, near, *movies[0], models[0], weight, gain, band, done, upper, lower, grown),
        (background, column, column, total), 8, 4,
    )
    return call(
        end_kernel, "annulus_end",
        (own, *movies[1], models[1], weight, weight_next, weight_prev, gain, band, done, upper,
         lower, grown),
        (background, gradient), 9, 4,
    )


def traces_kernel(capacity, stripe, slow, fast, step, traces, inbox, out):
    count, frames = traces.shape
    slots = inbox.shape[0]

    def upended(row):
        return jnp.broadcast_to(row[...].astype(F32), (LANES, count)).T

    before = lax.broadcasted_iota(jnp.int32, (count, count), 1) < lax.broadcasted_iota(
        jnp.int32, (count, count), 0
    )
    named = upended(stripe)
    same = (named == stripe[...].astype(F32)) & before
    rank = jnp.sum(jnp.where(same, 1.0, 0.0), axis=1, keepdims=True)
    slot = (named[:, 0:1] * capacity + rank).astype(jnp.int32)
    place = lax.broadcasted_iota(jnp.int32, (count, slots), 1)

    def onehot(shift):
        return jnp.where(place + shift == slot, 1.0, 0.0).astype(BF16)

    here = onehot(0)
    gradient = (
        dot(here, inbox[:, 0:frames])
        + dot(here, inbox[:, frames : 2 * frames])
        + dot(onehot(capacity), inbox[:, 2 * frames : 3 * frames])
        + dot(onehot(-capacity), inbox[:, 3 * frames : 4 * frames])
    )

    def wide(row):
        return jnp.concatenate([upended(row)] * (frames // LANES), axis=1)

    updated = traces[...].astype(F32) + wide(step) * gradient
    lane = lax.broadcasted_iota(jnp.int32, (count, frames), 1)

    def lagged(value, lag):
        return jnp.where(lane >= lag, pltpu.roll(value, lag, 1), 0.0)

    a, b = wide(slow), wide(fast)
    driven = updated - (a + b) * lagged(updated, 1) + (a * b) * lagged(updated, 2)
    value = jnp.maximum(driven - lam_floor, 0.0) * ((1.0 - a) * (1.0 - b))
    for root in (a, b):
        lag = 1
        while lag < frames:
            value = value + root * lagged(value, lag)
            root = root * root
            lag *= 2
    out[...] = value


def make_traces(stripe, slow, fast, step, traces, inbox, capacity):
    count, frames = traces.shape
    return pl.pallas_call(
        functools.partial(traces_kernel, capacity),
        out_shape=jax.ShapeDtypeStruct((count, frames), F32),
        compiler_params=params(),
        cost_estimate=cost(10 * count * frames * frames, 1),
        name="traces",
    )(stripe, slow, fast, step, traces, inbox)


def neighbours(axis):
    devices = lax.axis_size(axis)
    up = [(i, i + 1) for i in range(devices - 1)]
    return up, [(j, i) for i, j in up]


def on_device(movie, footprints, traces, stripe, column, annulus_gain, decay_slow, decay_fast):
    pix_count = lax.axis_size("pix")
    rows, cols, frames = movie.shape[1:]
    count = footprints.shape[1]
    capacity = max(2, 2 * count // pix_count)
    slots = pix_count * capacity
    pix_up, pix_down = neighbours("pix")
    plane_up, plane_down = neighbours("plane")

    stripe_row = stripe.reshape(1, count)
    outbox = make_outbox(stripe_row, column, footprints[0], traces[0], capacity, slots)
    inbox = lax.all_to_all(outbox, "pix", split_axis=0, concat_axis=0, tiled=True)
    cuts = [
        (movie[0, rows - (k + 1) * PER : rows - k * PER], movie[0, k * PER : (k + 1) * PER])
        for k in range(RAD // PER)
    ]

    def exchange(cut):
        return (lax.ppermute(cut[0], "pix", pix_up), lax.ppermute(cut[1], "pix", pix_down))

    near = exchange(cuts[0])
    cuts[1], inbox = lax.optimization_barrier((cuts[1], inbox))
    mid = exchange(cuts[1])
    cuts[2], near = lax.optimization_barrier((cuts[2], near))
    far = exchange(cuts[2])
    near_prev, near_next = near

    change = change_matrix(frames)
    foot_rows, residual, noise = make_residual(inbox, movie, change)
    near_rows, near_residual, near_noise = make_near(inbox, near_next, near_prev, change)
    noise = jnp.concatenate([near_noise[:NEAR], noise, near_noise[NEAR:]], axis=0)
    noise_before = lax.ppermute(noise, "plane", plane_up)
    noise_after = lax.ppermute(noise, "plane", plane_down)
    pooled = (noise_before + 2.0 * noise + noise_after) / 4.0
    scale = 1.0 / jnp.sqrt(pooled + noise_eps)

    weights = make_weights(foot_rows, near_rows, scale)
    models = make_outer_models(inbox, cols, frames)

    gain = jnp.broadcast_to((annulus_gain[0] / (8.0 * RAD))[:, None], (cols, LANES))
    background, gradient = make_annulus(
        residual, near_residual, (mid, far), models, weights, gain
    )
    home = lax.all_to_all(gradient, "pix", split_axis=0, concat_axis=0, tiled=True)
    foot_f = footprints[0].astype(F32)
    step = 1.0 / (jnp.sum(foot_f * foot_f, axis=1) + norm_eps)
    traces_new = make_traces(
        stripe_row, decay_slow, decay_fast, step[None], traces[0], home, capacity
    )
    return (background, traces_new[None])


def solution(mesh):
    placed = (
        P("plane", "pix", None, None),
        P("plane", "pix", None),
        P("plane", "pix", None),
        P("plane", "pix", None),
        P("plane", "pix"),
        P("plane", None),
        P("plane", "pix"),
        P("plane", "pix"),
    )
    return jax.shard_map(
        on_device,
        mesh=mesh,
        in_specs=placed,
        out_specs=(P("plane", "pix", None, None), P("plane", "pix", None)),
        check_vma=False,
    )
```

```python
import functools

import jax
import jax.numpy as jnp
import ml_dtypes
import numpy as np
from jax import lax
from jax.experimental import pallas as pl
from jax.experimental.pallas import tpu as pltpu
from jax.sharding import PartitionSpec as P

FOOT = 32
RAD = 12
GR = 3
LANES = 128
PER = LANES // FOOT
NEAR = PER

lam_floor = 0.1
noise_eps = 1e-05
norm_eps = 1e-05
sigma_twice = 4.5

F32 = jnp.float32
BF16 = jnp.bfloat16
MIB = 1 << 20
ANY = pl.BlockSpec(memory_space=pl.ANY)
VMEM = pl.BlockSpec(memory_space=pltpu.VMEM)


def tap_values():
    offsets = np.arange(-GR, GR + 1).astype(np.float32)
    raw = np.exp(-offsets * offsets / np.float32(sigma_twice)).astype(np.float32)
    return (raw / raw.sum(dtype=np.float32)).astype(ml_dtypes.bfloat16).astype(np.float32)


def params(mib=16):
    return pltpu.CompilerParams(vmem_limit_bytes=mib * MIB)


COST = pl.CostEstimate(flops=1, bytes_accessed=1, transcendentals=0)


def dot(a, b):
    return jnp.dot(a, b, preferred_element_type=F32)


def outbox_kernel(capacity, stripe, column, foot, traces, outbox):
    slots = outbox.shape[0]
    count, tiles = foot.shape
    frames = traces.shape[1]
    before = lax.broadcasted_iota(jnp.int32, (count, count), 0) < lax.broadcasted_iota(
        jnp.int32, (count, count), 1
    )
    named = jnp.broadcast_to(stripe[...].astype(F32), (count, count))
    same = (named == named.T) & before
    rank = jnp.sum(jnp.where(same, 1.0, 0.0), axis=0, keepdims=True).astype(jnp.int32)
    slot = stripe[...] * capacity + rank
    place = lax.broadcasted_iota(jnp.int32, (slots, count), 0)
    left = jnp.broadcast_to(column[...].astype(F32), (LANES, count)).T.astype(BF16)
    lane = lax.broadcasted_iota(jnp.int32, (slots, LANES), 1)
    edge = RAD * FOOT
    lefts = jnp.zeros((slots, LANES), F32)
    at = 3 * frames
    for k, (shift, first, width) in enumerate(
        ((0, 0, tiles), (capacity, 0, edge), (-capacity, tiles - edge, edge))
    ):
        hot = jnp.where(place + shift == slot, 1.0, 0.0).astype(BF16)
        outbox[:, k * frames : (k + 1) * frames] = dot(hot, traces[...]).astype(BF16)
        outbox[:, at : at + width] = dot(hot, foot[:, first : first + width]).astype(BF16)
        lefts = jnp.where(lane == k, dot(hot, left), lefts)
        at += width
    outbox[:, at:] = lefts.astype(BF16)


def make_outbox(stripe, column, foot, traces, capacity, slots):
    count, tiles = foot.shape
    frames = traces.shape[1]
    width = 3 * frames + tiles + 2 * RAD * FOOT + LANES
    return pl.pallas_call(
        functools.partial(outbox_kernel, capacity),
        out_shape=jax.ShapeDtypeStruct((slots, width), BF16),
        compiler_params=params(),
        cost_estimate=COST,
        name="outbox",
    )(stripe, column, foot, traces)


def spread(block, col):
    lane = lax.broadcasted_iota(jnp.int32, block.shape, 1)
    for k in range(7):
        block = jnp.where(((col >> k) & 1) == 1, pltpu.roll(block, 1 << k, 1), block)
    inside = ((lane - col) & (LANES - 1)) < FOOT
    left = inside & (lane >= col)
    right = inside & (lane < col)
    rows = []
    for q in range(PER):
        moved = block if q == 0 else pltpu.roll(block, LANES - q * FOOT, 1)
        rows.append(
            jnp.concatenate(
                [jnp.where(left, moved, 0.0), jnp.where(right, moved, 0.0)], axis=1
            ).astype(BF16)
        )
    return rows


def tile_rows(inbox, which, block, frames):
    lefts = inbox[:, inbox.shape[1] - LANES :].astype(F32)
    col = jnp.broadcast_to(lefts[:, which : which + 1], lefts.shape).astype(jnp.int32)
    start = 3 * frames + block * LANES
    if not isinstance(start, int):
        start = pl.multiple_of(start, LANES)
    return spread(inbox[:, pl.ds(start, LANES)].astype(F32), col)


def model_row(row, inbox, which, frames):
    traces = inbox[:, which * frames : (which + 1) * frames]
    return lax.dot_general(row, traces, (((0,), (0,)), ((), ())), preferred_element_type=F32)


def noise_row(left, change):
    frames = left.shape[1]
    steps = dot(left, change)
    steps = steps * steps
    part = steps[:, 0:LANES]
    for k in range(1, frames // LANES):
        part = part + steps[:, k * LANES : (k + 1) * LANES]
    return jnp.sum(part.T, axis=0, keepdims=True) / (frames - 1)


def change_matrix(frames):
    earlier, later = np.arange(frames)[:, None], np.arange(frames)[None, :]
    steps = (earlier == later + 1).astype(np.float32) - (earlier == later)
    return jnp.asarray(np.where(later < frames - 1, steps, 0.0).astype(ml_dtypes.bfloat16))


def residual_kernel(inbox, movie, change, foot_rows, residual, noise):
    rows, _, frames = movie.shape[1:]

    def group(g, carry):
        noises = []
        for q, row in enumerate(tile_rows(inbox, 0, g, frames)):
            y = g * PER + q
            foot_rows[y] = row
            left = (movie[0, y].astype(F32) - model_row(row, inbox, 0, frames)).astype(BF16)
            residual[y] = left
            noises.append(noise_row(left, change[...]))
        noise[g] = jnp.concatenate(noises, axis=0)
        return carry

    lax.fori_loop(0, rows // PER, group, 0)


def make_residual(inbox, movie, change):
    slots = inbox.shape[0]
    rows, cols, frames = movie.shape[1:]
    foot_rows, residual, noise = pl.pallas_call(
        residual_kernel,
        out_shape=(
            jax.ShapeDtypeStruct((rows, slots, cols), BF16),
            jax.ShapeDtypeStruct((rows, cols, frames), BF16),
            jax.ShapeDtypeStruct((rows // PER, PER, cols), F32),
        ),
        compiler_params=params(),
        cost_estimate=COST,
        name="residual",
    )(inbox, movie, change)
    return foot_rows, residual, noise.reshape(rows, cols)


def near_kernel(inbox, movie_next, movie_prev, change, foot_rows, residual, noise):
    frames = movie_next.shape[2]
    own = FOOT // PER
    for side, (block, movie) in enumerate(
        ((own, movie_next), (own + 2 * RAD // PER - 1, movie_prev))
    ):
        for q, row in enumerate(tile_rows(inbox, 1 + side, block, frames)):
            y = side * NEAR + q
            foot_rows[y] = row
            left = movie[q].astype(F32) - model_row(row, inbox, 1 + side, frames)
            left = left.astype(BF16)
            residual[y] = left
            noise[y : y + 1, :] = noise_row(left, change[...])


def make_near(inbox, movie_next, movie_prev, change):
    slots = inbox.shape[0]
    cols, frames = movie_next.shape[1:]
    return pl.pallas_call(
        near_kernel,
        out_shape=(
            jax.ShapeDtypeStruct((2 * NEAR, slots, cols), BF16),
            jax.ShapeDtypeStruct((2 * NEAR, cols, frames), BF16),
            jax.ShapeDtypeStruct((2 * NEAR, cols), F32),
        ),
        compiler_params=params(),
        cost_estimate=COST,
        name="near",
    )(inbox, movie_next, movie_prev, change)


def outer_kernel(inbox, *models):
    frames = models[0].shape[2]
    own = FOOT // PER
    groups = RAD // PER
    for piece, model in enumerate(models, 1):
        for side, block in enumerate((own + piece, own + 2 * groups - 1 - piece)):
            for q, row in enumerate(tile_rows(inbox, 1 + side, block, frames)):
                model[side * PER + q] = model_row(row, inbox, 1 + side, frames)


def make_outer_models(inbox, cols, frames):
    piece = jax.ShapeDtypeStruct((2 * PER, cols, frames), F32)
    return pl.pallas_call(
        outer_kernel,
        out_shape=(piece,) * (RAD // PER - 1),
        compiler_params=params(),
        cost_estimate=COST,
        name="outer_models",
    )(inbox)


def weights_kernel(taps, part, own, near, scale, band, out, out_next, out_prev):
    rows, slots, cols = own.shape

    def across(foot, inv):
        scaled = (foot.astype(F32) * inv[:, None, :]).astype(BF16)
        count = foot.shape[0]
        return dot(scaled.reshape(count * part, cols), band[...]).reshape(count, part, cols)

    def some(i, carry):
        these = pl.ds(pl.multiple_of(i * part, part), part)
        blurred = across(own[:, these, :], scale[NEAR : NEAR + rows])
        for r in range(rows):
            total = taps[GR] * blurred[r]
            for k in range(1, GR + 1):
                if r - k >= 0 and r + k < rows:
                    total = total + taps[GR + k] * (blurred[r - k] + blurred[r + k])
                elif r - k >= 0:
                    total = total + taps[GR + k] * blurred[r - k]
                elif r + k < rows:
                    total = total + taps[GR + k] * blurred[r + k]
            out[r, these, :] = total.astype(BF16)
        after = across(near[0:GR, these, :], scale[0:GR])
        ahead = across(near[2 * NEAR - GR : 2 * NEAR, these, :], scale[rows + 2 * NEAR - GR :])
        for a in range(GR):
            total = taps[2 * GR - a] * after[0]
            for r in range(1, a + 1):
                total = total + taps[2 * GR + r - a] * after[r]
            out_next[a, these, :] = total.astype(BF16)
            total = taps[2 * GR] * ahead[a]
            for b in range(a + 1, GR):
                total = total + taps[2 * GR + a - b] * ahead[b]
            out_prev[a, these, :] = total.astype(BF16)
        return carry

    lax.fori_loop(0, slots // part, some, 0)


def make_weights(foot_rows, near_rows, scale):
    rows, slots, cols = foot_rows.shape
    taps = tap_values()
    lag = np.arange(cols)[:, None] - np.arange(cols)[None, :]
    band = np.where(np.abs(lag) <= GR, taps[np.clip(lag + GR, 0, 2 * GR)], 0.0)
    band = jnp.asarray(band.astype(ml_dtypes.bfloat16))
    return pl.pallas_call(
        functools.partial(weights_kernel, [float(t) for t in taps], 32),
        out_shape=(
            jax.ShapeDtypeStruct((rows, slots, cols), BF16),
            jax.ShapeDtypeStruct((GR, slots, cols), BF16),
            jax.ShapeDtypeStruct((GR, slots, cols), BF16),
        ),
        compiler_params=params(),
        cost_estimate=COST,
        name="weights",
    )(foot_rows, near_rows, scale, band)


def annulus_group(g, own, leaving, entering, weight, gain, band, column, total, outgoing):
    cols, frames = own.shape[1:]
    top = lax.broadcasted_iota(jnp.int32, (cols // 8, 8, LANES), 1) < 4
    blank = jnp.zeros((2, 8, LANES), F32)
    outs = [leaving(q) for q in range(PER)]
    news = [entering(q) for q in range(PER)]
    levels = [dot(band, jnp.concatenate([o, n], axis=0)) for o, n in zip(outs, news)]
    column = list(column)
    dets = []
    for q in range(PER):
        det = []
        for h in range(frames // LANES):
            part = slice(h * LANES, (h + 1) * LANES)
            inner = column[h] - outs[q][:, part].astype(F32)
            column[h] = inner + news[q][:, part].astype(F32)
            turned = pltpu.roll(inner.reshape(cols // 8, 8, LANES), 4, 1)
            turned = jnp.concatenate([blank, turned, blank], axis=0)
            both = turned[0 : cols // 8 + 1] + turned[3 : cols // 8 + 4]
            sides = jnp.where(top, both[0 : cols // 8], both[1 : cols // 8 + 1])
            fit = (levels[q][:, part] + sides.reshape(cols, LANES)) * gain
            outgoing[g, q, :, part] = fit.astype(BF16)
            det.append((own[g * PER + q, :, part].astype(F32) - fit).astype(BF16))
        dets.append(jnp.concatenate(det, axis=1))
    weights = jnp.concatenate([weight[g * PER + q] for q in range(PER)], axis=1)
    total = total + dot(weights, jnp.concatenate(dets, axis=0))
    return column, total, dets


def halves(ref):
    return [ref[:, h * LANES : (h + 1) * LANES] for h in range(ref.shape[1] // LANES)]


def add_rows(column, rows, sign=1.0):
    for row in rows:
        column = [c + sign * r.astype(F32) for c, r in zip(column, halves(row))]
    return column


def put(ref, column):
    for h, value in enumerate(column):
        ref[:, h * LANES : (h + 1) * LANES] = value


def subtracted(movie, model, first):
    return [(movie[r].astype(F32) - model[first + r]).astype(BF16) for r in range(PER)]


def sender(outgoing, background, sems):
    def send(g, slot):
        return pltpu.make_async_copy(
            outgoing.at[g], background.at[0, pl.ds(g * PER, PER)], sems.at[slot]
        )

    return send


def middle_kernel(
    own, near, weight, gain, band, background, upper, lower, total, outgoing, sems
):
    rows, cols, frames = own.shape
    first, last = RAD // PER - 1, (rows - RAD) // PER + 1
    send = sender(outgoing, background, sems)
    column = add_rows([jnp.zeros((cols, LANES), F32)] * (frames // LANES), [
        near[NEAR + r] for r in range(NEAR)
    ])
    column = add_rows(column, [own[r] for r in range(RAD + NEAR)])
    put(upper, column)
    column = add_rows(column, [own[RAD + NEAR + r] for r in range(PER)])
    grown = jnp.zeros(total.shape, F32)
    for k, g in enumerate(range(first, last)):
        y = g * PER
        column, grown, _ = annulus_group(
            g,
            own,
            (lambda q: near[NEAR + q]) if g == first else (lambda q: own[y - RAD + q]),
            (lambda q: near[q]) if g == last - 1 else (lambda q: own[y + RAD + q]),
            weight, gain[...], band[...], column, grown, outgoing,
        )
        send(g, k).start()
    put(lower, column)
    total[...] = grown
    for k, g in enumerate(range(first, last)):
        send(g, k).wait()


def mid_kernel(
    own, near, movie_prev, movie_next, model, weight, gain, band, before, upper, lower, total,
    background, new_upper, new_lower, new_total, outgoing, sems,
):
    del before
    rows = own.shape[0]
    low, high = RAD // PER - 2, (rows - RAD) // PER + 1
    send = sender(outgoing, background, sems)
    above, below = subtracted(movie_prev, model, PER), subtracted(movie_next, model, 0)
    column = add_rows(halves(upper), above)
    put(new_upper, add_rows(column, [own[RAD + r] for r in range(PER)], -1.0))
    y = low * PER
    _, grown, _ = annulus_group(
        low, own, lambda q: above[q], lambda q: own[y + RAD + q],
        weight, gain[...], band[...], column, total[...], outgoing,
    )
    send(low, 0).start()
    z = high * PER
    column, grown, _ = annulus_group(
        high, own, lambda q: own[z - RAD + q], lambda q: below[q],
        weight, gain[...], band[...], halves(lower), grown, outgoing,
    )
    send(high, 1).start()
    put(new_lower, column)
    new_total[...] = grown
    send(low, 0).wait()
    send(high, 1).wait()


def end_kernel(
    own, movie_prev, movie_next, model, weight, weight_next, weight_prev, gain, band, before,
    upper, lower, total, background, gradient, outgoing, sems,
):
    del before
    rows, _, frames = own.shape
    low, high = 0, rows // PER - 1
    send = sender(outgoing, background, sems)
    above, below = subtracted(movie_prev, model, PER), subtracted(movie_next, model, 0)
    _, grown, low_dets = annulus_group(
        low, own, lambda q: above[q], lambda q: own[RAD + q],
        weight, gain[...], band[...], add_rows(halves(upper), above), total[...], outgoing,
    )
    send(low, 0).start()
    z = high * PER
    _, grown, high_dets = annulus_group(
        high, own, lambda q: own[z - RAD + q], lambda q: below[q],
        weight, gain[...], band[...], halves(lower), grown, outgoing,
    )
    send(high, 1).start()
    for at, edge, dets in ((2, weight_next, high_dets[PER - GR :]), (3, weight_prev, low_dets[:GR])):
        value = dot(
            jnp.concatenate([edge[a] for a in range(GR)], axis=1), jnp.concatenate(dets, axis=0)
        )
        gradient[:, at * frames : (at + 1) * frames] = value.astype(BF16)
    upper_half = grown.astype(BF16)
    gradient[:, 0:frames] = upper_half
    gradient[:, frames : 2 * frames] = (grown - upper_half.astype(F32)).astype(BF16)
    send(low, 0).wait()
    send(high, 1).wait()


def make_annulus(own, near, movies, models, weights, gain):
    rows, cols, frames = own.shape
    weight, weight_next, weight_prev = weights
    slots = weight.shape[1]
    lag = np.arange(cols)[:, None] - np.arange(cols)[None, :]
    band = (np.abs(lag) <= RAD).astype(ml_dtypes.bfloat16)
    band = jnp.asarray(np.concatenate([band, band], axis=1))
    background = jax.ShapeDtypeStruct((1, rows, cols, frames), BF16)
    column = jax.ShapeDtypeStruct((cols, frames), F32)
    total = jax.ShapeDtypeStruct((slots, frames), F32)
    gradient = jax.ShapeDtypeStruct((slots, 4 * frames), BF16)

    def call(kernel, name, args, outs, done):
        specs = [VMEM] * len(args)
        if done is not None:
            specs[done] = ANY
        return pl.pallas_call(
            kernel,
            in_specs=specs,
            out_specs=[ANY] + [VMEM] * (len(outs) - 1),
            out_shape=outs,
            scratch_shapes=[
                pltpu.VMEM((rows // PER, PER, cols, frames), BF16),
                pltpu.SemaphoreType.DMA((rows // PER,)),
            ],
            input_output_aliases={} if done is None else {done: 0},
            compiler_params=params(),
            cost_estimate=COST,
            name=name,
        )(*args)

    done, upper, lower, grown = call(
        middle_kernel, "annulus_middle", (own, near, weight, gain, band),
        (background, column, column, total), None,
    )
    done, upper, lower, grown = call(
        mid_kernel, "annulus_mid",
        (own, near, *movies[0], models[0], weight, gain, band, done, upper, lower, grown),
        (background, column, column, total), 8,
    )
    return call(
        end_kernel, "annulus_end",
        (own, *movies[1], models[1], weight, weight_next, weight_prev, gain, band, done, upper,
         lower, grown),
        (background, gradient), 9,
    )


def traces_kernel(capacity, stripe, slow, fast, step, traces, inbox, out):
    count, frames = traces.shape
    slots = inbox.shape[0]

    def upended(row):
        return jnp.broadcast_to(row[...].astype(F32), (LANES, count)).T

    before = lax.broadcasted_iota(jnp.int32, (count, count), 1) < lax.broadcasted_iota(
        jnp.int32, (count, count), 0
    )
    named = upended(stripe)
    same = (named == stripe[...].astype(F32)) & before
    rank = jnp.sum(jnp.where(same, 1.0, 0.0), axis=1, keepdims=True)
    slot = (named[:, 0:1] * capacity + rank).astype(jnp.int32)
    place = lax.broadcasted_iota(jnp.int32, (count, slots), 1)

    def onehot(shift):
        return jnp.where(place + shift == slot, 1.0, 0.0).astype(BF16)

    here = onehot(0)
    gradient = (
        dot(here, inbox[:, 0:frames])
        + dot(here, inbox[:, frames : 2 * frames])
        + dot(onehot(capacity), inbox[:, 2 * frames : 3 * frames])
        + dot(onehot(-capacity), inbox[:, 3 * frames : 4 * frames])
    )

    def wide(row):
        return jnp.concatenate([upended(row)] * (frames // LANES), axis=1)

    updated = traces[...].astype(F32) + wide(step) * gradient
    lane = lax.broadcasted_iota(jnp.int32, (count, frames), 1)

    def lagged(value, lag):
        return jnp.where(lane >= lag, pltpu.roll(value, lag, 1), 0.0)

    a, b = wide(slow), wide(fast)
    driven = updated - (a + b) * lagged(updated, 1) + (a * b) * lagged(updated, 2)
    value = jnp.maximum(driven - lam_floor, 0.0) * ((1.0 - a) * (1.0 - b))
    for root in (a, b):
        lag = 1
        while lag < frames:
            value = value + root * lagged(value, lag)
            root = root * root
            lag *= 2
    out[...] = value


def make_traces(stripe, slow, fast, step, traces, inbox, capacity):
    count, frames = traces.shape
    return pl.pallas_call(
        functools.partial(traces_kernel, capacity),
        out_shape=jax.ShapeDtypeStruct((count, frames), F32),
        compiler_params=params(),
        cost_estimate=COST,
        name="traces",
    )(stripe, slow, fast, step, traces, inbox)


def neighbours(axis):
    devices = lax.axis_size(axis)
    up = [(i, i + 1) for i in range(devices - 1)]
    return up, [(j, i) for i, j in up]


def on_device(movie, footprints, traces, stripe, column, annulus_gain, decay_slow, decay_fast):
    pix_count = lax.axis_size("pix")
    rows, cols, frames = movie.shape[1:]
    count = footprints.shape[1]
    capacity = max(2, 2 * count // pix_count)
    slots = pix_count * capacity
    pix_up, pix_down = neighbours("pix")
    plane_up, plane_down = neighbours("plane")

    stripe_row = stripe.reshape(1, count)
    outbox = make_outbox(stripe_row, column, footprints[0], traces[0], capacity, slots)
    cuts = [
        (movie[0, rows - (k + 1) * PER : rows - k * PER], movie[0, k * PER : (k + 1) * PER])
        for k in range(RAD // PER)
    ]

    cuts[1:], outbox = lax.optimization_barrier((cuts[1:], outbox))
    inbox = lax.all_to_all(outbox, "pix", split_axis=0, concat_axis=0, tiled=True)

    def exchange(cut):
        return (lax.ppermute(cut[0], "pix", pix_up), lax.ppermute(cut[1], "pix", pix_down))

    near_prev, near_next = exchange(cuts[0])
    mid, far = exchange(cuts[1]), exchange(cuts[2])

    change = change_matrix(frames)
    foot_rows, residual, noise = make_residual(inbox, movie, change)
    near_rows, near_residual, near_noise = make_near(inbox, near_next, near_prev, change)
    noise = jnp.concatenate([near_noise[:NEAR], noise, near_noise[NEAR:]], axis=0)
    noise_before = lax.ppermute(noise, "plane", plane_up)
    noise_after = lax.ppermute(noise, "plane", plane_down)
    pooled = (noise_before + 2.0 * noise + noise_after) / 4.0
    scale = 1.0 / jnp.sqrt(pooled + noise_eps)

    weights = make_weights(foot_rows, near_rows, scale)
    models = make_outer_models(inbox, cols, frames)

    gain = jnp.broadcast_to((annulus_gain[0] / (8.0 * RAD))[:, None], (cols, LANES))
    background, gradient = make_annulus(
        residual, near_residual, (mid, far), models, weights, gain
    )
    home = lax.all_to_all(gradient, "pix", split_axis=0, concat_axis=0, tiled=True)
    foot_f = footprints[0].astype(F32)
    step = 1.0 / (jnp.sum(foot_f * foot_f, axis=1) + norm_eps)
    traces_new = make_traces(
        stripe_row, decay_slow, decay_fast, step[None], traces[0], home, capacity
    )
    return (background, traces_new[None])


def solution(mesh):
    placed = (
        P("plane", "pix", None, None),
        P("plane", "pix", None),
        P("plane", "pix", None),
        P("plane", "pix", None),
        P("plane", "pix"),
        P("plane", None),
        P("plane", "pix"),
        P("plane", "pix"),
    )
    return jax.shard_map(
        on_device,
        mesh=mesh,
        in_specs=placed,
        out_specs=(P("plane", "pix", None, None), P("plane", "pix", None)),
        check_vma=False,
    )
```

```python
import functools

import jax
import jax.numpy as jnp
import ml_dtypes
import numpy as np
from jax import lax
from jax.experimental import pallas as pl
from jax.experimental.pallas import tpu as pltpu
from jax.sharding import PartitionSpec as P

FOOT = 32
RAD = 12
GR = 3
LANES = 128
PER = LANES // FOOT
NEAR = PER

lam_floor = 0.1
noise_eps = 1e-05
norm_eps = 1e-05
sigma_twice = 4.5

F32 = jnp.float32
BF16 = jnp.bfloat16
MIB = 1 << 20
HBM = pl.BlockSpec(memory_space=pltpu.HBM)
VMEM = pl.BlockSpec(memory_space=pltpu.VMEM)


def tap_values():
    offsets = np.arange(-GR, GR + 1).astype(np.float32)
    raw = np.exp(-offsets * offsets / np.float32(sigma_twice)).astype(np.float32)
    return (raw / raw.sum(dtype=np.float32)).astype(ml_dtypes.bfloat16).astype(np.float32)


def params(mib=16):
    return pltpu.CompilerParams(vmem_limit_bytes=mib * MIB)


COST = pl.CostEstimate(flops=1, bytes_accessed=1, transcendentals=0)


def dot(a, b):
    return jnp.dot(a, b, preferred_element_type=F32)


def outbox_kernel(capacity, *refs):
    sources, outbox, places, sems = refs[0:4], refs[4], refs[5:9], refs[9]
    copies = [
        pltpu.make_async_copy(source, place, sems.at[k])
        for k, (source, place) in enumerate(zip(sources, places))
    ]
    for copy in copies:
        copy.start()
    for copy in copies:
        copy.wait()
    stripe, column, foot, traces = places
    slots = outbox.shape[0]
    count, tiles = foot.shape
    frames = traces.shape[1]
    before = lax.broadcasted_iota(jnp.int32, (count, count), 0) < lax.broadcasted_iota(
        jnp.int32, (count, count), 1
    )
    named = jnp.broadcast_to(stripe[...].astype(F32), (count, count))
    same = (named == named.T) & before
    rank = jnp.sum(jnp.where(same, 1.0, 0.0), axis=0, keepdims=True).astype(jnp.int32)
    slot = stripe[...] * capacity + rank
    place = lax.broadcasted_iota(jnp.int32, (slots, count), 0)
    left = jnp.broadcast_to(column[...].astype(F32), (LANES, count)).T.astype(BF16)
    lane = lax.broadcasted_iota(jnp.int32, (slots, LANES), 1)
    edge = RAD * FOOT
    lefts = jnp.zeros((slots, LANES), F32)
    at = 3 * frames
    for k, (shift, first, width) in enumerate(
        ((0, 0, tiles), (capacity, 0, edge), (-capacity, tiles - edge, edge))
    ):
        hot = jnp.where(place + shift == slot, 1.0, 0.0).astype(BF16)
        outbox[:, k * frames : (k + 1) * frames] = dot(hot, traces[...]).astype(BF16)
        outbox[:, at : at + width] = dot(hot, foot[:, first : first + width]).astype(BF16)
        lefts = jnp.where(lane == k, dot(hot, left), lefts)
        at += width
    outbox[:, at:] = lefts.astype(BF16)


def make_outbox(stripe, column, foot, traces, capacity, slots):
    count, tiles = foot.shape
    frames = traces.shape[1]
    width = 3 * frames + tiles + 2 * RAD * FOOT + LANES
    args = (stripe, column, foot, traces)
    return pl.pallas_call(
        functools.partial(outbox_kernel, capacity),
        in_specs=[HBM] * len(args),
        out_shape=jax.ShapeDtypeStruct((slots, width), BF16),
        scratch_shapes=[pltpu.VMEM(a.shape, a.dtype) for a in args]
        + [pltpu.SemaphoreType.DMA((len(args),))],
        compiler_params=params(56),
        cost_estimate=COST,
        name="outbox",
    )(*args)


def spread(block, col):
    lane = lax.broadcasted_iota(jnp.int32, block.shape, 1)
    for k in range(7):
        block = jnp.where(((col >> k) & 1) == 1, pltpu.roll(block, 1 << k, 1), block)
    inside = ((lane - col) & (LANES - 1)) < FOOT
    left = inside & (lane >= col)
    right = inside & (lane < col)
    rows = []
    for q in range(PER):
        moved = block if q == 0 else pltpu.roll(block, LANES - q * FOOT, 1)
        rows.append(
            jnp.concatenate(
                [jnp.where(left, moved, 0.0), jnp.where(right, moved, 0.0)], axis=1
            ).astype(BF16)
        )
    return rows


def tile_rows(inbox, which, block, frames):
    lefts = inbox[:, inbox.shape[1] - LANES :].astype(F32)
    col = jnp.broadcast_to(lefts[:, which : which + 1], lefts.shape).astype(jnp.int32)
    start = 3 * frames + block * LANES
    if not isinstance(start, int):
        start = pl.multiple_of(start, LANES)
    return spread(inbox[:, pl.ds(start, LANES)].astype(F32), col)


def model_row(row, inbox, which, frames):
    traces = inbox[:, which * frames : (which + 1) * frames]
    return lax.dot_general(row, traces, (((0,), (0,)), ((), ())), preferred_element_type=F32)


def noise_row(left, change):
    frames = left.shape[1]
    steps = dot(left, change)
    steps = steps * steps
    part = steps[:, 0:LANES]
    for k in range(1, frames // LANES):
        part = part + steps[:, k * LANES : (k + 1) * LANES]
    return jnp.sum(part.T, axis=0, keepdims=True) / (frames - 1)


def lag_table(size):
    shape = (size, size)
    return lax.broadcasted_iota(jnp.int32, shape, 1) - lax.broadcasted_iota(jnp.int32, shape, 0)


def change_matrix(frames):
    lag = lag_table(frames)
    steps = jnp.where(lag == -1, 1.0, 0.0) - jnp.where(lag == 0, 1.0, 0.0)
    later = lax.broadcasted_iota(jnp.int32, lag.shape, 1)
    return jnp.where(later < frames - 1, steps, 0.0).astype(BF16)


def residual_kernel(
    inbox, movie, foot_rows, residual, noise, change, movie_slots, foot_slots, left_slots, sems
):
    rows, _, frames = movie.shape[1:]
    groups = rows // PER
    change[...] = change_matrix(frames)

    def fetch(g, slot):
        rows_g = pl.ds(g * PER, PER)
        return pltpu.make_async_copy(movie.at[0, rows_g], movie_slots.at[slot], sems.at[0, slot])

    def sends(g, slot):
        rows_g = pl.ds(g * PER, PER)
        return (
            pltpu.make_async_copy(foot_slots.at[slot], foot_rows.at[rows_g], sems.at[1, slot]),
            pltpu.make_async_copy(left_slots.at[slot], residual.at[rows_g], sems.at[2, slot]),
        )

    fetch(0, 0).start()

    def group(g, carry):
        slot = lax.rem(g, 2)

        @pl.when(g + 1 < groups)
        def _():
            fetch(g + 1, 1 - slot).start()

        fetch(g, slot).wait()

        @pl.when(g >= 2)
        def _():
            for copy in sends(g - 2, slot):
                copy.wait()

        noises = []
        for q, row in enumerate(tile_rows(inbox, 0, g, frames)):
            foot_slots[slot, q] = row
            left = movie_slots[slot, q].astype(F32) - model_row(row, inbox, 0, frames)
            left = left.astype(BF16)
            left_slots[slot, q] = left
            noises.append(noise_row(left, change[...]))
        noise[g] = jnp.concatenate(noises, axis=0)
        for copy in sends(g, slot):
            copy.start()
        return carry

    lax.fori_loop(0, groups, group, 0)
    for g in (groups - 2, groups - 1):
        for copy in sends(g, g % 2):
            copy.wait()


def make_residual(inbox, movie):
    slots = inbox.shape[0]
    rows, cols, frames = movie.shape[1:]
    return pl.pallas_call(
        residual_kernel,
        in_specs=[VMEM, HBM],
        out_specs=[HBM, HBM, VMEM],
        out_shape=(
            jax.ShapeDtypeStruct((rows, slots, cols), BF16),
            jax.ShapeDtypeStruct((rows, cols, frames), BF16),
            jax.ShapeDtypeStruct((rows // PER, PER, cols), F32),
        ),
        scratch_shapes=[
            pltpu.VMEM((frames, frames), BF16),
            pltpu.VMEM((2, PER, cols, frames), BF16),
            pltpu.VMEM((2, PER, slots, cols), BF16),
            pltpu.VMEM((2, PER, cols, frames), BF16),
            pltpu.SemaphoreType.DMA((3, 2)),
        ],
        compiler_params=params(44),
        cost_estimate=COST,
        name="residual",
    )(inbox, movie)


def near_kernel(inbox, movie_next, movie_prev, own_noise, foot_rows, residual, noise):
    frames = movie_next.shape[2]
    groups = own_noise.shape[0]
    own = FOOT // PER
    change = change_matrix(frames)
    for g in range(groups):
        noise[NEAR + g * PER : NEAR + (g + 1) * PER, :] = own_noise[g]
    for side, (block, movie, first) in enumerate(
        ((own, movie_next, 0), (own + 2 * RAD // PER - 1, movie_prev, NEAR + groups * PER))
    ):
        for q, row in enumerate(tile_rows(inbox, 1 + side, block, frames)):
            y = side * NEAR + q
            foot_rows[y] = row
            left = movie[q].astype(F32) - model_row(row, inbox, 1 + side, frames)
            left = left.astype(BF16)
            residual[y] = left
            noise[first + q : first + q + 1, :] = noise_row(left, change)


def make_near(inbox, movie_next, movie_prev, noise):
    slots = inbox.shape[0]
    groups, per, _ = noise.shape
    cols, frames = movie_next.shape[1:]
    return pl.pallas_call(
        near_kernel,
        out_shape=(
            jax.ShapeDtypeStruct((2 * NEAR, slots, cols), BF16),
            jax.ShapeDtypeStruct((2 * NEAR, cols, frames), BF16),
            jax.ShapeDtypeStruct((2 * NEAR + groups * per, cols), F32),
        ),
        compiler_params=params(),
        cost_estimate=COST,
        name="near",
    )(inbox, movie_next, movie_prev, noise)


def outer_kernel(inbox, model):
    frames = model.shape[2]
    first = (FOOT + NEAR) // PER
    groups = (RAD - NEAR) // PER
    for side in range(2):
        for g in range(groups):
            k = side * groups + g
            for q, row in enumerate(tile_rows(inbox, 1 + side, first + k, frames)):
                model[k * PER + q] = model_row(row, inbox, 1 + side, frames)


def make_outer_model(inbox, cols, frames):
    return pl.pallas_call(
        outer_kernel,
        out_shape=jax.ShapeDtypeStruct((2 * (RAD - NEAR), cols, frames), F32),
        compiler_params=params(),
        cost_estimate=COST,
        name="outer_model",
    )(inbox)


def weights_kernel(
    taps, own, near, noise, noise_before, noise_after, out, out_next, out_prev,
    own_slots, scale, band, sems,
):
    rows, slots, cols = own.shape
    part = own_slots.shape[2]
    count = slots // part

    def fetch(i, slot):
        these = pl.ds(pl.multiple_of(i * part, part), part)
        return pltpu.make_async_copy(own.at[:, these, :], own_slots.at[slot], sems.at[slot])

    fetch(0, 0).start()
    pooled = (noise_before[...] + 2.0 * noise[...] + noise_after[...]) / 4.0
    scale[...] = 1.0 / jnp.sqrt(pooled + noise_eps)
    lag = jnp.abs(lag_table(cols))
    table = jnp.zeros(lag.shape, F32)
    for k in range(GR + 1):
        table = jnp.where(lag == k, taps[GR + k], table)
    band[...] = table.astype(BF16)

    def across(foot, inv):
        scaled = (foot.astype(F32) * inv[:, None, :]).astype(BF16)
        count = foot.shape[0]
        return dot(scaled.reshape(count * part, cols), band[...]).reshape(count, part, cols)

    def some(i, carry):
        slot = lax.rem(i, 2)

        @pl.when(i + 1 < count)
        def _():
            fetch(i + 1, 1 - slot).start()

        fetch(i, slot).wait()
        these = pl.ds(pl.multiple_of(i * part, part), part)
        blurred = across(own_slots[slot], scale[NEAR : NEAR + rows])
        for r in range(rows):
            total = taps[GR] * blurred[r]
            for k in range(1, GR + 1):
                if r - k >= 0 and r + k < rows:
                    total = total + taps[GR + k] * (blurred[r - k] + blurred[r + k])
                elif r - k >= 0:
                    total = total + taps[GR + k] * blurred[r - k]
                elif r + k < rows:
                    total = total + taps[GR + k] * blurred[r + k]
            out[r, these, :] = total.astype(BF16)
        after = across(near[0:GR, these, :], scale[0:GR])
        ahead = across(near[2 * NEAR - GR : 2 * NEAR, these, :], scale[rows + 2 * NEAR - GR :])
        for a in range(GR):
            total = taps[2 * GR - a] * after[0]
            for r in range(1, a + 1):
                total = total + taps[2 * GR + r - a] * after[r]
            out_next[a, these, :] = total.astype(BF16)
            total = taps[2 * GR] * ahead[a]
            for b in range(a + 1, GR):
                total = total + taps[2 * GR + a - b] * ahead[b]
            out_prev[a, these, :] = total.astype(BF16)
        return carry

    lax.fori_loop(0, count, some, 0)


def make_weights(foot_rows, near_rows, noises):
    rows, slots, cols = foot_rows.shape
    part = 32
    return pl.pallas_call(
        functools.partial(weights_kernel, [float(t) for t in tap_values()]),
        in_specs=[HBM] + [VMEM] * (1 + len(noises)),
        out_shape=(
            jax.ShapeDtypeStruct((rows, slots, cols), BF16),
            jax.ShapeDtypeStruct((GR, slots, cols), BF16),
            jax.ShapeDtypeStruct((GR, slots, cols), BF16),
        ),
        scratch_shapes=[
            pltpu.VMEM((2, rows, part, cols), BF16),
            pltpu.VMEM(noises[0].shape, F32),
            pltpu.VMEM((cols, cols), BF16),
            pltpu.SemaphoreType.DMA((2,)),
        ],
        compiler_params=params(32),
        cost_estimate=COST,
        name="weights",
    )(foot_rows, near_rows, *noises)


def annulus_group(g, own, leaving, entering, weight, gain, band, column, total, outgoing):
    cols, frames = own.shape[1:]
    top = lax.broadcasted_iota(jnp.int32, (cols // 8, 8, LANES), 1) < 4
    blank = jnp.zeros((2, 8, LANES), F32)
    outs = [leaving(q) for q in range(PER)]
    news = [entering(q) for q in range(PER)]
    levels = [dot(band, jnp.concatenate([o, n], axis=0)) for o, n in zip(outs, news)]
    column = list(column)
    dets = []
    for q in range(PER):
        det = []
        for h in range(frames // LANES):
            part = slice(h * LANES, (h + 1) * LANES)
            inner = column[h] - outs[q][:, part].astype(F32)
            column[h] = inner + news[q][:, part].astype(F32)
            turned = pltpu.roll(inner.reshape(cols // 8, 8, LANES), 4, 1)
            turned = jnp.concatenate([blank, turned, blank], axis=0)
            both = turned[0 : cols // 8 + 1] + turned[3 : cols // 8 + 4]
            sides = jnp.where(top, both[0 : cols // 8], both[1 : cols // 8 + 1])
            fit = (levels[q][:, part] + sides.reshape(cols, LANES)) * gain
            outgoing[g, q, :, part] = fit.astype(BF16)
            det.append((own[g * PER + q, :, part].astype(F32) - fit).astype(BF16))
        dets.append(jnp.concatenate(det, axis=1))
    weights = jnp.concatenate([weight[g * PER + q] for q in range(PER)], axis=1)
    total = total + dot(weights, jnp.concatenate(dets, axis=0))
    return column, total, dets


def halves(ref):
    return [ref[:, h * LANES : (h + 1) * LANES] for h in range(ref.shape[1] // LANES)]


def add_rows(column, rows, sign=1.0):
    for row in rows:
        column = [c + sign * r.astype(F32) for c, r in zip(column, halves(row))]
    return column


def put(ref, column):
    for h, value in enumerate(column):
        ref[:, h * LANES : (h + 1) * LANES] = value


def sender(outgoing, background, sems):
    def send(g):
        return pltpu.make_async_copy(
            outgoing.at[g], background.at[0, pl.ds(g * PER, PER)], sems.at[g]
        )

    return send


def tables(gain):
    cols = gain.shape[1]
    band = jnp.where(jnp.abs(lag_table(cols)) <= RAD, 1.0, 0.0).astype(BF16)
    return (
        jnp.broadcast_to(gain[...], (LANES, cols)).T / (8.0 * RAD),
        jnp.concatenate([band, band], axis=1),
    )


def middle_kernel(own, near, weight, gain, background, upper, lower, total, outgoing, sems):
    rows, cols, frames = own.shape
    groups = range((RAD - NEAR) // PER, (rows - RAD + NEAR) // PER)
    send = sender(outgoing, background, sems)
    gains, band = tables(gain)
    column = [jnp.zeros((cols, LANES), F32)] * (frames // LANES)
    column = add_rows(column, [near[NEAR + r] for r in range(NEAR)])
    column = add_rows(column, [own[r] for r in range(RAD)])
    put(upper, column)
    column = add_rows(column, [own[RAD + r] for r in range(2 * RAD - NEAR - RAD)])
    grown = jnp.zeros(total.shape, F32)
    for g in groups:
        y = g * PER
        column, grown, _ = annulus_group(
            g,
            own,
            (lambda q: near[NEAR + y - RAD + NEAR + q])
            if y < RAD
            else (lambda q: own[y - RAD + q]),
            (lambda q: near[y + RAD - rows + q])
            if y + RAD >= rows
            else (lambda q: own[y + RAD + q]),
            weight, gains, band, column, grown, outgoing,
        )
        send(g).start()
    put(lower, column)
    total[...] = grown
    for g in groups:
        send(g).wait()


def ends_kernel(
    own, movie_prev, movie_next, model, weight, weight_next, weight_prev, gain, before,
    upper, lower, total, background, gradient, outgoing, sems,
):
    del before
    rows, _, frames = own.shape
    outer = RAD - NEAR
    count = outer // PER
    send = sender(outgoing, background, sems)
    gains, band = tables(gain)
    above, below = [
        [(movie[r].astype(F32) - model[first + r]).astype(BF16) for r in range(outer)]
        for movie, first in ((movie_prev, outer), (movie_next, 0))
    ]
    high, low = add_rows(halves(upper), above), halves(lower)
    grown = total[...]
    dets = {}
    for k in range(count):
        y, z = k * PER, rows - outer + k * PER
        high, grown, dets[y] = annulus_group(
            y // PER, own, lambda q: above[y + q], lambda q: own[y + RAD + q],
            weight, gains, band, high, grown, outgoing,
        )
        send(y // PER).start()
        low, grown, dets[z] = annulus_group(
            z // PER, own, lambda q: own[z - RAD + q], lambda q: below[k * PER + q],
            weight, gains, band, low, grown, outgoing,
        )
        send(z // PER).start()
    edges = ((2, weight_next, dets[rows - PER][PER - GR :]), (3, weight_prev, dets[0][:GR]))
    for at, edge, parts in edges:
        value = dot(
            jnp.concatenate([edge[a] for a in range(GR)], axis=1), jnp.concatenate(parts, axis=0)
        )
        gradient[:, at * frames : (at + 1) * frames] = value.astype(BF16)
    coarse = grown.astype(BF16)
    gradient[:, 0:frames] = coarse
    gradient[:, frames : 2 * frames] = (grown - coarse.astype(F32)).astype(BF16)
    for k in range(count):
        send(k).wait()
        send(rows // PER - 1 - k).wait()


def make_annulus(own, near, outer_prev, outer_next, model, weights, gain):
    rows, cols, frames = own.shape
    weight, weight_next, weight_prev = weights
    slots = weight.shape[1]
    background = jax.ShapeDtypeStruct((1, rows, cols, frames), BF16)
    column = jax.ShapeDtypeStruct((cols, frames), F32)
    total = jax.ShapeDtypeStruct((slots, frames), F32)
    gradient = jax.ShapeDtypeStruct((slots, 4 * frames), BF16)

    def call(kernel, name, args, outs, done):
        specs = [VMEM] * len(args)
        if done is not None:
            specs[done] = HBM
        return pl.pallas_call(
            kernel,
            in_specs=specs,
            out_specs=[HBM] + [VMEM] * (len(outs) - 1),
            out_shape=outs,
            scratch_shapes=[
                pltpu.VMEM((rows // PER, PER, cols, frames), BF16),
                pltpu.SemaphoreType.DMA((rows // PER,)),
            ],
            input_output_aliases={} if done is None else {done: 0},
            compiler_params=params(),
            cost_estimate=COST,
            name=name,
        )(*args)

    done, upper, lower, grown = call(
        middle_kernel, "annulus_middle", (own, near, weight, gain),
        (background, column, column, total), None,
    )
    return call(
        ends_kernel, "annulus_ends",
        (own, outer_prev, outer_next, model, weight, weight_next, weight_prev, gain, done, upper,
         lower, grown),
        (background, gradient), 8,
    )


def traces_kernel(capacity, stripe, slow, fast, step, traces, inbox, out):
    count, frames = traces.shape
    slots = inbox.shape[0]

    def upended(row):
        return jnp.broadcast_to(row[...].astype(F32), (LANES, count)).T

    before = lax.broadcasted_iota(jnp.int32, (count, count), 1) < lax.broadcasted_iota(
        jnp.int32, (count, count), 0
    )
    named = upended(stripe)
    same = (named == stripe[...].astype(F32)) & before
    rank = jnp.sum(jnp.where(same, 1.0, 0.0), axis=1, keepdims=True)
    slot = (named[:, 0:1] * capacity + rank).astype(jnp.int32)
    place = lax.broadcasted_iota(jnp.int32, (count, slots), 1)

    def onehot(shift):
        return jnp.where(place + shift == slot, 1.0, 0.0).astype(BF16)

    here = onehot(0)
    gradient = (
        dot(here, inbox[:, 0:frames])
        + dot(here, inbox[:, frames : 2 * frames])
        + dot(onehot(capacity), inbox[:, 2 * frames : 3 * frames])
        + dot(onehot(-capacity), inbox[:, 3 * frames : 4 * frames])
    )

    def wide(row):
        return jnp.concatenate([upended(row)] * (frames // LANES), axis=1)

    updated = traces[...].astype(F32) + wide(step) * gradient
    lane = lax.broadcasted_iota(jnp.int32, (count, frames), 1)

    def lagged(value, lag):
        return jnp.where(lane >= lag, pltpu.roll(value, lag, 1), 0.0)

    a, b = wide(slow), wide(fast)
    driven = updated - (a + b) * lagged(updated, 1) + (a * b) * lagged(updated, 2)
    value = jnp.maximum(driven - lam_floor, 0.0) * ((1.0 - a) * (1.0 - b))
    for root in (a, b):
        lag = 1
        while lag < frames:
            value = value + root * lagged(value, lag)
            root = root * root
            lag *= 2
    out[...] = value


def make_traces(stripe, slow, fast, step, traces, inbox, capacity):
    count, frames = traces.shape
    return pl.pallas_call(
        functools.partial(traces_kernel, capacity),
        out_shape=jax.ShapeDtypeStruct((count, frames), F32),
        compiler_params=params(),
        cost_estimate=COST,
        name="traces",
    )(stripe, slow, fast, step, traces, inbox)


def neighbours(axis):
    devices = lax.axis_size(axis)
    up = [(i, i + 1) for i in range(devices - 1)]
    return up, [(j, i) for i, j in up]


def on_device(movie, footprints, traces, stripe, column, annulus_gain, decay_slow, decay_fast):
    pix_count = lax.axis_size("pix")
    rows, cols, frames = movie.shape[1:]
    count = footprints.shape[1]
    capacity = max(2, 2 * count // pix_count)
    slots = pix_count * capacity
    pix_up, pix_down = neighbours("pix")
    plane_up, plane_down = neighbours("plane")

    stripe_row = stripe.reshape(1, count)
    outbox = make_outbox(stripe_row, column, footprints[0], traces[0], capacity, slots)
    frames_in, outbox = lax.optimization_barrier((movie, outbox))
    inbox = lax.all_to_all(outbox, "pix", split_axis=0, concat_axis=0, tiled=True)

    def exchange(cut):
        return (lax.ppermute(cut[0], "pix", pix_up), lax.ppermute(cut[1], "pix", pix_down))

    near = exchange((frames_in[0, rows - NEAR :], frames_in[0, :NEAR]))
    cut, near = lax.optimization_barrier(
        ((frames_in[0, rows - RAD : rows - NEAR], frames_in[0, NEAR:RAD]), near)
    )
    outer_prev, outer_next = exchange(cut)
    near_prev, near_next = near

    foot_rows, residual, noise = make_residual(inbox, movie)
    near_rows, near_residual, noise = make_near(inbox, near_next, near_prev, noise)
    noises = (
        noise,
        lax.ppermute(noise, "plane", plane_up),
        lax.ppermute(noise, "plane", plane_down),
    )
    weights = make_weights(foot_rows, near_rows, noises)
    model = make_outer_model(inbox, cols, frames)
    background, gradient = make_annulus(
        residual, near_residual, outer_prev, outer_next, model, weights, annulus_gain
    )
    home = lax.all_to_all(gradient, "pix", split_axis=0, concat_axis=0, tiled=True)
    foot_f = footprints[0].astype(F32)
    step = 1.0 / (jnp.sum(foot_f * foot_f, axis=1) + norm_eps)
    traces_new = make_traces(
        stripe_row, decay_slow, decay_fast, step[None], traces[0], home, capacity
    )
    return (background, traces_new[None])


def solution(mesh):
    placed = (
        P("plane", "pix", None, None),
        P("plane", "pix", None),
        P("plane", "pix", None),
        P("plane", "pix", None),
        P("plane", "pix"),
        P("plane", None),
        P("plane", "pix"),
        P("plane", "pix"),
    )
    return jax.shard_map(
        on_device,
        mesh=mesh,
        in_specs=placed,
        out_specs=(P("plane", "pix", None, None), P("plane", "pix", None)),
        check_vma=False,
    )
```

```python
import functools

import jax
import jax.numpy as jnp
import ml_dtypes
import numpy as np
from jax import lax
from jax.experimental import pallas as pl
from jax.experimental.pallas import tpu as pltpu
from jax.sharding import PartitionSpec as P

FOOT = 32
RAD = 12
GR = 3
LANES = 128
PER = LANES // FOOT
NEAR = PER

lam_floor = 0.1
noise_eps = 1e-05
norm_eps = 1e-05
sigma_twice = 4.5

F32 = jnp.float32
BF16 = jnp.bfloat16
MIB = 1 << 20
HBM = pl.BlockSpec(memory_space=pltpu.HBM)
VMEM = pl.BlockSpec(memory_space=pltpu.VMEM)


def tap_values():
    offsets = np.arange(-GR, GR + 1).astype(np.float32)
    raw = np.exp(-offsets * offsets / np.float32(sigma_twice)).astype(np.float32)
    return (raw / raw.sum(dtype=np.float32)).astype(ml_dtypes.bfloat16).astype(np.float32)


def params(mib=16):
    return pltpu.CompilerParams(vmem_limit_bytes=mib * MIB)


COST = pl.CostEstimate(flops=1, bytes_accessed=1, transcendentals=0)


def dot(a, b):
    return jnp.dot(a, b, preferred_element_type=F32)


def cut_kernel(movie, near_prev, near_next, up, down, sems):
    del near_prev, near_next
    rows, count = movie.shape[1], up.shape[0]
    copies = [
        pltpu.make_async_copy(movie.at[0, pl.ds(first, count)], out, sems.at[k])
        for k, (first, out) in enumerate(((rows - NEAR - count, up), (NEAR, down)))
    ]
    for copy in copies:
        copy.start()
    for copy in copies:
        copy.wait()


def cut_outer(movie, near_prev, near_next):
    cols, frames = movie.shape[2:]
    piece = jax.ShapeDtypeStruct((RAD - NEAR, cols, frames), BF16)
    return pl.pallas_call(
        cut_kernel,
        in_specs=[HBM, HBM, HBM],
        out_specs=[VMEM, VMEM],
        out_shape=(piece, piece),
        scratch_shapes=[pltpu.SemaphoreType.DMA((2,))],
        compiler_params=params(),
        cost_estimate=pl.CostEstimate(flops=9 * 10**9, bytes_accessed=1, transcendentals=0),
        name="cut_outer",
    )(movie, near_prev, near_next)


def outbox_kernel(capacity, *refs):
    sources, outbox, places, sems = refs[0:4], refs[4], refs[5:9], refs[9]
    copies = [
        pltpu.make_async_copy(source, place, sems.at[k])
        for k, (source, place) in enumerate(zip(sources, places))
    ]
    for copy in copies:
        copy.start()
    for copy in copies:
        copy.wait()
    stripe, column, foot, traces = places
    slots = outbox.shape[0]
    count, tiles = foot.shape
    frames = traces.shape[1]
    before = lax.broadcasted_iota(jnp.int32, (count, count), 0) < lax.broadcasted_iota(
        jnp.int32, (count, count), 1
    )
    named = jnp.broadcast_to(stripe[...].astype(F32), (count, count))
    same = (named == named.T) & before
    rank = jnp.sum(jnp.where(same, 1.0, 0.0), axis=0, keepdims=True).astype(jnp.int32)
    slot = stripe[...] * capacity + rank
    place = lax.broadcasted_iota(jnp.int32, (slots, count), 0)
    left = jnp.broadcast_to(column[...].astype(F32), (LANES, count)).T.astype(BF16)
    lane = lax.broadcasted_iota(jnp.int32, (slots, LANES), 1)
    edge = RAD * FOOT
    lefts = jnp.zeros((slots, LANES), F32)
    at = 3 * frames
    for k, (shift, first, width) in enumerate(
        ((0, 0, tiles), (capacity, 0, edge), (-capacity, tiles - edge, edge))
    ):
        hot = jnp.where(place + shift == slot, 1.0, 0.0).astype(BF16)
        outbox[:, k * frames : (k + 1) * frames] = dot(hot, traces[...]).astype(BF16)
        outbox[:, at : at + width] = dot(hot, foot[:, first : first + width]).astype(BF16)
        lefts = jnp.where(lane == k, dot(hot, left), lefts)
        at += width
    outbox[:, at:] = lefts.astype(BF16)


def make_outbox(stripe, column, foot, traces, capacity, slots):
    count, tiles = foot.shape
    frames = traces.shape[1]
    width = 3 * frames + tiles + 2 * RAD * FOOT + LANES
    args = (stripe, column, foot, traces)
    return pl.pallas_call(
        functools.partial(outbox_kernel, capacity),
        in_specs=[HBM] * len(args),
        out_shape=jax.ShapeDtypeStruct((slots, width), BF16),
        scratch_shapes=[pltpu.VMEM(a.shape, a.dtype) for a in args]
        + [pltpu.SemaphoreType.DMA((len(args),))],
        compiler_params=params(56),
        cost_estimate=COST,
        name="outbox",
    )(*args)


def spread(block, col):
    lane = lax.broadcasted_iota(jnp.int32, block.shape, 1)
    for k in range(7):
        block = jnp.where(((col >> k) & 1) == 1, pltpu.roll(block, 1 << k, 1), block)
    inside = ((lane - col) & (LANES - 1)) < FOOT
    left = inside & (lane >= col)
    right = inside & (lane < col)
    rows = []
    for q in range(PER):
        moved = block if q == 0 else pltpu.roll(block, LANES - q * FOOT, 1)
        rows.append(
            jnp.concatenate(
                [jnp.where(left, moved, 0.0), jnp.where(right, moved, 0.0)], axis=1
            ).astype(BF16)
        )
    return rows


def tile_rows(inbox, which, block, frames):
    lefts = inbox[:, inbox.shape[1] - LANES :].astype(F32)
    col = jnp.broadcast_to(lefts[:, which : which + 1], lefts.shape).astype(jnp.int32)
    start = 3 * frames + block * LANES
    if not isinstance(start, int):
        start = pl.multiple_of(start, LANES)
    return spread(inbox[:, pl.ds(start, LANES)].astype(F32), col)


def model_row(row, inbox, which, frames):
    traces = inbox[:, which * frames : (which + 1) * frames]
    return lax.dot_general(row, traces, (((0,), (0,)), ((), ())), preferred_element_type=F32)


def noise_row(left, change):
    frames = left.shape[1]
    steps = dot(left, change)
    steps = steps * steps
    part = steps[:, 0:LANES]
    for k in range(1, frames // LANES):
        part = part + steps[:, k * LANES : (k + 1) * LANES]
    return jnp.sum(part.T, axis=0, keepdims=True) / (frames - 1)


def lag_table(size):
    shape = (size, size)
    return lax.broadcasted_iota(jnp.int32, shape, 1) - lax.broadcasted_iota(jnp.int32, shape, 0)


def change_matrix(frames):
    lag = lag_table(frames)
    steps = jnp.where(lag == -1, 1.0, 0.0) - jnp.where(lag == 0, 1.0, 0.0)
    later = lax.broadcasted_iota(jnp.int32, lag.shape, 1)
    return jnp.where(later < frames - 1, steps, 0.0).astype(BF16)


def residual_kernel(
    inbox, movie, foot_rows, residual, noise, change, movie_slots, foot_slots, left_slots, sems
):
    rows, _, frames = movie.shape[1:]
    groups = rows // PER
    change[...] = change_matrix(frames)

    def fetch(g, slot):
        rows_g = pl.ds(g * PER, PER)
        return pltpu.make_async_copy(movie.at[0, rows_g], movie_slots.at[slot], sems.at[0, slot])

    def sends(g, slot):
        rows_g = pl.ds(g * PER, PER)
        return (
            pltpu.make_async_copy(foot_slots.at[slot], foot_rows.at[rows_g], sems.at[1, slot]),
            pltpu.make_async_copy(left_slots.at[slot], residual.at[rows_g], sems.at[2, slot]),
        )

    fetch(0, 0).start()

    def group(g, carry):
        slot = lax.rem(g, 2)

        @pl.when(g + 1 < groups)
        def _():
            fetch(g + 1, 1 - slot).start()

        fetch(g, slot).wait()

        @pl.when(g >= 2)
        def _():
            for copy in sends(g - 2, slot):
                copy.wait()

        noises = []
        for q, row in enumerate(tile_rows(inbox, 0, g, frames)):
            foot_slots[slot, q] = row
            left = movie_slots[slot, q].astype(F32) - model_row(row, inbox, 0, frames)
            left = left.astype(BF16)
            left_slots[slot, q] = left
            noises.append(noise_row(left, change[...]))
        noise[g] = jnp.concatenate(noises, axis=0)
        for copy in sends(g, slot):
            copy.start()
        return carry

    lax.fori_loop(0, groups, group, 0)
    for g in (groups - 2, groups - 1):
        for copy in sends(g, g % 2):
            copy.wait()


def make_residual(inbox, movie):
    slots = inbox.shape[0]
    rows, cols, frames = movie.shape[1:]
    return pl.pallas_call(
        residual_kernel,
        in_specs=[VMEM, HBM],
        out_specs=[HBM, HBM, VMEM],
        out_shape=(
            jax.ShapeDtypeStruct((rows, slots, cols), BF16),
            jax.ShapeDtypeStruct((rows, cols, frames), BF16),
            jax.ShapeDtypeStruct((rows // PER, PER, cols), F32),
        ),
        scratch_shapes=[
            pltpu.VMEM((frames, frames), BF16),
            pltpu.VMEM((2, PER, cols, frames), BF16),
            pltpu.VMEM((2, PER, slots, cols), BF16),
            pltpu.VMEM((2, PER, cols, frames), BF16),
            pltpu.SemaphoreType.DMA((3, 2)),
        ],
        compiler_params=params(44),
        cost_estimate=COST,
        name="residual",
    )(inbox, movie)


def near_kernel(inbox, movie_next, movie_prev, own_noise, foot_rows, residual, noise):
    frames = movie_next.shape[2]
    groups = own_noise.shape[0]
    own = FOOT // PER
    change = change_matrix(frames)
    for g in range(groups):
        noise[NEAR + g * PER : NEAR + (g + 1) * PER, :] = own_noise[g]
    for side, (block, movie, first) in enumerate(
        ((own, movie_next, 0), (own + 2 * RAD // PER - 1, movie_prev, NEAR + groups * PER))
    ):
        for q, row in enumerate(tile_rows(inbox, 1 + side, block, frames)):
            y = side * NEAR + q
            foot_rows[y] = row
            left = movie[q].astype(F32) - model_row(row, inbox, 1 + side, frames)
            left = left.astype(BF16)
            residual[y] = left
            noise[first + q : first + q + 1, :] = noise_row(left, change)


def make_near(inbox, movie_next, movie_prev, noise):
    slots = inbox.shape[0]
    groups, per, _ = noise.shape
    cols, frames = movie_next.shape[1:]
    return pl.pallas_call(
        near_kernel,
        out_shape=(
            jax.ShapeDtypeStruct((2 * NEAR, slots, cols), BF16),
            jax.ShapeDtypeStruct((2 * NEAR, cols, frames), BF16),
            jax.ShapeDtypeStruct((2 * NEAR + groups * per, cols), F32),
        ),
        compiler_params=params(),
        cost_estimate=COST,
        name="near",
    )(inbox, movie_next, movie_prev, noise)


def outer_kernel(inbox, model):
    frames = model.shape[2]
    first = (FOOT + NEAR) // PER
    groups = (RAD - NEAR) // PER
    for side in range(2):
        for g in range(groups):
            k = side * groups + g
            for q, row in enumerate(tile_rows(inbox, 1 + side, first + k, frames)):
                model[k * PER + q] = model_row(row, inbox, 1 + side, frames)


def make_outer_model(inbox, cols, frames):
    return pl.pallas_call(
        outer_kernel,
        out_shape=jax.ShapeDtypeStruct((2 * (RAD - NEAR), cols, frames), F32),
        compiler_params=params(),
        cost_estimate=COST,
        name="outer_model",
    )(inbox)


def weights_kernel(
    taps, own, near, noise, noise_before, noise_after, out, out_next, out_prev,
    own_slots, scale, band, sems,
):
    rows, slots, cols = own.shape
    part = own_slots.shape[2]
    count = slots // part

    def fetch(i, slot):
        these = pl.ds(pl.multiple_of(i * part, part), part)
        return pltpu.make_async_copy(own.at[:, these, :], own_slots.at[slot], sems.at[slot])

    fetch(0, 0).start()
    pooled = (noise_before[...] + 2.0 * noise[...] + noise_after[...]) / 4.0
    scale[...] = 1.0 / jnp.sqrt(pooled + noise_eps)
    lag = jnp.abs(lag_table(cols))
    table = jnp.zeros(lag.shape, F32)
    for k in range(GR + 1):
        table = jnp.where(lag == k, taps[GR + k], table)
    band[...] = table.astype(BF16)

    def across(foot, inv):
        scaled = (foot.astype(F32) * inv[:, None, :]).astype(BF16)
        count = foot.shape[0]
        return dot(scaled.reshape(count * part, cols), band[...]).reshape(count, part, cols)

    def some(i, carry):
        slot = lax.rem(i, 2)

        @pl.when(i + 1 < count)
        def _():
            fetch(i + 1, 1 - slot).start()

        fetch(i, slot).wait()
        these = pl.ds(pl.multiple_of(i * part, part), part)
        blurred = across(own_slots[slot], scale[NEAR : NEAR + rows])
        for r in range(rows):
            total = taps[GR] * blurred[r]
            for k in range(1, GR + 1):
                if r - k >= 0 and r + k < rows:
                    total = total + taps[GR + k] * (blurred[r - k] + blurred[r + k])
                elif r - k >= 0:
                    total = total + taps[GR + k] * blurred[r - k]
                elif r + k < rows:
                    total = total + taps[GR + k] * blurred[r + k]
            out[r, these, :] = total.astype(BF16)
        after = across(near[0:GR, these, :], scale[0:GR])
        ahead = across(near[2 * NEAR - GR : 2 * NEAR, these, :], scale[rows + 2 * NEAR - GR :])
        for a in range(GR):
            total = taps[2 * GR - a] * after[0]
            for r in range(1, a + 1):
                total = total + taps[2 * GR + r - a] * after[r]
            out_next[a, these, :] = total.astype(BF16)
            total = taps[2 * GR] * ahead[a]
            for b in range(a + 1, GR):
                total = total + taps[2 * GR + a - b] * ahead[b]
            out_prev[a, these, :] = total.astype(BF16)
        return carry

    lax.fori_loop(0, count, some, 0)


def make_weights(foot_rows, near_rows, noises):
    rows, slots, cols = foot_rows.shape
    part = 32
    return pl.pallas_call(
        functools.partial(weights_kernel, [float(t) for t in tap_values()]),
        in_specs=[HBM] + [VMEM] * (1 + len(noises)),
        out_shape=(
            jax.ShapeDtypeStruct((rows, slots, cols), BF16),
            jax.ShapeDtypeStruct((GR, slots, cols), BF16),
            jax.ShapeDtypeStruct((GR, slots, cols), BF16),
        ),
        scratch_shapes=[
            pltpu.VMEM((2, rows, part, cols), BF16),
            pltpu.VMEM(noises[0].shape, F32),
            pltpu.VMEM((cols, cols), BF16),
            pltpu.SemaphoreType.DMA((2,)),
        ],
        compiler_params=params(32),
        cost_estimate=COST,
        name="weights",
    )(foot_rows, near_rows, *noises)


def annulus_group(g, own, leaving, entering, weight, gain, band, column, total, outgoing):
    cols, frames = own.shape[1:]
    top = lax.broadcasted_iota(jnp.int32, (cols // 8, 8, LANES), 1) < 4
    blank = jnp.zeros((2, 8, LANES), F32)
    outs = [leaving(q) for q in range(PER)]
    news = [entering(q) for q in range(PER)]
    levels = [dot(band, jnp.concatenate([o, n], axis=0)) for o, n in zip(outs, news)]
    column = list(column)
    dets = []
    for q in range(PER):
        det = []
        for h in range(frames // LANES):
            part = slice(h * LANES, (h + 1) * LANES)
            inner = column[h] - outs[q][:, part].astype(F32)
            column[h] = inner + news[q][:, part].astype(F32)
            turned = pltpu.roll(inner.reshape(cols // 8, 8, LANES), 4, 1)
            turned = jnp.concatenate([blank, turned, blank], axis=0)
            both = turned[0 : cols // 8 + 1] + turned[3 : cols // 8 + 4]
            sides = jnp.where(top, both[0 : cols // 8], both[1 : cols // 8 + 1])
            fit = (levels[q][:, part] + sides.reshape(cols, LANES)) * gain
            outgoing[g, q, :, part] = fit.astype(BF16)
            det.append((own[g * PER + q, :, part].astype(F32) - fit).astype(BF16))
        dets.append(jnp.concatenate(det, axis=1))
    weights = jnp.concatenate([weight[g * PER + q] for q in range(PER)], axis=1)
    total = total + dot(weights, jnp.concatenate(dets, axis=0))
    return column, total, dets


def halves(ref):
    return [ref[:, h * LANES : (h + 1) * LANES] for h in range(ref.shape[1] // LANES)]


def add_rows(column, rows, sign=1.0):
    for row in rows:
        column = [c + sign * r.astype(F32) for c, r in zip(column, halves(row))]
    return column


def put(ref, column):
    for h, value in enumerate(column):
        ref[:, h * LANES : (h + 1) * LANES] = value


def sender(outgoing, background, sems):
    def send(g):
        return pltpu.make_async_copy(
            outgoing.at[g], background.at[0, pl.ds(g * PER, PER)], sems.at[g]
        )

    return send


def tables(gain):
    cols = gain.shape[1]
    band = jnp.where(jnp.abs(lag_table(cols)) <= RAD, 1.0, 0.0).astype(BF16)
    return (
        jnp.broadcast_to(gain[...], (LANES, cols)).T / (8.0 * RAD),
        jnp.concatenate([band, band], axis=1),
    )


def middle_kernel(own, near, weight, gain, background, upper, lower, total, outgoing, sems):
    rows, cols, frames = own.shape
    groups = range((RAD - NEAR) // PER, (rows - RAD + NEAR) // PER)
    send = sender(outgoing, background, sems)
    gains, band = tables(gain)
    column = [jnp.zeros((cols, LANES), F32)] * (frames // LANES)
    column = add_rows(column, [near[NEAR + r] for r in range(NEAR)])
    column = add_rows(column, [own[r] for r in range(RAD)])
    put(upper, column)
    column = add_rows(column, [own[RAD + r] for r in range(2 * RAD - NEAR - RAD)])
    grown = jnp.zeros(total.shape, F32)
    for g in groups:
        y = g * PER
        column, grown, _ = annulus_group(
            g,
            own,
            (lambda q: near[NEAR + y - RAD + NEAR + q])
            if y < RAD
            else (lambda q: own[y - RAD + q]),
            (lambda q: near[y + RAD - rows + q])
            if y + RAD >= rows
            else (lambda q: own[y + RAD + q]),
            weight, gains, band, column, grown, outgoing,
        )
        send(g).start()
    put(lower, column)
    total[...] = grown
    for g in groups:
        send(g).wait()


def ends_kernel(
    own, movie_prev, movie_next, model, weight, weight_next, weight_prev, gain, before,
    upper, lower, total, background, gradient, outgoing, sems,
):
    del before
    rows, _, frames = own.shape
    outer = RAD - NEAR
    count = outer // PER
    send = sender(outgoing, background, sems)
    gains, band = tables(gain)
    above, below = [
        [(movie[r].astype(F32) - model[first + r]).astype(BF16) for r in range(outer)]
        for movie, first in ((movie_prev, outer), (movie_next, 0))
    ]
    high, low = add_rows(halves(upper), above), halves(lower)
    grown = total[...]
    dets = {}
    for k in range(count):
        y, z = k * PER, rows - outer + k * PER
        high, grown, dets[y] = annulus_group(
            y // PER, own, lambda q: above[y + q], lambda q: own[y + RAD + q],
            weight, gains, band, high, grown, outgoing,
        )
        send(y // PER).start()
        low, grown, dets[z] = annulus_group(
            z // PER, own, lambda q: own[z - RAD + q], lambda q: below[k * PER + q],
            weight, gains, band, low, grown, outgoing,
        )
        send(z // PER).start()
    edges = ((2, weight_next, dets[rows - PER][PER - GR :]), (3, weight_prev, dets[0][:GR]))
    for at, edge, parts in edges:
        value = dot(
            jnp.concatenate([edge[a] for a in range(GR)], axis=1), jnp.concatenate(parts, axis=0)
        )
        gradient[:, at * frames : (at + 1) * frames] = value.astype(BF16)
    coarse = grown.astype(BF16)
    gradient[:, 0:frames] = coarse
    gradient[:, frames : 2 * frames] = (grown - coarse.astype(F32)).astype(BF16)
    for k in range(count):
        send(k).wait()
        send(rows // PER - 1 - k).wait()


def make_annulus(own, near, outer_prev, outer_next, model, weights, gain):
    rows, cols, frames = own.shape
    weight, weight_next, weight_prev = weights
    slots = weight.shape[1]
    background = jax.ShapeDtypeStruct((1, rows, cols, frames), BF16)
    column = jax.ShapeDtypeStruct((cols, frames), F32)
    total = jax.ShapeDtypeStruct((slots, frames), F32)
    gradient = jax.ShapeDtypeStruct((slots, 4 * frames), BF16)

    def call(kernel, name, args, outs, done):
        specs = [VMEM] * len(args)
        if done is not None:
            specs[done] = HBM
        return pl.pallas_call(
            kernel,
            in_specs=specs,
            out_specs=[HBM] + [VMEM] * (len(outs) - 1),
            out_shape=outs,
            scratch_shapes=[
                pltpu.VMEM((rows // PER, PER, cols, frames), BF16),
                pltpu.SemaphoreType.DMA((rows // PER,)),
            ],
            input_output_aliases={} if done is None else {done: 0},
            compiler_params=params(),
            cost_estimate=COST,
            name=name,
        )(*args)

    done, upper, lower, grown = call(
        middle_kernel, "annulus_middle", (own, near, weight, gain),
        (background, column, column, total), None,
    )
    return call(
        ends_kernel, "annulus_ends",
        (own, outer_prev, outer_next, model, weight, weight_next, weight_prev, gain, done, upper,
         lower, grown),
        (background, gradient), 8,
    )


def traces_kernel(capacity, stripe, slow, fast, step, traces, inbox, out):
    count, frames = traces.shape
    slots = inbox.shape[0]

    def upended(row):
        return jnp.broadcast_to(row[...].astype(F32), (LANES, count)).T

    before = lax.broadcasted_iota(jnp.int32, (count, count), 1) < lax.broadcasted_iota(
        jnp.int32, (count, count), 0
    )
    named = upended(stripe)
    same = (named == stripe[...].astype(F32)) & before
    rank = jnp.sum(jnp.where(same, 1.0, 0.0), axis=1, keepdims=True)
    slot = (named[:, 0:1] * capacity + rank).astype(jnp.int32)
    place = lax.broadcasted_iota(jnp.int32, (count, slots), 1)

    def onehot(shift):
        return jnp.where(place + shift == slot, 1.0, 0.0).astype(BF16)

    here = onehot(0)
    gradient = (
        dot(here, inbox[:, 0:frames])
        + dot(here, inbox[:, frames : 2 * frames])
        + dot(onehot(capacity), inbox[:, 2 * frames : 3 * frames])
        + dot(onehot(-capacity), inbox[:, 3 * frames : 4 * frames])
    )

    def wide(row):
        return jnp.concatenate([upended(row)] * (frames // LANES), axis=1)

    updated = traces[...].astype(F32) + wide(step) * gradient
    lane = lax.broadcasted_iota(jnp.int32, (count, frames), 1)

    def lagged(value, lag):
        return jnp.where(lane >= lag, pltpu.roll(value, lag, 1), 0.0)

    a, b = wide(slow), wide(fast)
    driven = updated - (a + b) * lagged(updated, 1) + (a * b) * lagged(updated, 2)
    value = jnp.maximum(driven - lam_floor, 0.0) * ((1.0 - a) * (1.0 - b))
    for root in (a, b):
        lag = 1
        while lag < frames:
            value = value + root * lagged(value, lag)
            root = root * root
            lag *= 2
    out[...] = value


def make_traces(stripe, slow, fast, step, traces, inbox, capacity):
    count, frames = traces.shape
    return pl.pallas_call(
        functools.partial(traces_kernel, capacity),
        out_shape=jax.ShapeDtypeStruct((count, frames), F32),
        compiler_params=params(),
        cost_estimate=COST,
        name="traces",
    )(stripe, slow, fast, step, traces, inbox)


def neighbours(axis):
    devices = lax.axis_size(axis)
    up = [(i, i + 1) for i in range(devices - 1)]
    return up, [(j, i) for i, j in up]


def on_device(movie, footprints, traces, stripe, column, annulus_gain, decay_slow, decay_fast):
    pix_count = lax.axis_size("pix")
    rows, cols, frames = movie.shape[1:]
    count = footprints.shape[1]
    capacity = max(2, 2 * count // pix_count)
    slots = pix_count * capacity
    pix_up, pix_down = neighbours("pix")
    plane_up, plane_down = neighbours("plane")

    stripe_row = stripe.reshape(1, count)
    outbox = make_outbox(stripe_row, column, footprints[0], traces[0], capacity, slots)
    def exchange(cut):
        return (lax.ppermute(cut[0], "pix", pix_up), lax.ppermute(cut[1], "pix", pix_down))

    near_prev, near_next = exchange((movie[0, rows - NEAR :], movie[0, :NEAR]))
    outer_prev, outer_next = exchange(cut_outer(movie, near_prev, near_next))
    inbox = lax.all_to_all(outbox, "pix", split_axis=0, concat_axis=0, tiled=True)

    foot_rows, residual, noise = make_residual(inbox, movie)
    near_rows, near_residual, noise = make_near(inbox, near_next, near_prev, noise)
    noises = (
        noise,
        lax.ppermute(noise, "plane", plane_up),
        lax.ppermute(noise, "plane", plane_down),
    )
    weights = make_weights(foot_rows, near_rows, noises)
    model = make_outer_model(inbox, cols, frames)
    background, gradient = make_annulus(
        residual, near_residual, outer_prev, outer_next, model, weights, annulus_gain
    )
    home = lax.all_to_all(gradient, "pix", split_axis=0, concat_axis=0, tiled=True)
    foot_f = footprints[0].astype(F32)
    step = 1.0 / (jnp.sum(foot_f * foot_f, axis=1) + norm_eps)
    traces_new = make_traces(
        stripe_row, decay_slow, decay_fast, step[None], traces[0], home, capacity
    )
    return (background, traces_new[None])


def solution(mesh):
    placed = (
        P("plane", "pix", None, None),
        P("plane", "pix", None),
        P("plane", "pix", None),
        P("plane", "pix", None),
        P("plane", "pix"),
        P("plane", None),
        P("plane", "pix"),
        P("plane", "pix"),
    )
    return jax.shard_map(
        on_device,
        mesh=mesh,
        in_specs=placed,
        out_specs=(P("plane", "pix", None, None), P("plane", "pix", None)),
        check_vma=False,
    )
```

```python
import functools

import jax
import jax.numpy as jnp
import ml_dtypes
import numpy as np
from jax import lax
from jax.experimental import pallas as pl
from jax.experimental.pallas import tpu as pltpu
from jax.sharding import PartitionSpec as P

FOOT = 32
RAD = 12
GR = 3
LANES = 128
PER = LANES // FOOT
NEAR = PER

lam_floor = 0.1
noise_eps = 1e-05
norm_eps = 1e-05
sigma_twice = 4.5

F32 = jnp.float32
BF16 = jnp.bfloat16
MIB = 1 << 20
HBM = pl.BlockSpec(memory_space=pltpu.HBM)
VMEM = pl.BlockSpec(memory_space=pltpu.VMEM)


def tap_values():
    offsets = np.arange(-GR, GR + 1).astype(np.float32)
    raw = np.exp(-offsets * offsets / np.float32(sigma_twice)).astype(np.float32)
    return (raw / raw.sum(dtype=np.float32)).astype(ml_dtypes.bfloat16).astype(np.float32)


def params(mib=16):
    return pltpu.CompilerParams(vmem_limit_bytes=mib * MIB)


COST = pl.CostEstimate(flops=1, bytes_accessed=1, transcendentals=0)


def dot(a, b):
    return jnp.dot(a, b, preferred_element_type=F32)


def outbox_kernel(capacity, *refs):
    sources, outbox, places, sems = refs[0:4], refs[4], refs[5:9], refs[9]
    copies = [
        pltpu.make_async_copy(source, place, sems.at[k])
        for k, (source, place) in enumerate(zip(sources, places))
    ]
    for copy in copies:
        copy.start()
    for copy in copies:
        copy.wait()
    stripe, column, foot, traces = places
    slots = outbox.shape[0]
    count, tiles = foot.shape
    frames = traces.shape[1]
    before = lax.broadcasted_iota(jnp.int32, (count, count), 0) < lax.broadcasted_iota(
        jnp.int32, (count, count), 1
    )
    named = jnp.broadcast_to(stripe[...].astype(F32), (count, count))
    same = (named == named.T) & before
    rank = jnp.sum(jnp.where(same, 1.0, 0.0), axis=0, keepdims=True).astype(jnp.int32)
    slot = stripe[...] * capacity + rank
    place = lax.broadcasted_iota(jnp.int32, (slots, count), 0)
    left = jnp.broadcast_to(column[...].astype(F32), (LANES, count)).T.astype(BF16)
    lane = lax.broadcasted_iota(jnp.int32, (slots, LANES), 1)
    edge = RAD * FOOT
    lefts = jnp.zeros((slots, LANES), F32)
    at = 3 * frames
    for k, (shift, first, width) in enumerate(
        ((0, 0, tiles), (capacity, 0, edge), (-capacity, tiles - edge, edge))
    ):
        hot = jnp.where(place + shift == slot, 1.0, 0.0).astype(BF16)
        outbox[:, k * frames : (k + 1) * frames] = dot(hot, traces[...]).astype(BF16)
        outbox[:, at : at + width] = dot(hot, foot[:, first : first + width]).astype(BF16)
        lefts = jnp.where(lane == k, dot(hot, left), lefts)
        at += width
    outbox[:, at:] = lefts.astype(BF16)


def make_outbox(stripe, column, foot, traces, capacity, slots):
    count, tiles = foot.shape
    frames = traces.shape[1]
    width = 3 * frames + tiles + 2 * RAD * FOOT + LANES
    args = (stripe, column, foot, traces)
    return pl.pallas_call(
        functools.partial(outbox_kernel, capacity),
        in_specs=[HBM] * len(args),
        out_shape=jax.ShapeDtypeStruct((slots, width), BF16),
        scratch_shapes=[pltpu.VMEM(a.shape, a.dtype) for a in args]
        + [pltpu.SemaphoreType.DMA((len(args),))],
        compiler_params=params(56),
        cost_estimate=COST,
        name="outbox",
    )(*args)


def spread(block, col):
    lane = lax.broadcasted_iota(jnp.int32, block.shape, 1)
    for k in range(7):
        block = jnp.where(((col >> k) & 1) == 1, pltpu.roll(block, 1 << k, 1), block)
    inside = ((lane - col) & (LANES - 1)) < FOOT
    left = inside & (lane >= col)
    right = inside & (lane < col)
    rows = []
    for q in range(PER):
        moved = block if q == 0 else pltpu.roll(block, LANES - q * FOOT, 1)
        rows.append(
            jnp.concatenate(
                [jnp.where(left, moved, 0.0), jnp.where(right, moved, 0.0)], axis=1
            ).astype(BF16)
        )
    return rows


def tile_rows(inbox, which, block, frames):
    lefts = inbox[:, inbox.shape[1] - LANES :].astype(F32)
    col = jnp.broadcast_to(lefts[:, which : which + 1], lefts.shape).astype(jnp.int32)
    start = 3 * frames + block * LANES
    if not isinstance(start, int):
        start = pl.multiple_of(start, LANES)
    return spread(inbox[:, pl.ds(start, LANES)].astype(F32), col)


def model_row(row, inbox, which, frames):
    traces = inbox[:, which * frames : (which + 1) * frames]
    return lax.dot_general(row, traces, (((0,), (0,)), ((), ())), preferred_element_type=F32)


def noise_row(left, change):
    frames = left.shape[1]
    steps = dot(left, change)
    steps = steps * steps
    part = steps[:, 0:LANES]
    for k in range(1, frames // LANES):
        part = part + steps[:, k * LANES : (k + 1) * LANES]
    return jnp.sum(part.T, axis=0, keepdims=True) / (frames - 1)


def lag_table(size):
    shape = (size, size)
    return lax.broadcasted_iota(jnp.int32, shape, 1) - lax.broadcasted_iota(jnp.int32, shape, 0)


def change_matrix(frames):
    lag = lag_table(frames)
    steps = jnp.where(lag == -1, 1.0, 0.0) - jnp.where(lag == 0, 1.0, 0.0)
    later = lax.broadcasted_iota(jnp.int32, lag.shape, 1)
    return jnp.where(later < frames - 1, steps, 0.0).astype(BF16)


def residual_kernel(
    inbox, movie, foot_rows, residual, noise, change, movie_slots, foot_slots, left_slots, sems
):
    rows, _, frames = movie.shape[1:]
    groups = rows // PER
    change[...] = change_matrix(frames)

    def fetch(g, slot):
        rows_g = pl.ds(g * PER, PER)
        return pltpu.make_async_copy(movie.at[0, rows_g], movie_slots.at[slot], sems.at[0, slot])

    def sends(g, slot):
        rows_g = pl.ds(g * PER, PER)
        return (
            pltpu.make_async_copy(foot_slots.at[slot], foot_rows.at[rows_g], sems.at[1, slot]),
            pltpu.make_async_copy(left_slots.at[slot], residual.at[rows_g], sems.at[2, slot]),
        )

    fetch(0, 0).start()

    def group(g, carry):
        slot = lax.rem(g, 2)

        @pl.when(g + 1 < groups)
        def _():
            fetch(g + 1, 1 - slot).start()

        fetch(g, slot).wait()

        @pl.when(g >= 2)
        def _():
            for copy in sends(g - 2, slot):
                copy.wait()

        noises = []
        for q, row in enumerate(tile_rows(inbox, 0, g, frames)):
            foot_slots[slot, q] = row
            left = movie_slots[slot, q].astype(F32) - model_row(row, inbox, 0, frames)
            left = left.astype(BF16)
            left_slots[slot, q] = left
            noises.append(noise_row(left, change[...]))
        noise[g] = jnp.concatenate(noises, axis=0)
        for copy in sends(g, slot):
            copy.start()
        return carry

    lax.fori_loop(0, groups, group, 0)
    for g in (groups - 2, groups - 1):
        for copy in sends(g, g % 2):
            copy.wait()


def make_residual(inbox, movie):
    slots = inbox.shape[0]
    rows, cols, frames = movie.shape[1:]
    return pl.pallas_call(
        residual_kernel,
        in_specs=[VMEM, HBM],
        out_specs=[HBM, HBM, VMEM],
        out_shape=(
            jax.ShapeDtypeStruct((rows, slots, cols), BF16),
            jax.ShapeDtypeStruct((rows, cols, frames), BF16),
            jax.ShapeDtypeStruct((rows // PER, PER, cols), F32),
        ),
        scratch_shapes=[
            pltpu.VMEM((frames, frames), BF16),
            pltpu.VMEM((2, PER, cols, frames), BF16),
            pltpu.VMEM((2, PER, slots, cols), BF16),
            pltpu.VMEM((2, PER, cols, frames), BF16),
            pltpu.SemaphoreType.DMA((3, 2)),
        ],
        compiler_params=params(44),
        cost_estimate=COST,
        name="residual",
    )(inbox, movie)


def near_kernel(inbox, movie_next, movie_prev, own_noise, foot_rows, residual, noise):
    frames = movie_next.shape[2]
    groups = own_noise.shape[0]
    own = FOOT // PER
    change = change_matrix(frames)
    for g in range(groups):
        noise[NEAR + g * PER : NEAR + (g + 1) * PER, :] = own_noise[g]
    for side, (block, movie, first) in enumerate(
        ((own, movie_next, 0), (own + 2 * RAD // PER - 1, movie_prev, NEAR + groups * PER))
    ):
        for q, row in enumerate(tile_rows(inbox, 1 + side, block, frames)):
            y = side * NEAR + q
            foot_rows[y] = row
            left = movie[q].astype(F32) - model_row(row, inbox, 1 + side, frames)
            left = left.astype(BF16)
            residual[y] = left
            noise[first + q : first + q + 1, :] = noise_row(left, change)


def make_near(inbox, movie_next, movie_prev, noise):
    slots = inbox.shape[0]
    groups, per, _ = noise.shape
    cols, frames = movie_next.shape[1:]
    return pl.pallas_call(
        near_kernel,
        out_shape=(
            jax.ShapeDtypeStruct((2 * NEAR, slots, cols), BF16),
            jax.ShapeDtypeStruct((2 * NEAR, cols, frames), BF16),
            jax.ShapeDtypeStruct((2 * NEAR + groups * per, cols), F32),
        ),
        compiler_params=params(),
        cost_estimate=COST,
        name="near",
    )(inbox, movie_next, movie_prev, noise)


def outer_kernel(inbox, model):
    frames = model.shape[2]
    first = (FOOT + NEAR) // PER
    groups = (RAD - NEAR) // PER
    for side in range(2):
        for g in range(groups):
            k = side * groups + g
            for q, row in enumerate(tile_rows(inbox, 1 + side, first + k, frames)):
                model[k * PER + q] = model_row(row, inbox, 1 + side, frames)


def make_outer_model(inbox, cols, frames):
    return pl.pallas_call(
        outer_kernel,
        out_shape=jax.ShapeDtypeStruct((2 * (RAD - NEAR), cols, frames), F32),
        compiler_params=params(),
        cost_estimate=COST,
        name="outer_model",
    )(inbox)


def weights_kernel(
    taps, own, near, noise, noise_before, noise_after, out, out_next, out_prev,
    own_slots, scale, band, sems,
):
    rows, slots, cols = own.shape
    part = own_slots.shape[2]
    count = slots // part

    def fetch(i, slot):
        these = pl.ds(pl.multiple_of(i * part, part), part)
        return pltpu.make_async_copy(own.at[:, these, :], own_slots.at[slot], sems.at[slot])

    fetch(0, 0).start()
    pooled = (noise_before[...] + 2.0 * noise[...] + noise_after[...]) / 4.0
    scale[...] = 1.0 / jnp.sqrt(pooled + noise_eps)
    lag = jnp.abs(lag_table(cols))
    table = jnp.zeros(lag.shape, F32)
    for k in range(GR + 1):
        table = jnp.where(lag == k, taps[GR + k], table)
    band[...] = table.astype(BF16)

    def across(foot, inv):
        scaled = (foot.astype(F32) * inv[:, None, :]).astype(BF16)
        count = foot.shape[0]
        return dot(scaled.reshape(count * part, cols), band[...]).reshape(count, part, cols)

    def some(i, carry):
        slot = lax.rem(i, 2)

        @pl.when(i + 1 < count)
        def _():
            fetch(i + 1, 1 - slot).start()

        fetch(i, slot).wait()
        these = pl.ds(pl.multiple_of(i * part, part), part)
        blurred = across(own_slots[slot], scale[NEAR : NEAR + rows])
        for r in range(rows):
            total = taps[GR] * blurred[r]
            for k in range(1, GR + 1):
                if r - k >= 0 and r + k < rows:
                    total = total + taps[GR + k] * (blurred[r - k] + blurred[r + k])
                elif r - k >= 0:
                    total = total + taps[GR + k] * blurred[r - k]
                elif r + k < rows:
                    total = total + taps[GR + k] * blurred[r + k]
            out[r, these, :] = total.astype(BF16)
        after = across(near[0:GR, these, :], scale[0:GR])
        ahead = across(near[2 * NEAR - GR : 2 * NEAR, these, :], scale[rows + 2 * NEAR - GR :])
        for a in range(GR):
            total = taps[2 * GR - a] * after[0]
            for r in range(1, a + 1):
                total = total + taps[2 * GR + r - a] * after[r]
            out_next[a, these, :] = total.astype(BF16)
            total = taps[2 * GR] * ahead[a]
            for b in range(a + 1, GR):
                total = total + taps[2 * GR + a - b] * ahead[b]
            out_prev[a, these, :] = total.astype(BF16)
        return carry

    lax.fori_loop(0, count, some, 0)


def make_weights(foot_rows, near_rows, noises):
    rows, slots, cols = foot_rows.shape
    part = 32
    return pl.pallas_call(
        functools.partial(weights_kernel, [float(t) for t in tap_values()]),
        in_specs=[HBM] + [VMEM] * (1 + len(noises)),
        out_shape=(
            jax.ShapeDtypeStruct((rows, slots, cols), BF16),
            jax.ShapeDtypeStruct((GR, slots, cols), BF16),
            jax.ShapeDtypeStruct((GR, slots, cols), BF16),
        ),
        scratch_shapes=[
            pltpu.VMEM((2, rows, part, cols), BF16),
            pltpu.VMEM(noises[0].shape, F32),
            pltpu.VMEM((cols, cols), BF16),
            pltpu.SemaphoreType.DMA((2,)),
        ],
        compiler_params=params(32),
        cost_estimate=COST,
        name="weights",
    )(foot_rows, near_rows, *noises)


def annulus_group(g, own, leaving, entering, weight, gain, band, column, total, outgoing):
    cols, frames = own.shape[1:]
    top = lax.broadcasted_iota(jnp.int32, (cols // 8, 8, LANES), 1) < 4
    blank = jnp.zeros((2, 8, LANES), F32)
    outs = [leaving(q) for q in range(PER)]
    news = [entering(q) for q in range(PER)]
    levels = [dot(band, jnp.concatenate([o, n], axis=0)) for o, n in zip(outs, news)]
    column = list(column)
    dets = []
    for q in range(PER):
        det = []
        for h in range(frames // LANES):
            part = slice(h * LANES, (h + 1) * LANES)
            inner = column[h] - outs[q][:, part].astype(F32)
            column[h] = inner + news[q][:, part].astype(F32)
            turned = pltpu.roll(inner.reshape(cols // 8, 8, LANES), 4, 1)
            turned = jnp.concatenate([blank, turned, blank], axis=0)
            both = turned[0 : cols // 8 + 1] + turned[3 : cols // 8 + 4]
            sides = jnp.where(top, both[0 : cols // 8], both[1 : cols // 8 + 1])
            fit = (levels[q][:, part] + sides.reshape(cols, LANES)) * gain
            outgoing[g, q, :, part] = fit.astype(BF16)
            det.append((own[g * PER + q, :, part].astype(F32) - fit).astype(BF16))
        dets.append(jnp.concatenate(det, axis=1))
    weights = jnp.concatenate([weight[g * PER + q] for q in range(PER)], axis=1)
    total = total + dot(weights, jnp.concatenate(dets, axis=0))
    return column, total, dets


def halves(ref):
    return [ref[:, h * LANES : (h + 1) * LANES] for h in range(ref.shape[1] // LANES)]


def add_rows(column, rows, sign=1.0):
    for row in rows:
        column = [c + sign * r.astype(F32) for c, r in zip(column, halves(row))]
    return column


def put(ref, column):
    for h, value in enumerate(column):
        ref[:, h * LANES : (h + 1) * LANES] = value


def sender(outgoing, background, sems):
    def send(g):
        return pltpu.make_async_copy(
            outgoing.at[g], background.at[0, pl.ds(g * PER, PER)], sems.at[g]
        )

    return send


def tables(gain):
    cols = gain.shape[1]
    band = jnp.where(jnp.abs(lag_table(cols)) <= RAD, 1.0, 0.0).astype(BF16)
    return (
        jnp.broadcast_to(gain[...], (LANES, cols)).T / (8.0 * RAD),
        jnp.concatenate([band, band], axis=1),
    )


def middle_kernel(own, near, weight, gain, background, upper, lower, total, outgoing, sems):
    rows, cols, frames = own.shape
    groups = range((RAD - NEAR) // PER, (rows - RAD + NEAR) // PER)
    send = sender(outgoing, background, sems)
    gains, band = tables(gain)
    column = [jnp.zeros((cols, LANES), F32)] * (frames // LANES)
    column = add_rows(column, [near[NEAR + r] for r in range(NEAR)])
    column = add_rows(column, [own[r] for r in range(RAD)])
    put(upper, column)
    column = add_rows(column, [own[RAD + r] for r in range(2 * RAD - NEAR - RAD)])
    grown = jnp.zeros(total.shape, F32)
    for g in groups:
        y = g * PER
        column, grown, _ = annulus_group(
            g,
            own,
            (lambda q: near[NEAR + y - RAD + NEAR + q])
            if y < RAD
            else (lambda q: own[y - RAD + q]),
            (lambda q: near[y + RAD - rows + q])
            if y + RAD >= rows
            else (lambda q: own[y + RAD + q]),
            weight, gains, band, column, grown, outgoing,
        )
        send(g).start()
    put(lower, column)
    total[...] = grown
    for g in groups:
        send(g).wait()


def ends_kernel(
    own, movie_prev, movie_next, model, weight, weight_next, weight_prev, gain, before,
    upper, lower, total, background, gradient, outgoing, sems,
):
    del before
    rows, _, frames = own.shape
    outer = RAD - NEAR
    count = outer // PER
    send = sender(outgoing, background, sems)
    gains, band = tables(gain)
    above, below = [
        [(movie[r].astype(F32) - model[first + r]).astype(BF16) for r in range(outer)]
        for movie, first in ((movie_prev, outer), (movie_next, 0))
    ]
    high, low = add_rows(halves(upper), above), halves(lower)
    grown = total[...]
    dets = {}
    for k in range(count):
        y, z = k * PER, rows - outer + k * PER
        high, grown, dets[y] = annulus_group(
            y // PER, own, lambda q: above[y + q], lambda q: own[y + RAD + q],
            weight, gains, band, high, grown, outgoing,
        )
        send(y // PER).start()
        low, grown, dets[z] = annulus_group(
            z // PER, own, lambda q: own[z - RAD + q], lambda q: below[k * PER + q],
            weight, gains, band, low, grown, outgoing,
        )
        send(z // PER).start()
    edges = ((2, weight_next, dets[rows - PER][PER - GR :]), (3, weight_prev, dets[0][:GR]))
    for at, edge, parts in edges:
        value = dot(
            jnp.concatenate([edge[a] for a in range(GR)], axis=1), jnp.concatenate(parts, axis=0)
        )
        gradient[:, at * frames : (at + 1) * frames] = value.astype(BF16)
    coarse = grown.astype(BF16)
    gradient[:, 0:frames] = coarse
    gradient[:, frames : 2 * frames] = (grown - coarse.astype(F32)).astype(BF16)
    for k in range(count):
        send(k).wait()
        send(rows // PER - 1 - k).wait()


def make_annulus(own, near, outer_prev, outer_next, model, weights, gain):
    rows, cols, frames = own.shape
    weight, weight_next, weight_prev = weights
    slots = weight.shape[1]
    background = jax.ShapeDtypeStruct((1, rows, cols, frames), BF16)
    column = jax.ShapeDtypeStruct((cols, frames), F32)
    total = jax.ShapeDtypeStruct((slots, frames), F32)
    gradient = jax.ShapeDtypeStruct((slots, 4 * frames), BF16)

    def call(kernel, name, args, outs, done):
        specs = [VMEM] * len(args)
        if done is not None:
            specs[done] = HBM
        return pl.pallas_call(
            kernel,
            in_specs=specs,
            out_specs=[HBM] + [VMEM] * (len(outs) - 1),
            out_shape=outs,
            scratch_shapes=[
                pltpu.VMEM((rows // PER, PER, cols, frames), BF16),
                pltpu.SemaphoreType.DMA((rows // PER,)),
            ],
            input_output_aliases={} if done is None else {done: 0},
            compiler_params=params(),
            cost_estimate=COST,
            name=name,
        )(*args)

    done, upper, lower, grown = call(
        middle_kernel, "annulus_middle", (own, near, weight, gain),
        (background, column, column, total), None,
    )
    return call(
        ends_kernel, "annulus_ends",
        (own, outer_prev, outer_next, model, weight, weight_next, weight_prev, gain, done, upper,
         lower, grown),
        (background, gradient), 8,
    )


def traces_kernel(capacity, stripe, slow, fast, step, traces, inbox, out):
    count, frames = traces.shape
    slots = inbox.shape[0]

    def upended(row):
        return jnp.broadcast_to(row[...].astype(F32), (LANES, count)).T

    before = lax.broadcasted_iota(jnp.int32, (count, count), 1) < lax.broadcasted_iota(
        jnp.int32, (count, count), 0
    )
    named = upended(stripe)
    same = (named == stripe[...].astype(F32)) & before
    rank = jnp.sum(jnp.where(same, 1.0, 0.0), axis=1, keepdims=True)
    slot = (named[:, 0:1] * capacity + rank).astype(jnp.int32)
    place = lax.broadcasted_iota(jnp.int32, (count, slots), 1)

    def onehot(shift):
        return jnp.where(place + shift == slot, 1.0, 0.0).astype(BF16)

    here = onehot(0)
    gradient = (
        dot(here, inbox[:, 0:frames])
        + dot(here, inbox[:, frames : 2 * frames])
        + dot(onehot(capacity), inbox[:, 2 * frames : 3 * frames])
        + dot(onehot(-capacity), inbox[:, 3 * frames : 4 * frames])
    )

    def wide(row):
        return jnp.concatenate([upended(row)] * (frames // LANES), axis=1)

    updated = traces[...].astype(F32) + wide(step) * gradient
    lane = lax.broadcasted_iota(jnp.int32, (count, frames), 1)

    def lagged(value, lag):
        return jnp.where(lane >= lag, pltpu.roll(value, lag, 1), 0.0)

    a, b = wide(slow), wide(fast)
    driven = updated - (a + b) * lagged(updated, 1) + (a * b) * lagged(updated, 2)
    spikes = jnp.maximum(driven - lam_floor, 0.0)
    sums = [spikes, spikes]
    roots = [a, b]
    lag = 1
    while lag < frames:
        sums = [value + root * lagged(value, lag) for value, root in zip(sums, roots)]
        roots = [root * root for root in roots]
        lag *= 2
    share = (1.0 - a) * (1.0 - b) / (a - b)
    out[...] = share * (a * sums[0] - b * sums[1])


def make_traces(stripe, slow, fast, step, traces, inbox, capacity):
    count, frames = traces.shape
    return pl.pallas_call(
        functools.partial(traces_kernel, capacity),
        out_shape=jax.ShapeDtypeStruct((count, frames), F32),
        compiler_params=params(),
        cost_estimate=COST,
        name="traces",
    )(stripe, slow, fast, step, traces, inbox)


def neighbours(axis):
    devices = lax.axis_size(axis)
    up = [(i, i + 1) for i in range(devices - 1)]
    return up, [(j, i) for i, j in up]


def on_device(movie, footprints, traces, stripe, column, annulus_gain, decay_slow, decay_fast):
    pix_count = lax.axis_size("pix")
    rows, cols, frames = movie.shape[1:]
    count = footprints.shape[1]
    capacity = max(2, 2 * count // pix_count)
    slots = pix_count * capacity
    pix_up, pix_down = neighbours("pix")
    plane_up, plane_down = neighbours("plane")

    stripe_row = stripe.reshape(1, count)
    outbox = make_outbox(stripe_row, column, footprints[0], traces[0], capacity, slots)
    frames_in, outbox = lax.optimization_barrier((movie, outbox))
    inbox = lax.all_to_all(outbox, "pix", split_axis=0, concat_axis=0, tiled=True)

    def exchange(cut):
        return (lax.ppermute(cut[0], "pix", pix_up), lax.ppermute(cut[1], "pix", pix_down))

    near_prev, near_next = exchange((frames_in[0, rows - NEAR :], frames_in[0, :NEAR]))
    outer_prev, outer_next = exchange(
        (frames_in[0, rows - RAD : rows - NEAR], frames_in[0, NEAR:RAD])
    )

    foot_rows, residual, noise = make_residual(inbox, movie)
    near_rows, near_residual, noise = make_near(inbox, near_next, near_prev, noise)
    noises = (
        noise,
        lax.ppermute(noise, "plane", plane_up),
        lax.ppermute(noise, "plane", plane_down),
    )
    weights = make_weights(foot_rows, near_rows, noises)
    model = make_outer_model(inbox, cols, frames)
    background, gradient = make_annulus(
        residual, near_residual, outer_prev, outer_next, model, weights, annulus_gain
    )
    home = lax.all_to_all(gradient, "pix", split_axis=0, concat_axis=0, tiled=True)
    foot_f = footprints[0].astype(F32)
    step = 1.0 / (jnp.sum(foot_f * foot_f, axis=1) + norm_eps)
    traces_new = make_traces(
        stripe_row, decay_slow, decay_fast, step[None], traces[0], home, capacity
    )
    return (background, traces_new[None])


def solution(mesh):
    placed = (
        P("plane", "pix", None, None),
        P("plane", "pix", None),
        P("plane", "pix", None),
        P("plane", "pix", None),
        P("plane", "pix"),
        P("plane", None),
        P("plane", "pix"),
        P("plane", "pix"),
    )
    return jax.shard_map(
        on_device,
        mesh=mesh,
        in_specs=placed,
        out_specs=(P("plane", "pix", None, None), P("plane", "pix", None)),
        check_vma=False,
    )
```

```python
import functools

import jax
import jax.numpy as jnp
import ml_dtypes
import numpy as np
from jax import lax
from jax.experimental import pallas as pl
from jax.experimental.pallas import tpu as pltpu
from jax.sharding import PartitionSpec as P

FOOT = 32
RAD = 12
GR = 3
LANES = 128
PER = LANES // FOOT
NEAR = PER

lam_floor = 0.1
noise_eps = 1e-05
norm_eps = 1e-05
sigma_twice = 4.5

F32 = jnp.float32
BF16 = jnp.bfloat16
MIB = 1 << 20
HBM = pl.BlockSpec(memory_space=pltpu.HBM)
VMEM = pl.BlockSpec(memory_space=pltpu.VMEM)


def tap_values():
    offsets = np.arange(-GR, GR + 1).astype(np.float32)
    raw = np.exp(-offsets * offsets / np.float32(sigma_twice)).astype(np.float32)
    return (raw / raw.sum(dtype=np.float32)).astype(ml_dtypes.bfloat16).astype(np.float32)


def params(mib=16):
    return pltpu.CompilerParams(vmem_limit_bytes=mib * MIB)


COST = pl.CostEstimate(flops=1, bytes_accessed=1, transcendentals=0)


def dot(a, b):
    return jnp.dot(a, b, preferred_element_type=F32)


def outbox_kernel(capacity, *refs):
    sources, outbox, places, sems = refs[0:4], refs[4], refs[5:9], refs[9]
    copies = [
        pltpu.make_async_copy(source, place, sems.at[k])
        for k, (source, place) in enumerate(zip(sources, places))
    ]
    for copy in copies:
        copy.start()
    for copy in copies:
        copy.wait()
    stripe, column, foot, traces = places
    slots = outbox.shape[0]
    count, tiles = foot.shape
    frames = traces.shape[1]
    before = lax.broadcasted_iota(jnp.int32, (count, count), 0) < lax.broadcasted_iota(
        jnp.int32, (count, count), 1
    )
    named = jnp.broadcast_to(stripe[...].astype(F32), (count, count))
    same = (named == named.T) & before
    rank = jnp.sum(jnp.where(same, 1.0, 0.0), axis=0, keepdims=True).astype(jnp.int32)
    slot = stripe[...] * capacity + rank
    place = lax.broadcasted_iota(jnp.int32, (slots, count), 0)
    left = jnp.broadcast_to(column[...].astype(F32), (LANES, count)).T.astype(BF16)
    lane = lax.broadcasted_iota(jnp.int32, (slots, LANES), 1)
    edge = RAD * FOOT
    lefts = jnp.zeros((slots, LANES), F32)
    at = 3 * frames
    for k, (shift, first, width) in enumerate(
        ((0, 0, tiles), (capacity, 0, edge), (-capacity, tiles - edge, edge))
    ):
        hot = jnp.where(place + shift == slot, 1.0, 0.0).astype(BF16)
        outbox[:, k * frames : (k + 1) * frames] = dot(hot, traces[...]).astype(BF16)
        outbox[:, at : at + width] = dot(hot, foot[:, first : first + width]).astype(BF16)
        lefts = jnp.where(lane == k, dot(hot, left), lefts)
        at += width
    outbox[:, at:] = lefts.astype(BF16)


def make_outbox(stripe, column, foot, traces, capacity, slots):
    count, tiles = foot.shape
    frames = traces.shape[1]
    width = 3 * frames + tiles + 2 * RAD * FOOT + LANES
    args = (stripe, column, foot, traces)
    return pl.pallas_call(
        functools.partial(outbox_kernel, capacity),
        in_specs=[HBM] * len(args),
        out_shape=jax.ShapeDtypeStruct((slots, width), BF16),
        scratch_shapes=[pltpu.VMEM(a.shape, a.dtype) for a in args]
        + [pltpu.SemaphoreType.DMA((len(args),))],
        compiler_params=params(56),
        cost_estimate=COST,
        name="outbox",
    )(*args)


def spread(block, col):
    lane = lax.broadcasted_iota(jnp.int32, block.shape, 1)
    for k in range(7):
        block = jnp.where(((col >> k) & 1) == 1, pltpu.roll(block, 1 << k, 1), block)
    inside = ((lane - col) & (LANES - 1)) < FOOT
    left = inside & (lane >= col)
    right = inside & (lane < col)
    rows = []
    for q in range(PER):
        moved = block if q == 0 else pltpu.roll(block, LANES - q * FOOT, 1)
        rows.append(
            jnp.concatenate(
                [jnp.where(left, moved, 0.0), jnp.where(right, moved, 0.0)], axis=1
            ).astype(BF16)
        )
    return rows


def tile_rows(inbox, which, block, frames):
    lefts = inbox[:, inbox.shape[1] - LANES :].astype(F32)
    col = jnp.broadcast_to(lefts[:, which : which + 1], lefts.shape).astype(jnp.int32)
    start = 3 * frames + block * LANES
    if not isinstance(start, int):
        start = pl.multiple_of(start, LANES)
    return spread(inbox[:, pl.ds(start, LANES)].astype(F32), col)


def model_row(row, inbox, which, frames):
    traces = inbox[:, which * frames : (which + 1) * frames]
    return lax.dot_general(row, traces, (((0,), (0,)), ((), ())), preferred_element_type=F32)


def noise_row(left, change):
    frames = left.shape[1]
    steps = dot(left, change)
    steps = steps * steps
    part = steps[:, 0:LANES]
    for k in range(1, frames // LANES):
        part = part + steps[:, k * LANES : (k + 1) * LANES]
    return jnp.sum(part.T, axis=0, keepdims=True) / (frames - 1)


def lag_table(size):
    shape = (size, size)
    return lax.broadcasted_iota(jnp.int32, shape, 1) - lax.broadcasted_iota(jnp.int32, shape, 0)


def change_matrix(frames):
    lag = lag_table(frames)
    steps = jnp.where(lag == -1, 1.0, 0.0) - jnp.where(lag == 0, 1.0, 0.0)
    later = lax.broadcasted_iota(jnp.int32, lag.shape, 1)
    return jnp.where(later < frames - 1, steps, 0.0).astype(BF16)


def residual_kernel(
    inbox, movie, foot_rows, residual, noise, change, movie_slots, foot_slots, left_slots, sems
):
    rows, _, frames = movie.shape[1:]
    groups = rows // PER
    change[...] = change_matrix(frames)

    def fetch(g, slot):
        rows_g = pl.ds(g * PER, PER)
        return pltpu.make_async_copy(movie.at[0, rows_g], movie_slots.at[slot], sems.at[0, slot])

    def sends(g, slot):
        rows_g = pl.ds(g * PER, PER)
        return (
            pltpu.make_async_copy(foot_slots.at[slot], foot_rows.at[rows_g], sems.at[1, slot]),
            pltpu.make_async_copy(left_slots.at[slot], residual.at[rows_g], sems.at[2, slot]),
        )

    fetch(0, 0).start()

    def group(g, carry):
        slot = lax.rem(g, 2)

        @pl.when(g + 1 < groups)
        def _():
            fetch(g + 1, 1 - slot).start()

        fetch(g, slot).wait()

        @pl.when(g >= 2)
        def _():
            for copy in sends(g - 2, slot):
                copy.wait()

        noises = []
        for q, row in enumerate(tile_rows(inbox, 0, g, frames)):
            foot_slots[slot, q] = row
            left = movie_slots[slot, q].astype(F32) - model_row(row, inbox, 0, frames)
            left = left.astype(BF16)
            left_slots[slot, q] = left
            noises.append(noise_row(left, change[...]))
        noise[g] = jnp.concatenate(noises, axis=0)
        for copy in sends(g, slot):
            copy.start()
        return carry

    lax.fori_loop(0, groups, group, 0)
    for g in (groups - 2, groups - 1):
        for copy in sends(g, g % 2):
            copy.wait()


def make_residual(inbox, movie):
    slots = inbox.shape[0]
    rows, cols, frames = movie.shape[1:]
    return pl.pallas_call(
        residual_kernel,
        in_specs=[VMEM, HBM],
        out_specs=[HBM, HBM, VMEM],
        out_shape=(
            jax.ShapeDtypeStruct((rows, slots, cols), BF16),
            jax.ShapeDtypeStruct((rows, cols, frames), BF16),
            jax.ShapeDtypeStruct((rows // PER, PER, cols), F32),
        ),
        scratch_shapes=[
            pltpu.VMEM((frames, frames), BF16),
            pltpu.VMEM((2, PER, cols, frames), BF16),
            pltpu.VMEM((2, PER, slots, cols), BF16),
            pltpu.VMEM((2, PER, cols, frames), BF16),
            pltpu.SemaphoreType.DMA((3, 2)),
        ],
        compiler_params=params(44),
        cost_estimate=COST,
        name="residual",
    )(inbox, movie)


def near_kernel(inbox, movie_next, movie_prev, own_noise, foot_rows, residual, noise):
    frames = movie_next.shape[2]
    groups = own_noise.shape[0]
    own = FOOT // PER
    change = change_matrix(frames)
    for g in range(groups):
        noise[NEAR + g * PER : NEAR + (g + 1) * PER, :] = own_noise[g]
    for side, (block, movie, first) in enumerate(
        ((own, movie_next, 0), (own + 2 * RAD // PER - 1, movie_prev, NEAR + groups * PER))
    ):
        for q, row in enumerate(tile_rows(inbox, 1 + side, block, frames)):
            y = side * NEAR + q
            foot_rows[y] = row
            left = movie[q].astype(F32) - model_row(row, inbox, 1 + side, frames)
            left = left.astype(BF16)
            residual[y] = left
            noise[first + q : first + q + 1, :] = noise_row(left, change)


def make_near(inbox, movie_next, movie_prev, noise):
    slots = inbox.shape[0]
    groups, per, _ = noise.shape
    cols, frames = movie_next.shape[1:]
    return pl.pallas_call(
        near_kernel,
        out_shape=(
            jax.ShapeDtypeStruct((2 * NEAR, slots, cols), BF16),
            jax.ShapeDtypeStruct((2 * NEAR, cols, frames), BF16),
            jax.ShapeDtypeStruct((2 * NEAR + groups * per, cols), F32),
        ),
        compiler_params=params(),
        cost_estimate=COST,
        name="near",
    )(inbox, movie_next, movie_prev, noise)


def outer_kernel(inbox, model):
    frames = model.shape[2]
    first = (FOOT + NEAR) // PER
    groups = (RAD - NEAR) // PER
    for side in range(2):
        for g in range(groups):
            k = side * groups + g
            for q, row in enumerate(tile_rows(inbox, 1 + side, first + k, frames)):
                model[k * PER + q] = model_row(row, inbox, 1 + side, frames)


def make_outer_model(inbox, cols, frames):
    return pl.pallas_call(
        outer_kernel,
        out_shape=jax.ShapeDtypeStruct((2 * (RAD - NEAR), cols, frames), F32),
        compiler_params=params(),
        cost_estimate=COST,
        name="outer_model",
    )(inbox)


def weights_kernel(
    taps, own, near, noise, noise_before, noise_after, out, out_next, out_prev,
    own_slots, scale, band, sems,
):
    rows, slots, cols = own.shape
    part = own_slots.shape[2]
    count = slots // part

    def fetch(i, slot):
        these = pl.ds(pl.multiple_of(i * part, part), part)
        return pltpu.make_async_copy(own.at[:, these, :], own_slots.at[slot], sems.at[slot])

    fetch(0, 0).start()
    pooled = (noise_before[...] + 2.0 * noise[...] + noise_after[...]) / 4.0
    scale[...] = 1.0 / jnp.sqrt(pooled + noise_eps)
    lag = jnp.abs(lag_table(cols))
    table = jnp.zeros(lag.shape, F32)
    for k in range(GR + 1):
        table = jnp.where(lag == k, taps[GR + k], table)
    band[...] = table.astype(BF16)

    def across(foot, inv):
        scaled = (foot.astype(F32) * inv[:, None, :]).astype(BF16)
        count = foot.shape[0]
        return dot(scaled.reshape(count * part, cols), band[...]).reshape(count, part, cols)

    def some(i, carry):
        slot = lax.rem(i, 2)

        @pl.when(i + 1 < count)
        def _():
            fetch(i + 1, 1 - slot).start()

        fetch(i, slot).wait()
        these = pl.ds(pl.multiple_of(i * part, part), part)
        blurred = across(own_slots[slot], scale[NEAR : NEAR + rows])
        for r in range(rows):
            total = taps[GR] * blurred[r]
            for k in range(1, GR + 1):
                if r - k >= 0 and r + k < rows:
                    total = total + taps[GR + k] * (blurred[r - k] + blurred[r + k])
                elif r - k >= 0:
                    total = total + taps[GR + k] * blurred[r - k]
                elif r + k < rows:
                    total = total + taps[GR + k] * blurred[r + k]
            out[r, these, :] = total.astype(BF16)
        after = across(near[0:GR, these, :], scale[0:GR])
        ahead = across(near[2 * NEAR - GR : 2 * NEAR, these, :], scale[rows + 2 * NEAR - GR :])
        for a in range(GR):
            total = taps[2 * GR - a] * after[0]
            for r in range(1, a + 1):
                total = total + taps[2 * GR + r - a] * after[r]
            out_next[a, these, :] = total.astype(BF16)
            total = taps[2 * GR] * ahead[a]
            for b in range(a + 1, GR):
                total = total + taps[2 * GR + a - b] * ahead[b]
            out_prev[a, these, :] = total.astype(BF16)
        return carry

    lax.fori_loop(0, count, some, 0)


def make_weights(foot_rows, near_rows, noises):
    rows, slots, cols = foot_rows.shape
    part = 32
    return pl.pallas_call(
        functools.partial(weights_kernel, [float(t) for t in tap_values()]),
        in_specs=[HBM] + [VMEM] * (1 + len(noises)),
        out_shape=(
            jax.ShapeDtypeStruct((rows, slots, cols), BF16),
            jax.ShapeDtypeStruct((GR, slots, cols), BF16),
            jax.ShapeDtypeStruct((GR, slots, cols), BF16),
        ),
        scratch_shapes=[
            pltpu.VMEM((2, rows, part, cols), BF16),
            pltpu.VMEM(noises[0].shape, F32),
            pltpu.VMEM((cols, cols), BF16),
            pltpu.SemaphoreType.DMA((2,)),
        ],
        compiler_params=params(32),
        cost_estimate=COST,
        name="weights",
    )(foot_rows, near_rows, *noises)


def annulus_group(g, own, leaving, entering, weight, gain, band, column, total, outgoing):
    cols, frames = own.shape[1:]
    top = lax.broadcasted_iota(jnp.int32, (cols // 8, 8, LANES), 1) < 4
    blank = jnp.zeros((2, 8, LANES), F32)
    outs = [leaving(q) for q in range(PER)]
    news = [entering(q) for q in range(PER)]
    levels = [dot(band, jnp.concatenate([o, n], axis=0)) for o, n in zip(outs, news)]
    column = list(column)
    dets = []
    for q in range(PER):
        det = []
        for h in range(frames // LANES):
            part = slice(h * LANES, (h + 1) * LANES)
            inner = column[h] - outs[q][:, part].astype(F32)
            column[h] = inner + news[q][:, part].astype(F32)
            turned = pltpu.roll(inner.reshape(cols // 8, 8, LANES), 4, 1)
            turned = jnp.concatenate([blank, turned, blank], axis=0)
            both = turned[0 : cols // 8 + 1] + turned[3 : cols // 8 + 4]
            sides = jnp.where(top, both[0 : cols // 8], both[1 : cols // 8 + 1])
            fit = (levels[q][:, part] + sides.reshape(cols, LANES)) * gain
            outgoing[g, q, :, part] = fit.astype(BF16)
            det.append((own[g * PER + q, :, part].astype(F32) - fit).astype(BF16))
        dets.append(jnp.concatenate(det, axis=1))
    weights = jnp.concatenate([weight[g * PER + q] for q in range(PER)], axis=1)
    total = total + dot(weights, jnp.concatenate(dets, axis=0))
    return column, total, dets


def halves(ref):
    return [ref[:, h * LANES : (h + 1) * LANES] for h in range(ref.shape[1] // LANES)]


def add_rows(column, rows, sign=1.0):
    for row in rows:
        column = [c + sign * r.astype(F32) for c, r in zip(column, halves(row))]
    return column


def put(ref, column):
    for h, value in enumerate(column):
        ref[:, h * LANES : (h + 1) * LANES] = value


def sender(outgoing, background, sems):
    def send(g):
        return pltpu.make_async_copy(
            outgoing.at[g], background.at[0, pl.ds(g * PER, PER)], sems.at[g]
        )

    return send


def tables(gain):
    cols = gain.shape[1]
    band = jnp.where(jnp.abs(lag_table(cols)) <= RAD, 1.0, 0.0).astype(BF16)
    return (
        jnp.broadcast_to(gain[...], (LANES, cols)).T / (8.0 * RAD),
        jnp.concatenate([band, band], axis=1),
    )


def middle_kernel(own, near, weight, gain, background, upper, lower, total, outgoing, sems):
    rows, cols, frames = own.shape
    groups = range((RAD - NEAR) // PER, (rows - RAD + NEAR) // PER)
    send = sender(outgoing, background, sems)
    gains, band = tables(gain)
    column = [jnp.zeros((cols, LANES), F32)] * (frames // LANES)
    column = add_rows(column, [near[NEAR + r] for r in range(NEAR)])
    column = add_rows(column, [own[r] for r in range(RAD)])
    put(upper, column)
    column = add_rows(column, [own[RAD + r] for r in range(2 * RAD - NEAR - RAD)])
    grown = jnp.zeros(total.shape, F32)
    for g in groups:
        y = g * PER
        column, grown, _ = annulus_group(
            g,
            own,
            (lambda q: near[NEAR + y - RAD + NEAR + q])
            if y < RAD
            else (lambda q: own[y - RAD + q]),
            (lambda q: near[y + RAD - rows + q])
            if y + RAD >= rows
            else (lambda q: own[y + RAD + q]),
            weight, gains, band, column, grown, outgoing,
        )
        send(g).start()
    put(lower, column)
    total[...] = grown
    for g in groups:
        send(g).wait()


def ends_kernel(
    own, movie_prev, movie_next, model, weight, weight_next, weight_prev, gain, before,
    upper, lower, total, background, gradient, outgoing, sems,
):
    del before
    rows, _, frames = own.shape
    outer = RAD - NEAR
    count = outer // PER
    send = sender(outgoing, background, sems)
    gains, band = tables(gain)
    above, below = [
        [(movie[r].astype(F32) - model[first + r]).astype(BF16) for r in range(outer)]
        for movie, first in ((movie_prev, outer), (movie_next, 0))
    ]
    high, low = add_rows(halves(upper), above), halves(lower)
    grown = total[...]
    dets = {}
    for k in range(count):
        y, z = k * PER, rows - outer + k * PER
        high, grown, dets[y] = annulus_group(
            y // PER, own, lambda q: above[y + q], lambda q: own[y + RAD + q],
            weight, gains, band, high, grown, outgoing,
        )
        send(y // PER).start()
        low, grown, dets[z] = annulus_group(
            z // PER, own, lambda q: own[z - RAD + q], lambda q: below[k * PER + q],
            weight, gains, band, low, grown, outgoing,
        )
        send(z // PER).start()
    edges = ((2, weight_next, dets[rows - PER][PER - GR :]), (3, weight_prev, dets[0][:GR]))
    for at, edge, parts in edges:
        value = dot(
            jnp.concatenate([edge[a] for a in range(GR)], axis=1), jnp.concatenate(parts, axis=0)
        )
        gradient[:, at * frames : (at + 1) * frames] = value.astype(BF16)
    coarse = grown.astype(BF16)
    gradient[:, 0:frames] = coarse
    gradient[:, frames : 2 * frames] = (grown - coarse.astype(F32)).astype(BF16)
    for k in range(count):
        send(k).wait()
        send(rows // PER - 1 - k).wait()


def make_annulus(own, near, outer_prev, outer_next, model, weights, gain):
    rows, cols, frames = own.shape
    weight, weight_next, weight_prev = weights
    slots = weight.shape[1]
    background = jax.ShapeDtypeStruct((1, rows, cols, frames), BF16)
    column = jax.ShapeDtypeStruct((cols, frames), F32)
    total = jax.ShapeDtypeStruct((slots, frames), F32)
    gradient = jax.ShapeDtypeStruct((slots, 4 * frames), BF16)

    def call(kernel, name, args, outs, done):
        specs = [VMEM] * len(args)
        if done is not None:
            specs[done] = HBM
        return pl.pallas_call(
            kernel,
            in_specs=specs,
            out_specs=[HBM] + [VMEM] * (len(outs) - 1),
            out_shape=outs,
            scratch_shapes=[
                pltpu.VMEM((rows // PER, PER, cols, frames), BF16),
                pltpu.SemaphoreType.DMA((rows // PER,)),
            ],
            input_output_aliases={} if done is None else {done: 0},
            compiler_params=params(),
            cost_estimate=COST,
            name=name,
        )(*args)

    done, upper, lower, grown = call(
        middle_kernel, "annulus_middle", (own, near, weight, gain),
        (background, column, column, total), None,
    )
    return call(
        ends_kernel, "annulus_ends",
        (own, outer_prev, outer_next, model, weight, weight_next, weight_prev, gain, done, upper,
         lower, grown),
        (background, gradient), 8,
    )


def traces_kernel(capacity, stripe, slow, fast, step, traces, inbox, out):
    count, frames = traces.shape
    slots = inbox.shape[0]

    def upended(row):
        return jnp.broadcast_to(row[...].astype(F32), (LANES, count)).T

    before = lax.broadcasted_iota(jnp.int32, (count, count), 1) < lax.broadcasted_iota(
        jnp.int32, (count, count), 0
    )
    named = upended(stripe)
    same = (named == stripe[...].astype(F32)) & before
    rank = jnp.sum(jnp.where(same, 1.0, 0.0), axis=1, keepdims=True)
    slot = (named[:, 0:1] * capacity + rank).astype(jnp.int32)
    place = lax.broadcasted_iota(jnp.int32, (count, slots), 1)

    def onehot(shift):
        return jnp.where(place + shift == slot, 1.0, 0.0).astype(BF16)

    here = onehot(0)
    gradient = (
        dot(here, inbox[:, 0:frames])
        + dot(here, inbox[:, frames : 2 * frames])
        + dot(onehot(capacity), inbox[:, 2 * frames : 3 * frames])
        + dot(onehot(-capacity), inbox[:, 3 * frames : 4 * frames])
    )

    def wide(row):
        return jnp.concatenate([upended(row)] * (frames // LANES), axis=1)

    updated = traces[...].astype(F32) + wide(step) * gradient
    lane = lax.broadcasted_iota(jnp.int32, (count, frames), 1)

    def lagged(value, lag):
        return jnp.where(lane >= lag, pltpu.roll(value, lag, 1), 0.0)

    a, b = wide(slow), wide(fast)
    driven = updated - (a + b) * lagged(updated, 1) + (a * b) * lagged(updated, 2)
    spikes = jnp.maximum(driven - lam_floor, 0.0)
    sums = [spikes, spikes]
    roots = [a, b]
    lag = 1
    while lag < frames:
        sums = [value + root * lagged(value, lag) for value, root in zip(sums, roots)]
        roots = [root * root for root in roots]
        lag *= 2
    share = (1.0 - a) * (1.0 - b) / (a - b)
    out[...] = share * (a * sums[0] - b * sums[1])


def make_traces(stripe, slow, fast, step, traces, inbox, capacity):
    count, frames = traces.shape
    return pl.pallas_call(
        functools.partial(traces_kernel, capacity),
        out_shape=jax.ShapeDtypeStruct((count, frames), F32),
        compiler_params=params(),
        cost_estimate=COST,
        name="traces",
    )(stripe, slow, fast, step, traces, inbox)


def neighbours(axis):
    devices = lax.axis_size(axis)
    up = [(i, i + 1) for i in range(devices - 1)]
    return up, [(j, i) for i, j in up]


def on_device(movie, footprints, traces, stripe, column, annulus_gain, decay_slow, decay_fast):
    pix_count = lax.axis_size("pix")
    rows, cols, frames = movie.shape[1:]
    count = footprints.shape[1]
    capacity = max(2, 2 * count // pix_count)
    slots = pix_count * capacity
    pix_up, pix_down = neighbours("pix")
    plane_up, plane_down = neighbours("plane")

    stripe_row = stripe.reshape(1, count)
    outbox = make_outbox(stripe_row, column, footprints[0], traces[0], capacity, slots)
    frames_in, outbox = lax.optimization_barrier((movie, outbox))
    inbox = lax.all_to_all(outbox, "pix", split_axis=0, concat_axis=0, tiled=True)

    def exchange(cut):
        return (lax.ppermute(cut[0], "pix", pix_up), lax.ppermute(cut[1], "pix", pix_down))

    near_prev, near_next = exchange((frames_in[0, rows - NEAR :], frames_in[0, :NEAR]))
    cut, inbox = lax.optimization_barrier(
        ((frames_in[0, rows - RAD : rows - NEAR], frames_in[0, NEAR:RAD]), inbox)
    )
    outer_prev, outer_next = exchange(cut)

    foot_rows, residual, noise = make_residual(inbox, movie)
    near_rows, near_residual, noise = make_near(inbox, near_next, near_prev, noise)
    noises = (
        noise,
        lax.ppermute(noise, "plane", plane_up),
        lax.ppermute(noise, "plane", plane_down),
    )
    weights = make_weights(foot_rows, near_rows, noises)
    model = make_outer_model(inbox, cols, frames)
    background, gradient = make_annulus(
        residual, near_residual, outer_prev, outer_next, model, weights, annulus_gain
    )
    home = lax.all_to_all(gradient, "pix", split_axis=0, concat_axis=0, tiled=True)
    foot_f = footprints[0].astype(F32)
    step = 1.0 / (jnp.sum(foot_f * foot_f, axis=1) + norm_eps)
    traces_new = make_traces(
        stripe_row, decay_slow, decay_fast, step[None], traces[0], home, capacity
    )
    return (background, traces_new[None])


def solution(mesh):
    placed = (
        P("plane", "pix", None, None),
        P("plane", "pix", None),
        P("plane", "pix", None),
        P("plane", "pix", None),
        P("plane", "pix"),
        P("plane", None),
        P("plane", "pix"),
        P("plane", "pix"),
    )
    return jax.shard_map(
        on_device,
        mesh=mesh,
        in_specs=placed,
        out_specs=(P("plane", "pix", None, None), P("plane", "pix", None)),
        check_vma=False,
    )
```

```python
import functools

import jax
import jax.numpy as jnp
import ml_dtypes
import numpy as np
from jax import lax
from jax.experimental import pallas as pl
from jax.experimental.pallas import tpu as pltpu
from jax.sharding import PartitionSpec as P

FOOT = 32
RAD = 12
GR = 3
LANES = 128
PER = LANES // FOOT
NEAR = PER

lam_floor = 0.1
noise_eps = 1e-05
norm_eps = 1e-05
sigma_twice = 4.5

F32 = jnp.float32
BF16 = jnp.bfloat16
MIB = 1 << 20
HBM = pl.BlockSpec(memory_space=pltpu.HBM)
VMEM = pl.BlockSpec(memory_space=pltpu.VMEM)


def tap_values():
    offsets = np.arange(-GR, GR + 1).astype(np.float32)
    raw = np.exp(-offsets * offsets / np.float32(sigma_twice)).astype(np.float32)
    return (raw / raw.sum(dtype=np.float32)).astype(ml_dtypes.bfloat16).astype(np.float32)


def params(mib=16):
    return pltpu.CompilerParams(vmem_limit_bytes=mib * MIB)


COST = pl.CostEstimate(flops=1, bytes_accessed=1, transcendentals=0)


def dot(a, b):
    return jnp.dot(a, b, preferred_element_type=F32)


def outbox_kernel(capacity, *refs):
    sources, outbox, places, sems = refs[0:4], refs[4], refs[5:9], refs[9]
    copies = [
        pltpu.make_async_copy(source, place, sems.at[k])
        for k, (source, place) in enumerate(zip(sources, places))
    ]
    for copy in copies:
        copy.start()
    for copy in copies:
        copy.wait()
    stripe, column, foot, traces = places
    slots = outbox.shape[0]
    count, tiles = foot.shape
    frames = traces.shape[1]
    before = lax.broadcasted_iota(jnp.int32, (count, count), 0) < lax.broadcasted_iota(
        jnp.int32, (count, count), 1
    )
    named = jnp.broadcast_to(stripe[...].astype(F32), (count, count))
    same = (named == named.T) & before
    rank = jnp.sum(jnp.where(same, 1.0, 0.0), axis=0, keepdims=True).astype(jnp.int32)
    slot = stripe[...] * capacity + rank
    place = lax.broadcasted_iota(jnp.int32, (slots, count), 0)
    left = jnp.broadcast_to(column[...].astype(F32), (LANES, count)).T.astype(BF16)
    lane = lax.broadcasted_iota(jnp.int32, (slots, LANES), 1)
    edge = RAD * FOOT
    lefts = jnp.zeros((slots, LANES), F32)
    at = 3 * frames
    for k, (shift, first, width) in enumerate(
        ((0, 0, tiles), (capacity, 0, edge), (-capacity, tiles - edge, edge))
    ):
        hot = jnp.where(place + shift == slot, 1.0, 0.0).astype(BF16)
        outbox[:, k * frames : (k + 1) * frames] = dot(hot, traces[...]).astype(BF16)
        outbox[:, at : at + width] = dot(hot, foot[:, first : first + width]).astype(BF16)
        lefts = jnp.where(lane == k, dot(hot, left), lefts)
        at += width
    outbox[:, at:] = lefts.astype(BF16)


def make_outbox(stripe, column, foot, traces, capacity, slots):
    count, tiles = foot.shape
    frames = traces.shape[1]
    width = 3 * frames + tiles + 2 * RAD * FOOT + LANES
    args = (stripe, column, foot, traces)
    return pl.pallas_call(
        functools.partial(outbox_kernel, capacity),
        in_specs=[HBM] * len(args),
        out_shape=jax.ShapeDtypeStruct((slots, width), BF16),
        scratch_shapes=[pltpu.VMEM(a.shape, a.dtype) for a in args]
        + [pltpu.SemaphoreType.DMA((len(args),))],
        compiler_params=params(56),
        cost_estimate=COST,
        name="outbox",
    )(*args)


def spread(block, col):
    lane = lax.broadcasted_iota(jnp.int32, block.shape, 1)
    for k in range(7):
        block = jnp.where(((col >> k) & 1) == 1, pltpu.roll(block, 1 << k, 1), block)
    inside = ((lane - col) & (LANES - 1)) < FOOT
    left = inside & (lane >= col)
    right = inside & (lane < col)
    rows = []
    for q in range(PER):
        moved = block if q == 0 else pltpu.roll(block, LANES - q * FOOT, 1)
        rows.append(
            jnp.concatenate(
                [jnp.where(left, moved, 0.0), jnp.where(right, moved, 0.0)], axis=1
            ).astype(BF16)
        )
    return rows


def tile_rows(inbox, which, block, frames):
    lefts = inbox[:, inbox.shape[1] - LANES :].astype(F32)
    col = jnp.broadcast_to(lefts[:, which : which + 1], lefts.shape).astype(jnp.int32)
    start = 3 * frames + block * LANES
    if not isinstance(start, int):
        start = pl.multiple_of(start, LANES)
    return spread(inbox[:, pl.ds(start, LANES)].astype(F32), col)


def model_row(row, inbox, which, frames):
    traces = inbox[:, which * frames : (which + 1) * frames]
    return lax.dot_general(row, traces, (((0,), (0,)), ((), ())), preferred_element_type=F32)


def noise_row(left, change):
    frames = left.shape[1]
    steps = dot(left, change)
    steps = steps * steps
    part = steps[:, 0:LANES]
    for k in range(1, frames // LANES):
        part = part + steps[:, k * LANES : (k + 1) * LANES]
    return jnp.sum(part.T, axis=0, keepdims=True) / (frames - 1)


def lag_table(size):
    shape = (size, size)
    return lax.broadcasted_iota(jnp.int32, shape, 1) - lax.broadcasted_iota(jnp.int32, shape, 0)


def change_matrix(frames):
    lag = lag_table(frames)
    steps = jnp.where(lag == -1, 1.0, 0.0) - jnp.where(lag == 0, 1.0, 0.0)
    later = lax.broadcasted_iota(jnp.int32, lag.shape, 1)
    return jnp.where(later < frames - 1, steps, 0.0).astype(BF16)


def residual_kernel(
    inbox, movie, foot_rows, residual, noise, change, movie_slots, foot_slots, left_slots, sems
):
    rows, _, frames = movie.shape[1:]
    groups = rows // PER
    change[...] = change_matrix(frames)

    def fetch(g, slot):
        rows_g = pl.ds(g * PER, PER)
        return pltpu.make_async_copy(movie.at[0, rows_g], movie_slots.at[slot], sems.at[0, slot])

    def sends(g, slot):
        rows_g = pl.ds(g * PER, PER)
        return (
            pltpu.make_async_copy(foot_slots.at[slot], foot_rows.at[rows_g], sems.at[1, slot]),
            pltpu.make_async_copy(left_slots.at[slot], residual.at[rows_g], sems.at[2, slot]),
        )

    fetch(0, 0).start()

    def group(g, carry):
        slot = lax.rem(g, 2)

        @pl.when(g + 1 < groups)
        def _():
            fetch(g + 1, 1 - slot).start()

        fetch(g, slot).wait()

        @pl.when(g >= 2)
        def _():
            for copy in sends(g - 2, slot):
                copy.wait()

        noises = []
        for q, row in enumerate(tile_rows(inbox, 0, g, frames)):
            foot_slots[slot, q] = row
            left = movie_slots[slot, q].astype(F32) - model_row(row, inbox, 0, frames)
            left = left.astype(BF16)
            left_slots[slot, q] = left
            noises.append(noise_row(left, change[...]))
        noise[g] = jnp.concatenate(noises, axis=0)
        for copy in sends(g, slot):
            copy.start()
        return carry

    lax.fori_loop(0, groups, group, 0)
    for g in (groups - 2, groups - 1):
        for copy in sends(g, g % 2):
            copy.wait()


def make_residual(inbox, movie):
    slots = inbox.shape[0]
    rows, cols, frames = movie.shape[1:]
    return pl.pallas_call(
        residual_kernel,
        in_specs=[VMEM, HBM],
        out_specs=[HBM, HBM, VMEM],
        out_shape=(
            jax.ShapeDtypeStruct((rows, slots, cols), BF16),
            jax.ShapeDtypeStruct((rows, cols, frames), BF16),
            jax.ShapeDtypeStruct((rows // PER, PER, cols), F32),
        ),
        scratch_shapes=[
            pltpu.VMEM((frames, frames), BF16),
            pltpu.VMEM((2, PER, cols, frames), BF16),
            pltpu.VMEM((2, PER, slots, cols), BF16),
            pltpu.VMEM((2, PER, cols, frames), BF16),
            pltpu.SemaphoreType.DMA((3, 2)),
        ],
        compiler_params=params(44),
        cost_estimate=COST,
        name="residual",
    )(inbox, movie)


def near_kernel(inbox, movie_next, movie_prev, own_noise, foot_rows, residual, noise):
    frames = movie_next.shape[2]
    groups = own_noise.shape[0]
    own = FOOT // PER
    change = change_matrix(frames)
    for g in range(groups):
        noise[NEAR + g * PER : NEAR + (g + 1) * PER, :] = own_noise[g]
    for side, (block, movie, first) in enumerate(
        ((own, movie_next, 0), (own + 2 * RAD // PER - 1, movie_prev, NEAR + groups * PER))
    ):
        for q, row in enumerate(tile_rows(inbox, 1 + side, block, frames)):
            y = side * NEAR + q
            foot_rows[y] = row
            left = movie[q].astype(F32) - model_row(row, inbox, 1 + side, frames)
            left = left.astype(BF16)
            residual[y] = left
            noise[first + q : first + q + 1, :] = noise_row(left, change)


def make_near(inbox, movie_next, movie_prev, noise):
    slots = inbox.shape[0]
    groups, per, _ = noise.shape
    cols, frames = movie_next.shape[1:]
    return pl.pallas_call(
        near_kernel,
        out_shape=(
            jax.ShapeDtypeStruct((2 * NEAR, slots, cols), BF16),
            jax.ShapeDtypeStruct((2 * NEAR, cols, frames), BF16),
            jax.ShapeDtypeStruct((2 * NEAR + groups * per, cols), F32),
        ),
        compiler_params=params(),
        cost_estimate=COST,
        name="near",
    )(inbox, movie_next, movie_prev, noise)


def outer_kernel(inbox, model):
    frames = model.shape[2]
    first = (FOOT + NEAR) // PER
    groups = (RAD - NEAR) // PER
    for side in range(2):
        for g in range(groups):
            k = side * groups + g
            for q, row in enumerate(tile_rows(inbox, 1 + side, first + k, frames)):
                model[k * PER + q] = model_row(row, inbox, 1 + side, frames)


def make_outer_model(inbox, cols, frames):
    return pl.pallas_call(
        outer_kernel,
        out_shape=jax.ShapeDtypeStruct((2 * (RAD - NEAR), cols, frames), F32),
        compiler_params=params(),
        cost_estimate=COST,
        name="outer_model",
    )(inbox)


def weights_kernel(
    taps, own, near, noise, noise_before, noise_after, out, out_next, out_prev,
    own_slots, scale, band, sems,
):
    rows, slots, cols = own.shape
    part = own_slots.shape[2]
    count = slots // part

    def fetch(i, slot):
        these = pl.ds(pl.multiple_of(i * part, part), part)
        return pltpu.make_async_copy(own.at[:, these, :], own_slots.at[slot], sems.at[slot])

    fetch(0, 0).start()
    pooled = (noise_before[...] + 2.0 * noise[...] + noise_after[...]) / 4.0
    scale[...] = 1.0 / jnp.sqrt(pooled + noise_eps)
    lag = jnp.abs(lag_table(cols))
    table = jnp.zeros(lag.shape, F32)
    for k in range(GR + 1):
        table = jnp.where(lag == k, taps[GR + k], table)
    band[...] = table.astype(BF16)

    def across(foot, inv):
        scaled = (foot.astype(F32) * inv[:, None, :]).astype(BF16)
        count = foot.shape[0]
        return dot(scaled.reshape(count * part, cols), band[...]).reshape(count, part, cols)

    def some(i, carry):
        slot = lax.rem(i, 2)

        @pl.when(i + 1 < count)
        def _():
            fetch(i + 1, 1 - slot).start()

        fetch(i, slot).wait()
        these = pl.ds(pl.multiple_of(i * part, part), part)
        blurred = across(own_slots[slot], scale[NEAR : NEAR + rows])
        for r in range(rows):
            total = taps[GR] * blurred[r]
            for k in range(1, GR + 1):
                if r - k >= 0 and r + k < rows:
                    total = total + taps[GR + k] * (blurred[r - k] + blurred[r + k])
                elif r - k >= 0:
                    total = total + taps[GR + k] * blurred[r - k]
                elif r + k < rows:
                    total = total + taps[GR + k] * blurred[r + k]
            out[r, these, :] = total.astype(BF16)
        after = across(near[0:GR, these, :], scale[0:GR])
        ahead = across(near[2 * NEAR - GR : 2 * NEAR, these, :], scale[rows + 2 * NEAR - GR :])
        for a in range(GR):
            total = taps[2 * GR - a] * after[0]
            for r in range(1, a + 1):
                total = total + taps[2 * GR + r - a] * after[r]
            out_next[a, these, :] = total.astype(BF16)
            total = taps[2 * GR] * ahead[a]
            for b in range(a + 1, GR):
                total = total + taps[2 * GR + a - b] * ahead[b]
            out_prev[a, these, :] = total.astype(BF16)
        return carry

    lax.fori_loop(0, count, some, 0)


def make_weights(foot_rows, near_rows, noises):
    rows, slots, cols = foot_rows.shape
    part = 32
    return pl.pallas_call(
        functools.partial(weights_kernel, [float(t) for t in tap_values()]),
        in_specs=[HBM] + [VMEM] * (1 + len(noises)),
        out_shape=(
            jax.ShapeDtypeStruct((rows, slots, cols), BF16),
            jax.ShapeDtypeStruct((GR, slots, cols), BF16),
            jax.ShapeDtypeStruct((GR, slots, cols), BF16),
        ),
        scratch_shapes=[
            pltpu.VMEM((2, rows, part, cols), BF16),
            pltpu.VMEM(noises[0].shape, F32),
            pltpu.VMEM((cols, cols), BF16),
            pltpu.SemaphoreType.DMA((2,)),
        ],
        compiler_params=params(32),
        cost_estimate=COST,
        name="weights",
    )(foot_rows, near_rows, *noises)


def annulus_group(g, own, leaving, entering, weight, gain, band, column, total, outgoing):
    cols, frames = own.shape[1:]
    top = lax.broadcasted_iota(jnp.int32, (cols // 8, 8, LANES), 1) < 4
    blank = jnp.zeros((2, 8, LANES), F32)
    outs = [leaving(q) for q in range(PER)]
    news = [entering(q) for q in range(PER)]
    levels = [dot(band, jnp.concatenate([o, n], axis=0)) for o, n in zip(outs, news)]
    column = list(column)
    dets = []
    for q in range(PER):
        det = []
        for h in range(frames // LANES):
            part = slice(h * LANES, (h + 1) * LANES)
            inner = column[h] - outs[q][:, part].astype(F32)
            column[h] = inner + news[q][:, part].astype(F32)
            turned = pltpu.roll(inner.reshape(cols // 8, 8, LANES), 4, 1)
            turned = jnp.concatenate([blank, turned, blank], axis=0)
            both = turned[0 : cols // 8 + 1] + turned[3 : cols // 8 + 4]
            sides = jnp.where(top, both[0 : cols // 8], both[1 : cols // 8 + 1])
            fit = (levels[q][:, part] + sides.reshape(cols, LANES)) * gain
            outgoing[g, q, :, part] = fit.astype(BF16)
            det.append((own[g * PER + q, :, part].astype(F32) - fit).astype(BF16))
        dets.append(jnp.concatenate(det, axis=1))
    weights = jnp.concatenate([weight[g * PER + q] for q in range(PER)], axis=1)
    total = total + dot(weights, jnp.concatenate(dets, axis=0))
    return column, total, dets


def halves(ref):
    return [ref[:, h * LANES : (h + 1) * LANES] for h in range(ref.shape[1] // LANES)]


def add_rows(column, rows, sign=1.0):
    for row in rows:
        column = [c + sign * r.astype(F32) for c, r in zip(column, halves(row))]
    return column


def put(ref, column):
    for h, value in enumerate(column):
        ref[:, h * LANES : (h + 1) * LANES] = value


def sender(outgoing, background, sems):
    def send(g):
        return pltpu.make_async_copy(
            outgoing.at[g], background.at[0, pl.ds(g * PER, PER)], sems.at[g]
        )

    return send


def tables(gain):
    cols = gain.shape[1]
    band = jnp.where(jnp.abs(lag_table(cols)) <= RAD, 1.0, 0.0).astype(BF16)
    return (
        jnp.broadcast_to(gain[...], (LANES, cols)).T / (8.0 * RAD),
        jnp.concatenate([band, band], axis=1),
    )


def middle_kernel(own, near, weight, gain, background, upper, lower, total, outgoing, sems):
    rows, cols, frames = own.shape
    groups = range((RAD - NEAR) // PER, (rows - RAD + NEAR) // PER)
    send = sender(outgoing, background, sems)
    gains, band = tables(gain)
    column = [jnp.zeros((cols, LANES), F32)] * (frames // LANES)
    column = add_rows(column, [near[NEAR + r] for r in range(NEAR)])
    column = add_rows(column, [own[r] for r in range(RAD)])
    put(upper, column)
    column = add_rows(column, [own[RAD + r] for r in range(2 * RAD - NEAR - RAD)])
    grown = jnp.zeros(total.shape, F32)
    for g in groups:
        y = g * PER
        column, grown, _ = annulus_group(
            g,
            own,
            (lambda q: near[NEAR + y - RAD + NEAR + q])
            if y < RAD
            else (lambda q: own[y - RAD + q]),
            (lambda q: near[y + RAD - rows + q])
            if y + RAD >= rows
            else (lambda q: own[y + RAD + q]),
            weight, gains, band, column, grown, outgoing,
        )
        send(g).start()
    put(lower, column)
    total[...] = grown
    for g in groups:
        send(g).wait()


def subtracted(movie, model, first):
    return [(movie[r].astype(F32) - model[first + r]).astype(BF16) for r in range(PER)]


def mid_kernel(
    own, movie_prev, movie_next, model, weight, gain, before, upper, lower, total,
    background, new_upper, new_lower, new_total, outgoing, sems,
):
    del before
    rows = own.shape[0]
    low, high = RAD // PER - 2, (rows - RAD) // PER + 1
    send = sender(outgoing, background, sems)
    gains, band = tables(gain)
    above = subtracted(movie_prev, model, model.shape[0] - PER)
    below = subtracted(movie_next, model, 0)
    column = add_rows(halves(upper), above)
    put(new_upper, column)
    column = add_rows(column, [own[RAD + r] for r in range(PER)])
    y, z = low * PER, high * PER
    _, grown, _ = annulus_group(
        low, own, lambda q: above[q], lambda q: own[y + RAD + q],
        weight, gains, band, column, total[...], outgoing,
    )
    send(low).start()
    column, grown, _ = annulus_group(
        high, own, lambda q: own[z - RAD + q], lambda q: below[q],
        weight, gains, band, halves(lower), grown, outgoing,
    )
    send(high).start()
    put(new_lower, column)
    new_total[...] = grown
    send(low).wait()
    send(high).wait()


def end_kernel(
    own, movie_prev, movie_next, model, weight, weight_next, weight_prev, gain, before,
    upper, lower, total, background, gradient, outgoing, sems,
):
    del before
    rows, _, frames = own.shape
    low, high = 0, rows // PER - 1
    half = model.shape[0] // 2
    send = sender(outgoing, background, sems)
    gains, band = tables(gain)
    above, below = subtracted(movie_prev, model, half), subtracted(movie_next, model, half - PER)
    z = high * PER
    _, grown, low_dets = annulus_group(
        low, own, lambda q: above[q], lambda q: own[RAD + q],
        weight, gains, band, add_rows(halves(upper), above), total[...], outgoing,
    )
    send(low).start()
    _, grown, high_dets = annulus_group(
        high, own, lambda q: own[z - RAD + q], lambda q: below[q],
        weight, gains, band, halves(lower), grown, outgoing,
    )
    send(high).start()
    edges = ((2, weight_next, high_dets[PER - GR :]), (3, weight_prev, low_dets[:GR]))
    for at, edge, parts in edges:
        value = dot(
            jnp.concatenate([edge[a] for a in range(GR)], axis=1), jnp.concatenate(parts, axis=0)
        )
        gradient[:, at * frames : (at + 1) * frames] = value.astype(BF16)
    coarse = grown.astype(BF16)
    gradient[:, 0:frames] = coarse
    gradient[:, frames : 2 * frames] = (grown - coarse.astype(F32)).astype(BF16)
    send(low).wait()
    send(high).wait()


def make_annulus(own, near, mid, far, model, weights, gain):
    rows, cols, frames = own.shape
    weight, weight_next, weight_prev = weights
    slots = weight.shape[1]
    background = jax.ShapeDtypeStruct((1, rows, cols, frames), BF16)
    column = jax.ShapeDtypeStruct((cols, frames), F32)
    total = jax.ShapeDtypeStruct((slots, frames), F32)
    gradient = jax.ShapeDtypeStruct((slots, 4 * frames), BF16)

    def call(kernel, name, args, outs, done, declared=COST):
        specs = [VMEM] * len(args)
        if done is not None:
            specs[done] = HBM
        return pl.pallas_call(
            kernel,
            in_specs=specs,
            out_specs=[HBM] + [VMEM] * (len(outs) - 1),
            out_shape=outs,
            scratch_shapes=[
                pltpu.VMEM((rows // PER, PER, cols, frames), BF16),
                pltpu.SemaphoreType.DMA((rows // PER,)),
            ],
            input_output_aliases={} if done is None else {done: 0},
            compiler_params=params(),
            cost_estimate=declared,
            name=name,
        )(*args)

    done, upper, lower, grown = call(
        middle_kernel, "annulus_middle", (own, near, weight, gain),
        (background, column, column, total), None,
    )
    done, upper, lower, grown = call(
        mid_kernel, "annulus_mid",
        (own, *mid, model, weight, gain, done, upper, lower, grown),
        (background, column, column, total), 6,
        pl.CostEstimate(
            flops=2 * rows * cols * cols * frames, bytes_accessed=5 * MIB, transcendentals=0
        ),
    )
    return call(
        end_kernel, "annulus_end",
        (own, *far, model, weight, weight_next, weight_prev, gain, done, upper, lower, grown),
        (background, gradient), 8,
    )


def traces_kernel(capacity, stripe, slow, fast, step, traces, inbox, out):
    count, frames = traces.shape
    slots = inbox.shape[0]

    def upended(row):
        return jnp.broadcast_to(row[...].astype(F32), (LANES, count)).T

    before = lax.broadcasted_iota(jnp.int32, (count, count), 1) < lax.broadcasted_iota(
        jnp.int32, (count, count), 0
    )
    named = upended(stripe)
    same = (named == stripe[...].astype(F32)) & before
    rank = jnp.sum(jnp.where(same, 1.0, 0.0), axis=1, keepdims=True)
    slot = (named[:, 0:1] * capacity + rank).astype(jnp.int32)
    place = lax.broadcasted_iota(jnp.int32, (count, slots), 1)

    def onehot(shift):
        return jnp.where(place + shift == slot, 1.0, 0.0).astype(BF16)

    here = onehot(0)
    gradient = (
        dot(here, inbox[:, 0:frames])
        + dot(here, inbox[:, frames : 2 * frames])
        + dot(onehot(capacity), inbox[:, 2 * frames : 3 * frames])
        + dot(onehot(-capacity), inbox[:, 3 * frames : 4 * frames])
    )

    def wide(row):
        return jnp.concatenate([upended(row)] * (frames // LANES), axis=1)

    updated = traces[...].astype(F32) + wide(step) * gradient
    lane = lax.broadcasted_iota(jnp.int32, (count, frames), 1)

    def lagged(value, lag):
        return jnp.where(lane >= lag, pltpu.roll(value, lag, 1), 0.0)

    a, b = wide(slow), wide(fast)
    driven = updated - (a + b) * lagged(updated, 1) + (a * b) * lagged(updated, 2)
    spikes = jnp.maximum(driven - lam_floor, 0.0)
    sums = [spikes, spikes]
    roots = [a, b]
    lag = 1
    while lag < frames:
        sums = [value + root * lagged(value, lag) for value, root in zip(sums, roots)]
        roots = [root * root for root in roots]
        lag *= 2
    share = (1.0 - a) * (1.0 - b) / (a - b)
    out[...] = share * (a * sums[0] - b * sums[1])


def make_traces(stripe, slow, fast, step, traces, inbox, capacity):
    count, frames = traces.shape
    return pl.pallas_call(
        functools.partial(traces_kernel, capacity),
        out_shape=jax.ShapeDtypeStruct((count, frames), F32),
        compiler_params=params(),
        cost_estimate=COST,
        name="traces",
    )(stripe, slow, fast, step, traces, inbox)


def neighbours(axis):
    devices = lax.axis_size(axis)
    up = [(i, i + 1) for i in range(devices - 1)]
    return up, [(j, i) for i, j in up]


def on_device(movie, footprints, traces, stripe, column, annulus_gain, decay_slow, decay_fast):
    pix_count = lax.axis_size("pix")
    rows, cols, frames = movie.shape[1:]
    count = footprints.shape[1]
    capacity = max(2, 2 * count // pix_count)
    slots = pix_count * capacity
    pix_up, pix_down = neighbours("pix")
    plane_up, plane_down = neighbours("plane")

    stripe_row = stripe.reshape(1, count)
    outbox = make_outbox(stripe_row, column, footprints[0], traces[0], capacity, slots)
    frames_in, outbox = lax.optimization_barrier((movie, outbox))
    inbox = lax.all_to_all(outbox, "pix", split_axis=0, concat_axis=0, tiled=True)
    cuts = [
        (frames_in[0, rows - k - PER : rows - k], frames_in[0, k : k + PER])
        for k in range(0, RAD, PER)
    ]
    cuts[1:], inbox = lax.optimization_barrier((cuts[1:], inbox))
    (near_prev, near_next), mid, far = [
        (lax.ppermute(above, "pix", pix_up), lax.ppermute(below, "pix", pix_down))
        for above, below in cuts
    ]

    foot_rows, residual, noise = make_residual(inbox, movie)
    near_rows, near_residual, noise = make_near(inbox, near_next, near_prev, noise)
    noises = (
        noise,
        lax.ppermute(noise, "plane", plane_up),
        lax.ppermute(noise, "plane", plane_down),
    )
    weights = make_weights(foot_rows, near_rows, noises)
    model = make_outer_model(inbox, cols, frames)
    background, gradient = make_annulus(
        residual, near_residual, mid, far, model, weights, annulus_gain
    )
    home = lax.all_to_all(gradient, "pix", split_axis=0, concat_axis=0, tiled=True)
    foot_f = footprints[0].astype(F32)
    step = 1.0 / (jnp.sum(foot_f * foot_f, axis=1) + norm_eps)
    traces_new = make_traces(
        stripe_row, decay_slow, decay_fast, step[None], traces[0], home, capacity
    )
    return (background, traces_new[None])


def solution(mesh):
    placed = (
        P("plane", "pix", None, None),
        P("plane", "pix", None),
        P("plane", "pix", None),
        P("plane", "pix", None),
        P("plane", "pix"),
        P("plane", None),
        P("plane", "pix"),
        P("plane", "pix"),
    )
    return jax.shard_map(
        on_device,
        mesh=mesh,
        in_specs=placed,
        out_specs=(P("plane", "pix", None, None), P("plane", "pix", None)),
        check_vma=False,
    )
```

```python
import functools

import jax
import jax.numpy as jnp
import ml_dtypes
import numpy as np
from jax import lax
from jax.experimental import pallas as pl
from jax.experimental.pallas import tpu as pltpu
from jax.sharding import PartitionSpec as P

FOOT = 32
RAD = 12
GR = 3
LANES = 128
PER = LANES // FOOT
NEAR = PER

lam_floor = 0.1
noise_eps = 1e-05
norm_eps = 1e-05
sigma_twice = 4.5

F32 = jnp.float32
BF16 = jnp.bfloat16
MIB = 1 << 20
HBM = pl.BlockSpec(memory_space=pltpu.HBM)
VMEM = pl.BlockSpec(memory_space=pltpu.VMEM)


def tap_values():
    offsets = np.arange(-GR, GR + 1).astype(np.float32)
    raw = np.exp(-offsets * offsets / np.float32(sigma_twice)).astype(np.float32)
    return (raw / raw.sum(dtype=np.float32)).astype(ml_dtypes.bfloat16).astype(np.float32)


def params(mib=16):
    return pltpu.CompilerParams(vmem_limit_bytes=mib * MIB)


COST = pl.CostEstimate(flops=1, bytes_accessed=1, transcendentals=0)


def dot(a, b):
    return jnp.dot(a, b, preferred_element_type=F32)


def outbox_kernel(capacity, *refs):
    sources, outbox, places, sems = refs[0:4], refs[4], refs[5:9], refs[9]
    copies = [
        pltpu.make_async_copy(source, place, sems.at[k])
        for k, (source, place) in enumerate(zip(sources, places))
    ]
    for copy in copies:
        copy.start()
    for copy in copies:
        copy.wait()
    stripe, column, foot, traces = places
    slots = outbox.shape[0]
    count, tiles = foot.shape
    frames = traces.shape[1]
    before = lax.broadcasted_iota(jnp.int32, (count, count), 0) < lax.broadcasted_iota(
        jnp.int32, (count, count), 1
    )
    named = jnp.broadcast_to(stripe[...].astype(F32), (count, count))
    same = (named == named.T) & before
    rank = jnp.sum(jnp.where(same, 1.0, 0.0), axis=0, keepdims=True).astype(jnp.int32)
    slot = stripe[...] * capacity + rank
    place = lax.broadcasted_iota(jnp.int32, (slots, count), 0)
    left = jnp.broadcast_to(column[...].astype(F32), (LANES, count)).T.astype(BF16)
    lane = lax.broadcasted_iota(jnp.int32, (slots, LANES), 1)
    edge = RAD * FOOT
    lefts = jnp.zeros((slots, LANES), F32)
    at = 3 * frames
    for k, (shift, first, width) in enumerate(
        ((0, 0, tiles), (capacity, 0, edge), (-capacity, tiles - edge, edge))
    ):
        hot = jnp.where(place + shift == slot, 1.0, 0.0).astype(BF16)
        outbox[:, k * frames : (k + 1) * frames] = dot(hot, traces[...]).astype(BF16)
        outbox[:, at : at + width] = dot(hot, foot[:, first : first + width]).astype(BF16)
        lefts = jnp.where(lane == k, dot(hot, left), lefts)
        at += width
    outbox[:, at:] = lefts.astype(BF16)


def make_outbox(stripe, column, foot, traces, capacity, slots):
    count, tiles = foot.shape
    frames = traces.shape[1]
    width = 3 * frames + tiles + 2 * RAD * FOOT + LANES
    args = (stripe, column, foot, traces)
    return pl.pallas_call(
        functools.partial(outbox_kernel, capacity),
        in_specs=[HBM] * len(args),
        out_shape=jax.ShapeDtypeStruct((slots, width), BF16),
        scratch_shapes=[pltpu.VMEM(a.shape, a.dtype) for a in args]
        + [pltpu.SemaphoreType.DMA((len(args),))],
        compiler_params=params(56),
        cost_estimate=COST,
        name="outbox",
    )(*args)


def spread(block, col):
    lane = lax.broadcasted_iota(jnp.int32, block.shape, 1)
    for k in range(7):
        block = jnp.where(((col >> k) & 1) == 1, pltpu.roll(block, 1 << k, 1), block)
    inside = ((lane - col) & (LANES - 1)) < FOOT
    left = inside & (lane >= col)
    right = inside & (lane < col)
    rows = []
    for q in range(PER):
        moved = block if q == 0 else pltpu.roll(block, LANES - q * FOOT, 1)
        rows.append(
            jnp.concatenate(
                [jnp.where(left, moved, 0.0), jnp.where(right, moved, 0.0)], axis=1
            ).astype(BF16)
        )
    return rows


def tile_rows(inbox, which, block, frames):
    lefts = inbox[:, inbox.shape[1] - LANES :].astype(F32)
    col = jnp.broadcast_to(lefts[:, which : which + 1], lefts.shape).astype(jnp.int32)
    start = 3 * frames + block * LANES
    if not isinstance(start, int):
        start = pl.multiple_of(start, LANES)
    return spread(inbox[:, pl.ds(start, LANES)].astype(F32), col)


def model_row(row, inbox, which, frames):
    traces = inbox[:, which * frames : (which + 1) * frames]
    return lax.dot_general(row, traces, (((0,), (0,)), ((), ())), preferred_element_type=F32)


def noise_row(left, change):
    frames = left.shape[1]
    steps = dot(left, change)
    steps = steps * steps
    part = steps[:, 0:LANES]
    for k in range(1, frames // LANES):
        part = part + steps[:, k * LANES : (k + 1) * LANES]
    return jnp.sum(part.T, axis=0, keepdims=True) / (frames - 1)


def lag_table(size):
    shape = (size, size)
    return lax.broadcasted_iota(jnp.int32, shape, 1) - lax.broadcasted_iota(jnp.int32, shape, 0)


def change_matrix(frames):
    lag = lag_table(frames)
    steps = jnp.where(lag == -1, 1.0, 0.0) - jnp.where(lag == 0, 1.0, 0.0)
    later = lax.broadcasted_iota(jnp.int32, lag.shape, 1)
    return jnp.where(later < frames - 1, steps, 0.0).astype(BF16)


def residual_kernel(
    inbox, movie, foot_rows, residual, noise, change, movie_slots, foot_slots, left_slots, sems
):
    rows, _, frames = movie.shape[1:]
    groups = rows // PER
    change[...] = change_matrix(frames)

    def fetch(g, slot):
        rows_g = pl.ds(g * PER, PER)
        return pltpu.make_async_copy(movie.at[0, rows_g], movie_slots.at[slot], sems.at[0, slot])

    def sends(g, slot):
        rows_g = pl.ds(g * PER, PER)
        return (
            pltpu.make_async_copy(foot_slots.at[slot], foot_rows.at[rows_g], sems.at[1, slot]),
            pltpu.make_async_copy(left_slots.at[slot], residual.at[rows_g], sems.at[2, slot]),
        )

    fetch(0, 0).start()

    def group(g, carry):
        slot = lax.rem(g, 2)

        @pl.when(g + 1 < groups)
        def _():
            fetch(g + 1, 1 - slot).start()

        fetch(g, slot).wait()

        @pl.when(g >= 2)
        def _():
            for copy in sends(g - 2, slot):
                copy.wait()

        noises = []
        for q, row in enumerate(tile_rows(inbox, 0, g, frames)):
            foot_slots[slot, q] = row
            left = movie_slots[slot, q].astype(F32) - model_row(row, inbox, 0, frames)
            left = left.astype(BF16)
            left_slots[slot, q] = left
            noises.append(noise_row(left, change[...]))
        noise[g] = jnp.concatenate(noises, axis=0)
        for copy in sends(g, slot):
            copy.start()
        return carry

    lax.fori_loop(0, groups, group, 0)
    for g in (groups - 2, groups - 1):
        for copy in sends(g, g % 2):
            copy.wait()


def make_residual(inbox, movie):
    slots = inbox.shape[0]
    rows, cols, frames = movie.shape[1:]
    return pl.pallas_call(
        residual_kernel,
        in_specs=[VMEM, HBM],
        out_specs=[HBM, HBM, VMEM],
        out_shape=(
            jax.ShapeDtypeStruct((rows, slots, cols), BF16),
            jax.ShapeDtypeStruct((rows, cols, frames), BF16),
            jax.ShapeDtypeStruct((rows // PER, PER, cols), F32),
        ),
        scratch_shapes=[
            pltpu.VMEM((frames, frames), BF16),
            pltpu.VMEM((2, PER, cols, frames), BF16),
            pltpu.VMEM((2, PER, slots, cols), BF16),
            pltpu.VMEM((2, PER, cols, frames), BF16),
            pltpu.SemaphoreType.DMA((3, 2)),
        ],
        compiler_params=params(44),
        cost_estimate=COST,
        name="residual",
    )(inbox, movie)


def near_kernel(inbox, movie_next, movie_prev, own_noise, foot_rows, residual, noise):
    frames = movie_next.shape[2]
    groups = own_noise.shape[0]
    own = FOOT // PER
    change = change_matrix(frames)
    for g in range(groups):
        noise[NEAR + g * PER : NEAR + (g + 1) * PER, :] = own_noise[g]
    for side, (block, movie, first) in enumerate(
        ((own, movie_next, 0), (own + 2 * RAD // PER - 1, movie_prev, NEAR + groups * PER))
    ):
        for q, row in enumerate(tile_rows(inbox, 1 + side, block, frames)):
            y = side * NEAR + q
            foot_rows[y] = row
            left = movie[q].astype(F32) - model_row(row, inbox, 1 + side, frames)
            left = left.astype(BF16)
            residual[y] = left
            noise[first + q : first + q + 1, :] = noise_row(left, change)


def make_near(inbox, movie_next, movie_prev, noise):
    slots = inbox.shape[0]
    groups, per, _ = noise.shape
    cols, frames = movie_next.shape[1:]
    return pl.pallas_call(
        near_kernel,
        out_shape=(
            jax.ShapeDtypeStruct((2 * NEAR, slots, cols), BF16),
            jax.ShapeDtypeStruct((2 * NEAR, cols, frames), BF16),
            jax.ShapeDtypeStruct((2 * NEAR + groups * per, cols), F32),
        ),
        compiler_params=params(),
        cost_estimate=COST,
        name="near",
    )(inbox, movie_next, movie_prev, noise)


def outer_kernel(inbox, model):
    frames = model.shape[2]
    first = (FOOT + NEAR) // PER
    groups = (RAD - NEAR) // PER
    for side in range(2):
        for g in range(groups):
            k = side * groups + g
            for q, row in enumerate(tile_rows(inbox, 1 + side, first + k, frames)):
                model[k * PER + q] = model_row(row, inbox, 1 + side, frames)


def make_outer_model(inbox, cols, frames):
    return pl.pallas_call(
        outer_kernel,
        out_shape=jax.ShapeDtypeStruct((2 * (RAD - NEAR), cols, frames), F32),
        compiler_params=params(),
        cost_estimate=COST,
        name="outer_model",
    )(inbox)


def weights_kernel(
    taps, own, near, noise, noise_before, noise_after, out, out_next, out_prev,
    own_slots, scale, band, sems,
):
    rows, slots, cols = own.shape
    part = own_slots.shape[2]
    count = slots // part

    def fetch(i, slot):
        these = pl.ds(pl.multiple_of(i * part, part), part)
        return pltpu.make_async_copy(own.at[:, these, :], own_slots.at[slot], sems.at[slot])

    fetch(0, 0).start()
    pooled = (noise_before[...] + 2.0 * noise[...] + noise_after[...]) / 4.0
    scale[...] = 1.0 / jnp.sqrt(pooled + noise_eps)
    lag = jnp.abs(lag_table(cols))
    table = jnp.zeros(lag.shape, F32)
    for k in range(GR + 1):
        table = jnp.where(lag == k, taps[GR + k], table)
    band[...] = table.astype(BF16)

    def across(foot, inv):
        scaled = (foot.astype(F32) * inv[:, None, :]).astype(BF16)
        count = foot.shape[0]
        return dot(scaled.reshape(count * part, cols), band[...]).reshape(count, part, cols)

    def some(i, carry):
        slot = lax.rem(i, 2)

        @pl.when(i + 1 < count)
        def _():
            fetch(i + 1, 1 - slot).start()

        fetch(i, slot).wait()
        these = pl.ds(pl.multiple_of(i * part, part), part)
        blurred = across(own_slots[slot], scale[NEAR : NEAR + rows])
        for r in range(rows):
            total = taps[GR] * blurred[r]
            for k in range(1, GR + 1):
                if r - k >= 0 and r + k < rows:
                    total = total + taps[GR + k] * (blurred[r - k] + blurred[r + k])
                elif r - k >= 0:
                    total = total + taps[GR + k] * blurred[r - k]
                elif r + k < rows:
                    total = total + taps[GR + k] * blurred[r + k]
            out[r, these, :] = total.astype(BF16)
        after = across(near[0:GR, these, :], scale[0:GR])
        ahead = across(near[2 * NEAR - GR : 2 * NEAR, these, :], scale[rows + 2 * NEAR - GR :])
        for a in range(GR):
            total = taps[2 * GR - a] * after[0]
            for r in range(1, a + 1):
                total = total + taps[2 * GR + r - a] * after[r]
            out_next[a, these, :] = total.astype(BF16)
            total = taps[2 * GR] * ahead[a]
            for b in range(a + 1, GR):
                total = total + taps[2 * GR + a - b] * ahead[b]
            out_prev[a, these, :] = total.astype(BF16)
        return carry

    lax.fori_loop(0, count, some, 0)


def make_weights(foot_rows, near_rows, noises):
    rows, slots, cols = foot_rows.shape
    part = 32
    return pl.pallas_call(
        functools.partial(weights_kernel, [float(t) for t in tap_values()]),
        in_specs=[HBM] + [VMEM] * (1 + len(noises)),
        out_shape=(
            jax.ShapeDtypeStruct((rows, slots, cols), BF16),
            jax.ShapeDtypeStruct((GR, slots, cols), BF16),
            jax.ShapeDtypeStruct((GR, slots, cols), BF16),
        ),
        scratch_shapes=[
            pltpu.VMEM((2, rows, part, cols), BF16),
            pltpu.VMEM(noises[0].shape, F32),
            pltpu.VMEM((cols, cols), BF16),
            pltpu.SemaphoreType.DMA((2,)),
        ],
        compiler_params=params(32),
        cost_estimate=COST,
        name="weights",
    )(foot_rows, near_rows, *noises)


def annulus_group(g, own, leaving, entering, weight, gain, band, column, total, outgoing):
    cols, frames = own.shape[1:]
    top = lax.broadcasted_iota(jnp.int32, (cols // 8, 8, LANES), 1) < 4
    blank = jnp.zeros((2, 8, LANES), F32)
    outs = [leaving(q) for q in range(PER)]
    news = [entering(q) for q in range(PER)]
    levels = [dot(band, jnp.concatenate([o, n], axis=0)) for o, n in zip(outs, news)]
    column = list(column)
    dets = []
    for q in range(PER):
        det = []
        for h in range(frames // LANES):
            part = slice(h * LANES, (h + 1) * LANES)
            inner = column[h] - outs[q][:, part].astype(F32)
            column[h] = inner + news[q][:, part].astype(F32)
            turned = pltpu.roll(inner.reshape(cols // 8, 8, LANES), 4, 1)
            turned = jnp.concatenate([blank, turned, blank], axis=0)
            both = turned[0 : cols // 8 + 1] + turned[3 : cols // 8 + 4]
            sides = jnp.where(top, both[0 : cols // 8], both[1 : cols // 8 + 1])
            fit = (levels[q][:, part] + sides.reshape(cols, LANES)) * gain
            outgoing[g, q, :, part] = fit.astype(BF16)
            det.append((own[g * PER + q, :, part].astype(F32) - fit).astype(BF16))
        dets.append(jnp.concatenate(det, axis=1))
    weights = jnp.concatenate([weight[g * PER + q] for q in range(PER)], axis=1)
    total = total + dot(weights, jnp.concatenate(dets, axis=0))
    return column, total, dets


def halves(ref):
    return [ref[:, h * LANES : (h + 1) * LANES] for h in range(ref.shape[1] // LANES)]


def add_rows(column, rows, sign=1.0):
    for row in rows:
        column = [c + sign * r.astype(F32) for c, r in zip(column, halves(row))]
    return column


def put(ref, column):
    for h, value in enumerate(column):
        ref[:, h * LANES : (h + 1) * LANES] = value


def sender(outgoing, background, sems):
    def send(g):
        return pltpu.make_async_copy(
            outgoing.at[g], background.at[0, pl.ds(g * PER, PER)], sems.at[g]
        )

    return send


def tables(gain):
    cols = gain.shape[1]
    band = jnp.where(jnp.abs(lag_table(cols)) <= RAD, 1.0, 0.0).astype(BF16)
    return (
        jnp.broadcast_to(gain[...], (LANES, cols)).T / (8.0 * RAD),
        jnp.concatenate([band, band], axis=1),
    )


def middle_kernel(own, near, weight, gain, background, upper, lower, total, outgoing, sems):
    rows, cols, frames = own.shape
    groups = range((RAD - NEAR) // PER, (rows - RAD + NEAR) // PER)
    send = sender(outgoing, background, sems)
    gains, band = tables(gain)
    column = [jnp.zeros((cols, LANES), F32)] * (frames // LANES)
    column = add_rows(column, [near[NEAR + r] for r in range(NEAR)])
    column = add_rows(column, [own[r] for r in range(RAD)])
    put(upper, column)
    column = add_rows(column, [own[RAD + r] for r in range(2 * RAD - NEAR - RAD)])
    grown = jnp.zeros(total.shape, F32)
    for g in groups:
        y = g * PER
        column, grown, _ = annulus_group(
            g,
            own,
            (lambda q: near[NEAR + y - RAD + NEAR + q])
            if y < RAD
            else (lambda q: own[y - RAD + q]),
            (lambda q: near[y + RAD - rows + q])
            if y + RAD >= rows
            else (lambda q: own[y + RAD + q]),
            weight, gains, band, column, grown, outgoing,
        )
        send(g).start()
    put(lower, column)
    total[...] = grown
    for g in groups:
        send(g).wait()


def subtracted(movie, model, first):
    return [(movie[r].astype(F32) - model[first + r]).astype(BF16) for r in range(PER)]


def mid_kernel(
    own, movie_prev, movie_next, model, weight, gain, before, upper, lower, total,
    background, new_upper, new_lower, new_total, outgoing, sems,
):
    del before
    rows = own.shape[0]
    low, high = RAD // PER - 2, (rows - RAD) // PER + 1
    send = sender(outgoing, background, sems)
    gains, band = tables(gain)
    above = subtracted(movie_prev, model, model.shape[0] - PER)
    below = subtracted(movie_next, model, 0)
    column = add_rows(halves(upper), above)
    put(new_upper, column)
    column = add_rows(column, [own[RAD + r] for r in range(PER)])
    y, z = low * PER, high * PER
    _, grown, _ = annulus_group(
        low, own, lambda q: above[q], lambda q: own[y + RAD + q],
        weight, gains, band, column, total[...], outgoing,
    )
    send(low).start()
    column, grown, _ = annulus_group(
        high, own, lambda q: own[z - RAD + q], lambda q: below[q],
        weight, gains, band, halves(lower), grown, outgoing,
    )
    send(high).start()
    put(new_lower, column)
    new_total[...] = grown
    send(low).wait()
    send(high).wait()


def end_kernel(
    own, movie_prev, movie_next, model, weight, weight_next, weight_prev, gain, before,
    upper, lower, total, background, gradient, outgoing, sems,
):
    del before
    rows, _, frames = own.shape
    low, high = 0, rows // PER - 1
    half = model.shape[0] // 2
    send = sender(outgoing, background, sems)
    gains, band = tables(gain)
    above, below = subtracted(movie_prev, model, half), subtracted(movie_next, model, half - PER)
    z = high * PER
    _, grown, low_dets = annulus_group(
        low, own, lambda q: above[q], lambda q: own[RAD + q],
        weight, gains, band, add_rows(halves(upper), above), total[...], outgoing,
    )
    send(low).start()
    _, grown, high_dets = annulus_group(
        high, own, lambda q: own[z - RAD + q], lambda q: below[q],
        weight, gains, band, halves(lower), grown, outgoing,
    )
    send(high).start()
    edges = ((2, weight_next, high_dets[PER - GR :]), (3, weight_prev, low_dets[:GR]))
    for at, edge, parts in edges:
        value = dot(
            jnp.concatenate([edge[a] for a in range(GR)], axis=1), jnp.concatenate(parts, axis=0)
        )
        gradient[:, at * frames : (at + 1) * frames] = value.astype(BF16)
    coarse = grown.astype(BF16)
    gradient[:, 0:frames] = coarse
    gradient[:, frames : 2 * frames] = (grown - coarse.astype(F32)).astype(BF16)
    send(low).wait()
    send(high).wait()


def make_annulus(own, near, mid, far, model, weights, gain):
    rows, cols, frames = own.shape
    weight, weight_next, weight_prev = weights
    slots = weight.shape[1]
    background = jax.ShapeDtypeStruct((1, rows, cols, frames), BF16)
    column = jax.ShapeDtypeStruct((cols, frames), F32)
    total = jax.ShapeDtypeStruct((slots, frames), F32)
    gradient = jax.ShapeDtypeStruct((slots, 4 * frames), BF16)

    def call(kernel, name, args, outs, done, declared=COST):
        specs = [VMEM] * len(args)
        if done is not None:
            specs[done] = HBM
        return pl.pallas_call(
            kernel,
            in_specs=specs,
            out_specs=[HBM] + [VMEM] * (len(outs) - 1),
            out_shape=outs,
            scratch_shapes=[
                pltpu.VMEM((rows // PER, PER, cols, frames), BF16),
                pltpu.SemaphoreType.DMA((rows // PER,)),
            ],
            input_output_aliases={} if done is None else {done: 0},
            compiler_params=params(),
            cost_estimate=declared,
            name=name,
        )(*args)

    done, upper, lower, grown = call(
        middle_kernel, "annulus_middle", (own, near, weight, gain),
        (background, column, column, total), None,
    )
    done, upper, lower, grown = call(
        mid_kernel, "annulus_mid",
        (own, *mid, model, weight, gain, done, upper, lower, grown),
        (background, column, column, total), 6,
        pl.CostEstimate(
            flops=2 * rows * cols * cols * frames, bytes_accessed=5 * MIB, transcendentals=0
        ),
    )
    return call(
        end_kernel, "annulus_end",
        (own, *far, model, weight, weight_next, weight_prev, gain, done, upper, lower, grown),
        (background, gradient), 8,
    )


def traces_kernel(capacity, stripe, slow, fast, step, traces, inbox, out):
    count, frames = traces.shape
    slots = inbox.shape[0]

    def upended(row):
        return jnp.broadcast_to(row[...].astype(F32), (LANES, count)).T

    before = lax.broadcasted_iota(jnp.int32, (count, count), 1) < lax.broadcasted_iota(
        jnp.int32, (count, count), 0
    )
    named = upended(stripe)
    same = (named == stripe[...].astype(F32)) & before
    rank = jnp.sum(jnp.where(same, 1.0, 0.0), axis=1, keepdims=True)
    slot = (named[:, 0:1] * capacity + rank).astype(jnp.int32)
    place = lax.broadcasted_iota(jnp.int32, (count, slots), 1)

    def onehot(shift):
        return jnp.where(place + shift == slot, 1.0, 0.0).astype(BF16)

    here = onehot(0)
    gradient = (
        dot(here, inbox[:, 0:frames])
        + dot(here, inbox[:, frames : 2 * frames])
        + dot(onehot(capacity), inbox[:, 2 * frames : 3 * frames])
        + dot(onehot(-capacity), inbox[:, 3 * frames : 4 * frames])
    )

    def wide(row):
        return jnp.concatenate([upended(row)] * (frames // LANES), axis=1)

    updated = traces[...].astype(F32) + wide(step) * gradient
    lane = lax.broadcasted_iota(jnp.int32, (count, frames), 1)

    def lagged(value, lag):
        return jnp.where(lane >= lag, pltpu.roll(value, lag, 1), 0.0)

    a, b = wide(slow), wide(fast)
    driven = updated - (a + b) * lagged(updated, 1) + (a * b) * lagged(updated, 2)
    spikes = jnp.maximum(driven - lam_floor, 0.0)
    sums = [spikes, spikes]
    roots = [a, b]
    lag = 1
    while lag < frames:
        sums = [value + root * lagged(value, lag) for value, root in zip(sums, roots)]
        roots = [root * root for root in roots]
        lag *= 2
    share = (1.0 - a) * (1.0 - b) / (a - b)
    out[...] = share * (a * sums[0] - b * sums[1])


def make_traces(stripe, slow, fast, step, traces, inbox, capacity):
    count, frames = traces.shape
    return pl.pallas_call(
        functools.partial(traces_kernel, capacity),
        out_shape=jax.ShapeDtypeStruct((count, frames), F32),
        compiler_params=params(),
        cost_estimate=COST,
        name="traces",
    )(stripe, slow, fast, step, traces, inbox)


def neighbours(axis):
    devices = lax.axis_size(axis)
    up = [(i, i + 1) for i in range(devices - 1)]
    return up, [(j, i) for i, j in up]


def on_device(movie, footprints, traces, stripe, column, annulus_gain, decay_slow, decay_fast):
    pix_count = lax.axis_size("pix")
    rows, cols, frames = movie.shape[1:]
    count = footprints.shape[1]
    capacity = max(2, 2 * count // pix_count)
    slots = pix_count * capacity
    pix_up, pix_down = neighbours("pix")
    plane_up, plane_down = neighbours("plane")

    stripe_row = stripe.reshape(1, count)
    outbox = make_outbox(stripe_row, column, footprints[0], traces[0], capacity, slots)
    frames_in, outbox = lax.optimization_barrier((movie, outbox))
    inbox = lax.all_to_all(outbox, "pix", split_axis=0, concat_axis=0, tiled=True)
    cuts = [
        (frames_in[0, rows - k - PER : rows - k], frames_in[0, k : k + PER])
        for k in range(0, RAD, PER)
    ]

    def exchange(cut):
        return (lax.ppermute(cut[0], "pix", pix_up), lax.ppermute(cut[1], "pix", pix_down))

    near_prev, near_next = exchange(cuts[0])
    cuts[1], inbox = lax.optimization_barrier((cuts[1], inbox))
    mid = exchange(cuts[1])

    foot_rows, residual, noise = make_residual(inbox, movie)
    near_rows, near_residual, noise = make_near(inbox, near_next, near_prev, noise)
    cuts[2], noise = lax.optimization_barrier((cuts[2], noise))
    far = exchange(cuts[2])
    noises = (
        noise,
        lax.ppermute(noise, "plane", plane_up),
        lax.ppermute(noise, "plane", plane_down),
    )
    weights = make_weights(foot_rows, near_rows, noises)
    model = make_outer_model(inbox, cols, frames)
    background, gradient = make_annulus(
        residual, near_residual, mid, far, model, weights, annulus_gain
    )
    home = lax.all_to_all(gradient, "pix", split_axis=0, concat_axis=0, tiled=True)
    foot_f = footprints[0].astype(F32)
    step = 1.0 / (jnp.sum(foot_f * foot_f, axis=1) + norm_eps)
    traces_new = make_traces(
        stripe_row, decay_slow, decay_fast, step[None], traces[0], home, capacity
    )
    return (background, traces_new[None])


def solution(mesh):
    placed = (
        P("plane", "pix", None, None),
        P("plane", "pix", None),
        P("plane", "pix", None),
        P("plane", "pix", None),
        P("plane", "pix"),
        P("plane", None),
        P("plane", "pix"),
        P("plane", "pix"),
    )
    return jax.shard_map(
        on_device,
        mesh=mesh,
        in_specs=placed,
        out_specs=(P("plane", "pix", None, None), P("plane", "pix", None)),
        check_vma=False,
    )
```

```python
import functools

import jax
import jax.numpy as jnp
import ml_dtypes
import numpy as np
from jax import lax
from jax.experimental import pallas as pl
from jax.experimental.pallas import tpu as pltpu
from jax.sharding import PartitionSpec as P

FOOT = 32
RAD = 12
GR = 3
LANES = 128
PER = LANES // FOOT
NEAR = PER

lam_floor = 0.1
noise_eps = 1e-05
norm_eps = 1e-05
sigma_twice = 4.5

F32 = jnp.float32
BF16 = jnp.bfloat16
MIB = 1 << 20
HBM = pl.BlockSpec(memory_space=pltpu.HBM)
VMEM = pl.BlockSpec(memory_space=pltpu.VMEM)


def tap_values():
    offsets = np.arange(-GR, GR + 1).astype(np.float32)
    raw = np.exp(-offsets * offsets / np.float32(sigma_twice)).astype(np.float32)
    return (raw / raw.sum(dtype=np.float32)).astype(ml_dtypes.bfloat16).astype(np.float32)


def params(mib=16):
    return pltpu.CompilerParams(vmem_limit_bytes=mib * MIB)


COST = pl.CostEstimate(flops=1, bytes_accessed=1, transcendentals=0)


def dot(a, b):
    return jnp.dot(a, b, preferred_element_type=F32)


def outbox_kernel(capacity, *refs):
    sources, outbox, places, sems = refs[0:4], refs[4], refs[5:9], refs[9]
    copies = [
        pltpu.make_async_copy(source, place, sems.at[k])
        for k, (source, place) in enumerate(zip(sources, places))
    ]
    for copy in copies:
        copy.start()
    for copy in copies:
        copy.wait()
    stripe, column, foot, traces = places
    slots = outbox.shape[0]
    count, tiles = foot.shape
    frames = traces.shape[1]
    before = lax.broadcasted_iota(jnp.int32, (count, count), 0) < lax.broadcasted_iota(
        jnp.int32, (count, count), 1
    )
    named = jnp.broadcast_to(stripe[...].astype(F32), (count, count))
    same = (named == named.T) & before
    rank = jnp.sum(jnp.where(same, 1.0, 0.0), axis=0, keepdims=True).astype(jnp.int32)
    slot = stripe[...] * capacity + rank
    place = lax.broadcasted_iota(jnp.int32, (slots, count), 0)
    left = jnp.broadcast_to(column[...].astype(F32), (LANES, count)).T.astype(BF16)
    lane = lax.broadcasted_iota(jnp.int32, (slots, LANES), 1)
    edge = NEAR * FOOT
    lefts = jnp.zeros((slots, LANES), F32)
    at = 3 * frames
    for k, (shift, first, width) in enumerate(
        ((0, 0, tiles), (capacity, 0, edge), (-capacity, tiles - edge, edge))
    ):
        hot = jnp.where(place + shift == slot, 1.0, 0.0).astype(BF16)
        outbox[:, k * frames : (k + 1) * frames] = dot(hot, traces[...]).astype(BF16)
        outbox[:, at : at + width] = dot(hot, foot[:, first : first + width]).astype(BF16)
        lefts = jnp.where(lane == k, dot(hot, left), lefts)
        at += width
    outbox[:, at:] = lefts.astype(BF16)


def make_outbox(stripe, column, foot, traces, capacity, slots):
    count, tiles = foot.shape
    frames = traces.shape[1]
    width = 3 * frames + tiles + 2 * NEAR * FOOT + LANES
    args = (stripe, column, foot, traces)
    return pl.pallas_call(
        functools.partial(outbox_kernel, capacity),
        in_specs=[HBM] * len(args),
        out_shape=jax.ShapeDtypeStruct((slots, width), BF16),
        scratch_shapes=[pltpu.VMEM(a.shape, a.dtype) for a in args]
        + [pltpu.SemaphoreType.DMA((len(args),))],
        compiler_params=params(56),
        cost_estimate=COST,
        name="outbox",
    )(*args)


def spread(block, col):
    lane = lax.broadcasted_iota(jnp.int32, block.shape, 1)
    for k in range(7):
        block = jnp.where(((col >> k) & 1) == 1, pltpu.roll(block, 1 << k, 1), block)
    inside = ((lane - col) & (LANES - 1)) < FOOT
    left = inside & (lane >= col)
    right = inside & (lane < col)
    rows = []
    for q in range(PER):
        moved = block if q == 0 else pltpu.roll(block, LANES - q * FOOT, 1)
        rows.append(
            jnp.concatenate(
                [jnp.where(left, moved, 0.0), jnp.where(right, moved, 0.0)], axis=1
            ).astype(BF16)
        )
    return rows


def tile_rows(inbox, which, block, frames):
    lefts = inbox[:, inbox.shape[1] - LANES :].astype(F32)
    col = jnp.broadcast_to(lefts[:, which : which + 1], lefts.shape).astype(jnp.int32)
    start = 3 * frames + block * LANES
    if not isinstance(start, int):
        start = pl.multiple_of(start, LANES)
    return spread(inbox[:, pl.ds(start, LANES)].astype(F32), col)


def model_row(row, inbox, which, frames):
    traces = inbox[:, which * frames : (which + 1) * frames]
    return lax.dot_general(row, traces, (((0,), (0,)), ((), ())), preferred_element_type=F32)


def noise_row(left, change):
    frames = left.shape[1]
    steps = dot(left, change)
    steps = steps * steps
    part = steps[:, 0:LANES]
    for k in range(1, frames // LANES):
        part = part + steps[:, k * LANES : (k + 1) * LANES]
    return jnp.sum(part.T, axis=0, keepdims=True) / (frames - 1)


def lag_table(size):
    shape = (size, size)
    return lax.broadcasted_iota(jnp.int32, shape, 1) - lax.broadcasted_iota(jnp.int32, shape, 0)


def change_matrix(frames):
    lag = lag_table(frames)
    steps = jnp.where(lag == -1, 1.0, 0.0) - jnp.where(lag == 0, 1.0, 0.0)
    later = lax.broadcasted_iota(jnp.int32, lag.shape, 1)
    return jnp.where(later < frames - 1, steps, 0.0).astype(BF16)


def residual_kernel(pick, low, high, first, inbox, movie, *refs):
    if not first:
        refs = refs[3:]
    (foot_rows, residual, noise, up, down) = refs[0:5]
    (change, movie_slots, foot_slots, left_slots, sems) = refs[5:]
    frames = movie.shape[3]
    count = pick(None)
    change[...] = change_matrix(frames)

    def fetch(i, slot):
        rows_g = pl.ds(pick(i) * PER, PER)
        return pltpu.make_async_copy(movie.at[0, rows_g], movie_slots.at[slot], sems.at[0, slot])

    def sends(i, slot):
        rows_g = pl.ds(pick(i) * PER, PER)
        return (
            pltpu.make_async_copy(foot_slots.at[slot], foot_rows.at[rows_g], sems.at[1, slot]),
            pltpu.make_async_copy(left_slots.at[slot], residual.at[rows_g], sems.at[2, slot]),
        )

    fetch(0, 0).start()

    def group(i, carry):
        slot = lax.rem(i, 2)
        g = pick(i)

        @pl.when(i + 1 < count)
        def _():
            fetch(i + 1, 1 - slot).start()

        fetch(i, slot).wait()

        @pl.when(i >= 2)
        def _():
            for copy in sends(i - 2, slot):
                copy.wait()

        noises = []
        for q, row in enumerate(tile_rows(inbox, 0, g, frames)):
            foot_slots[slot, q] = row
            left = movie_slots[slot, q].astype(F32) - model_row(row, inbox, 0, frames)
            left = left.astype(BF16)
            left_slots[slot, q] = left
            noises.append(noise_row(left, change[...]))
        noise[i] = jnp.concatenate(noises, axis=0)
        for copy in sends(i, slot):
            copy.start()

        @pl.when(g == low)
        def _():
            down[...] = left_slots[slot]

        @pl.when(g == high)
        def _():
            up[...] = left_slots[slot]

        return carry

    lax.fori_loop(0, count, group, 0)
    for i in (count - 2, count - 1):
        for copy in sends(i, i % 2):
            copy.wait()


def make_residual(inbox, movie, earlier=None):
    slots = inbox.shape[0]
    rows, cols, frames = movie.shape[1:]
    groups = rows // PER
    mids = (1, groups - 2)
    if earlier is None:
        low, high, count = *mids, 2

        def pick(i):
            return count if i is None else mids[0] + i * (mids[1] - mids[0])
    else:
        low, high, count = 2, groups - 3, groups - 2

        def pick(i):
            if i is None:
                return count
            if isinstance(i, int):
                return i + (i >= mids[0]) + (i + 1 >= mids[1])
            return i + jnp.where(i >= mids[0], 1, 0) + jnp.where(i + 1 >= mids[1], 1, 0)

    piece = jax.ShapeDtypeStruct((PER, cols, frames), BF16)
    more = () if earlier is None else earlier
    return pl.pallas_call(
        functools.partial(residual_kernel, pick, low, high, earlier is None),
        in_specs=[VMEM, HBM] + [HBM, HBM, VMEM][: len(more)],
        out_specs=[HBM, HBM, VMEM, VMEM, VMEM],
        out_shape=(
            jax.ShapeDtypeStruct((rows, slots, cols), BF16),
            jax.ShapeDtypeStruct((rows, cols, frames), BF16),
            jax.ShapeDtypeStruct((count, PER, cols), F32),
            piece,
            piece,
        ),
        scratch_shapes=[
            pltpu.VMEM((frames, frames), BF16),
            pltpu.VMEM((2, PER, cols, frames), BF16),
            pltpu.VMEM((2, PER, slots, cols), BF16),
            pltpu.VMEM((2, PER, cols, frames), BF16),
            pltpu.SemaphoreType.DMA((3, 2)),
        ],
        input_output_aliases={} if earlier is None else {2: 0, 3: 1},
        compiler_params=params(44),
        cost_estimate=COST,
        name="residual",
    )(inbox, movie, *more)


def near_kernel(
    inbox, movie_next, movie_prev, mid_noise, other_noise, foot_rows, residual, noise
):
    frames = movie_next.shape[2]
    groups = mid_noise.shape[0] + other_noise.shape[0]
    own = FOOT // PER
    change = change_matrix(frames)
    others = [g for g in range(groups) if g not in (1, groups - 2)]
    for order, part in (((1, groups - 2), mid_noise), (others, other_noise)):
        for i, g in enumerate(order):
            noise[NEAR + g * PER : NEAR + (g + 1) * PER, :] = part[i]
    for side, (block, movie, first) in enumerate(
        ((own, movie_next, 0), (own + NEAR // PER, movie_prev, NEAR + groups * PER))
    ):
        for q, row in enumerate(tile_rows(inbox, 1 + side, block, frames)):
            y = side * NEAR + q
            foot_rows[y] = row
            left = movie[q].astype(F32) - model_row(row, inbox, 1 + side, frames)
            left = left.astype(BF16)
            residual[y] = left
            noise[first + q : first + q + 1, :] = noise_row(left, change)


def make_near(inbox, movie_next, movie_prev, noises):
    slots = inbox.shape[0]
    cols, frames = movie_next.shape[1:]
    return pl.pallas_call(
        near_kernel,
        out_shape=(
            jax.ShapeDtypeStruct((2 * NEAR, slots, cols), BF16),
            jax.ShapeDtypeStruct((2 * NEAR, cols, frames), BF16),
            jax.ShapeDtypeStruct((2 * NEAR + PER * sum(n.shape[0] for n in noises), cols), F32),
        ),
        compiler_params=params(),
        cost_estimate=COST,
        name="near",
    )(inbox, movie_next, movie_prev, *noises)


def weights_kernel(
    taps, own, near, noise, noise_before, noise_after, out, out_next, out_prev,
    own_slots, scale, band, sems,
):
    rows, slots, cols = own.shape
    part = own_slots.shape[2]
    count = slots // part

    def fetch(i, slot):
        these = pl.ds(pl.multiple_of(i * part, part), part)
        return pltpu.make_async_copy(own.at[:, these, :], own_slots.at[slot], sems.at[slot])

    fetch(0, 0).start()
    pooled = (noise_before[...] + 2.0 * noise[...] + noise_after[...]) / 4.0
    scale[...] = 1.0 / jnp.sqrt(pooled + noise_eps)
    lag = jnp.abs(lag_table(cols))
    table = jnp.zeros(lag.shape, F32)
    for k in range(GR + 1):
        table = jnp.where(lag == k, taps[GR + k], table)
    band[...] = table.astype(BF16)

    def across(foot, inv):
        scaled = (foot.astype(F32) * inv[:, None, :]).astype(BF16)
        count = foot.shape[0]
        return dot(scaled.reshape(count * part, cols), band[...]).reshape(count, part, cols)

    def some(i, carry):
        slot = lax.rem(i, 2)

        @pl.when(i + 1 < count)
        def _():
            fetch(i + 1, 1 - slot).start()

        fetch(i, slot).wait()
        these = pl.ds(pl.multiple_of(i * part, part), part)
        blurred = across(own_slots[slot], scale[NEAR : NEAR + rows])
        for r in range(rows):
            total = taps[GR] * blurred[r]
            for k in range(1, GR + 1):
                if r - k >= 0 and r + k < rows:
                    total = total + taps[GR + k] * (blurred[r - k] + blurred[r + k])
                elif r - k >= 0:
                    total = total + taps[GR + k] * blurred[r - k]
                elif r + k < rows:
                    total = total + taps[GR + k] * blurred[r + k]
            out[r, these, :] = total.astype(BF16)
        after = across(near[0:GR, these, :], scale[0:GR])
        ahead = across(near[2 * NEAR - GR : 2 * NEAR, these, :], scale[rows + 2 * NEAR - GR :])
        for a in range(GR):
            total = taps[2 * GR - a] * after[0]
            for r in range(1, a + 1):
                total = total + taps[2 * GR + r - a] * after[r]
            out_next[a, these, :] = total.astype(BF16)
            total = taps[2 * GR] * ahead[a]
            for b in range(a + 1, GR):
                total = total + taps[2 * GR + a - b] * ahead[b]
            out_prev[a, these, :] = total.astype(BF16)
        return carry

    lax.fori_loop(0, count, some, 0)


def make_weights(foot_rows, near_rows, noises):
    rows, slots, cols = foot_rows.shape
    part = 32
    return pl.pallas_call(
        functools.partial(weights_kernel, [float(t) for t in tap_values()]),
        in_specs=[HBM] + [VMEM] * (1 + len(noises)),
        out_shape=(
            jax.ShapeDtypeStruct((rows, slots, cols), BF16),
            jax.ShapeDtypeStruct((GR, slots, cols), BF16),
            jax.ShapeDtypeStruct((GR, slots, cols), BF16),
        ),
        scratch_shapes=[
            pltpu.VMEM((2, rows, part, cols), BF16),
            pltpu.VMEM(noises[0].shape, F32),
            pltpu.VMEM((cols, cols), BF16),
            pltpu.SemaphoreType.DMA((2,)),
        ],
        compiler_params=params(32),
        cost_estimate=COST,
        name="weights",
    )(foot_rows, near_rows, *noises)


def annulus_group(g, own, leaving, entering, gain, band, column, outgoing):
    cols, frames = own.shape[1:]
    top = lax.broadcasted_iota(jnp.int32, (cols // 8, 8, LANES), 1) < 4
    blank = jnp.zeros((2, 8, LANES), F32)
    outs = [leaving(q) for q in range(PER)]
    news = [entering(q) for q in range(PER)]
    levels = [dot(band, jnp.concatenate([o, n], axis=0)) for o, n in zip(outs, news)]
    column = list(column)
    dets = []
    for q in range(PER):
        det = []
        for h in range(frames // LANES):
            part = slice(h * LANES, (h + 1) * LANES)
            inner = column[h] - outs[q][:, part].astype(F32)
            column[h] = inner + news[q][:, part].astype(F32)
            turned = pltpu.roll(inner.reshape(cols // 8, 8, LANES), 4, 1)
            turned = jnp.concatenate([blank, turned, blank], axis=0)
            both = turned[0 : cols // 8 + 1] + turned[3 : cols // 8 + 4]
            sides = jnp.where(top, both[0 : cols // 8], both[1 : cols // 8 + 1])
            fit = (levels[q][:, part] + sides.reshape(cols, LANES)) * gain
            outgoing[g, q, :, part] = fit.astype(BF16)
            det.append((own[g * PER + q, :, part].astype(F32) - fit).astype(BF16))
        dets.append(jnp.concatenate(det, axis=1))
    return column, dets


def grow(total, weight, g, dets):
    weights = jnp.concatenate([weight[g * PER + q] for q in range(PER)], axis=1)
    return total + dot(weights, jnp.concatenate(dets, axis=0))


def halves(ref):
    return [ref[:, h * LANES : (h + 1) * LANES] for h in range(ref.shape[1] // LANES)]


def add_rows(column, rows, sign=1.0):
    for row in rows:
        column = [c + sign * r.astype(F32) for c, r in zip(column, halves(row))]
    return column


def put(ref, column):
    for h, value in enumerate(column):
        ref[:, h * LANES : (h + 1) * LANES] = value


def sender(outgoing, background, sems):
    def send(g):
        return pltpu.make_async_copy(
            outgoing.at[g], background.at[0, pl.ds(g * PER, PER)], sems.at[g]
        )

    return send


def tables(gain):
    cols = gain.shape[1]
    band = jnp.where(jnp.abs(lag_table(cols)) <= RAD, 1.0, 0.0).astype(BF16)
    return (
        jnp.broadcast_to(gain[...], (LANES, cols)).T / (8.0 * RAD),
        jnp.concatenate([band, band], axis=1),
    )


def middle_kernel(own, near, weight, gain, background, upper, lower, total, outgoing, sems):
    rows, cols, frames = own.shape
    groups = range((RAD - NEAR) // PER, (rows - RAD + NEAR) // PER)
    send = sender(outgoing, background, sems)
    gains, band = tables(gain)
    column = [jnp.zeros((cols, LANES), F32)] * (frames // LANES)
    column = add_rows(column, [near[NEAR + r] for r in range(NEAR)])
    column = add_rows(column, [own[r] for r in range(RAD)])
    put(upper, column)
    column = add_rows(column, [own[RAD + r] for r in range(2 * RAD - NEAR - RAD)])
    grown = jnp.zeros(total.shape, F32)
    for g in groups:
        y = g * PER
        column, dets = annulus_group(
            g,
            own,
            (lambda q: near[NEAR + y - RAD + NEAR + q])
            if y < RAD
            else (lambda q: own[y - RAD + q]),
            (lambda q: near[y + RAD - rows + q])
            if y + RAD >= rows
            else (lambda q: own[y + RAD + q]),
            gains, band, column, outgoing,
        )
        send(g).start()
        grown = grow(grown, weight, g, dets)
    put(lower, column)
    total[...] = grown
    for g in groups:
        send(g).wait()


def mid_kernel(
    own, above, below, weight, gain, before, upper, lower, total,
    background, new_upper, new_lower, new_total, outgoing, sems,
):
    del before
    rows = own.shape[0]
    low, high = RAD // PER - 2, (rows - RAD) // PER + 1
    y, z = low * PER, high * PER
    send = sender(outgoing, background, sems)
    gains, band = tables(gain)
    column = add_rows(halves(upper), [above[r] for r in range(PER)])
    put(new_upper, column)
    column = add_rows(column, [own[RAD + r] for r in range(PER)])
    _, low_dets = annulus_group(
        low, own, lambda q: above[q], lambda q: own[y + RAD + q], gains, band, column, outgoing
    )
    send(low).start()
    column, high_dets = annulus_group(
        high, own, lambda q: own[z - RAD + q], lambda q: below[q], gains, band, halves(lower),
        outgoing,
    )
    send(high).start()
    put(new_lower, column)
    new_total[...] = grow(grow(total[...], weight, low, low_dets), weight, high, high_dets)
    send(low).wait()
    send(high).wait()


def end_kernel(
    own, above, below, weight, weight_next, weight_prev, gain, before,
    upper, lower, total, background, gradient, outgoing, sems,
):
    del before
    rows, _, frames = own.shape
    low, high = 0, rows // PER - 1
    z = high * PER
    send = sender(outgoing, background, sems)
    gains, band = tables(gain)
    _, low_dets = annulus_group(
        low, own, lambda q: above[q], lambda q: own[RAD + q], gains, band,
        add_rows(halves(upper), [above[r] for r in range(PER)]), outgoing,
    )
    send(low).start()
    _, high_dets = annulus_group(
        high, own, lambda q: own[z - RAD + q], lambda q: below[q], gains, band, halves(lower),
        outgoing,
    )
    send(high).start()
    grown = grow(grow(total[...], weight, low, low_dets), weight, high, high_dets)
    edges = ((2, weight_next, high_dets[PER - GR :]), (3, weight_prev, low_dets[:GR]))
    for at, edge, parts in edges:
        value = dot(
            jnp.concatenate([edge[a] for a in range(GR)], axis=1), jnp.concatenate(parts, axis=0)
        )
        gradient[:, at * frames : (at + 1) * frames] = value.astype(BF16)
    coarse = grown.astype(BF16)
    gradient[:, 0:frames] = coarse
    gradient[:, frames : 2 * frames] = (grown - coarse.astype(F32)).astype(BF16)
    send(low).wait()
    send(high).wait()


def make_annulus(own, near, mid, far, weights, gain):
    rows, cols, frames = own.shape
    weight, weight_next, weight_prev = weights
    slots = weight.shape[1]
    background = jax.ShapeDtypeStruct((1, rows, cols, frames), BF16)
    column = jax.ShapeDtypeStruct((cols, frames), F32)
    total = jax.ShapeDtypeStruct((slots, frames), F32)
    gradient = jax.ShapeDtypeStruct((slots, 4 * frames), BF16)

    def call(kernel, name, args, outs, done, declared=COST):
        specs = [VMEM] * len(args)
        if done is not None:
            specs[done] = HBM
        return pl.pallas_call(
            kernel,
            in_specs=specs,
            out_specs=[HBM] + [VMEM] * (len(outs) - 1),
            out_shape=outs,
            scratch_shapes=[
                pltpu.VMEM((rows // PER, PER, cols, frames), BF16),
                pltpu.SemaphoreType.DMA((rows // PER,)),
            ],
            input_output_aliases={} if done is None else {done: 0},
            compiler_params=params(),
            cost_estimate=declared,
            name=name,
        )(*args)

    done, upper, lower, grown = call(
        middle_kernel, "annulus_middle", (own, near, weight, gain),
        (background, column, column, total), None,
    )
    done, upper, lower, grown = call(
        mid_kernel, "annulus_mid",
        (own, *mid, weight, gain, done, upper, lower, grown),
        (background, column, column, total), 5,
        pl.CostEstimate(
            flops=2 * rows * cols * cols * frames, bytes_accessed=5 * MIB, transcendentals=0
        ),
    )
    return call(
        end_kernel, "annulus_end",
        (own, *far, weight, weight_next, weight_prev, gain, done, upper, lower, grown),
        (background, gradient), 7,
    )


def traces_kernel(capacity, stripe, slow, fast, step, traces, inbox, out):
    count, frames = traces.shape
    slots = inbox.shape[0]

    def upended(row):
        return jnp.broadcast_to(row[...].astype(F32), (LANES, count)).T

    before = lax.broadcasted_iota(jnp.int32, (count, count), 1) < lax.broadcasted_iota(
        jnp.int32, (count, count), 0
    )
    named = upended(stripe)
    same = (named == stripe[...].astype(F32)) & before
    rank = jnp.sum(jnp.where(same, 1.0, 0.0), axis=1, keepdims=True)
    slot = (named[:, 0:1] * capacity + rank).astype(jnp.int32)
    place = lax.broadcasted_iota(jnp.int32, (count, slots), 1)

    def onehot(shift):
        return jnp.where(place + shift == slot, 1.0, 0.0).astype(BF16)

    here = onehot(0)
    gradient = (
        dot(here, inbox[:, 0:frames])
        + dot(here, inbox[:, frames : 2 * frames])
        + dot(onehot(capacity), inbox[:, 2 * frames : 3 * frames])
        + dot(onehot(-capacity), inbox[:, 3 * frames : 4 * frames])
    )

    def wide(row):
        return jnp.concatenate([upended(row)] * (frames // LANES), axis=1)

    updated = traces[...].astype(F32) + wide(step) * gradient
    lane = lax.broadcasted_iota(jnp.int32, (count, frames), 1)

    def lagged(value, lag):
        return jnp.where(lane >= lag, pltpu.roll(value, lag, 1), 0.0)

    a, b = wide(slow), wide(fast)
    driven = updated - (a + b) * lagged(updated, 1) + (a * b) * lagged(updated, 2)
    spikes = jnp.maximum(driven - lam_floor, 0.0)
    sums = [spikes, spikes]
    roots = [a, b]
    lag = 1
    while lag < frames:
        sums = [value + root * lagged(value, lag) for value, root in zip(sums, roots)]
        roots = [root * root for root in roots]
        lag *= 2
    share = (1.0 - a) * (1.0 - b) / (a - b)
    out[...] = share * (a * sums[0] - b * sums[1])


def make_traces(stripe, slow, fast, step, traces, inbox, capacity):
    count, frames = traces.shape
    return pl.pallas_call(
        functools.partial(traces_kernel, capacity),
        out_shape=jax.ShapeDtypeStruct((count, frames), F32),
        compiler_params=params(),
        cost_estimate=COST,
        name="traces",
    )(stripe, slow, fast, step, traces, inbox)


def neighbours(axis):
    devices = lax.axis_size(axis)
    up = [(i, i + 1) for i in range(devices - 1)]
    return up, [(j, i) for i, j in up]


def on_device(movie, footprints, traces, stripe, column, annulus_gain, decay_slow, decay_fast):
    pix_count = lax.axis_size("pix")
    rows, cols, frames = movie.shape[1:]
    count = footprints.shape[1]
    capacity = max(2, 2 * count // pix_count)
    slots = pix_count * capacity
    pix_up, pix_down = neighbours("pix")
    plane_up, plane_down = neighbours("plane")

    stripe_row = stripe.reshape(1, count)
    outbox = make_outbox(stripe_row, column, footprints[0], traces[0], capacity, slots)
    def exchange(up, down):
        return (lax.ppermute(up, "pix", pix_up), lax.ppermute(down, "pix", pix_down))

    frames_in, outbox = lax.optimization_barrier((movie, outbox))
    inbox = lax.all_to_all(outbox, "pix", split_axis=0, concat_axis=0, tiled=True)
    near_prev, near_next = exchange(frames_in[0, rows - NEAR :], frames_in[0, :NEAR])
    *started, mid_noise, up, down = make_residual(inbox, movie)
    mid = exchange(up, down)
    foot_rows, residual, other_noise, up, down = make_residual(
        inbox, movie, (*started, mid_noise)
    )
    near_rows, near_residual, noise = make_near(
        inbox, near_next, near_prev, (mid_noise, other_noise)
    )
    up, down, noise = lax.optimization_barrier((up, down, noise))
    far = exchange(up, down)
    noises = (
        noise,
        lax.ppermute(noise, "plane", plane_up),
        lax.ppermute(noise, "plane", plane_down),
    )
    weights = make_weights(foot_rows, near_rows, noises)
    background, gradient = make_annulus(
        residual, near_residual, mid, far, weights, annulus_gain
    )
    home = lax.all_to_all(gradient, "pix", split_axis=0, concat_axis=0, tiled=True)
    foot_f = footprints[0].astype(F32)
    step = 1.0 / (jnp.sum(foot_f * foot_f, axis=1) + norm_eps)
    traces_new = make_traces(
        stripe_row, decay_slow, decay_fast, step[None], traces[0], home, capacity
    )
    return (background, traces_new[None])


def solution(mesh):
    placed = (
        P("plane", "pix", None, None),
        P("plane", "pix", None),
        P("plane", "pix", None),
        P("plane", "pix", None),
        P("plane", "pix"),
        P("plane", None),
        P("plane", "pix"),
        P("plane", "pix"),
    )
    return jax.shard_map(
        on_device,
        mesh=mesh,
        in_specs=placed,
        out_specs=(P("plane", "pix", None, None), P("plane", "pix", None)),
        check_vma=False,
    )
```

```python
import functools

import jax
import jax.numpy as jnp
import ml_dtypes
import numpy as np
from jax import lax
from jax.experimental import pallas as pl
from jax.experimental.pallas import tpu as pltpu
from jax.sharding import PartitionSpec as P

FOOT = 32
RAD = 12
GR = 3
LANES = 128
PER = LANES // FOOT
NEAR = PER

lam_floor = 0.1
noise_eps = 1e-05
norm_eps = 1e-05
sigma_twice = 4.5

F32 = jnp.float32
BF16 = jnp.bfloat16
MIB = 1 << 20
HBM = pl.BlockSpec(memory_space=pltpu.HBM)
VMEM = pl.BlockSpec(memory_space=pltpu.VMEM)


def tap_values():
    offsets = np.arange(-GR, GR + 1).astype(np.float32)
    raw = np.exp(-offsets * offsets / np.float32(sigma_twice)).astype(np.float32)
    return (raw / raw.sum(dtype=np.float32)).astype(ml_dtypes.bfloat16).astype(np.float32)


def params(mib=16):
    return pltpu.CompilerParams(vmem_limit_bytes=mib * MIB)


COST = pl.CostEstimate(flops=1, bytes_accessed=1, transcendentals=0)


def dot(a, b):
    return jnp.dot(a, b, preferred_element_type=F32)


def outbox_kernel(capacity, *refs):
    sources, outbox, places, sems = refs[0:4], refs[4], refs[5:9], refs[9]
    copies = [
        pltpu.make_async_copy(source, place, sems.at[k])
        for k, (source, place) in enumerate(zip(sources, places))
    ]
    for copy in copies:
        copy.start()
    for copy in copies[0:2]:
        copy.wait()
    stripe, column, foot, traces = places
    slots = outbox.shape[0]
    count, tiles = foot.shape
    frames = traces.shape[1]
    before = lax.broadcasted_iota(jnp.int32, (count, count), 0) < lax.broadcasted_iota(
        jnp.int32, (count, count), 1
    )
    named = jnp.broadcast_to(stripe[...].astype(F32), (count, count))
    same = (named == named.T) & before
    rank = jnp.sum(jnp.where(same, 1.0, 0.0), axis=0, keepdims=True).astype(jnp.int32)
    slot = stripe[...] * capacity + rank
    place = lax.broadcasted_iota(jnp.int32, (slots, count), 0)
    left = jnp.broadcast_to(column[...].astype(F32), (LANES, count)).T.astype(BF16)
    lane = lax.broadcasted_iota(jnp.int32, (slots, LANES), 1)
    edge = NEAR * FOOT
    lefts = jnp.zeros((slots, LANES), F32)
    at = 3 * frames
    hots = [
        jnp.where(place + shift == slot, 1.0, 0.0).astype(BF16)
        for shift in (0, capacity, -capacity)
    ]
    for copy in copies[2:]:
        copy.wait()
    for k, (hot, first, width) in enumerate(
        zip(hots, (0, 0, tiles - edge), (tiles, edge, edge))
    ):
        outbox[:, k * frames : (k + 1) * frames] = dot(hot, traces[...]).astype(BF16)
        outbox[:, at : at + width] = dot(hot, foot[:, first : first + width]).astype(BF16)
        lefts = jnp.where(lane == k, dot(hot, left), lefts)
        at += width
    outbox[:, at:] = lefts.astype(BF16)


def make_outbox(stripe, column, foot, traces, capacity, slots):
    count, tiles = foot.shape
    frames = traces.shape[1]
    width = 3 * frames + tiles + 2 * NEAR * FOOT + LANES
    args = (stripe, column, foot, traces)
    return pl.pallas_call(
        functools.partial(outbox_kernel, capacity),
        in_specs=[HBM] * len(args),
        out_shape=jax.ShapeDtypeStruct((slots, width), BF16),
        scratch_shapes=[pltpu.VMEM(a.shape, a.dtype) for a in args]
        + [pltpu.SemaphoreType.DMA((len(args),))],
        compiler_params=params(56),
        cost_estimate=COST,
        name="outbox",
    )(*args)


def spread(block, col):
    lane = lax.broadcasted_iota(jnp.int32, block.shape, 1)
    for k in range(7):
        block = jnp.where(((col >> k) & 1) == 1, pltpu.roll(block, 1 << k, 1), block)
    inside = ((lane - col) & (LANES - 1)) < FOOT
    left = inside & (lane >= col)
    right = inside & (lane < col)
    rows = []
    for q in range(PER):
        moved = block if q == 0 else pltpu.roll(block, LANES - q * FOOT, 1)
        rows.append(
            jnp.concatenate(
                [jnp.where(left, moved, 0.0), jnp.where(right, moved, 0.0)], axis=1
            ).astype(BF16)
        )
    return rows


def tile_rows(inbox, which, block, frames):
    lefts = inbox[:, inbox.shape[1] - LANES :].astype(F32)
    col = jnp.broadcast_to(lefts[:, which : which + 1], lefts.shape).astype(jnp.int32)
    start = 3 * frames + block * LANES
    if not isinstance(start, int):
        start = pl.multiple_of(start, LANES)
    return spread(inbox[:, pl.ds(start, LANES)].astype(F32), col)


def model_row(row, inbox, which, frames):
    traces = inbox[:, which * frames : (which + 1) * frames]
    return lax.dot_general(row, traces, (((0,), (0,)), ((), ())), preferred_element_type=F32)


def noise_row(left, change):
    frames = left.shape[1]
    steps = dot(left, change)
    steps = steps * steps
    part = steps[:, 0:LANES]
    for k in range(1, frames // LANES):
        part = part + steps[:, k * LANES : (k + 1) * LANES]
    return jnp.sum(part.T, axis=0, keepdims=True) / (frames - 1)


def lag_table(size):
    shape = (size, size)
    return lax.broadcasted_iota(jnp.int32, shape, 1) - lax.broadcasted_iota(jnp.int32, shape, 0)


def change_matrix(frames):
    lag = lag_table(frames)
    steps = jnp.where(lag == -1, 1.0, 0.0) - jnp.where(lag == 0, 1.0, 0.0)
    later = lax.broadcasted_iota(jnp.int32, lag.shape, 1)
    return jnp.where(later < frames - 1, steps, 0.0).astype(BF16)


def residual_kernel(pick, low, high, first, inbox, movie, *refs):
    if not first:
        refs = refs[3:]
    (foot_rows, residual, noise, up, down) = refs[0:5]
    (change, movie_slots, foot_slots, left_slots, sems) = refs[5:]
    frames = movie.shape[3]
    count = pick(None)
    change[...] = change_matrix(frames)

    def fetch(i, slot):
        rows_g = pl.ds(pick(i) * PER, PER)
        return pltpu.make_async_copy(movie.at[0, rows_g], movie_slots.at[slot], sems.at[0, slot])

    def sends(i, slot):
        rows_g = pl.ds(pick(i) * PER, PER)
        return (
            pltpu.make_async_copy(foot_slots.at[slot], foot_rows.at[rows_g], sems.at[1, slot]),
            pltpu.make_async_copy(left_slots.at[slot], residual.at[rows_g], sems.at[2, slot]),
        )

    fetch(0, 0).start()

    def group(i, carry):
        slot = lax.rem(i, 2)
        g = pick(i)

        @pl.when(i + 1 < count)
        def _():
            fetch(i + 1, 1 - slot).start()

        fetch(i, slot).wait()

        @pl.when(i >= 2)
        def _():
            for copy in sends(i - 2, slot):
                copy.wait()

        noises = []
        for q, row in enumerate(tile_rows(inbox, 0, g, frames)):
            foot_slots[slot, q] = row
            left = movie_slots[slot, q].astype(F32) - model_row(row, inbox, 0, frames)
            left = left.astype(BF16)
            left_slots[slot, q] = left
            noises.append(noise_row(left, change[...]))
        noise[i] = jnp.concatenate(noises, axis=0)
        for copy in sends(i, slot):
            copy.start()

        @pl.when(g == low)
        def _():
            down[...] = left_slots[slot]

        @pl.when(g == high)
        def _():
            up[...] = left_slots[slot]

        return carry

    lax.fori_loop(0, count, group, 0)
    for i in (count - 2, count - 1):
        for copy in sends(i, i % 2):
            copy.wait()


def make_residual(inbox, movie, earlier=None):
    slots = inbox.shape[0]
    rows, cols, frames = movie.shape[1:]
    groups = rows // PER
    mids = (1, groups - 2)
    if earlier is None:
        low, high, count = *mids, 2

        def pick(i):
            return count if i is None else mids[0] + i * (mids[1] - mids[0])
    else:
        low, high, count = 2, groups - 3, groups - 2

        def pick(i):
            if i is None:
                return count
            if isinstance(i, int):
                return i + (i >= mids[0]) + (i + 1 >= mids[1])
            return i + jnp.where(i >= mids[0], 1, 0) + jnp.where(i + 1 >= mids[1], 1, 0)

    piece = jax.ShapeDtypeStruct((PER, cols, frames), BF16)
    more = () if earlier is None else earlier
    return pl.pallas_call(
        functools.partial(residual_kernel, pick, low, high, earlier is None),
        in_specs=[VMEM, HBM] + [HBM, HBM, VMEM][: len(more)],
        out_specs=[HBM, HBM, VMEM, VMEM, VMEM],
        out_shape=(
            jax.ShapeDtypeStruct((rows, slots, cols), BF16),
            jax.ShapeDtypeStruct((rows, cols, frames), BF16),
            jax.ShapeDtypeStruct((count, PER, cols), F32),
            piece,
            piece,
        ),
        scratch_shapes=[
            pltpu.VMEM((frames, frames), BF16),
            pltpu.VMEM((2, PER, cols, frames), BF16),
            pltpu.VMEM((2, PER, slots, cols), BF16),
            pltpu.VMEM((2, PER, cols, frames), BF16),
            pltpu.SemaphoreType.DMA((3, 2)),
        ],
        input_output_aliases={} if earlier is None else {2: 0, 3: 1},
        compiler_params=params(44),
        cost_estimate=COST,
        name="residual",
    )(inbox, movie, *more)


def near_kernel(
    inbox, movie_next, movie_prev, mid_noise, other_noise, foot_rows, residual, noise
):
    frames = movie_next.shape[2]
    groups = mid_noise.shape[0] + other_noise.shape[0]
    own = FOOT // PER
    change = change_matrix(frames)
    others = [g for g in range(groups) if g not in (1, groups - 2)]
    for order, part in (((1, groups - 2), mid_noise), (others, other_noise)):
        for i, g in enumerate(order):
            noise[NEAR + g * PER : NEAR + (g + 1) * PER, :] = part[i]
    for side, (block, movie, first) in enumerate(
        ((own, movie_next, 0), (own + NEAR // PER, movie_prev, NEAR + groups * PER))
    ):
        for q, row in enumerate(tile_rows(inbox, 1 + side, block, frames)):
            y = side * NEAR + q
            foot_rows[y] = row
            left = movie[q].astype(F32) - model_row(row, inbox, 1 + side, frames)
            left = left.astype(BF16)
            residual[y] = left
            noise[first + q : first + q + 1, :] = noise_row(left, change)


def make_near(inbox, movie_next, movie_prev, noises):
    slots = inbox.shape[0]
    cols, frames = movie_next.shape[1:]
    return pl.pallas_call(
        near_kernel,
        out_shape=(
            jax.ShapeDtypeStruct((2 * NEAR, slots, cols), BF16),
            jax.ShapeDtypeStruct((2 * NEAR, cols, frames), BF16),
            jax.ShapeDtypeStruct((2 * NEAR + PER * sum(n.shape[0] for n in noises), cols), F32),
        ),
        compiler_params=params(),
        cost_estimate=COST,
        name="near",
    )(inbox, movie_next, movie_prev, *noises)


def weights_kernel(
    taps, own, near, noise, noise_before, noise_after, out, out_next, out_prev,
    own_slots, scale, band, sems,
):
    rows, slots, cols = own.shape
    part = own_slots.shape[2]
    count = slots // part

    def fetch(i, slot):
        these = pl.ds(pl.multiple_of(i * part, part), part)
        return pltpu.make_async_copy(own.at[:, these, :], own_slots.at[slot], sems.at[slot])

    fetch(0, 0).start()
    pooled = (noise_before[...] + 2.0 * noise[...] + noise_after[...]) / 4.0
    scale[...] = 1.0 / jnp.sqrt(pooled + noise_eps)
    lag = jnp.abs(lag_table(cols))
    table = jnp.zeros(lag.shape, F32)
    for k in range(GR + 1):
        table = jnp.where(lag == k, taps[GR + k], table)
    band[...] = table.astype(BF16)

    def across(foot, inv):
        scaled = (foot.astype(F32) * inv[:, None, :]).astype(BF16)
        count = foot.shape[0]
        return dot(scaled.reshape(count * part, cols), band[...]).reshape(count, part, cols)

    def some(i, carry):
        slot = lax.rem(i, 2)

        @pl.when(i + 1 < count)
        def _():
            fetch(i + 1, 1 - slot).start()

        fetch(i, slot).wait()
        these = pl.ds(pl.multiple_of(i * part, part), part)
        blurred = across(own_slots[slot], scale[NEAR : NEAR + rows])
        for r in range(rows):
            total = taps[GR] * blurred[r]
            for k in range(1, GR + 1):
                if r - k >= 0 and r + k < rows:
                    total = total + taps[GR + k] * (blurred[r - k] + blurred[r + k])
                elif r - k >= 0:
                    total = total + taps[GR + k] * blurred[r - k]
                elif r + k < rows:
                    total = total + taps[GR + k] * blurred[r + k]
            out[r, these, :] = total.astype(BF16)
        after = across(near[0:GR, these, :], scale[0:GR])
        ahead = across(near[2 * NEAR - GR : 2 * NEAR, these, :], scale[rows + 2 * NEAR - GR :])
        for a in range(GR):
            total = taps[2 * GR - a] * after[0]
            for r in range(1, a + 1):
                total = total + taps[2 * GR + r - a] * after[r]
            out_next[a, these, :] = total.astype(BF16)
            total = taps[2 * GR] * ahead[a]
            for b in range(a + 1, GR):
                total = total + taps[2 * GR + a - b] * ahead[b]
            out_prev[a, these, :] = total.astype(BF16)
        return carry

    lax.fori_loop(0, count, some, 0)


def make_weights(foot_rows, near_rows, noises):
    rows, slots, cols = foot_rows.shape
    part = 32
    return pl.pallas_call(
        functools.partial(weights_kernel, [float(t) for t in tap_values()]),
        in_specs=[HBM] + [VMEM] * (1 + len(noises)),
        out_shape=(
            jax.ShapeDtypeStruct((rows, slots, cols), BF16),
            jax.ShapeDtypeStruct((GR, slots, cols), BF16),
            jax.ShapeDtypeStruct((GR, slots, cols), BF16),
        ),
        scratch_shapes=[
            pltpu.VMEM((2, rows, part, cols), BF16),
            pltpu.VMEM(noises[0].shape, F32),
            pltpu.VMEM((cols, cols), BF16),
            pltpu.SemaphoreType.DMA((2,)),
        ],
        compiler_params=params(32),
        cost_estimate=COST,
        name="weights",
    )(foot_rows, near_rows, *noises)


def annulus_group(g, own, leaving, entering, gain, band, column, outgoing, slot=None):
    cols, frames = own.shape[1:]
    top = lax.broadcasted_iota(jnp.int32, (cols // 8, 8, LANES), 1) < 4
    blank = jnp.zeros((2, 8, LANES), F32)
    slot = g if slot is None else slot
    outs = [leaving(q) for q in range(PER)]
    news = [entering(q) for q in range(PER)]
    levels = [dot(band, jnp.concatenate([o, n], axis=0)) for o, n in zip(outs, news)]
    column = list(column)
    dets = []
    for q in range(PER):
        det = []
        for h in range(frames // LANES):
            part = slice(h * LANES, (h + 1) * LANES)
            inner = column[h] - outs[q][:, part].astype(F32)
            column[h] = inner + news[q][:, part].astype(F32)
            turned = pltpu.roll(inner.reshape(cols // 8, 8, LANES), 4, 1)
            turned = jnp.concatenate([blank, turned, blank], axis=0)
            both = turned[0 : cols // 8 + 1] + turned[3 : cols // 8 + 4]
            sides = jnp.where(top, both[0 : cols // 8], both[1 : cols // 8 + 1])
            fit = (levels[q][:, part] + sides.reshape(cols, LANES)) * gain
            outgoing[slot, q, :, part] = fit.astype(BF16)
            det.append((own[g * PER + q, :, part].astype(F32) - fit).astype(BF16))
        dets.append(jnp.concatenate(det, axis=1))
    return column, dets


def grow(total, weight, g, dets):
    weights = jnp.concatenate([weight[g * PER + q] for q in range(PER)], axis=1)
    return total + dot(weights, jnp.concatenate(dets, axis=0))


def halves(ref):
    return [ref[:, h * LANES : (h + 1) * LANES] for h in range(ref.shape[1] // LANES)]


def add_rows(column, rows, sign=1.0):
    for row in rows:
        column = [c + sign * r.astype(F32) for c, r in zip(column, halves(row))]
    return column


def put(ref, column):
    for h, value in enumerate(column):
        ref[:, h * LANES : (h + 1) * LANES] = value


def sender(outgoing, background, sems):
    def send(g):
        return pltpu.make_async_copy(
            outgoing.at[g], background.at[0, pl.ds(g * PER, PER)], sems.at[g]
        )

    return send


def tables(gain):
    cols = gain.shape[1]
    band = jnp.where(jnp.abs(lag_table(cols)) <= RAD, 1.0, 0.0).astype(BF16)
    return (
        jnp.broadcast_to(gain[...], (LANES, cols)).T / (8.0 * RAD),
        jnp.concatenate([band, band], axis=1),
    )


def middle_kernel(own, near, weight, gain, background, upper, lower, total, outgoing, sems):
    rows, cols, frames = own.shape
    groups = range((RAD - NEAR) // PER, (rows - RAD + NEAR) // PER)
    send = sender(outgoing, background, sems)
    gains, band = tables(gain)
    column = [jnp.zeros((cols, LANES), F32)] * (frames // LANES)
    column = add_rows(column, [near[NEAR + r] for r in range(NEAR)])
    column = add_rows(column, [own[r] for r in range(RAD)])
    put(upper, column)
    column = add_rows(column, [own[RAD + r] for r in range(2 * RAD - NEAR - RAD)])
    grown = jnp.zeros(total.shape, F32)
    for g in groups:
        y = g * PER
        column, dets = annulus_group(
            g,
            own,
            (lambda q: near[NEAR + y - RAD + NEAR + q])
            if y < RAD
            else (lambda q: own[y - RAD + q]),
            (lambda q: near[y + RAD - rows + q])
            if y + RAD >= rows
            else (lambda q: own[y + RAD + q]),
            gains, band, column, outgoing,
        )
        send(g).start()
        grown = grow(grown, weight, g, dets)
    put(lower, column)
    total[...] = grown
    for g in groups:
        send(g).wait()


def mid_kernel(
    own, above, below, weight, gain, before, upper, lower, total,
    background, new_upper, new_lower, new_total, outgoing, sems,
):
    del before
    rows = own.shape[0]
    low, high = RAD // PER - 2, (rows - RAD) // PER + 1
    y, z = low * PER, high * PER
    send = sender(outgoing, background, sems)
    gains, band = tables(gain)
    column = add_rows(halves(upper), [above[r] for r in range(PER)])
    put(new_upper, column)
    column = add_rows(column, [own[RAD + r] for r in range(PER)])
    _, low_dets = annulus_group(
        low, own, lambda q: above[q], lambda q: own[y + RAD + q], gains, band, column, outgoing
    )
    send(low).start()
    column, high_dets = annulus_group(
        high, own, lambda q: own[z - RAD + q], lambda q: below[q], gains, band, halves(lower),
        outgoing,
    )
    send(high).start()
    put(new_lower, column)
    new_total[...] = grow(grow(total[...], weight, low, low_dets), weight, high, high_dets)
    send(low).wait()
    send(high).wait()


def end_kernel(
    own, above, below, weight, weight_next, weight_prev, gain, upper, lower, total,
    gradient, late,
):
    rows, _, frames = own.shape
    low, high = 0, rows // PER - 1
    z = high * PER
    gains, band = tables(gain)
    _, low_dets = annulus_group(
        low, own, lambda q: above[q], lambda q: own[RAD + q], gains, band,
        add_rows(halves(upper), [above[r] for r in range(PER)]), late, 0,
    )
    _, high_dets = annulus_group(
        high, own, lambda q: own[z - RAD + q], lambda q: below[q], gains, band, halves(lower),
        late, 1,
    )
    grown = grow(grow(total[...], weight, low, low_dets), weight, high, high_dets)
    edges = ((2, weight_next, high_dets[PER - GR :]), (3, weight_prev, low_dets[:GR]))
    for at, edge, parts in edges:
        value = dot(
            jnp.concatenate([edge[a] for a in range(GR)], axis=1), jnp.concatenate(parts, axis=0)
        )
        gradient[:, at * frames : (at + 1) * frames] = value.astype(BF16)
    coarse = grown.astype(BF16)
    gradient[:, 0:frames] = coarse
    gradient[:, frames : 2 * frames] = (grown - coarse.astype(F32)).astype(BF16)


def late_kernel(late, before, background, sems):
    del before
    rows = background.shape[1]
    copies = [
        pltpu.make_async_copy(late.at[k], background.at[0, pl.ds(first, PER)], sems.at[k])
        for k, first in enumerate((0, rows - PER))
    ]
    for copy in copies:
        copy.start()
    for copy in copies:
        copy.wait()


def make_annulus(own, near, mid, far, weights, gain):
    rows, cols, frames = own.shape
    weight, weight_next, weight_prev = weights
    slots = weight.shape[1]
    background = jax.ShapeDtypeStruct((1, rows, cols, frames), BF16)
    column = jax.ShapeDtypeStruct((cols, frames), F32)
    total = jax.ShapeDtypeStruct((slots, frames), F32)
    gradient = jax.ShapeDtypeStruct((slots, 4 * frames), BF16)

    def call(kernel, name, args, outs, done, declared=COST):
        specs = [VMEM] * len(args)
        if done is not None:
            specs[done] = HBM
        return pl.pallas_call(
            kernel,
            in_specs=specs,
            out_specs=[HBM] + [VMEM] * (len(outs) - 1),
            out_shape=outs,
            scratch_shapes=[
                pltpu.VMEM((rows // PER, PER, cols, frames), BF16),
                pltpu.SemaphoreType.DMA((rows // PER,)),
            ],
            input_output_aliases={} if done is None else {done: 0},
            compiler_params=params(),
            cost_estimate=declared,
            name=name,
        )(*args)

    done, upper, lower, grown = call(
        middle_kernel, "annulus_middle", (own, near, weight, gain),
        (background, column, column, total), None,
    )
    done, upper, lower, grown = call(
        mid_kernel, "annulus_mid",
        (own, *mid, weight, gain, done, upper, lower, grown),
        (background, column, column, total), 5,
        pl.CostEstimate(
            flops=2 * rows * cols * cols * frames, bytes_accessed=5 * MIB, transcendentals=0
        ),
    )
    args = (own, *far, weight, weight_next, weight_prev, gain, upper, lower, grown)
    gradient, late = pl.pallas_call(
        end_kernel,
        in_specs=[VMEM] * len(args),
        out_shape=(gradient, jax.ShapeDtypeStruct((2, PER, cols, frames), BF16)),
        compiler_params=params(),
        cost_estimate=COST,
        name="annulus_end",
    )(*args)
    background = pl.pallas_call(
        late_kernel,
        in_specs=[VMEM, HBM],
        out_specs=HBM,
        out_shape=background,
        scratch_shapes=[pltpu.SemaphoreType.DMA((2,))],
        input_output_aliases={1: 0},
        compiler_params=params(),
        cost_estimate=COST,
        name="late_rows",
    )(late, done)
    return background, gradient


def prepare_kernel(capacity, stripe, slow, fast, step, hots, tables):
    count = stripe.shape[1]
    frames = tables.shape[2]
    slots = hots.shape[1] // 4

    def upended(row):
        return jnp.broadcast_to(row[...].astype(F32), (LANES, count)).T

    before = lax.broadcasted_iota(jnp.int32, (count, count), 1) < lax.broadcasted_iota(
        jnp.int32, (count, count), 0
    )
    named = upended(stripe)
    same = (named == stripe[...].astype(F32)) & before
    rank = jnp.sum(jnp.where(same, 1.0, 0.0), axis=1, keepdims=True)
    slot = (named[:, 0:1] * capacity + rank).astype(jnp.int32)
    place = lax.broadcasted_iota(jnp.int32, (count, slots), 1)
    for k, shift in enumerate((0, 0, capacity, -capacity)):
        hots[:, k * slots : (k + 1) * slots] = jnp.where(place + shift == slot, 1.0, 0.0).astype(
            BF16
        )
    a, b = upended(slow), upended(fast)
    for k, part in enumerate((upended(step), a, b, (1.0 - a) * (1.0 - b) / (a - b))):
        tables[k] = jnp.concatenate([part] * (frames // LANES), axis=1)


def prepare_traces(stripe, slow, fast, step, frames, slots, capacity):
    count = stripe.shape[1]
    return pl.pallas_call(
        functools.partial(prepare_kernel, capacity),
        out_shape=(
            jax.ShapeDtypeStruct((count, 4 * slots), BF16),
            jax.ShapeDtypeStruct((4, count, frames), F32),
        ),
        compiler_params=params(),
        cost_estimate=COST,
        name="prepare",
    )(stripe, slow, fast, step)


def traces_kernel(hots, tables, traces, inbox, out):
    count, frames = traces.shape
    parts = [inbox[:, k * frames : (k + 1) * frames] for k in range(4)]
    gradient = dot(hots[...], jnp.concatenate(parts, axis=0))
    updated = traces[...].astype(F32) + tables[0] * gradient
    lane = lax.broadcasted_iota(jnp.int32, (count, frames), 1)

    def lagged(value, lag):
        return jnp.where(lane >= lag, pltpu.roll(value, lag, 1), 0.0)

    a, b = tables[1], tables[2]
    driven = updated - (a + b) * lagged(updated, 1) + (a * b) * lagged(updated, 2)
    spikes = jnp.maximum(driven - lam_floor, 0.0)
    sums = [spikes, spikes]
    roots = [a, b]
    lag = 1
    while lag < frames:
        sums = [value + root * lagged(value, lag) for value, root in zip(sums, roots)]
        roots = [root * root for root in roots]
        lag *= 2
    out[...] = tables[3] * (a * sums[0] - b * sums[1])


def make_traces(hots, tables, traces, inbox):
    count, frames = traces.shape
    return pl.pallas_call(
        traces_kernel,
        out_shape=jax.ShapeDtypeStruct((count, frames), F32),
        compiler_params=params(),
        cost_estimate=COST,
        name="traces",
    )(hots, tables, traces, inbox)


def neighbours(axis):
    devices = lax.axis_size(axis)
    up = [(i, i + 1) for i in range(devices - 1)]
    return up, [(j, i) for i, j in up]


def on_device(movie, footprints, traces, stripe, column, annulus_gain, decay_slow, decay_fast):
    pix_count = lax.axis_size("pix")
    rows, cols, frames = movie.shape[1:]
    count = footprints.shape[1]
    capacity = max(2, 2 * count // pix_count)
    slots = pix_count * capacity
    pix_up, pix_down = neighbours("pix")
    plane_up, plane_down = neighbours("plane")

    stripe_row = stripe.reshape(1, count)
    outbox = make_outbox(stripe_row, column, footprints[0], traces[0], capacity, slots)
    def exchange(up, down):
        return (lax.ppermute(up, "pix", pix_up), lax.ppermute(down, "pix", pix_down))

    frames_in, outbox = lax.optimization_barrier((movie, outbox))
    inbox = lax.all_to_all(outbox, "pix", split_axis=0, concat_axis=0, tiled=True)
    near_prev, near_next = exchange(frames_in[0, rows - NEAR :], frames_in[0, :NEAR])
    *started, mid_noise, up, down = make_residual(inbox, movie)
    mid = exchange(up, down)
    foot_rows, residual, other_noise, up, down = make_residual(
        inbox, movie, (*started, mid_noise)
    )
    near_rows, near_residual, noise = make_near(
        inbox, near_next, near_prev, (mid_noise, other_noise)
    )
    foot_f = footprints[0].astype(F32)
    step = 1.0 / (jnp.sum(foot_f * foot_f, axis=1) + norm_eps)
    step_row, up, down, noise = lax.optimization_barrier((step[None], up, down, noise))
    far = exchange(up, down)
    noises = (
        noise,
        lax.ppermute(noise, "plane", plane_up),
        lax.ppermute(noise, "plane", plane_down),
    )
    hots, tables = prepare_traces(
        stripe_row, decay_slow, decay_fast, step_row, frames, slots, capacity
    )
    weights = make_weights(foot_rows, near_rows, noises)
    background, gradient = make_annulus(
        residual, near_residual, mid, far, weights, annulus_gain
    )
    home = lax.all_to_all(gradient, "pix", split_axis=0, concat_axis=0, tiled=True)
    traces_new = make_traces(hots, tables, traces[0], home)
    return (background, traces_new[None])


def solution(mesh):
    placed = (
        P("plane", "pix", None, None),
        P("plane", "pix", None),
        P("plane", "pix", None),
        P("plane", "pix", None),
        P("plane", "pix"),
        P("plane", None),
        P("plane", "pix"),
        P("plane", "pix"),
    )
    return jax.shard_map(
        on_device,
        mesh=mesh,
        in_specs=placed,
        out_specs=(P("plane", "pix", None, None), P("plane", "pix", None)),
        check_vma=False,
    )
```

```python
import functools

import jax
import jax.numpy as jnp
import ml_dtypes
import numpy as np
from jax import lax
from jax.experimental import pallas as pl
from jax.experimental.pallas import tpu as pltpu
from jax.sharding import PartitionSpec as P

FOOT = 32
RAD = 12
GR = 3
LANES = 128
PER = LANES // FOOT
NEAR = PER

lam_floor = 0.1
noise_eps = 1e-05
norm_eps = 1e-05
sigma_twice = 4.5

F32 = jnp.float32
BF16 = jnp.bfloat16
MIB = 1 << 20
HBM = pl.BlockSpec(memory_space=pltpu.HBM)
VMEM = pl.BlockSpec(memory_space=pltpu.VMEM)


def tap_values():
    offsets = np.arange(-GR, GR + 1).astype(np.float32)
    raw = np.exp(-offsets * offsets / np.float32(sigma_twice)).astype(np.float32)
    return (raw / raw.sum(dtype=np.float32)).astype(ml_dtypes.bfloat16).astype(np.float32)


def params(mib=16):
    return pltpu.CompilerParams(vmem_limit_bytes=mib * MIB)


COST = pl.CostEstimate(flops=1, bytes_accessed=1, transcendentals=0)


def dot(a, b):
    return jnp.dot(a, b, preferred_element_type=F32)


def outbox_kernel(capacity, *refs):
    sources, result, places, outbox, sems = refs[0:4], refs[4], refs[5:9], refs[9], refs[10]
    copies = [
        pltpu.make_async_copy(source, place, sems.at[k])
        for k, (source, place) in enumerate(zip(sources, places))
    ]
    for copy in copies:
        copy.start()
    for copy in copies[0:2]:
        copy.wait()
    stripe, column, foot, traces = places
    slots = outbox.shape[0]
    count, tiles = foot.shape
    frames = traces.shape[1]
    before = lax.broadcasted_iota(jnp.int32, (count, count), 0) < lax.broadcasted_iota(
        jnp.int32, (count, count), 1
    )
    named = jnp.broadcast_to(stripe[...].astype(F32), (count, count))
    same = (named == named.T) & before
    rank = jnp.sum(jnp.where(same, 1.0, 0.0), axis=0, keepdims=True).astype(jnp.int32)
    slot = stripe[...] * capacity + rank
    place = lax.broadcasted_iota(jnp.int32, (slots, count), 0)
    left = jnp.broadcast_to(column[...].astype(F32), (LANES, count)).T.astype(BF16)
    lane = lax.broadcasted_iota(jnp.int32, (slots, LANES), 1)
    edge = NEAR * FOOT
    lefts = jnp.zeros((slots, LANES), F32)
    at = 3 * frames
    hots = [
        jnp.where(place + shift == slot, 1.0, 0.0).astype(BF16)
        for shift in (0, capacity, -capacity)
    ]
    for copy in copies[2:]:
        copy.wait()
    leaving = []

    def leave(start, width):
        lanes = pl.ds(start, width)
        copy = pltpu.make_async_copy(
            outbox.at[:, lanes], result.at[:, lanes], sems.at[len(copies) + len(leaving)]
        )
        copy.start()
        leaving.append(copy)

    for k, (hot, first, width) in enumerate(
        zip(hots, (0, 0, tiles - edge), (tiles, edge, edge))
    ):
        outbox[:, at : at + width] = dot(hot, foot[:, first : first + width]).astype(BF16)
        if k == 0:
            leave(at, width)
        outbox[:, k * frames : (k + 1) * frames] = dot(hot, traces[...]).astype(BF16)
        lefts = jnp.where(lane == k, dot(hot, left), lefts)
        at += width
    leave(0, 3 * frames)
    outbox[:, at:] = lefts.astype(BF16)
    leave(3 * frames + tiles, outbox.shape[1] - 3 * frames - tiles)
    for copy in leaving:
        copy.wait()


def make_outbox(stripe, column, foot, traces, capacity, slots):
    count, tiles = foot.shape
    frames = traces.shape[1]
    width = 3 * frames + tiles + 2 * NEAR * FOOT + LANES
    args = (stripe, column, foot, traces)
    return pl.pallas_call(
        functools.partial(outbox_kernel, capacity),
        in_specs=[HBM] * len(args),
        out_specs=HBM,
        out_shape=jax.ShapeDtypeStruct((slots, width), BF16),
        scratch_shapes=[pltpu.VMEM(a.shape, a.dtype) for a in args]
        + [pltpu.VMEM((slots, width), BF16), pltpu.SemaphoreType.DMA((len(args) + 3,))],
        compiler_params=params(56),
        cost_estimate=COST,
        name="outbox",
    )(*args)


def spread(block, col):
    lane = lax.broadcasted_iota(jnp.int32, block.shape, 1)
    for k in range(7):
        block = jnp.where(((col >> k) & 1) == 1, pltpu.roll(block, 1 << k, 1), block)
    inside = ((lane - col) & (LANES - 1)) < FOOT
    left = inside & (lane >= col)
    right = inside & (lane < col)
    rows = []
    for q in range(PER):
        moved = block if q == 0 else pltpu.roll(block, LANES - q * FOOT, 1)
        rows.append(
            jnp.concatenate(
                [jnp.where(left, moved, 0.0), jnp.where(right, moved, 0.0)], axis=1
            ).astype(BF16)
        )
    return rows


def tile_rows(inbox, which, block, frames):
    lefts = inbox[:, inbox.shape[1] - LANES :].astype(F32)
    col = jnp.broadcast_to(lefts[:, which : which + 1], lefts.shape).astype(jnp.int32)
    start = 3 * frames + block * LANES
    if not isinstance(start, int):
        start = pl.multiple_of(start, LANES)
    return spread(inbox[:, pl.ds(start, LANES)].astype(F32), col)


def model_row(row, inbox, which, frames):
    traces = inbox[:, which * frames : (which + 1) * frames]
    return lax.dot_general(row, traces, (((0,), (0,)), ((), ())), preferred_element_type=F32)


def noise_row(left, change):
    frames = left.shape[1]
    steps = dot(left, change)
    steps = steps * steps
    part = steps[:, 0:LANES]
    for k in range(1, frames // LANES):
        part = part + steps[:, k * LANES : (k + 1) * LANES]
    return jnp.sum(part.T, axis=0, keepdims=True) / (frames - 1)


def lag_table(size):
    shape = (size, size)
    return lax.broadcasted_iota(jnp.int32, shape, 1) - lax.broadcasted_iota(jnp.int32, shape, 0)


def change_matrix(frames):
    lag = lag_table(frames)
    steps = jnp.where(lag == -1, 1.0, 0.0) - jnp.where(lag == 0, 1.0, 0.0)
    later = lax.broadcasted_iota(jnp.int32, lag.shape, 1)
    return jnp.where(later < frames - 1, steps, 0.0).astype(BF16)


def residual_kernel(pick, low, high, first, inbox, movie, *refs):
    if not first:
        refs = refs[3:]
    (foot_rows, residual, noise, up, down) = refs[0:5]
    (change, movie_slots, foot_slots, left_slots, sems) = refs[5:]
    frames = movie.shape[3]
    count = pick(None)
    change[...] = change_matrix(frames)

    def fetch(i, slot):
        rows_g = pl.ds(pick(i) * PER, PER)
        return pltpu.make_async_copy(movie.at[0, rows_g], movie_slots.at[slot], sems.at[0, slot])

    def sends(i, slot):
        rows_g = pl.ds(pick(i) * PER, PER)
        return (
            pltpu.make_async_copy(foot_slots.at[slot], foot_rows.at[rows_g], sems.at[1, slot]),
            pltpu.make_async_copy(left_slots.at[slot], residual.at[rows_g], sems.at[2, slot]),
        )

    fetch(0, 0).start()

    def group(i, carry):
        slot = lax.rem(i, 2)
        g = pick(i)

        @pl.when(i + 1 < count)
        def _():
            fetch(i + 1, 1 - slot).start()

        fetch(i, slot).wait()

        @pl.when(i >= 2)
        def _():
            for copy in sends(i - 2, slot):
                copy.wait()

        noises = []
        for q, row in enumerate(tile_rows(inbox, 0, g, frames)):
            foot_slots[slot, q] = row
            left = movie_slots[slot, q].astype(F32) - model_row(row, inbox, 0, frames)
            left = left.astype(BF16)
            left_slots[slot, q] = left
            noises.append(noise_row(left, change[...]))
        noise[i] = jnp.concatenate(noises, axis=0)
        for copy in sends(i, slot):
            copy.start()

        @pl.when(g == low)
        def _():
            down[...] = left_slots[slot]

        @pl.when(g == high)
        def _():
            up[...] = left_slots[slot]

        return carry

    lax.fori_loop(0, count, group, 0)
    for i in (count - 2, count - 1):
        for copy in sends(i, i % 2):
            copy.wait()


def make_residual(inbox, movie, earlier=None):
    slots = inbox.shape[0]
    rows, cols, frames = movie.shape[1:]
    groups = rows // PER
    mids = (1, groups - 2)
    if earlier is None:
        low, high, count = *mids, 2

        def pick(i):
            return count if i is None else mids[0] + i * (mids[1] - mids[0])
    else:
        low, high, count = 2, groups - 3, groups - 2

        def pick(i):
            if i is None:
                return count
            if isinstance(i, int):
                return i + (i >= mids[0]) + (i + 1 >= mids[1])
            return i + jnp.where(i >= mids[0], 1, 0) + jnp.where(i + 1 >= mids[1], 1, 0)

    piece = jax.ShapeDtypeStruct((PER, cols, frames), BF16)
    more = () if earlier is None else earlier
    return pl.pallas_call(
        functools.partial(residual_kernel, pick, low, high, earlier is None),
        in_specs=[VMEM, HBM] + [HBM, HBM, VMEM][: len(more)],
        out_specs=[HBM, HBM, VMEM, VMEM, VMEM],
        out_shape=(
            jax.ShapeDtypeStruct((rows, slots, cols), BF16),
            jax.ShapeDtypeStruct((rows, cols, frames), BF16),
            jax.ShapeDtypeStruct((count, PER, cols), F32),
            piece,
            piece,
        ),
        scratch_shapes=[
            pltpu.VMEM((frames, frames), BF16),
            pltpu.VMEM((2, PER, cols, frames), BF16),
            pltpu.VMEM((2, PER, slots, cols), BF16),
            pltpu.VMEM((2, PER, cols, frames), BF16),
            pltpu.SemaphoreType.DMA((3, 2)),
        ],
        input_output_aliases={} if earlier is None else {2: 0, 3: 1},
        compiler_params=params(44),
        cost_estimate=COST,
        name="residual",
    )(inbox, movie, *more)


def near_kernel(
    inbox, movie_next, movie_prev, mid_noise, other_noise, foot_rows, residual, noise
):
    frames = movie_next.shape[2]
    groups = mid_noise.shape[0] + other_noise.shape[0]
    own = FOOT // PER
    change = change_matrix(frames)
    others = [g for g in range(groups) if g not in (1, groups - 2)]
    for order, part in (((1, groups - 2), mid_noise), (others, other_noise)):
        for i, g in enumerate(order):
            noise[NEAR + g * PER : NEAR + (g + 1) * PER, :] = part[i]
    for side, (block, movie, first) in enumerate(
        ((own, movie_next, 0), (own + NEAR // PER, movie_prev, NEAR + groups * PER))
    ):
        for q, row in enumerate(tile_rows(inbox, 1 + side, block, frames)):
            y = side * NEAR + q
            foot_rows[y] = row
            left = movie[q].astype(F32) - model_row(row, inbox, 1 + side, frames)
            left = left.astype(BF16)
            residual[y] = left
            noise[first + q : first + q + 1, :] = noise_row(left, change)


def make_near(inbox, movie_next, movie_prev, noises):
    slots = inbox.shape[0]
    cols, frames = movie_next.shape[1:]
    return pl.pallas_call(
        near_kernel,
        out_shape=(
            jax.ShapeDtypeStruct((2 * NEAR, slots, cols), BF16),
            jax.ShapeDtypeStruct((2 * NEAR, cols, frames), BF16),
            jax.ShapeDtypeStruct((2 * NEAR + PER * sum(n.shape[0] for n in noises), cols), F32),
        ),
        compiler_params=params(),
        cost_estimate=COST,
        name="near",
    )(inbox, movie_next, movie_prev, *noises)


def weights_kernel(
    taps, own, near, noise, noise_before, noise_after, out, out_next, out_prev,
    own_slots, scale, band, sems,
):
    rows, slots, cols = own.shape
    part = own_slots.shape[2]
    count = slots // part

    def fetch(i, slot):
        these = pl.ds(pl.multiple_of(i * part, part), part)
        return pltpu.make_async_copy(own.at[:, these, :], own_slots.at[slot], sems.at[slot])

    fetch(0, 0).start()
    pooled = (noise_before[...] + 2.0 * noise[...] + noise_after[...]) / 4.0
    scale[...] = 1.0 / jnp.sqrt(pooled + noise_eps)
    lag = jnp.abs(lag_table(cols))
    table = jnp.zeros(lag.shape, F32)
    for k in range(GR + 1):
        table = jnp.where(lag == k, taps[GR + k], table)
    band[...] = table.astype(BF16)

    def across(foot, inv):
        scaled = (foot.astype(F32) * inv[:, None, :]).astype(BF16)
        count = foot.shape[0]
        return dot(scaled.reshape(count * part, cols), band[...]).reshape(count, part, cols)

    def some(i, carry):
        slot = lax.rem(i, 2)

        @pl.when(i + 1 < count)
        def _():
            fetch(i + 1, 1 - slot).start()

        fetch(i, slot).wait()
        these = pl.ds(pl.multiple_of(i * part, part), part)
        blurred = across(own_slots[slot], scale[NEAR : NEAR + rows])
        for r in range(rows):
            total = taps[GR] * blurred[r]
            for k in range(1, GR + 1):
                if r - k >= 0 and r + k < rows:
                    total = total + taps[GR + k] * (blurred[r - k] + blurred[r + k])
                elif r - k >= 0:
                    total = total + taps[GR + k] * blurred[r - k]
                elif r + k < rows:
                    total = total + taps[GR + k] * blurred[r + k]
            out[r, these, :] = total.astype(BF16)
        after = across(near[0:GR, these, :], scale[0:GR])
        ahead = across(near[2 * NEAR - GR : 2 * NEAR, these, :], scale[rows + 2 * NEAR - GR :])
        for a in range(GR):
            total = taps[2 * GR - a] * after[0]
            for r in range(1, a + 1):
                total = total + taps[2 * GR + r - a] * after[r]
            out_next[a, these, :] = total.astype(BF16)
            total = taps[2 * GR] * ahead[a]
            for b in range(a + 1, GR):
                total = total + taps[2 * GR + a - b] * ahead[b]
            out_prev[a, these, :] = total.astype(BF16)
        return carry

    lax.fori_loop(0, count, some, 0)


def make_weights(foot_rows, near_rows, noises):
    rows, slots, cols = foot_rows.shape
    part = 32
    return pl.pallas_call(
        functools.partial(weights_kernel, [float(t) for t in tap_values()]),
        in_specs=[HBM] + [VMEM] * (1 + len(noises)),
        out_shape=(
            jax.ShapeDtypeStruct((rows, slots, cols), BF16),
            jax.ShapeDtypeStruct((GR, slots, cols), BF16),
            jax.ShapeDtypeStruct((GR, slots, cols), BF16),
        ),
        scratch_shapes=[
            pltpu.VMEM((2, rows, part, cols), BF16),
            pltpu.VMEM(noises[0].shape, F32),
            pltpu.VMEM((cols, cols), BF16),
            pltpu.SemaphoreType.DMA((2,)),
        ],
        compiler_params=params(32),
        cost_estimate=COST,
        name="weights",
    )(foot_rows, near_rows, *noises)


def side_sum(column):
    cols = column.shape[0]
    top = lax.broadcasted_iota(jnp.int32, (cols // 8, 8, LANES), 1) < 4
    blank = jnp.zeros((2, 8, LANES), F32)
    turned = pltpu.roll(column.reshape(cols // 8, 8, LANES), 4, 1)
    turned = jnp.concatenate([blank, turned, blank], axis=0)
    both = turned[0 : cols // 8 + 1] + turned[3 : cols // 8 + 4]
    sides = jnp.where(top, both[0 : cols // 8], both[1 : cols // 8 + 1])
    return sides.reshape(cols, LANES)


def annulus_group(g, own, leaving, entering, gain, band, column, outgoing):
    frames = own.shape[2]
    outs = [leaving(q) for q in range(PER)]
    news = [entering(q) for q in range(PER)]
    levels = [dot(band, jnp.concatenate([o, n], axis=0)) for o, n in zip(outs, news)]
    column = list(column)
    dets = []
    for q in range(PER):
        det = []
        for h in range(frames // LANES):
            part = slice(h * LANES, (h + 1) * LANES)
            inner = column[h] - outs[q][:, part].astype(F32)
            column[h] = inner + news[q][:, part].astype(F32)
            fit = (levels[q][:, part] + side_sum(inner)) * gain
            outgoing[g, q, :, part] = fit.astype(BF16)
            det.append((own[g * PER + q, :, part].astype(F32) - fit).astype(BF16))
        dets.append(jnp.concatenate(det, axis=1))
    return column, dets


def grow(total, weight, g, dets):
    weights = jnp.concatenate([weight[g * PER + q] for q in range(PER)], axis=1)
    return total + dot(weights, jnp.concatenate(dets, axis=0))


def halves(ref):
    return [ref[:, h * LANES : (h + 1) * LANES] for h in range(ref.shape[1] // LANES)]


def add_rows(column, rows, sign=1.0):
    for row in rows:
        column = [c + sign * r.astype(F32) for c, r in zip(column, halves(row))]
    return column


def put(ref, column):
    for h, value in enumerate(column):
        ref[:, h * LANES : (h + 1) * LANES] = value


def sender(outgoing, background, sems):
    def send(g):
        return pltpu.make_async_copy(
            outgoing.at[g], background.at[0, pl.ds(g * PER, PER)], sems.at[g]
        )

    return send


def tables(gain):
    cols = gain.shape[1]
    band = jnp.where(jnp.abs(lag_table(cols)) <= RAD, 1.0, 0.0).astype(BF16)
    return (
        jnp.broadcast_to(gain[...], (LANES, cols)).T / (8.0 * RAD),
        jnp.concatenate([band, band], axis=1),
    )


def middle_kernel(own, near, weight, gain, background, upper, lower, total, outgoing, sems):
    rows, cols, frames = own.shape
    groups = range((RAD - NEAR) // PER, (rows - RAD + NEAR) // PER)
    send = sender(outgoing, background, sems)
    gains, band = tables(gain)
    column = [jnp.zeros((cols, LANES), F32)] * (frames // LANES)
    column = add_rows(column, [near[NEAR + r] for r in range(NEAR)])
    column = add_rows(column, [own[r] for r in range(RAD)])
    put(upper, column)
    column = add_rows(column, [own[RAD + r] for r in range(2 * RAD - NEAR - RAD)])
    grown = jnp.zeros(total.shape, F32)
    for g in groups:
        y = g * PER
        column, dets = annulus_group(
            g,
            own,
            (lambda q: near[NEAR + y - RAD + NEAR + q])
            if y < RAD
            else (lambda q: own[y - RAD + q]),
            (lambda q: near[y + RAD - rows + q])
            if y + RAD >= rows
            else (lambda q: own[y + RAD + q]),
            gains, band, column, outgoing,
        )
        send(g).start()
        grown = grow(grown, weight, g, dets)
    put(lower, column)
    total[...] = grown
    for g in groups:
        send(g).wait()


def mid_kernel(
    own, above, below, weight, gain, before, upper, lower, total,
    background, new_total, base, gain_table, band_table, outgoing, sems,
):
    del before
    rows = own.shape[0]
    low, high = RAD // PER - 2, (rows - RAD) // PER + 1
    y, z = low * PER, high * PER
    send = sender(outgoing, background, sems)
    gains, band = tables(gain)
    first = add_rows(halves(upper), [above[r] for r in range(PER)])
    column = add_rows(first, [own[RAD + r] for r in range(PER)])
    _, low_dets = annulus_group(
        low, own, lambda q: above[q], lambda q: own[y + RAD + q], gains, band, column, outgoing
    )
    send(low).start()
    column, high_dets = annulus_group(
        high, own, lambda q: own[z - RAD + q], lambda q: below[q], gains, band, halves(lower),
        outgoing,
    )
    send(high).start()
    new_total[...] = grow(grow(total[...], weight, low, low_dets), weight, high, high_dets)
    gain_table[...] = gains
    band_table[...] = band[:, : own.shape[1]]
    for q in range(PER):
        if q > 0:
            first = add_rows(first, [own[RAD + q - 1]])
        inner = own[z + PER - RAD + q]
        column = add_rows(column, [inner], -1.0)
        for k, (sums, row) in enumerate(((first, own[RAD + q]), (column, inner))):
            level = dot(band_table[...], row)
            for h, value in enumerate(sums):
                part = slice(h * LANES, (h + 1) * LANES)
                base[k, q, :, part] = level[:, part] + side_sum(value)
    send(low).wait()
    send(high).wait()


def end_kernel(
    own, above, below, weight, weight_next, weight_prev, total, base, gain, band, gradient, late
):
    rows, cols, frames = own.shape
    low, high = 0, rows // PER - 1
    blank = [jnp.zeros((cols, LANES), F32)] * (frames // LANES)
    dets = []
    for k, (g, far, order) in enumerate(
        ((low, above, range(PER - 1, -1, -1)), (high, below, range(PER)))
    ):
        column, mine = blank, [None] * PER
        for i, q in enumerate(order):
            row = far[q]
            level = dot(band[...], row)
            det = []
            for h in range(frames // LANES):
                part = slice(h * LANES, (h + 1) * LANES)
                fit = base[k, q, :, part] + level[:, part]
                if i > 0:
                    fit = fit + side_sum(column[h])
                fit = fit * gain[...]
                late[k, q, :, part] = fit.astype(BF16)
                det.append((own[g * PER + q, :, part].astype(F32) - fit).astype(BF16))
            mine[q] = jnp.concatenate(det, axis=1)
            column = add_rows(column, [row])
        dets.append(mine)
    low_dets, high_dets = dets
    grown = grow(grow(total[...], weight, low, low_dets), weight, high, high_dets)
    edges = ((2, weight_next, high_dets[PER - GR :]), (3, weight_prev, low_dets[:GR]))
    for at, edge, parts in edges:
        value = dot(
            jnp.concatenate([edge[a] for a in range(GR)], axis=1), jnp.concatenate(parts, axis=0)
        )
        gradient[:, at * frames : (at + 1) * frames] = value.astype(BF16)
    coarse = grown.astype(BF16)
    gradient[:, 0:frames] = coarse
    gradient[:, frames : 2 * frames] = (grown - coarse.astype(F32)).astype(BF16)


def late_kernel(late, before, background, sems):
    del before
    rows = background.shape[1]
    copies = [
        pltpu.make_async_copy(late.at[k], background.at[0, pl.ds(first, PER)], sems.at[k])
        for k, first in enumerate((0, rows - PER))
    ]
    for copy in copies:
        copy.start()
    for copy in copies:
        copy.wait()


def make_annulus(own, near, mid, far, weights, gain):
    rows, cols, frames = own.shape
    weight, weight_next, weight_prev = weights
    slots = weight.shape[1]
    background = jax.ShapeDtypeStruct((1, rows, cols, frames), BF16)
    column = jax.ShapeDtypeStruct((cols, frames), F32)
    total = jax.ShapeDtypeStruct((slots, frames), F32)
    gradient = jax.ShapeDtypeStruct((slots, 4 * frames), BF16)

    def call(kernel, name, args, outs, done, declared=COST):
        specs = [VMEM] * len(args)
        if done is not None:
            specs[done] = HBM
        return pl.pallas_call(
            kernel,
            in_specs=specs,
            out_specs=[HBM] + [VMEM] * (len(outs) - 1),
            out_shape=outs,
            scratch_shapes=[
                pltpu.VMEM((rows // PER, PER, cols, frames), BF16),
                pltpu.SemaphoreType.DMA((rows // PER,)),
            ],
            input_output_aliases={} if done is None else {done: 0},
            compiler_params=params(),
            cost_estimate=declared,
            name=name,
        )(*args)

    done, upper, lower, grown = call(
        middle_kernel, "annulus_middle", (own, near, weight, gain),
        (background, column, column, total), None,
    )
    prepared = (
        jax.ShapeDtypeStruct((2, PER, cols, frames), F32),
        jax.ShapeDtypeStruct((cols, LANES), F32),
        jax.ShapeDtypeStruct((cols, cols), BF16),
    )
    done, grown, *prepared = call(
        mid_kernel, "annulus_mid",
        (own, *mid, weight, gain, done, upper, lower, grown),
        (background, total, *prepared), 5,
        pl.CostEstimate(
            flops=2 * rows * cols * cols * frames, bytes_accessed=5 * MIB, transcendentals=0
        ),
    )
    args = (own, *far, weight, weight_next, weight_prev, grown, *prepared)
    gradient, late = pl.pallas_call(
        end_kernel,
        in_specs=[VMEM] * len(args),
        out_shape=(gradient, jax.ShapeDtypeStruct((2, PER, cols, frames), BF16)),
        compiler_params=params(),
        cost_estimate=COST,
        name="annulus_end",
    )(*args)
    background = pl.pallas_call(
        late_kernel,
        in_specs=[VMEM, HBM],
        out_specs=HBM,
        out_shape=background,
        scratch_shapes=[pltpu.SemaphoreType.DMA((2,))],
        input_output_aliases={1: 0},
        compiler_params=params(),
        cost_estimate=COST,
        name="late_rows",
    )(late, done)
    return background, gradient


def prepare_kernel(capacity, stripe, slow, fast, step, hots, tables):
    count = stripe.shape[1]
    frames = tables.shape[2]
    slots = hots.shape[1] // 4

    def upended(row):
        return jnp.broadcast_to(row[...].astype(F32), (LANES, count)).T

    before = lax.broadcasted_iota(jnp.int32, (count, count), 1) < lax.broadcasted_iota(
        jnp.int32, (count, count), 0
    )
    named = upended(stripe)
    same = (named == stripe[...].astype(F32)) & before
    rank = jnp.sum(jnp.where(same, 1.0, 0.0), axis=1, keepdims=True)
    slot = (named[:, 0:1] * capacity + rank).astype(jnp.int32)
    place = lax.broadcasted_iota(jnp.int32, (count, slots), 1)
    for k, shift in enumerate((0, 0, capacity, -capacity)):
        hots[:, k * slots : (k + 1) * slots] = jnp.where(place + shift == slot, 1.0, 0.0).astype(
            BF16
        )
    a, b = upended(slow), upended(fast)
    for k, part in enumerate((upended(step), a, b, (1.0 - a) * (1.0 - b) / (a - b))):
        tables[k] = jnp.concatenate([part] * (frames // LANES), axis=1)


def prepare_traces(stripe, slow, fast, step, frames, slots, capacity):
    count = stripe.shape[1]
    return pl.pallas_call(
        functools.partial(prepare_kernel, capacity),
        out_shape=(
            jax.ShapeDtypeStruct((count, 4 * slots), BF16),
            jax.ShapeDtypeStruct((4, count, frames), F32),
        ),
        compiler_params=params(),
        cost_estimate=COST,
        name="prepare",
    )(stripe, slow, fast, step)


def traces_kernel(hots, tables, traces, inbox, out):
    count, frames = traces.shape
    parts = [inbox[:, k * frames : (k + 1) * frames] for k in range(4)]
    gradient = dot(hots[...], jnp.concatenate(parts, axis=0))
    updated = traces[...].astype(F32) + tables[0] * gradient
    lane = lax.broadcasted_iota(jnp.int32, (count, frames), 1)

    def lagged(value, lag):
        return jnp.where(lane >= lag, pltpu.roll(value, lag, 1), 0.0)

    a, b = tables[1], tables[2]
    driven = updated - (a + b) * lagged(updated, 1) + (a * b) * lagged(updated, 2)
    spikes = jnp.maximum(driven - lam_floor, 0.0)
    sums = [spikes, spikes]
    roots = [a, b]
    lag = 1
    while lag < frames:
        sums = [value + root * lagged(value, lag) for value, root in zip(sums, roots)]
        roots = [root * root for root in roots]
        lag *= 2
    out[...] = tables[3] * (a * sums[0] - b * sums[1])


def make_traces(hots, tables, traces, inbox):
    count, frames = traces.shape
    return pl.pallas_call(
        traces_kernel,
        out_shape=jax.ShapeDtypeStruct((count, frames), F32),
        compiler_params=params(),
        cost_estimate=COST,
        name="traces",
    )(hots, tables, traces, inbox)


def neighbours(axis):
    devices = lax.axis_size(axis)
    up = [(i, i + 1) for i in range(devices - 1)]
    return up, [(j, i) for i, j in up]


def on_device(movie, footprints, traces, stripe, column, annulus_gain, decay_slow, decay_fast):
    pix_count = lax.axis_size("pix")
    rows, cols, frames = movie.shape[1:]
    count = footprints.shape[1]
    capacity = max(2, 2 * count // pix_count)
    slots = pix_count * capacity
    pix_up, pix_down = neighbours("pix")
    plane_up, plane_down = neighbours("plane")

    stripe_row = stripe.reshape(1, count)
    outbox = make_outbox(stripe_row, column, footprints[0], traces[0], capacity, slots)
    def exchange(up, down):
        return (lax.ppermute(up, "pix", pix_up), lax.ppermute(down, "pix", pix_down))

    frames_in, outbox = lax.optimization_barrier((movie, outbox))
    inbox = lax.all_to_all(outbox, "pix", split_axis=0, concat_axis=0, tiled=True)
    near_prev, near_next = exchange(frames_in[0, rows - NEAR :], frames_in[0, :NEAR])
    *started, mid_noise, up, down = make_residual(inbox, movie)
    mid = exchange(up, down)
    foot_rows, residual, other_noise, up, down = make_residual(
        inbox, movie, (*started, mid_noise)
    )
    near_rows, near_residual, noise = make_near(
        inbox, near_next, near_prev, (mid_noise, other_noise)
    )
    foot_f = footprints[0].astype(F32)
    step = 1.0 / (jnp.sum(foot_f * foot_f, axis=1) + norm_eps)
    step_row, up, down, noise = lax.optimization_barrier((step[None], up, down, noise))
    far = exchange(up, down)
    noises = (
        noise,
        lax.ppermute(noise, "plane", plane_up),
        lax.ppermute(noise, "plane", plane_down),
    )
    hots, tables = prepare_traces(
        stripe_row, decay_slow, decay_fast, step_row, frames, slots, capacity
    )
    weights = make_weights(foot_rows, near_rows, noises)
    background, gradient = make_annulus(
        residual, near_residual, mid, far, weights, annulus_gain
    )
    home = lax.all_to_all(gradient, "pix", split_axis=0, concat_axis=0, tiled=True)
    traces_new = make_traces(hots, tables, traces[0], home)
    return (background, traces_new[None])


def solution(mesh):
    placed = (
        P("plane", "pix", None, None),
        P("plane", "pix", None),
        P("plane", "pix", None),
        P("plane", "pix", None),
        P("plane", "pix"),
        P("plane", None),
        P("plane", "pix"),
        P("plane", "pix"),
    )
    return jax.shard_map(
        on_device,
        mesh=mesh,
        in_specs=placed,
        out_specs=(P("plane", "pix", None, None), P("plane", "pix", None)),
        check_vma=False,
    )
```

```python
import functools

import jax
import jax.numpy as jnp
import ml_dtypes
import numpy as np
from jax import lax
from jax.experimental import pallas as pl
from jax.experimental.pallas import tpu as pltpu
from jax.sharding import PartitionSpec as P

FOOT = 32
RAD = 12
GR = 3
LANES = 128
PER = LANES // FOOT
NEAR = PER

lam_floor = 0.1
noise_eps = 1e-05
norm_eps = 1e-05
sigma_twice = 4.5

F32 = jnp.float32
BF16 = jnp.bfloat16
MIB = 1 << 20
HBM = pl.BlockSpec(memory_space=pltpu.HBM)
VMEM = pl.BlockSpec(memory_space=pltpu.VMEM)


def tap_values():
    offsets = np.arange(-GR, GR + 1).astype(np.float32)
    raw = np.exp(-offsets * offsets / np.float32(sigma_twice)).astype(np.float32)
    return (raw / raw.sum(dtype=np.float32)).astype(ml_dtypes.bfloat16).astype(np.float32)


def params(mib=16):
    return pltpu.CompilerParams(vmem_limit_bytes=mib * MIB)


COST = pl.CostEstimate(flops=1, bytes_accessed=1, transcendentals=0)


def dot(a, b):
    return jnp.dot(a, b, preferred_element_type=F32)


def outbox_kernel(capacity, *refs):
    sources, result, places, outbox, sems = refs[0:4], refs[4], refs[5:9], refs[9], refs[10]
    copies = [
        pltpu.make_async_copy(source, place, sems.at[k])
        for k, (source, place) in enumerate(zip(sources, places))
    ]
    for copy in copies:
        copy.start()
    for copy in copies[0:2]:
        copy.wait()
    stripe, column, foot, traces = places
    slots = outbox.shape[0]
    count, tiles = foot.shape
    frames = traces.shape[1]
    before = lax.broadcasted_iota(jnp.int32, (count, count), 0) < lax.broadcasted_iota(
        jnp.int32, (count, count), 1
    )
    named = jnp.broadcast_to(stripe[...].astype(F32), (count, count))
    same = (named == named.T) & before
    rank = jnp.sum(jnp.where(same, 1.0, 0.0), axis=0, keepdims=True).astype(jnp.int32)
    slot = stripe[...] * capacity + rank
    place = lax.broadcasted_iota(jnp.int32, (slots, count), 0)
    left = jnp.broadcast_to(column[...].astype(F32), (LANES, count)).T.astype(BF16)
    lane = lax.broadcasted_iota(jnp.int32, (slots, LANES), 1)
    edge = NEAR * FOOT
    lefts = jnp.zeros((slots, LANES), F32)
    at = 3 * frames
    hots = [
        jnp.where(place + shift == slot, 1.0, 0.0).astype(BF16)
        for shift in (0, capacity, -capacity)
    ]
    for copy in copies[2:]:
        copy.wait()
    leaving = []

    def leave(start, width):
        lanes = pl.ds(start, width)
        copy = pltpu.make_async_copy(
            outbox.at[:, lanes], result.at[:, lanes], sems.at[len(copies) + len(leaving)]
        )
        copy.start()
        leaving.append(copy)

    for k, (hot, first, width) in enumerate(
        zip(hots, (0, 0, tiles - edge), (tiles, edge, edge))
    ):
        outbox[:, at : at + width] = dot(hot, foot[:, first : first + width]).astype(BF16)
        if k == 0:
            leave(at, width)
        outbox[:, k * frames : (k + 1) * frames] = dot(hot, traces[...]).astype(BF16)
        lefts = jnp.where(lane == k, dot(hot, left), lefts)
        at += width
    leave(0, 3 * frames)
    outbox[:, at:] = lefts.astype(BF16)
    leave(3 * frames + tiles, outbox.shape[1] - 3 * frames - tiles)
    for copy in leaving:
        copy.wait()


def make_outbox(stripe, column, foot, traces, capacity, slots):
    count, tiles = foot.shape
    frames = traces.shape[1]
    width = 3 * frames + tiles + 2 * NEAR * FOOT + LANES
    args = (stripe, column, foot, traces)
    return pl.pallas_call(
        functools.partial(outbox_kernel, capacity),
        in_specs=[HBM] * len(args),
        out_specs=HBM,
        out_shape=jax.ShapeDtypeStruct((slots, width), BF16),
        scratch_shapes=[pltpu.VMEM(a.shape, a.dtype) for a in args]
        + [pltpu.VMEM((slots, width), BF16), pltpu.SemaphoreType.DMA((len(args) + 3,))],
        compiler_params=params(56),
        cost_estimate=COST,
        name="outbox",
    )(*args)


def spread(block, col):
    lane = lax.broadcasted_iota(jnp.int32, block.shape, 1)
    for k in range(7):
        block = jnp.where(((col >> k) & 1) == 1, pltpu.roll(block, 1 << k, 1), block)
    inside = ((lane - col) & (LANES - 1)) < FOOT
    left = inside & (lane >= col)
    right = inside & (lane < col)
    rows = []
    for q in range(PER):
        moved = block if q == 0 else pltpu.roll(block, LANES - q * FOOT, 1)
        rows.append(
            jnp.concatenate(
                [jnp.where(left, moved, 0.0), jnp.where(right, moved, 0.0)], axis=1
            ).astype(BF16)
        )
    return rows


def tile_rows(inbox, which, block, frames):
    lefts = inbox[:, inbox.shape[1] - LANES :].astype(F32)
    col = jnp.broadcast_to(lefts[:, which : which + 1], lefts.shape).astype(jnp.int32)
    start = 3 * frames + block * LANES
    if not isinstance(start, int):
        start = pl.multiple_of(start, LANES)
    return spread(inbox[:, pl.ds(start, LANES)].astype(F32), col)


def model_row(row, inbox, which, frames):
    traces = inbox[:, which * frames : (which + 1) * frames]
    return lax.dot_general(row, traces, (((0,), (0,)), ((), ())), preferred_element_type=F32)


def noise_row(left, change):
    frames = left.shape[1]
    steps = dot(left, change)
    steps = steps * steps
    part = steps[:, 0:LANES]
    for k in range(1, frames // LANES):
        part = part + steps[:, k * LANES : (k + 1) * LANES]
    return jnp.sum(part.T, axis=0, keepdims=True) / (frames - 1)


def lag_table(size):
    shape = (size, size)
    return lax.broadcasted_iota(jnp.int32, shape, 1) - lax.broadcasted_iota(jnp.int32, shape, 0)


def change_matrix(frames):
    lag = lag_table(frames)
    steps = jnp.where(lag == -1, 1.0, 0.0) - jnp.where(lag == 0, 1.0, 0.0)
    later = lax.broadcasted_iota(jnp.int32, lag.shape, 1)
    return jnp.where(later < frames - 1, steps, 0.0).astype(BF16)


def residual_kernel(pick, low, high, first, inbox, movie, *refs):
    if not first:
        refs = refs[3:]
    (foot_rows, residual, noise, up, down) = refs[0:5]
    (change, movie_slots, foot_slots, left_slots, sems) = refs[5:]
    frames = movie.shape[3]
    count = pick(None)
    change[...] = change_matrix(frames)

    def fetch(i, slot):
        rows_g = pl.ds(pick(i) * PER, PER)
        return pltpu.make_async_copy(movie.at[0, rows_g], movie_slots.at[slot], sems.at[0, slot])

    def sends(i, slot):
        rows_g = pl.ds(pick(i) * PER, PER)
        return (
            pltpu.make_async_copy(foot_slots.at[slot], foot_rows.at[rows_g], sems.at[1, slot]),
            pltpu.make_async_copy(left_slots.at[slot], residual.at[rows_g], sems.at[2, slot]),
        )

    fetch(0, 0).start()

    def group(i, carry):
        slot = lax.rem(i, 2)
        g = pick(i)

        @pl.when(i + 1 < count)
        def _():
            fetch(i + 1, 1 - slot).start()

        fetch(i, slot).wait()

        @pl.when(i >= 2)
        def _():
            for copy in sends(i - 2, slot):
                copy.wait()

        noises = []
        for q, row in enumerate(tile_rows(inbox, 0, g, frames)):
            foot_slots[slot, q] = row
            left = movie_slots[slot, q].astype(F32) - model_row(row, inbox, 0, frames)
            left = left.astype(BF16)
            left_slots[slot, q] = left
            noises.append(noise_row(left, change[...]))
        noise[i] = jnp.concatenate(noises, axis=0)
        for copy in sends(i, slot):
            copy.start()

        @pl.when(g == low)
        def _():
            down[...] = left_slots[slot]

        @pl.when(g == high)
        def _():
            up[...] = left_slots[slot]

        return carry

    lax.fori_loop(0, count, group, 0)
    for i in (count - 2, count - 1):
        for copy in sends(i, i % 2):
            copy.wait()


def make_residual(inbox, movie, earlier=None):
    slots = inbox.shape[0]
    rows, cols, frames = movie.shape[1:]
    groups = rows // PER
    mids = (1, groups - 2)
    if earlier is None:
        low, high, count = *mids, 2

        def pick(i):
            return count if i is None else mids[0] + i * (mids[1] - mids[0])
    else:
        low, high, count = 2, groups - 3, groups - 2

        def pick(i):
            if i is None:
                return count
            if isinstance(i, int):
                return i + (i >= mids[0]) + (i + 1 >= mids[1])
            return i + jnp.where(i >= mids[0], 1, 0) + jnp.where(i + 1 >= mids[1], 1, 0)

    piece = jax.ShapeDtypeStruct((PER, cols, frames), BF16)
    more = () if earlier is None else earlier
    return pl.pallas_call(
        functools.partial(residual_kernel, pick, low, high, earlier is None),
        in_specs=[VMEM, HBM] + [HBM, HBM, VMEM][: len(more)],
        out_specs=[HBM, HBM, VMEM, VMEM, VMEM],
        out_shape=(
            jax.ShapeDtypeStruct((rows, slots, cols), BF16),
            jax.ShapeDtypeStruct((rows, cols, frames), BF16),
            jax.ShapeDtypeStruct((count, PER, cols), F32),
            piece,
            piece,
        ),
        scratch_shapes=[
            pltpu.VMEM((frames, frames), BF16),
            pltpu.VMEM((2, PER, cols, frames), BF16),
            pltpu.VMEM((2, PER, slots, cols), BF16),
            pltpu.VMEM((2, PER, cols, frames), BF16),
            pltpu.SemaphoreType.DMA((3, 2)),
        ],
        input_output_aliases={} if earlier is None else {2: 0, 3: 1},
        compiler_params=params(44),
        cost_estimate=COST,
        name="residual",
    )(inbox, movie, *more)


def near_kernel(
    inbox, even, pair, diag_next, diag_prev, mid_noise, other_noise, foot_rows, residual, noise
):
    frames = pair.shape[3]
    first_of_pair = even[0] == 1
    groups = mid_noise.shape[0] + other_noise.shape[0]
    own = FOOT // PER
    change = change_matrix(frames)
    others = [g for g in range(groups) if g not in (1, groups - 2)]
    for order, part in (((1, groups - 2), mid_noise), (others, other_noise)):
        for i, g in enumerate(order):
            noise[NEAR + g * PER : NEAR + (g + 1) * PER, :] = part[i]
    for side, (block, direct, diagonal, first) in enumerate(
        (
            (own, first_of_pair, diag_next, 0),
            (own + NEAR // PER, ~first_of_pair, diag_prev, NEAR + groups * PER),
        )
    ):
        for q, row in enumerate(tile_rows(inbox, 1 + side, block, frames)):
            y = side * NEAR + q
            foot_rows[y] = row
            movie = jnp.where(direct, pair[1 - side, q].astype(F32), diagonal[q].astype(F32))
            left = (movie - model_row(row, inbox, 1 + side, frames)).astype(BF16)
            residual[y] = left
            noise[first + q : first + q + 1, :] = noise_row(left, change)


def make_near(inbox, even, pair, diag_next, diag_prev, noises):
    slots = inbox.shape[0]
    cols, frames = diag_next.shape[1:]
    return pl.pallas_call(
        near_kernel,
        in_specs=[VMEM, pl.BlockSpec(memory_space=pltpu.SMEM)] + [VMEM] * (3 + len(noises)),
        out_shape=(
            jax.ShapeDtypeStruct((2 * NEAR, slots, cols), BF16),
            jax.ShapeDtypeStruct((2 * NEAR, cols, frames), BF16),
            jax.ShapeDtypeStruct((2 * NEAR + PER * sum(n.shape[0] for n in noises), cols), F32),
        ),
        compiler_params=params(),
        cost_estimate=COST,
        name="near",
    )(inbox, even, pair, diag_next, diag_prev, *noises)


def weights_kernel(
    taps, own, near, noise, noise_before, noise_after, out, out_next, out_prev,
    own_slots, scale, band, sems,
):
    rows, slots, cols = own.shape
    part = own_slots.shape[2]
    count = slots // part

    def fetch(i, slot):
        these = pl.ds(pl.multiple_of(i * part, part), part)
        return pltpu.make_async_copy(own.at[:, these, :], own_slots.at[slot], sems.at[slot])

    fetch(0, 0).start()
    pooled = (noise_before[...] + 2.0 * noise[...] + noise_after[...]) / 4.0
    scale[...] = 1.0 / jnp.sqrt(pooled + noise_eps)
    lag = jnp.abs(lag_table(cols))
    table = jnp.zeros(lag.shape, F32)
    for k in range(GR + 1):
        table = jnp.where(lag == k, taps[GR + k], table)
    band[...] = table.astype(BF16)

    def across(foot, inv):
        scaled = (foot.astype(F32) * inv[:, None, :]).astype(BF16)
        count = foot.shape[0]
        return dot(scaled.reshape(count * part, cols), band[...]).reshape(count, part, cols)

    def some(i, carry):
        slot = lax.rem(i, 2)

        @pl.when(i + 1 < count)
        def _():
            fetch(i + 1, 1 - slot).start()

        fetch(i, slot).wait()
        these = pl.ds(pl.multiple_of(i * part, part), part)
        blurred = across(own_slots[slot], scale[NEAR : NEAR + rows])
        for r in range(rows):
            total = taps[GR] * blurred[r]
            for k in range(1, GR + 1):
                if r - k >= 0 and r + k < rows:
                    total = total + taps[GR + k] * (blurred[r - k] + blurred[r + k])
                elif r - k >= 0:
                    total = total + taps[GR + k] * blurred[r - k]
                elif r + k < rows:
                    total = total + taps[GR + k] * blurred[r + k]
            out[r, these, :] = total.astype(BF16)
        after = across(near[0:GR, these, :], scale[0:GR])
        ahead = across(near[2 * NEAR - GR : 2 * NEAR, these, :], scale[rows + 2 * NEAR - GR :])
        for a in range(GR):
            total = taps[2 * GR - a] * after[0]
            for r in range(1, a + 1):
                total = total + taps[2 * GR + r - a] * after[r]
            out_next[a, these, :] = total.astype(BF16)
            total = taps[2 * GR] * ahead[a]
            for b in range(a + 1, GR):
                total = total + taps[2 * GR + a - b] * ahead[b]
            out_prev[a, these, :] = total.astype(BF16)
        return carry

    lax.fori_loop(0, count, some, 0)


def make_weights(foot_rows, near_rows, noises):
    rows, slots, cols = foot_rows.shape
    part = 32
    return pl.pallas_call(
        functools.partial(weights_kernel, [float(t) for t in tap_values()]),
        in_specs=[HBM] + [VMEM] * (1 + len(noises)),
        out_shape=(
            jax.ShapeDtypeStruct((rows, slots, cols), BF16),
            jax.ShapeDtypeStruct((GR, slots, cols), BF16),
            jax.ShapeDtypeStruct((GR, slots, cols), BF16),
        ),
        scratch_shapes=[
            pltpu.VMEM((2, rows, part, cols), BF16),
            pltpu.VMEM(noises[0].shape, F32),
            pltpu.VMEM((cols, cols), BF16),
            pltpu.SemaphoreType.DMA((2,)),
        ],
        compiler_params=params(32),
        cost_estimate=COST,
        name="weights",
    )(foot_rows, near_rows, *noises)


def side_sum(column):
    cols = column.shape[0]
    top = lax.broadcasted_iota(jnp.int32, (cols // 8, 8, LANES), 1) < 4
    blank = jnp.zeros((2, 8, LANES), F32)
    turned = pltpu.roll(column.reshape(cols // 8, 8, LANES), 4, 1)
    turned = jnp.concatenate([blank, turned, blank], axis=0)
    both = turned[0 : cols // 8 + 1] + turned[3 : cols // 8 + 4]
    sides = jnp.where(top, both[0 : cols // 8], both[1 : cols // 8 + 1])
    return sides.reshape(cols, LANES)


def annulus_group(g, own, leaving, entering, gain, band, column, outgoing):
    frames = own.shape[2]
    outs = [leaving(q) for q in range(PER)]
    news = [entering(q) for q in range(PER)]
    levels = [dot(band, jnp.concatenate([o, n], axis=0)) for o, n in zip(outs, news)]
    column = list(column)
    dets = []
    for q in range(PER):
        det = []
        for h in range(frames // LANES):
            part = slice(h * LANES, (h + 1) * LANES)
            inner = column[h] - outs[q][:, part].astype(F32)
            column[h] = inner + news[q][:, part].astype(F32)
            fit = (levels[q][:, part] + side_sum(inner)) * gain
            outgoing[g, q, :, part] = fit.astype(BF16)
            det.append((own[g * PER + q, :, part].astype(F32) - fit).astype(BF16))
        dets.append(jnp.concatenate(det, axis=1))
    return column, dets


def grow(total, weight, g, dets):
    weights = jnp.concatenate([weight[g * PER + q] for q in range(PER)], axis=1)
    return total + dot(weights, jnp.concatenate(dets, axis=0))


def halves(ref):
    return [ref[:, h * LANES : (h + 1) * LANES] for h in range(ref.shape[1] // LANES)]


def add_rows(column, rows, sign=1.0):
    for row in rows:
        column = [c + sign * r.astype(F32) for c, r in zip(column, halves(row))]
    return column


def put(ref, column):
    for h, value in enumerate(column):
        ref[:, h * LANES : (h + 1) * LANES] = value


def sender(outgoing, background, sems):
    def send(g):
        return pltpu.make_async_copy(
            outgoing.at[g], background.at[0, pl.ds(g * PER, PER)], sems.at[g]
        )

    return send


def tables(gain):
    cols = gain.shape[1]
    band = jnp.where(jnp.abs(lag_table(cols)) <= RAD, 1.0, 0.0).astype(BF16)
    return (
        jnp.broadcast_to(gain[...], (LANES, cols)).T / (8.0 * RAD),
        jnp.concatenate([band, band], axis=1),
    )


def middle_kernel(own, near, weight, gain, background, upper, lower, total, outgoing, sems):
    rows, cols, frames = own.shape
    groups = range((RAD - NEAR) // PER, (rows - RAD + NEAR) // PER)
    send = sender(outgoing, background, sems)
    gains, band = tables(gain)
    column = [jnp.zeros((cols, LANES), F32)] * (frames // LANES)
    column = add_rows(column, [near[NEAR + r] for r in range(NEAR)])
    column = add_rows(column, [own[r] for r in range(RAD)])
    put(upper, column)
    column = add_rows(column, [own[RAD + r] for r in range(2 * RAD - NEAR - RAD)])
    grown = jnp.zeros(total.shape, F32)
    for g in groups:
        y = g * PER
        column, dets = annulus_group(
            g,
            own,
            (lambda q: near[NEAR + y - RAD + NEAR + q])
            if y < RAD
            else (lambda q: own[y - RAD + q]),
            (lambda q: near[y + RAD - rows + q])
            if y + RAD >= rows
            else (lambda q: own[y + RAD + q]),
            gains, band, column, outgoing,
        )
        send(g).start()
        grown = grow(grown, weight, g, dets)
    put(lower, column)
    total[...] = grown
    for g in groups:
        send(g).wait()


def mid_kernel(
    own, above, below, weight, gain, before, upper, lower, total,
    background, new_total, base, gain_table, band_table, outgoing, sems,
):
    del before
    rows = own.shape[0]
    low, high = RAD // PER - 2, (rows - RAD) // PER + 1
    y, z = low * PER, high * PER
    send = sender(outgoing, background, sems)
    gains, band = tables(gain)
    first = add_rows(halves(upper), [above[r] for r in range(PER)])
    column = add_rows(first, [own[RAD + r] for r in range(PER)])
    _, low_dets = annulus_group(
        low, own, lambda q: above[q], lambda q: own[y + RAD + q], gains, band, column, outgoing
    )
    send(low).start()
    column, high_dets = annulus_group(
        high, own, lambda q: own[z - RAD + q], lambda q: below[q], gains, band, halves(lower),
        outgoing,
    )
    send(high).start()
    new_total[...] = grow(grow(total[...], weight, low, low_dets), weight, high, high_dets)
    gain_table[...] = gains
    band_table[...] = band[:, : own.shape[1]]
    for q in range(PER):
        if q > 0:
            first = add_rows(first, [own[RAD + q - 1]])
        inner = own[z + PER - RAD + q]
        column = add_rows(column, [inner], -1.0)
        for k, (sums, row) in enumerate(((first, own[RAD + q]), (column, inner))):
            level = dot(band_table[...], row)
            for h, value in enumerate(sums):
                part = slice(h * LANES, (h + 1) * LANES)
                base[k, q, :, part] = level[:, part] + side_sum(value)
    send(low).wait()
    send(high).wait()


def end_kernel(
    own, above, below, weight, weight_next, weight_prev, total, base, gain, band, gradient, late
):
    rows, cols, frames = own.shape
    low, high = 0, rows // PER - 1
    blank = [jnp.zeros((cols, LANES), F32)] * (frames // LANES)
    dets = []
    for k, (g, far, order) in enumerate(
        ((low, above, range(PER - 1, -1, -1)), (high, below, range(PER)))
    ):
        column, mine = blank, [None] * PER
        for i, q in enumerate(order):
            row = far[q]
            level = dot(band[...], row)
            det = []
            for h in range(frames // LANES):
                part = slice(h * LANES, (h + 1) * LANES)
                fit = base[k, q, :, part] + level[:, part]
                if i > 0:
                    fit = fit + side_sum(column[h])
                fit = fit * gain[...]
                late[k, q, :, part] = fit.astype(BF16)
                det.append((own[g * PER + q, :, part].astype(F32) - fit).astype(BF16))
            mine[q] = jnp.concatenate(det, axis=1)
            column = add_rows(column, [row])
        dets.append(mine)
    low_dets, high_dets = dets
    grown = grow(grow(total[...], weight, low, low_dets), weight, high, high_dets)
    edges = ((2, weight_next, high_dets[PER - GR :]), (3, weight_prev, low_dets[:GR]))
    for at, edge, parts in edges:
        value = dot(
            jnp.concatenate([edge[a] for a in range(GR)], axis=1), jnp.concatenate(parts, axis=0)
        )
        gradient[:, at * frames : (at + 1) * frames] = value.astype(BF16)
    coarse = grown.astype(BF16)
    gradient[:, 0:frames] = coarse
    gradient[:, frames : 2 * frames] = (grown - coarse.astype(F32)).astype(BF16)


def late_kernel(late, before, background, sems):
    del before
    rows = background.shape[1]
    copies = [
        pltpu.make_async_copy(late.at[k], background.at[0, pl.ds(first, PER)], sems.at[k])
        for k, first in enumerate((0, rows - PER))
    ]
    for copy in copies:
        copy.start()
    for copy in copies:
        copy.wait()


def make_annulus(own, near, mid, far, weights, gain):
    rows, cols, frames = own.shape
    weight, weight_next, weight_prev = weights
    slots = weight.shape[1]
    background = jax.ShapeDtypeStruct((1, rows, cols, frames), BF16)
    column = jax.ShapeDtypeStruct((cols, frames), F32)
    total = jax.ShapeDtypeStruct((slots, frames), F32)
    gradient = jax.ShapeDtypeStruct((slots, 4 * frames), BF16)

    def call(kernel, name, args, outs, done, declared=COST):
        specs = [VMEM] * len(args)
        if done is not None:
            specs[done] = HBM
        return pl.pallas_call(
            kernel,
            in_specs=specs,
            out_specs=[HBM] + [VMEM] * (len(outs) - 1),
            out_shape=outs,
            scratch_shapes=[
                pltpu.VMEM((rows // PER, PER, cols, frames), BF16),
                pltpu.SemaphoreType.DMA((rows // PER,)),
            ],
            input_output_aliases={} if done is None else {done: 0},
            compiler_params=params(),
            cost_estimate=declared,
            name=name,
        )(*args)

    done, upper, lower, grown = call(
        middle_kernel, "annulus_middle", (own, near, weight, gain),
        (background, column, column, total), None,
    )
    prepared = (
        jax.ShapeDtypeStruct((2, PER, cols, frames), F32),
        jax.ShapeDtypeStruct((cols, LANES), F32),
        jax.ShapeDtypeStruct((cols, cols), BF16),
    )
    done, grown, *prepared = call(
        mid_kernel, "annulus_mid",
        (own, *mid, weight, gain, done, upper, lower, grown),
        (background, total, *prepared), 5,
        pl.CostEstimate(
            flops=2 * rows * cols * cols * frames, bytes_accessed=5 * MIB, transcendentals=0
        ),
    )
    args = (own, *far, weight, weight_next, weight_prev, grown, *prepared)
    gradient, late = pl.pallas_call(
        end_kernel,
        in_specs=[VMEM] * len(args),
        out_shape=(gradient, jax.ShapeDtypeStruct((2, PER, cols, frames), BF16)),
        compiler_params=params(),
        cost_estimate=COST,
        name="annulus_end",
    )(*args)
    background = pl.pallas_call(
        late_kernel,
        in_specs=[VMEM, HBM],
        out_specs=HBM,
        out_shape=background,
        scratch_shapes=[pltpu.SemaphoreType.DMA((2,))],
        input_output_aliases={1: 0},
        compiler_params=params(),
        cost_estimate=COST,
        name="late_rows",
    )(late, done)
    return background, gradient


def prepare_kernel(capacity, stripe, slow, fast, step, hots, tables):
    count = stripe.shape[1]
    frames = tables.shape[2]
    slots = hots.shape[1] // 4

    def upended(row):
        return jnp.broadcast_to(row[...].astype(F32), (LANES, count)).T

    before = lax.broadcasted_iota(jnp.int32, (count, count), 1) < lax.broadcasted_iota(
        jnp.int32, (count, count), 0
    )
    named = upended(stripe)
    same = (named == stripe[...].astype(F32)) & before
    rank = jnp.sum(jnp.where(same, 1.0, 0.0), axis=1, keepdims=True)
    slot = (named[:, 0:1] * capacity + rank).astype(jnp.int32)
    place = lax.broadcasted_iota(jnp.int32, (count, slots), 1)
    for k, shift in enumerate((0, 0, capacity, -capacity)):
        hots[:, k * slots : (k + 1) * slots] = jnp.where(place + shift == slot, 1.0, 0.0).astype(
            BF16
        )
    a, b = upended(slow), upended(fast)
    for k, part in enumerate((upended(step), a, b, (1.0 - a) * (1.0 - b) / (a - b))):
        tables[k] = jnp.concatenate([part] * (frames // LANES), axis=1)


def prepare_traces(stripe, slow, fast, step, frames, slots, capacity):
    count = stripe.shape[1]
    return pl.pallas_call(
        functools.partial(prepare_kernel, capacity),
        out_shape=(
            jax.ShapeDtypeStruct((count, 4 * slots), BF16),
            jax.ShapeDtypeStruct((4, count, frames), F32),
        ),
        compiler_params=params(),
        cost_estimate=COST,
        name="prepare",
    )(stripe, slow, fast, step)


def traces_kernel(hots, tables, traces, inbox, out):
    count, frames = traces.shape
    parts = [inbox[:, k * frames : (k + 1) * frames] for k in range(4)]
    gradient = dot(hots[...], jnp.concatenate(parts, axis=0))
    updated = traces[...].astype(F32) + tables[0] * gradient
    lane = lax.broadcasted_iota(jnp.int32, (count, frames), 1)

    def lagged(value, lag):
        return jnp.where(lane >= lag, pltpu.roll(value, lag, 1), 0.0)

    a, b = tables[1], tables[2]
    driven = updated - (a + b) * lagged(updated, 1) + (a * b) * lagged(updated, 2)
    spikes = jnp.maximum(driven - lam_floor, 0.0)
    sums = [spikes, spikes]
    roots = [a, b]
    lag = 1
    while lag < frames:
        sums = [value + root * lagged(value, lag) for value, root in zip(sums, roots)]
        roots = [root * root for root in roots]
        lag *= 2
    out[...] = tables[3] * (a * sums[0] - b * sums[1])


def make_traces(hots, tables, traces, inbox):
    count, frames = traces.shape
    return pl.pallas_call(
        traces_kernel,
        out_shape=jax.ShapeDtypeStruct((count, frames), F32),
        compiler_params=params(),
        cost_estimate=COST,
        name="traces",
    )(hots, tables, traces, inbox)


def neighbours(axis):
    devices = lax.axis_size(axis)
    up = [(i, i + 1) for i in range(devices - 1)]
    return up, [(j, i) for i, j in up]


def on_device(movie, footprints, traces, stripe, column, annulus_gain, decay_slow, decay_fast):
    pix_count = lax.axis_size("pix")
    rows, cols, frames = movie.shape[1:]
    count = footprints.shape[1]
    capacity = max(2, 2 * count // pix_count)
    slots = pix_count * capacity
    pix_up, pix_down = neighbours("pix")
    plane_up, plane_down = neighbours("plane")

    is_even = lax.axis_index("pix") % 2 == 0
    pair = lax.all_gather(
        jnp.where(is_even, movie[0, rows - NEAR :], movie[0, :NEAR]),
        "pix",
        axis_index_groups=[[i, i + 1] for i in range(0, pix_count, 2)],
    )
    even = is_even.astype(jnp.int32).reshape(1)
    stripe_row = stripe.reshape(1, count)
    outbox = make_outbox(stripe_row, column, footprints[0], traces[0], capacity, slots)
    def exchange(up, down):
        return (lax.ppermute(up, "pix", pix_up), lax.ppermute(down, "pix", pix_down))

    frames_in, outbox = lax.optimization_barrier((movie, outbox))
    inbox = lax.all_to_all(outbox, "pix", split_axis=0, concat_axis=0, tiled=True)
    diag_prev = lax.ppermute(frames_in[0, rows - NEAR :], "pix", pix_up[1::2])
    diag_next = lax.ppermute(frames_in[0, :NEAR], "pix", pix_down[1::2])
    *started, mid_noise, up, down = make_residual(inbox, movie)
    mid = exchange(up, down)
    foot_rows, residual, other_noise, up, down = make_residual(
        inbox, movie, (*started, mid_noise)
    )
    near_rows, near_residual, noise = make_near(
        inbox, even, pair, diag_next, diag_prev, (mid_noise, other_noise)
    )
    foot_f = footprints[0].astype(F32)
    step = 1.0 / (jnp.sum(foot_f * foot_f, axis=1) + norm_eps)
    step_row, up, down, noise = lax.optimization_barrier((step[None], up, down, noise))
    far = exchange(up, down)
    noises = (
        noise,
        lax.ppermute(noise, "plane", plane_up),
        lax.ppermute(noise, "plane", plane_down),
    )
    hots, tables = prepare_traces(
        stripe_row, decay_slow, decay_fast, step_row, frames, slots, capacity
    )
    weights = make_weights(foot_rows, near_rows, noises)
    background, gradient = make_annulus(
        residual, near_residual, mid, far, weights, annulus_gain
    )
    home = lax.all_to_all(gradient, "pix", split_axis=0, concat_axis=0, tiled=True)
    traces_new = make_traces(hots, tables, traces[0], home)
    return (background, traces_new[None])


def solution(mesh):
    placed = (
        P("plane", "pix", None, None),
        P("plane", "pix", None),
        P("plane", "pix", None),
        P("plane", "pix", None),
        P("plane", "pix"),
        P("plane", None),
        P("plane", "pix"),
        P("plane", "pix"),
    )
    return jax.shard_map(
        on_device,
        mesh=mesh,
        in_specs=placed,
        out_specs=(P("plane", "pix", None, None), P("plane", "pix", None)),
        check_vma=False,
    )
```

```python
import functools

import jax
import jax.numpy as jnp
import ml_dtypes
import numpy as np
from jax import lax
from jax.experimental import pallas as pl
from jax.experimental.pallas import tpu as pltpu
from jax.sharding import PartitionSpec as P

FOOT = 32
RAD = 12
GR = 3
LANES = 128
PER = LANES // FOOT
NEAR = PER

lam_floor = 0.1
noise_eps = 1e-05
norm_eps = 1e-05
sigma_twice = 4.5

F32 = jnp.float32
BF16 = jnp.bfloat16
MIB = 1 << 20
HBM = pl.BlockSpec(memory_space=pltpu.HBM)
VMEM = pl.BlockSpec(memory_space=pltpu.VMEM)


def tap_values():
    offsets = np.arange(-GR, GR + 1).astype(np.float32)
    raw = np.exp(-offsets * offsets / np.float32(sigma_twice)).astype(np.float32)
    return (raw / raw.sum(dtype=np.float32)).astype(ml_dtypes.bfloat16).astype(np.float32)


def params(mib=16):
    return pltpu.CompilerParams(vmem_limit_bytes=mib * MIB)


COST = pl.CostEstimate(flops=1, bytes_accessed=1, transcendentals=0)


def dot(a, b):
    return jnp.dot(a, b, preferred_element_type=F32)


def outbox_kernel(capacity, *refs):
    sources, result, places, outbox, sems = refs[0:4], refs[4], refs[5:9], refs[9], refs[10]
    copies = [
        pltpu.make_async_copy(source, place, sems.at[k])
        for k, (source, place) in enumerate(zip(sources, places))
    ]
    for copy in copies:
        copy.start()
    for copy in copies[0:2]:
        copy.wait()
    stripe, column, foot, traces = places
    slots = outbox.shape[0]
    count, tiles = foot.shape
    frames = traces.shape[1]
    before = lax.broadcasted_iota(jnp.int32, (count, count), 0) < lax.broadcasted_iota(
        jnp.int32, (count, count), 1
    )
    named = jnp.broadcast_to(stripe[...].astype(F32), (count, count))
    same = (named == named.T) & before
    rank = jnp.sum(jnp.where(same, 1.0, 0.0), axis=0, keepdims=True).astype(jnp.int32)
    slot = stripe[...] * capacity + rank
    place = lax.broadcasted_iota(jnp.int32, (slots, count), 0)
    left = jnp.broadcast_to(column[...].astype(F32), (LANES, count)).T.astype(BF16)
    lane = lax.broadcasted_iota(jnp.int32, (slots, LANES), 1)
    edge = NEAR * FOOT
    lefts = jnp.zeros((slots, LANES), F32)
    at = 3 * frames
    hots = [
        jnp.where(place + shift == slot, 1.0, 0.0).astype(BF16)
        for shift in (0, capacity, -capacity)
    ]
    for copy in copies[2:]:
        copy.wait()
    leaving = []

    def leave(start, width):
        lanes = pl.ds(start, width)
        copy = pltpu.make_async_copy(
            outbox.at[:, lanes], result.at[:, lanes], sems.at[len(copies) + len(leaving)]
        )
        copy.start()
        leaving.append(copy)

    for k, (hot, first, width) in enumerate(
        zip(hots, (0, 0, tiles - edge), (tiles, edge, edge))
    ):
        outbox[:, at : at + width] = dot(hot, foot[:, first : first + width]).astype(BF16)
        if k == 0:
            leave(at, width)
        outbox[:, k * frames : (k + 1) * frames] = dot(hot, traces[...]).astype(BF16)
        lefts = jnp.where(lane == k, dot(hot, left), lefts)
        at += width
    leave(0, 3 * frames)
    outbox[:, at:] = lefts.astype(BF16)
    leave(3 * frames + tiles, outbox.shape[1] - 3 * frames - tiles)
    for copy in leaving:
        copy.wait()


def make_outbox(stripe, column, foot, traces, capacity, slots):
    count, tiles = foot.shape
    frames = traces.shape[1]
    width = 3 * frames + tiles + 2 * NEAR * FOOT + LANES
    args = (stripe, column, foot, traces)
    return pl.pallas_call(
        functools.partial(outbox_kernel, capacity),
        in_specs=[HBM] * len(args),
        out_specs=HBM,
        out_shape=jax.ShapeDtypeStruct((slots, width), BF16),
        scratch_shapes=[pltpu.VMEM(a.shape, a.dtype) for a in args]
        + [pltpu.VMEM((slots, width), BF16), pltpu.SemaphoreType.DMA((len(args) + 3,))],
        compiler_params=params(56),
        cost_estimate=COST,
        name="outbox",
    )(*args)


def spread(block, col):
    lane = lax.broadcasted_iota(jnp.int32, block.shape, 1)
    for k in range(7):
        block = jnp.where(((col >> k) & 1) == 1, pltpu.roll(block, 1 << k, 1), block)
    inside = ((lane - col) & (LANES - 1)) < FOOT
    left = inside & (lane >= col)
    right = inside & (lane < col)
    rows = []
    for q in range(PER):
        moved = block if q == 0 else pltpu.roll(block, LANES - q * FOOT, 1)
        rows.append(
            jnp.concatenate(
                [jnp.where(left, moved, 0.0), jnp.where(right, moved, 0.0)], axis=1
            ).astype(BF16)
        )
    return rows


def tile_rows(inbox, which, block, frames):
    lefts = inbox[:, inbox.shape[1] - LANES :].astype(F32)
    col = jnp.broadcast_to(lefts[:, which : which + 1], lefts.shape).astype(jnp.int32)
    start = 3 * frames + block * LANES
    if not isinstance(start, int):
        start = pl.multiple_of(start, LANES)
    return spread(inbox[:, pl.ds(start, LANES)].astype(F32), col)


def model_row(row, inbox, which, frames):
    traces = inbox[:, which * frames : (which + 1) * frames]
    return lax.dot_general(row, traces, (((0,), (0,)), ((), ())), preferred_element_type=F32)


def noise_row(left, change):
    frames = left.shape[1]
    steps = dot(left, change)
    steps = steps * steps
    part = steps[:, 0:LANES]
    for k in range(1, frames // LANES):
        part = part + steps[:, k * LANES : (k + 1) * LANES]
    return jnp.sum(part.T, axis=0, keepdims=True) / (frames - 1)


def lag_table(size):
    shape = (size, size)
    return lax.broadcasted_iota(jnp.int32, shape, 1) - lax.broadcasted_iota(jnp.int32, shape, 0)


def change_matrix(frames):
    lag = lag_table(frames)
    steps = jnp.where(lag == -1, 1.0, 0.0) - jnp.where(lag == 0, 1.0, 0.0)
    later = lax.broadcasted_iota(jnp.int32, lag.shape, 1)
    return jnp.where(later < frames - 1, steps, 0.0).astype(BF16)


def residual_kernel(pick, low, high, first, inbox, movie, *refs):
    if not first:
        refs = refs[3:]
    (foot_rows, residual, noise, up, down) = refs[0:5]
    (change, movie_slots, foot_slots, left_slots, sems) = refs[5:]
    frames = movie.shape[3]
    count = pick(None)
    change[...] = change_matrix(frames)

    def fetch(i, slot):
        rows_g = pl.ds(pick(i) * PER, PER)
        return pltpu.make_async_copy(movie.at[0, rows_g], movie_slots.at[slot], sems.at[0, slot])

    def sends(i, slot):
        rows_g = pl.ds(pick(i) * PER, PER)
        return (
            pltpu.make_async_copy(foot_slots.at[slot], foot_rows.at[rows_g], sems.at[1, slot]),
            pltpu.make_async_copy(left_slots.at[slot], residual.at[rows_g], sems.at[2, slot]),
        )

    fetch(0, 0).start()

    def group(i, carry):
        slot = lax.rem(i, 2)
        g = pick(i)

        @pl.when(i + 1 < count)
        def _():
            fetch(i + 1, 1 - slot).start()

        fetch(i, slot).wait()

        @pl.when(i >= 2)
        def _():
            for copy in sends(i - 2, slot):
                copy.wait()

        noises = []
        for q, row in enumerate(tile_rows(inbox, 0, g, frames)):
            foot_slots[slot, q] = row
            left = movie_slots[slot, q].astype(F32) - model_row(row, inbox, 0, frames)
            left = left.astype(BF16)
            left_slots[slot, q] = left
            noises.append(noise_row(left, change[...]))
        noise[i] = jnp.concatenate(noises, axis=0)
        for copy in sends(i, slot):
            copy.start()

        @pl.when(g == low)
        def _():
            down[...] = left_slots[slot]

        @pl.when(g == high)
        def _():
            up[...] = left_slots[slot]

        return carry

    lax.fori_loop(0, count, group, 0)
    for i in (count - 2, count - 1):
        for copy in sends(i, i % 2):
            copy.wait()


def make_residual(inbox, movie, earlier=None):
    slots = inbox.shape[0]
    rows, cols, frames = movie.shape[1:]
    groups = rows // PER
    mids = (1, groups - 2)
    if earlier is None:
        low, high, count = *mids, 2

        def pick(i):
            return count if i is None else mids[0] + i * (mids[1] - mids[0])
    else:
        low, high, count = 2, groups - 3, groups - 2

        def pick(i):
            if i is None:
                return count
            if isinstance(i, int):
                return i + (i >= mids[0]) + (i + 1 >= mids[1])
            return i + jnp.where(i >= mids[0], 1, 0) + jnp.where(i + 1 >= mids[1], 1, 0)

    piece = jax.ShapeDtypeStruct((PER, cols, frames), BF16)
    more = () if earlier is None else earlier
    return pl.pallas_call(
        functools.partial(residual_kernel, pick, low, high, earlier is None),
        in_specs=[VMEM, HBM] + [HBM, HBM, VMEM][: len(more)],
        out_specs=[HBM, HBM, VMEM, VMEM, VMEM],
        out_shape=(
            jax.ShapeDtypeStruct((rows, slots, cols), BF16),
            jax.ShapeDtypeStruct((rows, cols, frames), BF16),
            jax.ShapeDtypeStruct((count, PER, cols), F32),
            piece,
            piece,
        ),
        scratch_shapes=[
            pltpu.VMEM((frames, frames), BF16),
            pltpu.VMEM((2, PER, cols, frames), BF16),
            pltpu.VMEM((2, PER, slots, cols), BF16),
            pltpu.VMEM((2, PER, cols, frames), BF16),
            pltpu.SemaphoreType.DMA((3, 2)),
        ],
        input_output_aliases={} if earlier is None else {2: 0, 3: 1},
        compiler_params=params(44),
        cost_estimate=COST,
        name="residual",
    )(inbox, movie, *more)


def near_kernel(
    inbox, movie_next, movie_prev, mid_noise, other_noise, foot_rows, residual, noise
):
    frames = movie_next.shape[2]
    groups = mid_noise.shape[0] + other_noise.shape[0]
    own = FOOT // PER
    change = change_matrix(frames)
    others = [g for g in range(groups) if g not in (1, groups - 2)]
    for order, part in (((1, groups - 2), mid_noise), (others, other_noise)):
        for i, g in enumerate(order):
            noise[NEAR + g * PER : NEAR + (g + 1) * PER, :] = part[i]
    for side, (block, movie, first) in enumerate(
        ((own, movie_next, 0), (own + NEAR // PER, movie_prev, NEAR + groups * PER))
    ):
        for q, row in enumerate(tile_rows(inbox, 1 + side, block, frames)):
            y = side * NEAR + q
            foot_rows[y] = row
            left = movie[q].astype(F32) - model_row(row, inbox, 1 + side, frames)
            left = left.astype(BF16)
            residual[y] = left
            noise[first + q : first + q + 1, :] = noise_row(left, change)


def make_near(inbox, movie_next, movie_prev, noises):
    slots = inbox.shape[0]
    cols, frames = movie_next.shape[1:]
    return pl.pallas_call(
        near_kernel,
        out_shape=(
            jax.ShapeDtypeStruct((2 * NEAR, slots, cols), BF16),
            jax.ShapeDtypeStruct((2 * NEAR, cols, frames), BF16),
            jax.ShapeDtypeStruct((2 * NEAR + PER * sum(n.shape[0] for n in noises), cols), F32),
        ),
        compiler_params=params(),
        cost_estimate=COST,
        name="near",
    )(inbox, movie_next, movie_prev, *noises)


def weights_kernel(
    taps, own, near, noise, noise_before, noise_after, out, out_next, out_prev,
    own_slots, scale, band, sems,
):
    rows, slots, cols = own.shape
    part = own_slots.shape[2]
    count = slots // part

    def fetch(i, slot):
        these = pl.ds(pl.multiple_of(i * part, part), part)
        return pltpu.make_async_copy(own.at[:, these, :], own_slots.at[slot], sems.at[slot])

    fetch(0, 0).start()
    pooled = (noise_before[...] + 2.0 * noise[...] + noise_after[...]) / 4.0
    scale[...] = 1.0 / jnp.sqrt(pooled + noise_eps)
    lag = jnp.abs(lag_table(cols))
    table = jnp.zeros(lag.shape, F32)
    for k in range(GR + 1):
        table = jnp.where(lag == k, taps[GR + k], table)
    band[...] = table.astype(BF16)

    def across(foot, inv):
        scaled = (foot.astype(F32) * inv[:, None, :]).astype(BF16)
        count = foot.shape[0]
        return dot(scaled.reshape(count * part, cols), band[...]).reshape(count, part, cols)

    def some(i, carry):
        slot = lax.rem(i, 2)

        @pl.when(i + 1 < count)
        def _():
            fetch(i + 1, 1 - slot).start()

        fetch(i, slot).wait()
        these = pl.ds(pl.multiple_of(i * part, part), part)
        blurred = across(own_slots[slot], scale[NEAR : NEAR + rows])
        for r in range(rows):
            total = taps[GR] * blurred[r]
            for k in range(1, GR + 1):
                if r - k >= 0 and r + k < rows:
                    total = total + taps[GR + k] * (blurred[r - k] + blurred[r + k])
                elif r - k >= 0:
                    total = total + taps[GR + k] * blurred[r - k]
                elif r + k < rows:
                    total = total + taps[GR + k] * blurred[r + k]
            out[r, these, :] = total.astype(BF16)
        after = across(near[0:GR, these, :], scale[0:GR])
        ahead = across(near[2 * NEAR - GR : 2 * NEAR, these, :], scale[rows + 2 * NEAR - GR :])
        for a in range(GR):
            total = taps[2 * GR - a] * after[0]
            for r in range(1, a + 1):
                total = total + taps[2 * GR + r - a] * after[r]
            out_next[a, these, :] = total.astype(BF16)
            total = taps[2 * GR] * ahead[a]
            for b in range(a + 1, GR):
                total = total + taps[2 * GR + a - b] * ahead[b]
            out_prev[a, these, :] = total.astype(BF16)
        return carry

    lax.fori_loop(0, count, some, 0)


def make_weights(foot_rows, near_rows, noises):
    rows, slots, cols = foot_rows.shape
    part = 32
    return pl.pallas_call(
        functools.partial(weights_kernel, [float(t) for t in tap_values()]),
        in_specs=[HBM] + [VMEM] * (1 + len(noises)),
        out_shape=(
            jax.ShapeDtypeStruct((rows, slots, cols), BF16),
            jax.ShapeDtypeStruct((GR, slots, cols), BF16),
            jax.ShapeDtypeStruct((GR, slots, cols), BF16),
        ),
        scratch_shapes=[
            pltpu.VMEM((2, rows, part, cols), BF16),
            pltpu.VMEM(noises[0].shape, F32),
            pltpu.VMEM((cols, cols), BF16),
            pltpu.SemaphoreType.DMA((2,)),
        ],
        compiler_params=params(32),
        cost_estimate=COST,
        name="weights",
    )(foot_rows, near_rows, *noises)


def side_sum(column):
    cols = column.shape[0]
    top = lax.broadcasted_iota(jnp.int32, (cols // 8, 8, LANES), 1) < 4
    blank = jnp.zeros((2, 8, LANES), F32)
    turned = pltpu.roll(column.reshape(cols // 8, 8, LANES), 4, 1)
    turned = jnp.concatenate([blank, turned, blank], axis=0)
    both = turned[0 : cols // 8 + 1] + turned[3 : cols // 8 + 4]
    sides = jnp.where(top, both[0 : cols // 8], both[1 : cols // 8 + 1])
    return sides.reshape(cols, LANES)


def annulus_group(g, own, leaving, entering, gain, band, column, outgoing):
    frames = own.shape[2]
    outs = [leaving(q) for q in range(PER)]
    news = [entering(q) for q in range(PER)]
    levels = [dot(band, jnp.concatenate([o, n], axis=0)) for o, n in zip(outs, news)]
    column = list(column)
    dets = []
    for q in range(PER):
        det = []
        for h in range(frames // LANES):
            part = slice(h * LANES, (h + 1) * LANES)
            inner = column[h] - outs[q][:, part].astype(F32)
            column[h] = inner + news[q][:, part].astype(F32)
            fit = (levels[q][:, part] + side_sum(inner)) * gain
            outgoing[g, q, :, part] = fit.astype(BF16)
            det.append((own[g * PER + q, :, part].astype(F32) - fit).astype(BF16))
        dets.append(jnp.concatenate(det, axis=1))
    return column, dets


def grow(total, weight, g, dets):
    weights = jnp.concatenate([weight[g * PER + q] for q in range(PER)], axis=1)
    return total + dot(weights, jnp.concatenate(dets, axis=0))


def halves(ref):
    return [ref[:, h * LANES : (h + 1) * LANES] for h in range(ref.shape[1] // LANES)]


def add_rows(column, rows, sign=1.0):
    for row in rows:
        column = [c + sign * r.astype(F32) for c, r in zip(column, halves(row))]
    return column


def put(ref, column):
    for h, value in enumerate(column):
        ref[:, h * LANES : (h + 1) * LANES] = value


def sender(outgoing, background, sems):
    def send(g):
        return pltpu.make_async_copy(
            outgoing.at[g], background.at[0, pl.ds(g * PER, PER)], sems.at[g]
        )

    return send


def tables(gain):
    cols = gain.shape[1]
    band = jnp.where(jnp.abs(lag_table(cols)) <= RAD, 1.0, 0.0).astype(BF16)
    return (
        jnp.broadcast_to(gain[...], (LANES, cols)).T / (8.0 * RAD),
        jnp.concatenate([band, band], axis=1),
    )


def middle_kernel(own, near, weight, gain, background, upper, lower, total, outgoing, sems):
    rows, cols, frames = own.shape
    groups = range((RAD - NEAR) // PER, (rows - RAD + NEAR) // PER)
    send = sender(outgoing, background, sems)
    gains, band = tables(gain)
    column = [jnp.zeros((cols, LANES), F32)] * (frames // LANES)
    column = add_rows(column, [near[NEAR + r] for r in range(NEAR)])
    column = add_rows(column, [own[r] for r in range(RAD)])
    put(upper, column)
    column = add_rows(column, [own[RAD + r] for r in range(2 * RAD - NEAR - RAD)])
    grown = jnp.zeros(total.shape, F32)
    for g in groups:
        y = g * PER
        column, dets = annulus_group(
            g,
            own,
            (lambda q: near[NEAR + y - RAD + NEAR + q])
            if y < RAD
            else (lambda q: own[y - RAD + q]),
            (lambda q: near[y + RAD - rows + q])
            if y + RAD >= rows
            else (lambda q: own[y + RAD + q]),
            gains, band, column, outgoing,
        )
        send(g).start()
        grown = grow(grown, weight, g, dets)
    put(lower, column)
    total[...] = grown
    for g in groups:
        send(g).wait()


def mid_kernel(
    own, above, below, weight, gain, before, upper, lower, total,
    background, new_total, base, gain_table, band_table, outgoing, sems,
):
    del before
    rows = own.shape[0]
    low, high = RAD // PER - 2, (rows - RAD) // PER + 1
    y, z = low * PER, high * PER
    send = sender(outgoing, background, sems)
    gains, band = tables(gain)
    first = add_rows(halves(upper), [above[r] for r in range(PER)])
    column = add_rows(first, [own[RAD + r] for r in range(PER)])
    _, low_dets = annulus_group(
        low, own, lambda q: above[q], lambda q: own[y + RAD + q], gains, band, column, outgoing
    )
    send(low).start()
    column, high_dets = annulus_group(
        high, own, lambda q: own[z - RAD + q], lambda q: below[q], gains, band, halves(lower),
        outgoing,
    )
    send(high).start()
    new_total[...] = grow(grow(total[...], weight, low, low_dets), weight, high, high_dets)
    gain_table[...] = gains
    band_table[...] = band[:, : own.shape[1]]
    for q in range(PER):
        if q > 0:
            first = add_rows(first, [own[RAD + q - 1]])
        inner = own[z + PER - RAD + q]
        column = add_rows(column, [inner], -1.0)
        for k, (sums, row) in enumerate(((first, own[RAD + q]), (column, inner))):
            level = dot(band_table[...], row)
            for h, value in enumerate(sums):
                part = slice(h * LANES, (h + 1) * LANES)
                base[k, q, :, part] = level[:, part] + side_sum(value)
    send(low).wait()
    send(high).wait()


def end_kernel(
    own, above, below, weight, weight_next, weight_prev, total, base, gain, band, gradient, late
):
    rows, cols, frames = own.shape
    low, high = 0, rows // PER - 1
    blank = [jnp.zeros((cols, LANES), F32)] * (frames // LANES)
    dets = []
    for k, (g, far, order) in enumerate(
        ((low, above, range(PER - 1, -1, -1)), (high, below, range(PER)))
    ):
        column, mine = blank, [None] * PER
        for i, q in enumerate(order):
            row = far[q]
            level = dot(band[...], row)
            det = []
            for h in range(frames // LANES):
                part = slice(h * LANES, (h + 1) * LANES)
                fit = base[k, q, :, part] + level[:, part]
                if i > 0:
                    fit = fit + side_sum(column[h])
                fit = fit * gain[...]
                late[k, q, :, part] = fit.astype(BF16)
                det.append((own[g * PER + q, :, part].astype(F32) - fit).astype(BF16))
            mine[q] = jnp.concatenate(det, axis=1)
            column = add_rows(column, [row])
        dets.append(mine)
    low_dets, high_dets = dets
    grown = grow(grow(total[...], weight, low, low_dets), weight, high, high_dets)
    edges = ((2, weight_next, high_dets[PER - GR :]), (3, weight_prev, low_dets[:GR]))
    for at, edge, parts in edges:
        value = dot(
            jnp.concatenate([edge[a] for a in range(GR)], axis=1), jnp.concatenate(parts, axis=0)
        )
        gradient[:, at * frames : (at + 1) * frames] = value.astype(BF16)
    coarse = grown.astype(BF16)
    gradient[:, 0:frames] = coarse
    gradient[:, frames : 2 * frames] = (grown - coarse.astype(F32)).astype(BF16)


def late_kernel(late, before, background, sems):
    del before
    rows = background.shape[1]
    copies = [
        pltpu.make_async_copy(late.at[k], background.at[0, pl.ds(first, PER)], sems.at[k])
        for k, first in enumerate((0, rows - PER))
    ]
    for copy in copies:
        copy.start()
    for copy in copies:
        copy.wait()


def make_annulus(own, near, mid, far, weights, gain):
    rows, cols, frames = own.shape
    weight, weight_next, weight_prev = weights
    slots = weight.shape[1]
    background = jax.ShapeDtypeStruct((1, rows, cols, frames), BF16)
    column = jax.ShapeDtypeStruct((cols, frames), F32)
    total = jax.ShapeDtypeStruct((slots, frames), F32)
    gradient = jax.ShapeDtypeStruct((slots, 4 * frames), BF16)

    def call(kernel, name, args, outs, done, declared=COST):
        specs = [VMEM] * len(args)
        if done is not None:
            specs[done] = HBM
        return pl.pallas_call(
            kernel,
            in_specs=specs,
            out_specs=[HBM] + [VMEM] * (len(outs) - 1),
            out_shape=outs,
            scratch_shapes=[
                pltpu.VMEM((rows // PER, PER, cols, frames), BF16),
                pltpu.SemaphoreType.DMA((rows // PER,)),
            ],
            input_output_aliases={} if done is None else {done: 0},
            compiler_params=params(),
            cost_estimate=declared,
            name=name,
        )(*args)

    done, upper, lower, grown = call(
        middle_kernel, "annulus_middle", (own, near, weight, gain),
        (background, column, column, total), None,
    )
    prepared = (
        jax.ShapeDtypeStruct((2, PER, cols, frames), F32),
        jax.ShapeDtypeStruct((cols, LANES), F32),
        jax.ShapeDtypeStruct((cols, cols), BF16),
    )
    done, grown, *prepared = call(
        mid_kernel, "annulus_mid",
        (own, *mid, weight, gain, done, upper, lower, grown),
        (background, total, *prepared), 5,
        pl.CostEstimate(
            flops=2 * rows * cols * cols * frames, bytes_accessed=5 * MIB, transcendentals=0
        ),
    )
    args = (own, *far, weight, weight_next, weight_prev, grown, *prepared)
    gradient, late = pl.pallas_call(
        end_kernel,
        in_specs=[VMEM] * len(args),
        out_shape=(gradient, jax.ShapeDtypeStruct((2, PER, cols, frames), BF16)),
        compiler_params=params(),
        cost_estimate=COST,
        name="annulus_end",
    )(*args)
    background = pl.pallas_call(
        late_kernel,
        in_specs=[VMEM, HBM],
        out_specs=HBM,
        out_shape=background,
        scratch_shapes=[pltpu.SemaphoreType.DMA((2,))],
        input_output_aliases={1: 0},
        compiler_params=params(),
        cost_estimate=COST,
        name="late_rows",
    )(late, done)
    return background, gradient


def prepare_kernel(capacity, stripe, slow, fast, step, hots, tables):
    count = stripe.shape[1]
    frames = tables.shape[2]
    slots = hots.shape[1] // 4

    def upended(row):
        return jnp.broadcast_to(row[...].astype(F32), (LANES, count)).T

    before = lax.broadcasted_iota(jnp.int32, (count, count), 1) < lax.broadcasted_iota(
        jnp.int32, (count, count), 0
    )
    named = upended(stripe)
    same = (named == stripe[...].astype(F32)) & before
    rank = jnp.sum(jnp.where(same, 1.0, 0.0), axis=1, keepdims=True)
    slot = (named[:, 0:1] * capacity + rank).astype(jnp.int32)
    place = lax.broadcasted_iota(jnp.int32, (count, slots), 1)
    for k, shift in enumerate((0, 0, capacity, -capacity)):
        hots[:, k * slots : (k + 1) * slots] = jnp.where(place + shift == slot, 1.0, 0.0).astype(
            BF16
        )
    a, b = upended(slow), upended(fast)
    for k, part in enumerate((upended(step), a, b, (1.0 - a) * (1.0 - b) / (a - b))):
        tables[k] = jnp.concatenate([part] * (frames // LANES), axis=1)


def prepare_traces(stripe, slow, fast, step, frames, slots, capacity):
    count = stripe.shape[1]
    return pl.pallas_call(
        functools.partial(prepare_kernel, capacity),
        out_shape=(
            jax.ShapeDtypeStruct((count, 4 * slots), BF16),
            jax.ShapeDtypeStruct((4, count, frames), F32),
        ),
        compiler_params=params(),
        cost_estimate=COST,
        name="prepare",
    )(stripe, slow, fast, step)


def traces_kernel(hots, tables, traces, inbox, out):
    count, frames = traces.shape
    parts = [inbox[:, k * frames : (k + 1) * frames] for k in range(4)]
    gradient = dot(hots[...], jnp.concatenate(parts, axis=0))
    updated = traces[...].astype(F32) + tables[0] * gradient
    lane = lax.broadcasted_iota(jnp.int32, (count, frames), 1)

    def lagged(value, lag):
        return jnp.where(lane >= lag, pltpu.roll(value, lag, 1), 0.0)

    a, b = tables[1], tables[2]
    driven = updated - (a + b) * lagged(updated, 1) + (a * b) * lagged(updated, 2)
    spikes = jnp.maximum(driven - lam_floor, 0.0)
    sums = [spikes, spikes]
    roots = [a, b]
    lag = 1
    while lag < frames:
        sums = [value + root * lagged(value, lag) for value, root in zip(sums, roots)]
        roots = [root * root for root in roots]
        lag *= 2
    out[...] = tables[3] * (a * sums[0] - b * sums[1])


def make_traces(hots, tables, traces, inbox):
    count, frames = traces.shape
    return pl.pallas_call(
        traces_kernel,
        out_shape=jax.ShapeDtypeStruct((count, frames), F32),
        compiler_params=params(),
        cost_estimate=COST,
        name="traces",
    )(hots, tables, traces, inbox)


def neighbours(axis):
    devices = lax.axis_size(axis)
    up = [(i, i + 1) for i in range(devices - 1)]
    return up, [(j, i) for i, j in up]


def on_device(movie, footprints, traces, stripe, column, annulus_gain, decay_slow, decay_fast):
    pix_count = lax.axis_size("pix")
    rows, cols, frames = movie.shape[1:]
    count = footprints.shape[1]
    capacity = max(2, 2 * count // pix_count)
    slots = pix_count * capacity
    pix_up, pix_down = neighbours("pix")
    plane_up, plane_down = neighbours("plane")

    stripe_row = stripe.reshape(1, count)
    outbox = make_outbox(stripe_row, column, footprints[0], traces[0], capacity, slots)
    def exchange(up, down):
        return (lax.ppermute(up, "pix", pix_up), lax.ppermute(down, "pix", pix_down))

    frames_in, outbox = lax.optimization_barrier((movie, outbox))
    inbox = lax.all_to_all(outbox, "pix", split_axis=0, concat_axis=0, tiled=True)
    near_prev, near_next = exchange(frames_in[0, rows - NEAR :], frames_in[0, :NEAR])
    *started, mid_noise, up, down = make_residual(inbox, movie)
    mid = exchange(up, down)
    foot_rows, residual, other_noise, up, down = make_residual(
        inbox, movie, (*started, mid_noise)
    )
    near_rows, near_residual, noise = make_near(
        inbox, near_next, near_prev, (mid_noise, other_noise)
    )
    foot_f = footprints[0].astype(F32)
    step = 1.0 / (jnp.sum(foot_f * foot_f, axis=1) + norm_eps)
    noise_before = lax.ppermute(noise, "plane", plane_up)
    noise_after = lax.ppermute(noise, "plane", plane_down)
    step_row, up, down, noise_before = lax.optimization_barrier(
        (step[None], up, down, noise_before)
    )
    far = exchange(up, down)
    noises = (noise, noise_before, noise_after)
    hots, tables = prepare_traces(
        stripe_row, decay_slow, decay_fast, step_row, frames, slots, capacity
    )
    weights = make_weights(foot_rows, near_rows, noises)
    background, gradient = make_annulus(
        residual, near_residual, mid, far, weights, annulus_gain
    )
    home = lax.all_to_all(gradient, "pix", split_axis=0, concat_axis=0, tiled=True)
    traces_new = make_traces(hots, tables, traces[0], home)
    return (background, traces_new[None])


def solution(mesh):
    placed = (
        P("plane", "pix", None, None),
        P("plane", "pix", None),
        P("plane", "pix", None),
        P("plane", "pix", None),
        P("plane", "pix"),
        P("plane", None),
        P("plane", "pix"),
        P("plane", "pix"),
    )
    return jax.shard_map(
        on_device,
        mesh=mesh,
        in_specs=placed,
        out_specs=(P("plane", "pix", None, None), P("plane", "pix", None)),
        check_vma=False,
    )
```

```python
import functools

import jax
import jax.numpy as jnp
import ml_dtypes
import numpy as np
from jax import lax
from jax.experimental import pallas as pl
from jax.experimental.pallas import tpu as pltpu
from jax.sharding import PartitionSpec as P

FOOT = 32
RAD = 12
GR = 3
LANES = 128
PER = LANES // FOOT
NEAR = PER

lam_floor = 0.1
noise_eps = 1e-05
norm_eps = 1e-05
sigma_twice = 4.5

F32 = jnp.float32
BF16 = jnp.bfloat16
MIB = 1 << 20
HBM = pl.BlockSpec(memory_space=pltpu.HBM)
VMEM = pl.BlockSpec(memory_space=pltpu.VMEM)


def tap_values():
    offsets = np.arange(-GR, GR + 1).astype(np.float32)
    raw = np.exp(-offsets * offsets / np.float32(sigma_twice)).astype(np.float32)
    return (raw / raw.sum(dtype=np.float32)).astype(ml_dtypes.bfloat16).astype(np.float32)


def params(mib=16):
    return pltpu.CompilerParams(vmem_limit_bytes=mib * MIB)


COST = pl.CostEstimate(flops=1, bytes_accessed=1, transcendentals=0)


def dot(a, b):
    return jnp.dot(a, b, preferred_element_type=F32)


def outbox_kernel(capacity, *refs):
    sources, result, places, outbox, sems = refs[0:4], refs[4], refs[5:9], refs[9], refs[10]
    copies = [
        pltpu.make_async_copy(source, place, sems.at[k])
        for k, (source, place) in enumerate(zip(sources, places))
    ]
    for copy in copies:
        copy.start()
    for copy in copies[0:2]:
        copy.wait()
    stripe, column, foot, traces = places
    slots = outbox.shape[0]
    count, tiles = foot.shape
    frames = traces.shape[1]
    before = lax.broadcasted_iota(jnp.int32, (count, count), 0) < lax.broadcasted_iota(
        jnp.int32, (count, count), 1
    )
    named = jnp.broadcast_to(stripe[...].astype(F32), (count, count))
    same = (named == named.T) & before
    rank = jnp.sum(jnp.where(same, 1.0, 0.0), axis=0, keepdims=True).astype(jnp.int32)
    slot = stripe[...] * capacity + rank
    place = lax.broadcasted_iota(jnp.int32, (slots, count), 0)
    left = jnp.broadcast_to(column[...].astype(F32), (LANES, count)).T.astype(BF16)
    lane = lax.broadcasted_iota(jnp.int32, (slots, LANES), 1)
    edge = NEAR * FOOT
    lefts = jnp.zeros((slots, LANES), F32)
    at = 3 * frames
    hots = [
        jnp.where(place + shift == slot, 1.0, 0.0).astype(BF16)
        for shift in (0, capacity, -capacity)
    ]
    leaving = []

    def leave(start, width):
        lanes = pl.ds(start, width)
        copy = pltpu.make_async_copy(
            outbox.at[:, lanes], result.at[:, lanes], sems.at[len(copies) + len(leaving)]
        )
        copy.start()
        leaving.append(copy)

    copies[3].wait()
    for k, hot in enumerate(hots):
        outbox[:, k * frames : (k + 1) * frames] = dot(hot, traces[...]).astype(BF16)
        lefts = jnp.where(lane == k, dot(hot, left), lefts)
    outbox[:, outbox.shape[1] - LANES :] = lefts.astype(BF16)
    leave(0, at)
    copies[2].wait()
    half = tiles // 2
    for hot, first, width in (
        (hots[0], 0, half),
        (hots[0], half, half),
        (hots[1], 0, edge),
        (hots[2], tiles - edge, edge),
    ):
        outbox[:, at : at + width] = dot(hot, foot[:, first : first + width]).astype(BF16)
        if width == half:
            leave(at, width)
        at += width
    leave(3 * frames + tiles, outbox.shape[1] - 3 * frames - tiles)
    for copy in leaving:
        copy.wait()


def make_outbox(stripe, column, foot, traces, capacity, slots):
    count, tiles = foot.shape
    frames = traces.shape[1]
    width = 3 * frames + tiles + 2 * NEAR * FOOT + LANES
    args = (stripe, column, foot, traces)
    return pl.pallas_call(
        functools.partial(outbox_kernel, capacity),
        in_specs=[HBM] * len(args),
        out_specs=HBM,
        out_shape=jax.ShapeDtypeStruct((slots, width), BF16),
        scratch_shapes=[pltpu.VMEM(a.shape, a.dtype) for a in args]
        + [pltpu.VMEM((slots, width), BF16), pltpu.SemaphoreType.DMA((len(args) + 4,))],
        compiler_params=params(56),
        cost_estimate=COST,
        name="outbox",
    )(*args)


def spread(block, col):
    lane = lax.broadcasted_iota(jnp.int32, block.shape, 1)
    for k in range(7):
        block = jnp.where(((col >> k) & 1) == 1, pltpu.roll(block, 1 << k, 1), block)
    inside = ((lane - col) & (LANES - 1)) < FOOT
    left = inside & (lane >= col)
    right = inside & (lane < col)
    rows = []
    for q in range(PER):
        moved = block if q == 0 else pltpu.roll(block, LANES - q * FOOT, 1)
        rows.append(
            jnp.concatenate(
                [jnp.where(left, moved, 0.0), jnp.where(right, moved, 0.0)], axis=1
            ).astype(BF16)
        )
    return rows


def tile_rows(inbox, which, block, frames):
    lefts = inbox[:, inbox.shape[1] - LANES :].astype(F32)
    col = jnp.broadcast_to(lefts[:, which : which + 1], lefts.shape).astype(jnp.int32)
    start = 3 * frames + block * LANES
    if not isinstance(start, int):
        start = pl.multiple_of(start, LANES)
    return spread(inbox[:, pl.ds(start, LANES)].astype(F32), col)


def model_row(row, inbox, which, frames):
    traces = inbox[:, which * frames : (which + 1) * frames]
    return lax.dot_general(row, traces, (((0,), (0,)), ((), ())), preferred_element_type=F32)


def noise_row(left, change):
    frames = left.shape[1]
    steps = dot(left, change)
    steps = steps * steps
    part = steps[:, 0:LANES]
    for k in range(1, frames // LANES):
        part = part + steps[:, k * LANES : (k + 1) * LANES]
    return jnp.sum(part.T, axis=0, keepdims=True) / (frames - 1)


def lag_table(size):
    shape = (size, size)
    return lax.broadcasted_iota(jnp.int32, shape, 1) - lax.broadcasted_iota(jnp.int32, shape, 0)


def change_matrix(frames):
    lag = lag_table(frames)
    steps = jnp.where(lag == -1, 1.0, 0.0) - jnp.where(lag == 0, 1.0, 0.0)
    later = lax.broadcasted_iota(jnp.int32, lag.shape, 1)
    return jnp.where(later < frames - 1, steps, 0.0).astype(BF16)


def residual_kernel(pick, low, high, first, inbox, movie, *refs):
    if not first:
        refs = refs[3:]
    (foot_rows, residual, noise, up, down) = refs[0:5]
    (change, movie_slots, foot_slots, left_slots, sems) = refs[5:]
    frames = movie.shape[3]
    count = pick(None)
    change[...] = change_matrix(frames)

    def fetch(i, slot):
        rows_g = pl.ds(pick(i) * PER, PER)
        return pltpu.make_async_copy(movie.at[0, rows_g], movie_slots.at[slot], sems.at[0, slot])

    def sends(i, slot):
        rows_g = pl.ds(pick(i) * PER, PER)
        return (
            pltpu.make_async_copy(foot_slots.at[slot], foot_rows.at[rows_g], sems.at[1, slot]),
            pltpu.make_async_copy(left_slots.at[slot], residual.at[rows_g], sems.at[2, slot]),
        )

    fetch(0, 0).start()

    def group(i, carry):
        slot = lax.rem(i, 2)
        g = pick(i)

        @pl.when(i + 1 < count)
        def _():
            fetch(i + 1, 1 - slot).start()

        fetch(i, slot).wait()

        @pl.when(i >= 2)
        def _():
            for copy in sends(i - 2, slot):
                copy.wait()

        noises = []
        for q, row in enumerate(tile_rows(inbox, 0, g, frames)):
            foot_slots[slot, q] = row
            left = movie_slots[slot, q].astype(F32) - model_row(row, inbox, 0, frames)
            left = left.astype(BF16)
            left_slots[slot, q] = left
            noises.append(noise_row(left, change[...]))
        noise[i] = jnp.concatenate(noises, axis=0)
        for copy in sends(i, slot):
            copy.start()

        @pl.when(g == low)
        def _():
            down[...] = left_slots[slot]

        @pl.when(g == high)
        def _():
            up[...] = left_slots[slot]

        return carry

    lax.fori_loop(0, count, group, 0)
    for i in (count - 2, count - 1):
        for copy in sends(i, i % 2):
            copy.wait()


def make_residual(inbox, movie, earlier=None):
    slots = inbox.shape[0]
    rows, cols, frames = movie.shape[1:]
    groups = rows // PER
    mids = (1, groups - 2)
    if earlier is None:
        low, high, count = *mids, 2

        def pick(i):
            return count if i is None else mids[0] + i * (mids[1] - mids[0])
    else:
        low, high, count = 2, groups - 3, groups - 2

        def pick(i):
            if i is None:
                return count
            if isinstance(i, int):
                return i + (i >= mids[0]) + (i + 1 >= mids[1])
            return i + jnp.where(i >= mids[0], 1, 0) + jnp.where(i + 1 >= mids[1], 1, 0)

    piece = jax.ShapeDtypeStruct((PER, cols, frames), BF16)
    more = () if earlier is None else earlier
    return pl.pallas_call(
        functools.partial(residual_kernel, pick, low, high, earlier is None),
        in_specs=[VMEM, HBM] + [HBM, HBM, VMEM][: len(more)],
        out_specs=[HBM, HBM, VMEM, VMEM, VMEM],
        out_shape=(
            jax.ShapeDtypeStruct((rows, slots, cols), BF16),
            jax.ShapeDtypeStruct((rows, cols, frames), BF16),
            jax.ShapeDtypeStruct((count, PER, cols), F32),
            piece,
            piece,
        ),
        scratch_shapes=[
            pltpu.VMEM((frames, frames), BF16),
            pltpu.VMEM((2, PER, cols, frames), BF16),
            pltpu.VMEM((2, PER, slots, cols), BF16),
            pltpu.VMEM((2, PER, cols, frames), BF16),
            pltpu.SemaphoreType.DMA((3, 2)),
        ],
        input_output_aliases={} if earlier is None else {2: 0, 3: 1},
        compiler_params=params(44),
        cost_estimate=COST,
        name="residual",
    )(inbox, movie, *more)


def near_kernel(
    inbox, movie_next, movie_prev, mid_noise, other_noise, foot_rows, residual, noise
):
    frames = movie_next.shape[2]
    groups = mid_noise.shape[0] + other_noise.shape[0]
    own = FOOT // PER
    change = change_matrix(frames)
    others = [g for g in range(groups) if g not in (1, groups - 2)]
    for order, part in (((1, groups - 2), mid_noise), (others, other_noise)):
        for i, g in enumerate(order):
            noise[NEAR + g * PER : NEAR + (g + 1) * PER, :] = part[i]
    for side, (block, movie, first) in enumerate(
        ((own, movie_next, 0), (own + NEAR // PER, movie_prev, NEAR + groups * PER))
    ):
        for q, row in enumerate(tile_rows(inbox, 1 + side, block, frames)):
            y = side * NEAR + q
            foot_rows[y] = row
            left = movie[q].astype(F32) - model_row(row, inbox, 1 + side, frames)
            left = left.astype(BF16)
            residual[y] = left
            noise[first + q : first + q + 1, :] = noise_row(left, change)


def make_near(inbox, movie_next, movie_prev, noises):
    slots = inbox.shape[0]
    cols, frames = movie_next.shape[1:]
    return pl.pallas_call(
        near_kernel,
        out_shape=(
            jax.ShapeDtypeStruct((2 * NEAR, slots, cols), BF16),
            jax.ShapeDtypeStruct((2 * NEAR, cols, frames), BF16),
            jax.ShapeDtypeStruct((2 * NEAR + PER * sum(n.shape[0] for n in noises), cols), F32),
        ),
        compiler_params=params(),
        cost_estimate=COST,
        name="near",
    )(inbox, movie_next, movie_prev, *noises)


def weights_kernel(
    taps, own, near, noise, noise_before, noise_after, out, out_next, out_prev,
    own_slots, scale, band, sems,
):
    rows, slots, cols = own.shape
    part = own_slots.shape[2]
    count = slots // part

    def fetch(i, slot):
        these = pl.ds(pl.multiple_of(i * part, part), part)
        return pltpu.make_async_copy(own.at[:, these, :], own_slots.at[slot], sems.at[slot])

    fetch(0, 0).start()
    pooled = (noise_before[...] + 2.0 * noise[...] + noise_after[...]) / 4.0
    scale[...] = 1.0 / jnp.sqrt(pooled + noise_eps)
    lag = jnp.abs(lag_table(cols))
    table = jnp.zeros(lag.shape, F32)
    for k in range(GR + 1):
        table = jnp.where(lag == k, taps[GR + k], table)
    band[...] = table.astype(BF16)

    def across(foot, inv):
        scaled = (foot.astype(F32) * inv[:, None, :]).astype(BF16)
        count = foot.shape[0]
        return dot(scaled.reshape(count * part, cols), band[...]).reshape(count, part, cols)

    def some(i, carry):
        slot = lax.rem(i, 2)

        @pl.when(i + 1 < count)
        def _():
            fetch(i + 1, 1 - slot).start()

        fetch(i, slot).wait()
        these = pl.ds(pl.multiple_of(i * part, part), part)
        blurred = across(own_slots[slot], scale[NEAR : NEAR + rows])
        for r in range(rows):
            total = taps[GR] * blurred[r]
            for k in range(1, GR + 1):
                if r - k >= 0 and r + k < rows:
                    total = total + taps[GR + k] * (blurred[r - k] + blurred[r + k])
                elif r - k >= 0:
                    total = total + taps[GR + k] * blurred[r - k]
                elif r + k < rows:
                    total = total + taps[GR + k] * blurred[r + k]
            out[r, these, :] = total.astype(BF16)
        after = across(near[0:GR, these, :], scale[0:GR])
        ahead = across(near[2 * NEAR - GR : 2 * NEAR, these, :], scale[rows + 2 * NEAR - GR :])
        for a in range(GR):
            total = taps[2 * GR - a] * after[0]
            for r in range(1, a + 1):
                total = total + taps[2 * GR + r - a] * after[r]
            out_next[a, these, :] = total.astype(BF16)
            total = taps[2 * GR] * ahead[a]
            for b in range(a + 1, GR):
                total = total + taps[2 * GR + a - b] * ahead[b]
            out_prev[a, these, :] = total.astype(BF16)
        return carry

    lax.fori_loop(0, count, some, 0)


def make_weights(foot_rows, near_rows, noises):
    rows, slots, cols = foot_rows.shape
    part = 32
    return pl.pallas_call(
        functools.partial(weights_kernel, [float(t) for t in tap_values()]),
        in_specs=[HBM] + [VMEM] * (1 + len(noises)),
        out_shape=(
            jax.ShapeDtypeStruct((rows, slots, cols), BF16),
            jax.ShapeDtypeStruct((GR, slots, cols), BF16),
            jax.ShapeDtypeStruct((GR, slots, cols), BF16),
        ),
        scratch_shapes=[
            pltpu.VMEM((2, rows, part, cols), BF16),
            pltpu.VMEM(noises[0].shape, F32),
            pltpu.VMEM((cols, cols), BF16),
            pltpu.SemaphoreType.DMA((2,)),
        ],
        compiler_params=params(32),
        cost_estimate=COST,
        name="weights",
    )(foot_rows, near_rows, *noises)


def side_sum(column):
    cols = column.shape[0]
    top = lax.broadcasted_iota(jnp.int32, (cols // 8, 8, LANES), 1) < 4
    blank = jnp.zeros((2, 8, LANES), F32)
    turned = pltpu.roll(column.reshape(cols // 8, 8, LANES), 4, 1)
    turned = jnp.concatenate([blank, turned, blank], axis=0)
    both = turned[0 : cols // 8 + 1] + turned[3 : cols // 8 + 4]
    sides = jnp.where(top, both[0 : cols // 8], both[1 : cols // 8 + 1])
    return sides.reshape(cols, LANES)


def annulus_group(g, own, leaving, entering, gain, band, column, outgoing):
    frames = own.shape[2]
    outs = [leaving(q) for q in range(PER)]
    news = [entering(q) for q in range(PER)]
    levels = [dot(band, jnp.concatenate([o, n], axis=0)) for o, n in zip(outs, news)]
    column = list(column)
    dets = []
    for q in range(PER):
        det = []
        for h in range(frames // LANES):
            part = slice(h * LANES, (h + 1) * LANES)
            inner = column[h] - outs[q][:, part].astype(F32)
            column[h] = inner + news[q][:, part].astype(F32)
            fit = (levels[q][:, part] + side_sum(inner)) * gain
            outgoing[g, q, :, part] = fit.astype(BF16)
            det.append((own[g * PER + q, :, part].astype(F32) - fit).astype(BF16))
        dets.append(jnp.concatenate(det, axis=1))
    return column, dets


def grow(total, weight, g, dets):
    weights = jnp.concatenate([weight[g * PER + q] for q in range(PER)], axis=1)
    return total + dot(weights, jnp.concatenate(dets, axis=0))


def halves(ref):
    return [ref[:, h * LANES : (h + 1) * LANES] for h in range(ref.shape[1] // LANES)]


def add_rows(column, rows, sign=1.0):
    for row in rows:
        column = [c + sign * r.astype(F32) for c, r in zip(column, halves(row))]
    return column


def put(ref, column):
    for h, value in enumerate(column):
        ref[:, h * LANES : (h + 1) * LANES] = value


def sender(outgoing, background, sems):
    def send(g):
        return pltpu.make_async_copy(
            outgoing.at[g], background.at[0, pl.ds(g * PER, PER)], sems.at[g]
        )

    return send


def tables(gain):
    cols = gain.shape[1]
    band = jnp.where(jnp.abs(lag_table(cols)) <= RAD, 1.0, 0.0).astype(BF16)
    return (
        jnp.broadcast_to(gain[...], (LANES, cols)).T / (8.0 * RAD),
        jnp.concatenate([band, band], axis=1),
    )


def middle_kernel(own, near, weight, gain, background, upper, lower, total, outgoing, sems):
    rows, cols, frames = own.shape
    groups = range((RAD - NEAR) // PER, (rows - RAD + NEAR) // PER)
    send = sender(outgoing, background, sems)
    gains, band = tables(gain)
    column = [jnp.zeros((cols, LANES), F32)] * (frames // LANES)
    column = add_rows(column, [near[NEAR + r] for r in range(NEAR)])
    column = add_rows(column, [own[r] for r in range(RAD)])
    put(upper, column)
    column = add_rows(column, [own[RAD + r] for r in range(2 * RAD - NEAR - RAD)])
    grown = jnp.zeros(total.shape, F32)
    for g in groups:
        y = g * PER
        column, dets = annulus_group(
            g,
            own,
            (lambda q: near[NEAR + y - RAD + NEAR + q])
            if y < RAD
            else (lambda q: own[y - RAD + q]),
            (lambda q: near[y + RAD - rows + q])
            if y + RAD >= rows
            else (lambda q: own[y + RAD + q]),
            gains, band, column, outgoing,
        )
        send(g).start()
        grown = grow(grown, weight, g, dets)
    put(lower, column)
    total[...] = grown
    for g in groups:
        send(g).wait()


def mid_kernel(
    own, above, below, weight, gain, before, upper, lower, total,
    background, new_total, base, gain_table, band_table, outgoing, sems,
):
    del before
    rows = own.shape[0]
    low, high = RAD // PER - 2, (rows - RAD) // PER + 1
    y, z = low * PER, high * PER
    send = sender(outgoing, background, sems)
    gains, band = tables(gain)
    first = add_rows(halves(upper), [above[r] for r in range(PER)])
    column = add_rows(first, [own[RAD + r] for r in range(PER)])
    _, low_dets = annulus_group(
        low, own, lambda q: above[q], lambda q: own[y + RAD + q], gains, band, column, outgoing
    )
    send(low).start()
    column, high_dets = annulus_group(
        high, own, lambda q: own[z - RAD + q], lambda q: below[q], gains, band, halves(lower),
        outgoing,
    )
    send(high).start()
    new_total[...] = grow(grow(total[...], weight, low, low_dets), weight, high, high_dets)
    gain_table[...] = gains
    band_table[...] = band[:, : own.shape[1]]
    for q in range(PER):
        if q > 0:
            first = add_rows(first, [own[RAD + q - 1]])
        inner = own[z + PER - RAD + q]
        column = add_rows(column, [inner], -1.0)
        for k, (sums, row) in enumerate(((first, own[RAD + q]), (column, inner))):
            level = dot(band_table[...], row)
            for h, value in enumerate(sums):
                part = slice(h * LANES, (h + 1) * LANES)
                base[k, q, :, part] = level[:, part] + side_sum(value)
    send(low).wait()
    send(high).wait()


def end_kernel(
    own, above, below, weight, weight_next, weight_prev, total, base, gain, band, result, late,
    gradient, sems,
):
    rows, cols, frames = own.shape
    low, high = 0, rows // PER - 1
    blank = [jnp.zeros((cols, LANES), F32)] * (frames // LANES)
    dets = []
    for k, (g, far, order) in enumerate(
        ((low, above, range(PER - 1, -1, -1)), (high, below, range(PER)))
    ):
        column, mine = blank, [None] * PER
        for i, q in enumerate(order):
            row = far[q]
            level = dot(band[...], row)
            det = []
            for h in range(frames // LANES):
                part = slice(h * LANES, (h + 1) * LANES)
                fit = base[k, q, :, part] + level[:, part]
                if i > 0:
                    fit = fit + side_sum(column[h])
                fit = fit * gain[...]
                late[k, q, :, part] = fit.astype(BF16)
                det.append((own[g * PER + q, :, part].astype(F32) - fit).astype(BF16))
            mine[q] = jnp.concatenate(det, axis=1)
            column = add_rows(column, [row])
        dets.append(mine)
    low_dets, high_dets = dets
    edges = ((2, weight_next, high_dets[PER - GR :]), (3, weight_prev, low_dets[:GR]))
    for at, edge, parts in edges:
        value = dot(
            jnp.concatenate([edge[a] for a in range(GR)], axis=1), jnp.concatenate(parts, axis=0)
        )
        gradient[:, at * frames : (at + 1) * frames] = value.astype(BF16)
    copies = [
        pltpu.make_async_copy(gradient.at[:, lanes], result.at[:, lanes], sems.at[k])
        for k, lanes in enumerate((pl.ds(2 * frames, 2 * frames), pl.ds(0, 2 * frames)))
    ]
    copies[0].start()
    grown = grow(grow(total[...], weight, low, low_dets), weight, high, high_dets)
    coarse = grown.astype(BF16)
    gradient[:, 0:frames] = coarse
    gradient[:, frames : 2 * frames] = (grown - coarse.astype(F32)).astype(BF16)
    copies[1].start()
    for copy in copies:
        copy.wait()


def late_kernel(late, before, background, sems):
    del before
    rows = background.shape[1]
    copies = [
        pltpu.make_async_copy(late.at[k], background.at[0, pl.ds(first, PER)], sems.at[k])
        for k, first in enumerate((0, rows - PER))
    ]
    for copy in copies:
        copy.start()
    for copy in copies:
        copy.wait()


def make_annulus(own, near, mid, far, weights, gain):
    rows, cols, frames = own.shape
    weight, weight_next, weight_prev = weights
    slots = weight.shape[1]
    background = jax.ShapeDtypeStruct((1, rows, cols, frames), BF16)
    column = jax.ShapeDtypeStruct((cols, frames), F32)
    total = jax.ShapeDtypeStruct((slots, frames), F32)
    gradient = jax.ShapeDtypeStruct((slots, 4 * frames), BF16)

    def call(kernel, name, args, outs, done, declared=COST):
        specs = [VMEM] * len(args)
        if done is not None:
            specs[done] = HBM
        return pl.pallas_call(
            kernel,
            in_specs=specs,
            out_specs=[HBM] + [VMEM] * (len(outs) - 1),
            out_shape=outs,
            scratch_shapes=[
                pltpu.VMEM((rows // PER, PER, cols, frames), BF16),
                pltpu.SemaphoreType.DMA((rows // PER,)),
            ],
            input_output_aliases={} if done is None else {done: 0},
            compiler_params=params(),
            cost_estimate=declared,
            name=name,
        )(*args)

    done, upper, lower, grown = call(
        middle_kernel, "annulus_middle", (own, near, weight, gain),
        (background, column, column, total), None,
    )
    prepared = (
        jax.ShapeDtypeStruct((2, PER, cols, frames), F32),
        jax.ShapeDtypeStruct((cols, LANES), F32),
        jax.ShapeDtypeStruct((cols, cols), BF16),
    )
    done, grown, *prepared = call(
        mid_kernel, "annulus_mid",
        (own, *mid, weight, gain, done, upper, lower, grown),
        (background, total, *prepared), 5,
        pl.CostEstimate(
            flops=2 * rows * cols * cols * frames, bytes_accessed=5 * MIB, transcendentals=0
        ),
    )
    args = (own, *far, weight, weight_next, weight_prev, grown, *prepared)
    gradient, late = pl.pallas_call(
        end_kernel,
        in_specs=[VMEM] * len(args),
        out_specs=[HBM, VMEM],
        out_shape=(gradient, jax.ShapeDtypeStruct((2, PER, cols, frames), BF16)),
        scratch_shapes=[
            pltpu.VMEM((slots, 4 * frames), BF16),
            pltpu.SemaphoreType.DMA((2,)),
        ],
        compiler_params=params(),
        cost_estimate=COST,
        name="annulus_end",
    )(*args)
    background = pl.pallas_call(
        late_kernel,
        in_specs=[VMEM, HBM],
        out_specs=HBM,
        out_shape=background,
        scratch_shapes=[pltpu.SemaphoreType.DMA((2,))],
        input_output_aliases={1: 0},
        compiler_params=params(),
        cost_estimate=COST,
        name="late_rows",
    )(late, done)
    return background, gradient


def prepare_kernel(capacity, stripe, slow, fast, step, hots, tables):
    count = stripe.shape[1]
    frames = tables.shape[2]
    slots = hots.shape[1] // 4

    def upended(row):
        return jnp.broadcast_to(row[...].astype(F32), (LANES, count)).T

    before = lax.broadcasted_iota(jnp.int32, (count, count), 1) < lax.broadcasted_iota(
        jnp.int32, (count, count), 0
    )
    named = upended(stripe)
    same = (named == stripe[...].astype(F32)) & before
    rank = jnp.sum(jnp.where(same, 1.0, 0.0), axis=1, keepdims=True)
    slot = (named[:, 0:1] * capacity + rank).astype(jnp.int32)
    place = lax.broadcasted_iota(jnp.int32, (count, slots), 1)
    for k, shift in enumerate((0, 0, capacity, -capacity)):
        hots[:, k * slots : (k + 1) * slots] = jnp.where(place + shift == slot, 1.0, 0.0).astype(
            BF16
        )
    a, b = upended(slow), upended(fast)
    for k, part in enumerate((upended(step), a, b, (1.0 - a) * (1.0 - b) / (a - b))):
        tables[k] = jnp.concatenate([part] * (frames // LANES), axis=1)


def prepare_traces(stripe, slow, fast, step, frames, slots, capacity):
    count = stripe.shape[1]
    return pl.pallas_call(
        functools.partial(prepare_kernel, capacity),
        out_shape=(
            jax.ShapeDtypeStruct((count, 4 * slots), BF16),
            jax.ShapeDtypeStruct((4, count, frames), F32),
        ),
        compiler_params=params(),
        cost_estimate=COST,
        name="prepare",
    )(stripe, slow, fast, step)


def traces_kernel(hots, tables, traces, inbox, out):
    count, frames = traces.shape
    parts = [inbox[:, k * frames : (k + 1) * frames] for k in range(4)]
    gradient = dot(hots[...], jnp.concatenate(parts, axis=0))
    updated = traces[...].astype(F32) + tables[0] * gradient
    lane = lax.broadcasted_iota(jnp.int32, (count, frames), 1)

    def lagged(value, lag):
        return jnp.where(lane >= lag, pltpu.roll(value, lag, 1), 0.0)

    a, b = tables[1], tables[2]
    driven = updated - (a + b) * lagged(updated, 1) + (a * b) * lagged(updated, 2)
    spikes = jnp.maximum(driven - lam_floor, 0.0)
    sums = [spikes, spikes]
    roots = [a, b]
    lag = 1
    while lag < frames:
        sums = [value + root * lagged(value, lag) for value, root in zip(sums, roots)]
        roots = [root * root for root in roots]
        lag *= 2
    out[...] = tables[3] * (a * sums[0] - b * sums[1])


def make_traces(hots, tables, traces, inbox):
    count, frames = traces.shape
    return pl.pallas_call(
        traces_kernel,
        out_shape=jax.ShapeDtypeStruct((count, frames), F32),
        compiler_params=params(),
        cost_estimate=COST,
        name="traces",
    )(hots, tables, traces, inbox)


def neighbours(axis):
    devices = lax.axis_size(axis)
    up = [(i, i + 1) for i in range(devices - 1)]
    return up, [(j, i) for i, j in up]


def on_device(movie, footprints, traces, stripe, column, annulus_gain, decay_slow, decay_fast):
    pix_count = lax.axis_size("pix")
    rows, cols, frames = movie.shape[1:]
    count = footprints.shape[1]
    capacity = max(2, 2 * count // pix_count)
    slots = pix_count * capacity
    pix_up, pix_down = neighbours("pix")
    plane_up, plane_down = neighbours("plane")

    stripe_row = stripe.reshape(1, count)
    outbox = make_outbox(stripe_row, column, footprints[0], traces[0], capacity, slots)
    def exchange(up, down):
        return (lax.ppermute(up, "pix", pix_up), lax.ppermute(down, "pix", pix_down))

    frames_in, outbox = lax.optimization_barrier((movie, outbox))
    inbox = lax.all_to_all(outbox, "pix", split_axis=0, concat_axis=0, tiled=True)
    near_prev, near_next = exchange(frames_in[0, rows - NEAR :], frames_in[0, :NEAR])
    *started, mid_noise, up, down = make_residual(inbox, movie)
    mid = exchange(up, down)
    foot_rows, residual, other_noise, up, down = make_residual(
        inbox, movie, (*started, mid_noise)
    )
    near_rows, near_residual, noise = make_near(
        inbox, near_next, near_prev, (mid_noise, other_noise)
    )
    foot_f = footprints[0].astype(F32)
    step = 1.0 / (jnp.sum(foot_f * foot_f, axis=1) + norm_eps)
    step_row, up, down, noise = lax.optimization_barrier((step[None], up, down, noise))
    far = exchange(up, down)
    noises = (
        noise,
        lax.ppermute(noise, "plane", plane_up),
        lax.ppermute(noise, "plane", plane_down),
    )
    hots, tables = prepare_traces(
        stripe_row, decay_slow, decay_fast, step_row, frames, slots, capacity
    )
    weights = make_weights(foot_rows, near_rows, noises)
    background, gradient = make_annulus(
        residual, near_residual, mid, far, weights, annulus_gain
    )
    home = lax.all_to_all(gradient, "pix", split_axis=0, concat_axis=0, tiled=True)
    traces_new = make_traces(hots, tables, traces[0], home)
    return (background, traces_new[None])


def solution(mesh):
    placed = (
        P("plane", "pix", None, None),
        P("plane", "pix", None),
        P("plane", "pix", None),
        P("plane", "pix", None),
        P("plane", "pix"),
        P("plane", None),
        P("plane", "pix"),
        P("plane", "pix"),
    )
    return jax.shard_map(
        on_device,
        mesh=mesh,
        in_specs=placed,
        out_specs=(P("plane", "pix", None, None), P("plane", "pix", None)),
        check_vma=False,
    )
```
